32 devices in a mesh: gx: 8 (over z, y), gy: 4 (over x, core).
Axes of the slice: x: 2, y: 2, z: 4, core: 2. Of those that a mesh axis runs over, the one named last changes fastest.
Arguments:
- head_old: float32 [10, 128, 2048], P(None, 'gx', 'gy'), may hold values from -4 to 4
- soil_type: int32 [10, 128, 2048], P(None, 'gx', 'gy'), may hold values from 0 to 11
- soil_table: float32 [3, 12], replicated, may hold values from 0.2 to 3, as said below
- forcing: float32 [4, 128, 2048], P(None, 'gx', 'gy'), may hold values from 0 to 2, as said below
- canopy: float32 [13, 65536], P(None, ('gx', 'gy')), may hold values from 0.05 to 6, as said below
- column_slot: int32 [128, 2048], P('gx', 'gy'), may hold values from -1 to 2047, as said below
Outputs:
- head_new: float32 [10, 128, 2048], P(None, 'gx', 'gy')
- surface_flux: float32 [2, 128, 2048], P(None, 'gx', 'gy')
The draws below stay inside these ranges and needn't reach their ends.
Inputs may be any that keep to these rules, and one draw needn't show every extreme that they name: `soil_table`: Rows: conductivity 0.2 to 2, steepness 0.5 to 3, capacity 0.2 to 0.5. `forcing`: Rows: sunlight 0.5 to 2, air temperature 0.8 to 1.2, humidity 0 to 0.5, rainfall 0.1 to 2. `canopy`: Rows: leaf area 0.5 to 6, albedo 0.1 to 0.3, resistance 0.2 to 5, root weights 0.05 to 1. `column_slot`: the land cells of one device's tile name distinct values; the value v sends the column to the device of index v // 64 along gx+gy into slot v % 64; in every draw some device uses every value.
All inputs are finite; a program needn't handle non-finite values.
Results may differ from the reference program's by a relative error of at most 0.00029.
Values sent between devices are 32-bit elements; how exact they have to be, the bound alone decides.
No kernel may reach another device: no remote copies, remote signals or barrier semaphores. Data moves between devices by JAX's collectives and lax.ppermute only.
A program may use at most 64 MiB of HBM per device.

```python
import math
import jax
import jax.numpy as jnp
from jax import lax

NZ = 10
CX = 16
CY = 512
CAP = 64
NSOIL = 12
NEWTON = 2
KRYLOV = 3
NX = 128
NY = 2048
SLOTS = 2048
COLS = 65536


def ranged(key, shape, lower, upper, logscale):
    unit = jax.random.uniform(key, shape, jnp.float32)
    if logscale:
        return jnp.exp(math.log(lower) + (math.log(upper) - math.log(lower)) * unit)
    return lower + (upper - lower) * unit


def draw_soil_table(key, part):
    keys = jax.random.split(key, 3)
    conduct = ranged(keys[0], (NSOIL,), 0.2, 2.0, True)
    steep = ranged(keys[1], (NSOIL,), 0.5, 3.0, True)
    capacity = ranged(keys[2], (NSOIL,), 0.2, 0.5, False)
    return jnp.stack([conduct, steep, capacity]).astype(jnp.float32)


def draw_forcing(key, part):
    keys = jax.random.split(key, 4)
    sunlight = ranged(keys[0], (NX, NY), 0.5, 2.0, False)
    air_temp = ranged(keys[1], (NX, NY), 0.8, 1.2, False)
    humidity = ranged(keys[2], (NX, NY), 0.0, 0.5, False)
    rainfall = ranged(keys[3], (NX, NY), 0.1, 2.0, True)
    return jnp.stack([sunlight, air_temp, humidity, rainfall]).astype(jnp.float32)


def draw_canopy(key, part):
    keys = jax.random.split(key, 4)
    leaf_area = ranged(keys[0], (1, COLS), 0.5, 6.0, True)
    albedo = ranged(keys[1], (1, COLS), 0.1, 0.3, False)
    resist = ranged(keys[2], (1, COLS), 0.2, 5.0, True)
    roots = ranged(keys[3], (NZ, COLS), 0.05, 1.0, True)
    return jnp.concatenate([leaf_area, albedo, resist, roots], axis=0).astype(jnp.float32)


def draw_column_slot(key, part):
    grid_x = NX // CX
    grid_y = NY // CY
    devices = grid_x * grid_y
    top = CX * CY
    keys = jax.random.split(key, 5)
    level = jax.random.randint(keys[0], (devices,), 2, 11)
    forced = jax.random.randint(keys[1], (), 0, devices)
    level = jnp.where(jnp.arange(devices) == forced, 10, level)
    chance = jax.random.randint(keys[2], (devices, top), 0, 10)
    candidate = chance < level[:, None]
    order = jax.vmap(lambda sub_key: jax.random.permutation(sub_key, top))(jax.random.split(keys[3], devices))
    shuffled = jax.vmap(lambda sub_key: jax.random.permutation(sub_key, SLOTS))(jax.random.split(keys[4], devices))
    ordered = jnp.take_along_axis(candidate, order, axis=1)
    rank = jnp.cumsum(ordered.astype(jnp.int32), axis=1) - 1
    kept = ordered & (rank < SLOTS)
    chosen = jnp.take_along_axis(shuffled, jnp.clip(rank, 0, SLOTS - 1), axis=1)
    values = jnp.where(kept, chosen, -1).astype(jnp.int32)
    placed = jax.vmap(lambda positions, entries: jnp.zeros((top,), jnp.int32).at[positions].set(entries))(order, values)
    return placed.reshape(grid_x, grid_y, CX, CY).transpose(0, 2, 1, 3).reshape(NX, NY).astype(jnp.int32)


def set_ends(result, stream_key, low, top_value):
    shape = result.shape
    spot = [jax.random.randint(jax.random.fold_in(stream_key, axis), (), 0, shape[axis]) for axis in range(len(shape))]
    result = result.at[tuple(spot)].set(low)
    longest = shape.index(max(shape))
    spot[longest] = (spot[longest] + 1) % shape[longest]
    return result.at[tuple(spot)].set(top_value)


def block_scale(own_key, extent, cuts, low, high):
    def one(dim, blocks):
        draws = jax.random.uniform(jax.random.fold_in(jax.random.fold_in(own_key, 6), dim), (blocks,), jnp.float32, low / len(cuts), high / len(cuts))
        return jnp.repeat(jnp.exp(draws), extent[dim] // blocks).reshape((-1,) + (1,) * (len(extent) - dim - 1))

    factor_of = one(*cuts[0])
    for cut in cuts[1:]:
        factor_of = factor_of * one(*cut)
    return factor_of


def scatter_about(rng, dims, width, reach, pieces=(), held_as=jnp.bfloat16):
    gain = block_scale(rng, dims, pieces, -0.22, 0.18) if pieces else 1.0
    drawn = jax.random.normal(rng, dims, jnp.float32) * width * gain
    return jnp.minimum(jnp.maximum(drawn, -reach), reach).astype(held_as)


def setup_inputs(seed: int = 0) -> dict:
    splits = jax.random.split(jax.random.key(seed), 7)
    return {
        "head_old": scatter_about(splits[0], (NZ, NX, NY), 1.0, 4.0, ((1, 8), (2, 4)), jnp.float32),
        "soil_type": set_ends(jax.random.randint(splits[1], (NZ, NX, NY), 0, NSOIL), jax.random.fold_in(splits[1], 1), 0, NSOIL - 1).astype(jnp.int32),
        "soil_table": draw_soil_table(jax.random.fold_in(splits[6], 71), 0),
        "forcing": draw_forcing(jax.random.fold_in(splits[6], 71), 0),
        "canopy": draw_canopy(jax.random.fold_in(splits[6], 71), 0),
        "column_slot": draw_column_slot(jax.random.fold_in(splits[6], 71), 0),
    }


storage_weight = 4.0
norm_epsilon = 1e-06

def soil_fields(soil_type, soil_table):
    conduct = jnp.zeros(soil_type.shape, jnp.float32)
    steep = jnp.zeros(soil_type.shape, jnp.float32)
    capacity = jnp.zeros(soil_type.shape, jnp.float32)
    for kind in range(soil_table.shape[1]):
        match = soil_type == kind
        conduct = jnp.where(match, soil_table[0, kind], conduct)
        steep = jnp.where(match, soil_table[1, kind], steep)
        capacity = jnp.where(match, soil_table[2, kind], capacity)
    return jnp.stack([conduct, steep, capacity])

def balance(padded, params, theta_old, source):
    sat = jax.nn.sigmoid(params[1] * padded)
    conduct = params[0] * (0.1 + 0.9 * sat * sat)
    head = padded[:, 1:-1, 1:-1]
    inner = conduct[:, 1:-1, 1:-1]
    theta = params[2][:, 1:-1, 1:-1] * sat[:, 1:-1, 1:-1]
    lateral = jnp.zeros_like(head)
    for near_head, near_cond in ((padded[:, 2:, 1:-1], conduct[:, 2:, 1:-1]), (padded[:, :-2, 1:-1], conduct[:, :-2, 1:-1]), (padded[:, 1:-1, 2:], conduct[:, 1:-1, 2:]), (padded[:, 1:-1, :-2], conduct[:, 1:-1, :-2])):
        lateral = lateral + 0.5 * (inner + near_cond) * (head - near_head)
    face = 0.5 * (inner[:-1] + inner[1:]) * (head[:-1] - head[1:] + 1.0)
    below = jnp.concatenate([face, inner[-1:]], axis=0)
    above = jnp.concatenate([jnp.zeros_like(head[:1]), face], axis=0)
    return storage_weight * (theta - theta_old) + lateral + below - above - source

def land_column(wet, ks_top, forcing, records):
    sunlight, air_temp, humidity, rainfall = (forcing[0], forcing[1], forcing[2], forcing[3])
    leaf_area, albedo, resist = (records[0], records[1], records[2])
    roots = records[3:]
    uptake = roots * wet
    total = lax.optimization_barrier(jnp.sum(uptake, axis=0))
    wetness = total / lax.optimization_barrier(jnp.sum(roots, axis=0))
    conductance = wetness * leaf_area / (leaf_area + resist)
    exchange_coef = 0.5 + 0.3 * leaf_area
    radiation = (1.0 - albedo) * sunlight + 0.3
    surface = air_temp
    for sweep_index in range(2):
        vapour = 0.5 * jnp.exp(2.0 * (surface - air_temp))
        square = surface * surface
        excess = radiation - 0.3 * square * square - exchange_coef * (surface - air_temp) - conductance * (vapour - humidity)
        slope = -1.2 * square * surface - exchange_coef - 2.0 * conductance * vapour
        surface = surface - excess / slope
    vapour = 0.5 * jnp.exp(2.0 * (surface - air_temp))
    evaporation = conductance * (vapour - humidity)
    infiltration = rainfall * ks_top / (rainfall + ks_top)
    sink = evaporation * uptake / total
    return (sink, evaporation, infiltration)

def surface_terms(land, sink, evaporation, infiltration):
    source = jnp.where(land, -sink, 0.0)
    source = source.at[0].add(jnp.where(land, infiltration, 0.0))
    flux = jnp.stack([jnp.where(land, evaporation, 0.0), jnp.where(land, infiltration, 0.0)])
    return (source, flux)

def small_solve(hessen, initial_norm):
    gram = jnp.dot(hessen.T, hessen, precision=lax.Precision.HIGHEST)
    target = hessen[0] * initial_norm
    factor = jnp.linalg.cholesky(gram)
    size = gram.shape[0]
    forward = []
    for row in range(size):
        value = target[row]
        for other in range(row):
            value = value - factor[row, other] * forward[other]
        forward.append(value / factor[row, row])
    backward = [None] * size
    for row in reversed(range(size)):
        value = forward[row]
        for other in range(row + 1, size):
            value = value - factor[other, row] * backward[other]
        backward[row] = value / factor[row, row]
    return jnp.stack(backward)

def pad_cells(field):
    return jnp.pad(field, ((0, 0), (1, 1), (1, 1)))

def reference(head_old, soil_type, soil_table, forcing, canopy, column_slot):
    params = soil_fields(soil_type, soil_table)
    wet = jax.nn.sigmoid(params[1] * head_old)
    theta_old = params[2] * wet
    land = column_slot >= 0
    slot = jnp.maximum(column_slot, 0)
    device = (jnp.arange(NX, dtype=jnp.int32) // CX)[:, None] * (NY // CY) + (jnp.arange(NY, dtype=jnp.int32) // CY)[None, :]
    record = slot // CAP * SLOTS + device * CAP + slot % CAP
    cell_records = jnp.take(canopy, record.reshape(-1).astype(jnp.int32), axis=1).reshape(-1, NX, NY)
    sink, evaporation, infiltration = land_column(wet, params[0, 0], forcing, cell_records)
    source, surface_flux = surface_terms(land, sink, evaporation, infiltration)
    padded_params = jnp.pad(params, ((0, 0), (0, 0), (1, 1), (1, 1)))
    head = head_old
    for newton_step in range(NEWTON):
        padded = pad_cells(head)

        def residual_of(field):
            return balance(field, padded_params, theta_old, source)
        residual_now = residual_of(padded)
        initial_norm = jnp.sqrt(jnp.sum(residual_now * residual_now) + norm_epsilon)
        basis = [residual_now / initial_norm]
        hessen = jnp.zeros((KRYLOV + 1, KRYLOV), jnp.float32)
        for krylov_step in range(KRYLOV):
            direction = jax.jvp(residual_of, (padded,), (pad_cells(basis[krylov_step]),))[1]
            for index, earlier in enumerate(basis):
                product = jnp.sum(direction * earlier)
                direction = direction - product * earlier
                hessen = hessen.at[index, krylov_step].set(product)
            length = jnp.sqrt(jnp.sum(direction * direction) + norm_epsilon)
            hessen = hessen.at[krylov_step + 1, krylov_step].set(length)
            if krylov_step + 1 < KRYLOV:
                basis.append(direction / length)
        weights = small_solve(hessen, initial_norm)
        for index, earlier in enumerate(basis):
            head = head - weights[index] * earlier
    return (head, surface_flux)
```

```python
import functools

import jax
import jax.numpy as jnp
from jax import lax
from jax.experimental import pallas as pl
from jax.experimental.pallas import tpu as pltpu
from jax.sharding import PartitionSpec as P

NEWTON = 2
KRYLOV = 3
HALO = 8
LANES = 128
SLOT = 64

storage_weight = 4.0
norm_epsilon = 1e-06

VMEM_LIMIT = 40 * 1024 * 1024
PAIRS = [(i, j) for i in range(KRYLOV + 1) for j in range(i, KRYLOV + 1)]
HALF = (len(PAIRS) + 1) // 2

f32 = jnp.float32
vmem = pl.BlockSpec(memory_space=pltpu.VMEM)
smem = pl.BlockSpec(memory_space=pltpu.SMEM)


def call(body, outs, n_in, scratch=(), in_specs=None, flops=1000000):
    return pl.pallas_call(
        body,
        out_shape=[jax.ShapeDtypeStruct(s, d) for s, d in outs],
        in_specs=in_specs or [vmem] * n_in,
        out_specs=[vmem] * len(outs),
        scratch_shapes=list(scratch),
        compiler_params=pltpu.CompilerParams(vmem_limit_bytes=VMEM_LIMIT),
        cost_estimate=pl.CostEstimate(flops=flops, bytes_accessed=1000000, transcendentals=0),
    )


def lane_iota(shape):
    return lax.broadcasted_iota(jnp.int32, shape, len(shape) - 1)


def pack_canopy(canopy_ref, out_ref):
    rows = canopy_ref.shape[0]
    tiles = canopy_ref.shape[1] // LANES
    low = lane_iota((8, LANES)) < SLOT

    def step(t, _):
        here = pl.ds(pl.multiple_of(t * LANES, LANES), LANES)
        first = canopy_ref[0:8, here]
        rest = canopy_ref[8:rows, here]
        rest = jnp.concatenate([rest, jnp.zeros((16 - rows, LANES), f32)], axis=0)
        out_ref[2 * t] = jnp.where(low, first, pltpu.roll(rest, SLOT, 1))
        out_ref[2 * t + 1] = jnp.where(low, pltpu.roll(first, SLOT, 1), rest)
        return 0

    lax.fori_loop(0, tiles, step, 0)


def pack_kernel(canopy_ref, head_ref, soil_ref, send_ref, down_ref, up_ref):
    layers, rows, _ = head_ref.shape
    down_ref[0:layers] = head_ref[:, 0:HALO, :]
    up_ref[0:layers] = head_ref[:, rows - HALO : rows, :]
    down_ref[layers : 2 * layers] = (soil_ref[:, 0:HALO, :] + 1).astype(f32)
    up_ref[layers : 2 * layers] = (soil_ref[:, rows - HALO : rows, :] + 1).astype(f32)
    pack_canopy(canopy_ref, send_ref)


def table_rows(table_ref, rows):
    lane = lane_iota((rows, LANES))
    out = []
    for field in range(table_ref.shape[0]):
        row = jnp.zeros((rows, LANES), f32)
        for kind in range(table_ref.shape[1]):
            row = jnp.where(lane == kind + 1, table_ref[field, kind], row)
        out.append(row)
    return out


def lookup(row, index):
    pieces = [
        jnp.take_along_axis(row, index[:, at : at + LANES], axis=1, mode="promise_in_bounds")
        for at in range(0, index.shape[1], LANES)
    ]
    return jnp.concatenate(pieces, axis=1)


def sigmoid(u):
    return 1.0 / (1.0 + jnp.exp(-u))


def source_kernel(
    table_ref, arrived_ref, head_ref, soil_ref, forcing_ref, slot_ref,
    source_ref, down_ref, up_ref, flux_ref, tab_ref,
):
    layers, rows, cols = head_ref.shape
    owners = arrived_ref.shape[0]
    low = lane_iota((8, LANES)) < SLOT
    records = 3 + layers

    def unpack(t, _):
        first = arrived_ref[2 * t]
        second = arrived_ref[2 * t + 1]
        tab_ref[t, 0:8] = jnp.where(low, first, pltpu.roll(second, SLOT, 1))
        tab_ref[t, 8:16] = jnp.where(low, pltpu.roll(first, SLOT, 1), second)
        return 0

    lax.fori_loop(0, owners // 2, unpack, 0)
    tables = table_rows(table_ref, 8)

    for at_x in range(0, rows, 8):
        for at_y in range(0, cols, LANES):
            here = (slice(at_x, at_x + 8), slice(at_y, at_y + LANES))
            slot = slot_ref[here]
            land = slot >= 0
            value = jnp.maximum(slot, 0)
            lane = value & (LANES - 1)
            tile = value >> 7

            def pick(t, held):
                match = tile == t
                out = []
                for k in range(records):
                    row = jnp.broadcast_to(tab_ref[t, k : k + 1, :], (8, LANES))
                    got = jnp.take_along_axis(row, lane, axis=1, mode="promise_in_bounds")
                    out.append(jnp.where(match, got, held[k]))
                return tuple(out)

            picked = lax.fori_loop(
                0, owners // 2, pick, tuple(jnp.ones((8, LANES), f32) for _ in range(records)),
                unroll=4,
            )
            leaf_area, albedo, resist = picked[:3]
            roots = picked[3:]
            uptake = []
            for k in range(layers):
                index = soil_ref[(k,) + here] + 1
                steep = lookup(tables[1], index)
                uptake.append(roots[k] * sigmoid(steep * head_ref[(k,) + here]))
                if k == 0:
                    ks_top = lookup(tables[0], index)
            total = functools.reduce(jnp.add, uptake)
            root_sum = functools.reduce(jnp.add, roots)
            sunlight, air_temp, humidity, rainfall = (forcing_ref[(i,) + here] for i in range(4))
            conductance = total / root_sum * (leaf_area / (leaf_area + resist))
            exchange_coef = 0.5 + 0.3 * leaf_area
            radiation = (1.0 - albedo) * sunlight + 0.3
            surface = air_temp
            for _ in range(2):
                vapour = 0.5 * jnp.exp(2.0 * (surface - air_temp))
                square = surface * surface
                excess = (
                    radiation
                    - 0.3 * square * square
                    - exchange_coef * (surface - air_temp)
                    - conductance * (vapour - humidity)
                )
                slope = -1.2 * square * surface - exchange_coef - 2.0 * conductance * vapour
                surface = surface - excess / slope
            vapour = 0.5 * jnp.exp(2.0 * (surface - air_temp))
            evaporation = conductance * (vapour - humidity)
            infiltration = rainfall * ks_top / (rainfall + ks_top)
            rate = evaporation / total
            evaporation = jnp.where(land, evaporation, 0.0)
            infiltration = jnp.where(land, infiltration, 0.0)
            rate = jnp.where(land, rate, 0.0)
            flux_ref[(0,) + here] = evaporation
            flux_ref[(1,) + here] = infiltration
            for k in range(layers):
                value = -rate * uptake[k]
                if k == 0:
                    value = value + infiltration
                source_ref[(k,) + here] = value
                if at_x < HALO:
                    down_ref[(k,) + here] = value
                if at_x >= rows - HALO:
                    up_ref[(k, slice(at_x - rows + HALO, at_x - rows + HALO + 8), here[1])] = value


def strips(top, above, below, at, shift_from):
    layers = top.shape[0]
    lane = lane_iota((top.shape[1] + 2 * HALO, LANES))
    packed = jnp.zeros(lane.shape, f32)
    for k in range(layers):
        plane = jnp.concatenate([top[k], above[k], below[k]], axis=0)
        shift = (HALO * k - shift_from) % LANES
        moved = pltpu.roll(plane, shift, 1) if shift else plane
        inside = (lane >= HALO * k) & (lane < HALO * (k + 1))
        packed = jnp.where(inside, moved, packed)
    return packed


def strip_kernel(head_ref, soil_ref, lo_ref, hi_ref, src_ref, slo_ref, shi_ref, down_ref, up_ref):
    layers, rows, cols = head_ref.shape
    for out_ref, at, shift_from in ((down_ref, 0, 0), (up_ref, cols - LANES, LANES - HALO)):
        part = slice(at, at + LANES)
        out_ref[0] = strips(
            head_ref[:, :, part], hi_ref[0:layers, :, part], lo_ref[0:layers, :, part], at, shift_from
        )
        out_ref[1] = strips(
            (soil_ref[:, :, part] + 1).astype(f32),
            hi_ref[layers : 2 * layers, :, part],
            lo_ref[layers : 2 * layers, :, part],
            at,
            shift_from,
        )
        out_ref[2] = strips(src_ref[:, :, part], shi_ref[:, :, part], slo_ref[:, :, part], at, shift_from)


def after(x, axis):
    return pltpu.roll(x, x.shape[axis] - 1, axis)


def before(x, axis):
    return pltpu.roll(x, 1, axis)


def krylov(head_ref, base_ref, index_ref, tables, basis, scratch, gram_ref, tile):
    layers = head_ref.shape[0]
    ax_ref, bx_ref, ay_ref, by_ref, az_ref, bz_ref, store_ref, cond_ref, deriv_ref, mask_ref = scratch
    for k in range(layers):
        index = index_ref[k]
        conduct, steep, capacity = (lookup(row, index) for row in tables)
        sat = sigmoid(steep * head_ref[k])
        slope = steep * sat * (1.0 - sat)
        cond_ref[k] = conduct * (0.1 + 0.9 * sat * sat)
        deriv_ref[k] = 0.9 * conduct * sat * slope
        store_ref[k] = storage_weight * capacity * slope
        mask_ref[k] = (index > 0).astype(f32)
        basis[0][k] = storage_weight * capacity * sat - base_ref[k]
    above = None
    for k in range(layers):
        head = head_ref[k]
        cond = cond_ref[k]
        deriv = deriv_ref[k]
        value = basis[0][k]
        for a_ref, b_ref, axis in ((ax_ref, bx_ref, 0), (ay_ref, by_ref, 1)):
            mean = 0.5 * (cond + after(cond, axis))
            drop = head - after(head, axis)
            a_ref[k] = mean + deriv * drop
            b_ref[k] = mean - after(deriv, axis) * drop
            face = mean * drop
            value = value + face - before(face, axis)
        if k + 1 < layers:
            mean = 0.5 * (cond + cond_ref[k + 1])
            drop = head - head_ref[k + 1] + 1.0
            az_ref[k] = mean + deriv * drop
            bz_ref[k] = mean - deriv_ref[k + 1] * drop
            face = mean * drop
        else:
            az_ref[k] = 2.0 * deriv
            face = cond
        value = value + face
        if above is not None:
            value = value - above
        above = face
        basis[0][k] = value * mask_ref[k]
    for j in range(KRYLOV):
        v_ref, w_ref = basis[j], basis[j + 1]
        above = None
        for k in range(layers):
            v = v_ref[k]
            value = store_ref[k] * v
            for a_ref, b_ref, axis in ((ax_ref, bx_ref, 0), (ay_ref, by_ref, 1)):
                face = a_ref[k] * v - b_ref[k] * after(v, axis)
                value = value + face - before(face, axis)
            face = az_ref[k] * v
            if k + 1 < layers:
                face = face - bz_ref[k] * v_ref[k + 1]
            value = value + face
            if above is not None:
                value = value - above
            above = face
            w_ref[k] = value * mask_ref[k]
    rows, cols = tile
    sums = [jnp.zeros((8, LANES), f32) for _ in PAIRS]
    for k in range(layers):
        for at_x in range(0, rows, 8):
            for at_y in range(0, cols, LANES):
                vs = [b[k, at_x : at_x + 8, at_y : at_y + LANES] for b in basis]
                for e, (i, j) in enumerate(PAIRS):
                    sums[e] = sums[e] + vs[i] * vs[j]
    halves = []
    for e in range(2 * HALF):
        row = jnp.sum(sums[e], axis=0, keepdims=True)
        halves.append(row + pltpu.roll(row, SLOT, 1))
    low = lane_iota((1, LANES)) < SLOT
    lines = [jnp.where(low, halves[e], halves[e + HALF]) for e in range(HALF)]
    block = jnp.concatenate(lines + [jnp.zeros((8 - HALF, LANES), f32)], axis=0)
    for d in range(gram_ref.shape[0]):
        gram_ref[d] = block


def solve(gram_ref):
    total = gram_ref[0]
    for d in range(1, gram_ref.shape[0]):
        total = total + gram_ref[d]
    low = lane_iota((8, LANES)) < SLOT
    scale = 1.0 / (LANES // SLOT)
    first = jnp.sum(jnp.where(low, total, 0.0), axis=1, keepdims=True)
    second = jnp.sum(jnp.where(low, 0.0, total), axis=1, keepdims=True)
    gram = {}
    for e, (i, j) in enumerate(PAIRS):
        part = first if e < HALF else second
        gram[i, j] = gram[j, i] = part[e % HALF : e % HALF + 1, :]

    def times_gram(c):
        out = []
        for i in range(KRYLOV + 1):
            out.append(functools.reduce(jnp.add, [gram[i, m] * c[m] for m in range(len(c))]))
        return out

    def dot(a, b):
        return functools.reduce(jnp.add, [x * y for x, y in zip(a, b)])

    beta = jnp.sqrt(gram[0, 0] + norm_epsilon)
    basis = [[1.0 / beta]]
    images = [times_gram(basis[0])]
    hessen = {}
    for j in range(KRYLOV):
        w = [jnp.zeros_like(beta)] + basis[j]
        for i in range(j + 1):
            product = dot(w, images[i])
            hessen[i, j] = product
            w = [w[m] - product * basis[i][m] if m < len(basis[i]) else w[m] for m in range(len(w))]
        square = jnp.maximum(dot(w, times_gram(w)), 0.0)
        length = jnp.sqrt(square + norm_epsilon)
        hessen[j + 1, j] = length
        if j + 1 < KRYLOV:
            inverse = 1.0 / length
            basis.append([x * inverse for x in w])
            images.append(times_gram(basis[-1]))
    n = KRYLOV
    normal = {}
    for a in range(n):
        for b in range(a + 1):
            normal[a, b] = functools.reduce(
                jnp.add,
                [hessen[i, a] * hessen[i, b] for i in range(n + 1) if (i, a) in hessen and (i, b) in hessen],
            )
    factor = {}
    inverse = []
    for a in range(n):
        for b in range(a + 1):
            value = normal[a, b]
            for m in range(b):
                value = value - factor[a, m] * factor[b, m]
            if a == b:
                inverse.append(lax.rsqrt(value))
            else:
                factor[a, b] = value * inverse[b]
    forward = []
    for a in range(n):
        value = hessen[0, a] * beta
        for m in range(a):
            value = value - factor[a, m] * forward[m]
        forward.append(value * inverse[a])
    backward = [None] * n
    for a in reversed(range(n)):
        value = forward[a]
        for m in range(a + 1, n):
            value = value - factor[m, a] * backward[m]
        backward[a] = value * inverse[a]
    return [
        functools.reduce(jnp.add, [backward[j] * basis[j][i] for j in range(i, n)]) for i in range(n)
    ]


def first_kernel(
    table_ref, head_ref, soil_ref, lo_ref, hi_ref, src_ref, slo_ref, shi_ref, ylo_ref, yhi_ref,
    ext_ref, index_ref, base_ref, p0_ref, p1_ref, p2_ref, gram_ref, p3_ref, *scratch,
):
    layers, rows, cols = head_ref.shape
    tall = rows + 2 * HALO
    tables = table_rows(table_ref, tall)
    lane = lane_iota((tall, LANES))

    def side(field, k):
        right = yhi_ref[field]
        left = ylo_ref[field]
        shift = (-HALO * k) % LANES
        right = pltpu.roll(right, shift, 1) if shift else right
        left = pltpu.roll(left, (LANES - HALO - HALO * k) % LANES, 1)
        return jnp.where(lane < HALO, right, jnp.where(lane >= LANES - HALO, left, 0.0))

    for k in range(layers):
        ext_ref[k, 0:rows, 0:cols] = head_ref[k]
        ext_ref[k, rows : rows + HALO, 0:cols] = hi_ref[k]
        ext_ref[k, rows + HALO : tall, 0:cols] = lo_ref[k]
        ext_ref[k, :, cols : cols + LANES] = side(0, k)
        index_ref[k, 0:rows, 0:cols] = soil_ref[k] + 1
        index_ref[k, rows : rows + HALO, 0:cols] = hi_ref[layers + k].astype(jnp.int32)
        index_ref[k, rows + HALO : tall, 0:cols] = lo_ref[layers + k].astype(jnp.int32)
        index_ref[k, :, cols : cols + LANES] = side(1, k).astype(jnp.int32)
        base_ref[k, 0:rows, 0:cols] = src_ref[k]
        base_ref[k, rows : rows + HALO, 0:cols] = shi_ref[k]
        base_ref[k, rows + HALO : tall, 0:cols] = slo_ref[k]
        base_ref[k, :, cols : cols + LANES] = side(2, k)
    for k in range(layers):
        index = index_ref[k]
        steep = lookup(tables[1], index)
        capacity = lookup(tables[2], index)
        theta_old = capacity * sigmoid(steep * ext_ref[k])
        base_ref[k] = base_ref[k] + storage_weight * theta_old
    krylov(
        ext_ref, base_ref, index_ref, tables, (p0_ref, p1_ref, p2_ref, p3_ref), scratch, gram_ref,
        (rows, cols),
    )


def second_kernel(
    table_ref, sums_ref, old_ref, index_ref, base_ref, q0_ref, q1_ref, q2_ref,
    part_ref, p0_ref, p1_ref, p2_ref, gram_ref, ext_ref, p3_ref, *scratch,
):
    layers, tall, wide = old_ref.shape
    rows, cols = part_ref.shape[1:]
    tables = table_rows(table_ref, tall)
    x = solve(sums_ref)
    for k in range(layers):
        ext_ref[k] = old_ref[k] - x[0] * q0_ref[k] - x[1] * q1_ref[k] - x[2] * q2_ref[k]
        part_ref[k] = ext_ref[k, 0:rows, 0:cols]
    krylov(
        ext_ref, base_ref, index_ref, tables, (p0_ref, p1_ref, p2_ref, p3_ref), scratch, gram_ref,
        (rows, cols),
    )


def last_kernel(sums_ref, part_ref, q0_ref, q1_ref, q2_ref, head_ref):
    layers, rows, cols = part_ref.shape
    x = solve(sums_ref)
    for k in range(layers):
        own = (k, slice(0, rows), slice(0, cols))
        head_ref[k] = part_ref[k] - x[0] * q0_ref[own] - x[1] * q1_ref[own] - x[2] * q2_ref[own]


def shards(head_old, soil_type, soil_table, forcing, canopy, column_slot):
    layers, rows, cols = head_old.shape
    both = ("gx", "gy")
    devices = lax.axis_size("gx") * lax.axis_size("gy")
    block = (devices, 8, LANES)

    def exchange(to_lower, to_upper, axis):
        size = lax.axis_size(axis)
        up = [(i, i + 1) for i in range(size - 1)]
        down = [(j, i) for i, j in up]
        return lax.ppermute(to_upper, axis, up), lax.ppermute(to_lower, axis, down)

    def spread(x):
        return lax.all_to_all(x, both, split_axis=0, concat_axis=0, tiled=True)

    send, down, up = call(
        pack_kernel,
        [(block, f32), ((2 * layers, HALO, cols), f32), ((2 * layers, HALO, cols), f32)],
        3,
    )(canopy, head_old, soil_type)
    arrived = spread(send)
    lo, hi = exchange(down, up, "gx")
    edge = ((layers, HALO, cols), f32)
    source, sdown, sup, flux = call(
        source_kernel,
        [((layers, rows, cols), f32), edge, edge, ((2, rows, cols), f32)],
        6,
        scratch=[pltpu.VMEM((devices // 2, 16, LANES), f32)],
        in_specs=[smem] + [vmem] * 5,
    )(soil_table, arrived, head_old, soil_type, forcing, column_slot)
    slo, shi = exchange(sdown, sup, "gx")
    tall = rows + 2 * HALO
    wide = cols + LANES
    ydown, yup = call(strip_kernel, [((3, tall, LANES), f32)] * 2, 7)(
        head_old, soil_type, lo, hi, source, slo, shi
    )
    ylo, yhi = exchange(ydown, yup, "gy")
    ext = ((layers, tall, wide), f32)
    held = [pltpu.VMEM((layers, tall, wide), f32)]
    old, index, base, p0, p1, p2, gram = call(
        first_kernel,
        [ext, ((layers, tall, wide), jnp.int32), ext, ext, ext, ext, (block, f32)],
        10,
        scratch=held * 11,
        in_specs=[smem] + [vmem] * 9,
    )(soil_table, head_old, soil_type, lo, hi, source, slo, shi, ylo, yhi)
    sums = spread(gram)
    part, q0, q1, q2, gram = call(
        second_kernel,
        [((layers, rows, cols), f32), ext, ext, ext, (block, f32)],
        8,
        scratch=held * 12,
        in_specs=[smem] + [vmem] * 7,
    )(soil_table, sums, old, index, base, p0, p1, p2)
    sums = spread(gram)
    (head,) = call(last_kernel, [((layers, rows, cols), f32)], 5)(sums, part, q0, q1, q2)
    return head, flux


def solution(mesh):
    return jax.shard_map(
        shards,
        mesh=mesh,
        in_specs=(
            P(None, "gx", "gy"),
            P(None, "gx", "gy"),
            P(),
            P(None, "gx", "gy"),
            P(None, ("gx", "gy")),
            P("gx", "gy"),
        ),
        out_specs=(P(None, "gx", "gy"), P(None, "gx", "gy")),
        check_vma=False,
    )
```

```python
import functools

import jax
import jax.numpy as jnp
from jax import lax
from jax.experimental import pallas as pl
from jax.experimental.pallas import tpu as pltpu
from jax.sharding import PartitionSpec as P

NEWTON = 2
KRYLOV = 3
HALO = 8
LANES = 128
SLOT = 64

storage_weight = 4.0
norm_epsilon = 1e-06

VMEM_LIMIT = 40 * 1024 * 1024
PAIRS = [(i, j) for i in range(KRYLOV + 1) for j in range(i, KRYLOV + 1)]

f32 = jnp.float32
vmem = pl.BlockSpec(memory_space=pltpu.VMEM)
smem = pl.BlockSpec(memory_space=pltpu.SMEM)


def call(body, outs, n_in, scratch=(), in_specs=None, flops=1000000):
    return pl.pallas_call(
        body,
        out_shape=[jax.ShapeDtypeStruct(s, d) for s, d in outs],
        in_specs=in_specs or [vmem] * n_in,
        out_specs=[vmem] * len(outs),
        scratch_shapes=list(scratch),
        compiler_params=pltpu.CompilerParams(vmem_limit_bytes=VMEM_LIMIT),
        cost_estimate=pl.CostEstimate(flops=flops, bytes_accessed=1000000, transcendentals=0),
    )


def lane_iota(shape):
    return lax.broadcasted_iota(jnp.int32, shape, len(shape) - 1)


def pack_kernel(canopy_ref, out_ref):
    rows = canopy_ref.shape[0]
    low = lane_iota((8, LANES)) < SLOT

    def step(t, _):
        here = pl.ds(pl.multiple_of(t * LANES, LANES), LANES)
        first = canopy_ref[0:8, here]
        rest = canopy_ref[8:rows, here]
        rest = jnp.concatenate([rest, jnp.zeros((16 - rows, LANES), f32)], axis=0)
        out_ref[2 * t] = jnp.where(low, first, pltpu.roll(rest, SLOT, 1))
        out_ref[2 * t + 1] = jnp.where(low, pltpu.roll(first, SLOT, 1), rest)
        return 0

    lax.fori_loop(0, canopy_ref.shape[1] // LANES, step, 0, unroll=4)


def edge_kernel(head_ref, soil_ref, down_ref, up_ref):
    layers, rows, _ = head_ref.shape
    for out_ref, at in ((down_ref, 0), (up_ref, rows - HALO)):
        for k in range(layers):
            out_ref[k] = head_ref[k, at : at + HALO, :]
            out_ref[layers + k] = (soil_ref[k, at : at + HALO, :] + 1).astype(f32)


def table_rows(table_ref, rows):
    lane = lane_iota((rows, LANES))
    out = []
    for field in range(table_ref.shape[0]):
        row = jnp.zeros((rows, LANES), f32)
        for kind in range(table_ref.shape[1]):
            row = jnp.where(lane == kind + 1, table_ref[field, kind], row)
        out.append(row)
    return out


def lookup(row, index):
    pieces = [
        jnp.take_along_axis(row, index[:, at : at + LANES], axis=1, mode="promise_in_bounds")
        for at in range(0, index.shape[1], LANES)
    ]
    return jnp.concatenate(pieces, axis=1)


def sigmoid(u):
    return 1.0 / (1.0 + jnp.exp(-u))


def source_kernel(
    table_ref, arrived_ref, head_ref, soil_ref, forcing_ref, slot_ref,
    source_ref, down_ref, up_ref, flux_ref, tab_ref,
):
    layers, rows, cols = head_ref.shape
    owners = arrived_ref.shape[0]
    low = lane_iota((8, LANES)) < SLOT
    line = lax.broadcasted_iota(jnp.int32, (16, LANES), 0)
    is_root = (line >= 3) & (line < 3 + layers)

    def unpack(t, _):
        first = arrived_ref[2 * t]
        second = arrived_ref[2 * t + 1]
        both = jnp.concatenate(
            [
                jnp.where(low, first, pltpu.roll(second, SLOT, 1)),
                jnp.where(low, pltpu.roll(first, SLOT, 1), second),
            ],
            axis=0,
        )
        leaf_area, albedo, resist = both[0:1], both[1:2], both[2:3]
        root_sum = jnp.sum(jnp.where(is_root, both, 0.0), axis=0, keepdims=True)
        both = both * (leaf_area / ((leaf_area + resist) * root_sum))
        tab_ref[t, 0] = jnp.broadcast_to(0.5 + 0.3 * leaf_area, (8, LANES))
        tab_ref[t, 1] = jnp.broadcast_to(1.0 - albedo, (8, LANES))
        for k in range(layers):
            tab_ref[t, 2 + k] = jnp.broadcast_to(both[3 + k : 4 + k], (8, LANES))
        return 0

    lax.fori_loop(0, owners // 2, unpack, 0, unroll=4)
    tables = table_rows(table_ref, 8)

    for at_x in range(0, rows, 8):

        def column(j, _):
            here = (slice(at_x, at_x + 8), pl.ds(pl.multiple_of(j * LANES, LANES), LANES))
            slot = slot_ref[here]
            land = slot >= 0
            value = jnp.maximum(slot, 0)
            lane = value & (LANES - 1)
            tile = value >> 7

            def pick(t, held):
                match = tile == t
                return tuple(
                    jnp.where(match, lookup(tab_ref[t, k], lane), held[k]) for k in range(2 + layers)
                )

            start = tuple(jnp.ones((8, LANES), f32) for _ in range(2 + layers))
            exchange_coef, absorbed, *roots = lax.fori_loop(0, owners // 2, pick, start, unroll=8)
            uptake = []
            for k in range(layers):
                index = soil_ref[(k,) + here] + 1
                steep = lookup(tables[1], index)
                uptake.append(roots[k] * sigmoid(steep * head_ref[(k,) + here]))
                if k == 0:
                    ks_top = lookup(tables[0], index)
            conductance = functools.reduce(jnp.add, uptake)
            sunlight, air_temp, humidity, rainfall = (forcing_ref[(i,) + here] for i in range(4))
            radiation = absorbed * sunlight + 0.3
            square = air_temp * air_temp
            excess = radiation - 0.3 * square * square - conductance * (0.5 - humidity)
            slope = -1.2 * square * air_temp - exchange_coef - conductance
            rise = -excess / slope
            surface = air_temp + rise
            vapour = 0.5 * jnp.exp(2.0 * rise)
            square = surface * surface
            excess = (
                radiation
                - 0.3 * square * square
                - exchange_coef * rise
                - conductance * (vapour - humidity)
            )
            slope = -1.2 * square * surface - exchange_coef - 2.0 * conductance * vapour
            rise = rise - excess / slope
            rate = 0.5 * jnp.exp(2.0 * rise) - humidity
            infiltration = rainfall * ks_top / (rainfall + ks_top)
            infiltration = jnp.where(land, infiltration, 0.0)
            rate = jnp.where(land, rate, 0.0)
            flux_ref[(0,) + here] = conductance * rate
            flux_ref[(1,) + here] = infiltration
            for k in range(layers):
                value = -rate * uptake[k]
                if k == 0:
                    value = value + infiltration
                source_ref[(k,) + here] = value
                if at_x < HALO:
                    down_ref[(k, slice(0, 8), here[1])] = value
                if at_x >= rows - HALO:
                    up_ref[(k, slice(0, 8), here[1])] = value
            return 0

        lax.fori_loop(0, cols // LANES, column, 0)


def strips(top, above, below, at, shift_from):
    layers = top.shape[0]
    lane = lane_iota((top.shape[1] + 2 * HALO, LANES))
    packed = jnp.zeros(lane.shape, f32)
    for k in range(layers):
        plane = jnp.concatenate([top[k], above[k], below[k]], axis=0)
        shift = (HALO * k - shift_from) % LANES
        moved = pltpu.roll(plane, shift, 1) if shift else plane
        inside = (lane >= HALO * k) & (lane < HALO * (k + 1))
        packed = jnp.where(inside, moved, packed)
    return packed


def strip_kernel(head_ref, soil_ref, lo_ref, hi_ref, src_ref, slo_ref, shi_ref, down_ref, up_ref):
    layers, rows, cols = head_ref.shape
    for out_ref, at, shift_from in ((down_ref, 0, 0), (up_ref, cols - LANES, LANES - HALO)):
        part = slice(at, at + LANES)
        out_ref[0] = strips(
            head_ref[:, :, part], hi_ref[0:layers, :, part], lo_ref[0:layers, :, part], at, shift_from
        )
        out_ref[1] = strips(
            (soil_ref[:, :, part] + 1).astype(f32),
            hi_ref[layers : 2 * layers, :, part],
            lo_ref[layers : 2 * layers, :, part],
            at,
            shift_from,
        )
        out_ref[2] = strips(src_ref[:, :, part], shi_ref[:, :, part], slo_ref[:, :, part], at, shift_from)


class Field:
    def __init__(self, main, side):
        self.main, self.side = main, side
        self.tiles = main.shape[-1] // LANES + 1

    def place(self, k, j):
        if j == self.tiles - 1:
            return self.side, (k,)
        return self.main, (k, slice(None), slice(j * LANES, (j + 1) * LANES))

    def get(self, k, j):
        ref, at = self.place(k, j)
        return ref[at]

    def set(self, k, j, value):
        ref, at = self.place(k, j)
        ref[at] = value


def after_x(x):
    return pltpu.roll(x, x.shape[0] - 1, 0)


def before_x(x):
    return pltpu.roll(x, 1, 0)


def up_one(x):
    return pltpu.roll(x, LANES - 1, 1)


def down_one(x):
    return pltpu.roll(x, 1, 1)


def pointwise(head, conduct, steep, capacity):
    sat = 0.5 + 0.5 * jnp.tanh(0.5 * (steep * head))
    slope = steep * sat * (1.0 - sat)
    cond = conduct * (0.1 + 0.9 * sat * sat)
    deriv = 0.9 * conduct * sat * slope
    weighted = storage_weight * capacity
    return cond, deriv, weighted * slope, weighted * sat


def krylov(head, water, base, cond, deriv, store, mask, basis, faces, zface, gram_ref, tile):
    layers = head.main.shape[0]
    rows, _ = tile
    tiles = head.tiles
    order = [tiles - 1] + list(range(tiles - 1))
    tall = head.main.shape[1]
    lane = lane_iota((tall, LANES))
    is_first, is_last = lane == 0, lane == LANES - 1
    (ax, bx), (ay, by), (az, bz) = faces

    def masked(value, j):
        edge = mask.get(0, j)
        if j == tiles - 1:
            return value * edge
        return jnp.concatenate([value[:rows], value[rows:] * edge[rows:]], axis=0)

    def sweep(read, flux, finish, k, last, own=False):
        rolled = {}
        pending = None
        previous = None
        wrapped = {}

        def shifted(j):
            if j not in wrapped:
                wrapped[j] = [up_one(x) for x in read(k, j)]
            return wrapped[j]

        for j in order:
            here = read(k, j)
            ahead = [
                jnp.where(is_last, b, a)
                for a, b in zip(shifted(j), shifted((j + 1) % tiles))
            ]
            face_y = flux(1, k, j, here, ahead)
            moved = down_one(face_y)
            if own and j == tiles - 1:
                previous = moved
                continue
            face_x = flux(0, k, j, here, [after_x(x) for x in here])
            value = face_x - before_x(face_x) + face_y
            below = flux(2, k, j, here, None if last else read(k + 1, j))
            value = value + (below - zface.get(0, j))
            zface.set(0, j, below)
            if previous is None:
                pending = (value, moved)
            else:
                finish(k, j, value - jnp.where(is_first, previous, moved))
            previous = moved
        if pending is not None:
            value, moved = pending
            finish(k, tiles - 1, value - jnp.where(is_first, previous, moved))

    def run(read, flux, finish, own=False):
        for j in range(tiles):
            zface.set(0, j, jnp.zeros((tall, LANES), f32))

        def step(k, _):
            sweep(read, flux, finish, k, False, own)
            return 0

        lax.fori_loop(0, layers - 1, step, 0)
        sweep(read, flux, finish, layers - 1, True, own)

    def read_state(k, j):
        return [head.get(k, j), cond.get(k, j), deriv.get(k, j)]

    def flux_state(axis, k, j, here, ahead):
        if ahead is None:
            az.set(k, j, 2.0 * here[2])
            return here[1]
        mean = 0.5 * (here[1] + ahead[1])
        drop = here[0] - ahead[0]
        if axis == 2:
            drop = drop + 1.0
        a, b = faces[axis]
        a.set(k, j, mean + here[2] * drop)
        b.set(k, j, mean - ahead[2] * drop)
        return mean * drop

    def finish_state(k, j, value):
        basis[0].set(k, j, masked(value + (water.get(k, j) - base.get(k, j)), j))

    run(read_state, flux_state, finish_state)

    def flux_of(axis, k, j, here, ahead):
        a, b = faces[axis]
        face = a.get(k, j) * here[0]
        if ahead is None:
            return face
        return face - b.get(k, j) * ahead[0]

    for step in range(KRYLOV - 1):

        def read_vector(k, j):
            return [basis[step].get(k, j)]

        def finish_vector(k, j, value):
            basis[step + 1].set(k, j, masked(value + store.get(k, j) * basis[step].get(k, j), j))

        run(read_vector, flux_of, finish_vector)

    for e in range(len(PAIRS)):
        gram_ref[e] = jnp.zeros((8, LANES), f32)

    def read_last(k, j):
        return [basis[-1].get(k, j)]

    def finish_last(k, j, value):
        value = value + store.get(k, j) * basis[-1].get(k, j)
        tops = [b.get(k, j) for b in basis] + [value]
        for e, (a, b) in enumerate(PAIRS):
            total = gram_ref[e]
            for at in range(0, rows, 8):
                total = total + tops[a][at : at + 8] * tops[b][at : at + 8]
            gram_ref[e] = total

    run(read_last, flux_of, finish_last, own=True)


def emit_gram(sums_ref, out_ref):
    lines = [jnp.sum(sums_ref[e], axis=0, keepdims=True) for e in range(len(PAIRS))]
    lines.append(jnp.zeros((16 - len(PAIRS), LANES), f32))
    block = jnp.sum(jnp.concatenate(lines, axis=0), axis=1, keepdims=True)
    line = lax.broadcasted_iota(jnp.int32, (16, LANES), 0)
    flat = jnp.sum(jnp.where(lane_iota((16, LANES)) == line, block, 0.0), axis=0, keepdims=True)
    for d in range(out_ref.shape[0]):
        out_ref[d] = flat


def solve(gram_ref):
    total = gram_ref[0]
    for d in range(1, gram_ref.shape[0]):
        total = total + gram_ref[d]
    line = lax.broadcasted_iota(jnp.int32, (16, LANES), 0)
    spread = jnp.broadcast_to(total, (16, LANES))
    column = jnp.sum(jnp.where(lane_iota((16, LANES)) == line, spread, 0.0), axis=1, keepdims=True)
    gram = {}
    for e, (i, j) in enumerate(PAIRS):
        gram[i, j] = gram[j, i] = column[e : e + 1, :]

    def times_gram(c):
        out = []
        for i in range(KRYLOV + 1):
            out.append(functools.reduce(jnp.add, [gram[i, m] * c[m] for m in range(len(c))]))
        return out

    def dot(a, b):
        return functools.reduce(jnp.add, [x * y for x, y in zip(a, b)])

    beta = jnp.sqrt(gram[0, 0] + norm_epsilon)
    basis = [[1.0 / beta]]
    images = [times_gram(basis[0])]
    hessen = {}
    for j in range(KRYLOV):
        w = [jnp.zeros_like(beta)] + basis[j]
        for i in range(j + 1):
            product = dot(w, images[i])
            hessen[i, j] = product
            w = [w[m] - product * basis[i][m] if m < len(basis[i]) else w[m] for m in range(len(w))]
        square = jnp.maximum(dot(w, times_gram(w)), 0.0)
        length = jnp.sqrt(square + norm_epsilon)
        hessen[j + 1, j] = length
        if j + 1 < KRYLOV:
            inverse = 1.0 / length
            basis.append([x * inverse for x in w])
            images.append(times_gram(basis[-1]))
    n = KRYLOV
    normal = {}
    for a in range(n):
        for b in range(a + 1):
            normal[a, b] = functools.reduce(
                jnp.add,
                [hessen[i, a] * hessen[i, b] for i in range(n + 1) if (i, a) in hessen and (i, b) in hessen],
            )
    factor = {}
    inverse = []
    for a in range(n):
        for b in range(a + 1):
            value = normal[a, b]
            for m in range(b):
                value = value - factor[a, m] * factor[b, m]
            if a == b:
                inverse.append(lax.rsqrt(value))
            else:
                factor[a, b] = value * inverse[b]
    forward = []
    for a in range(n):
        value = hessen[0, a] * beta
        for m in range(a):
            value = value - factor[a, m] * forward[m]
        forward.append(value * inverse[a])
    backward = [None] * n
    for a in reversed(range(n)):
        value = forward[a]
        for m in range(a + 1, n):
            value = value - factor[m, a] * backward[m]
        backward[a] = value * inverse[a]
    return [
        functools.reduce(jnp.add, [backward[j] * basis[j][i] for j in range(i, n)]) for i in range(n)
    ]


def soil_kernel(
    table_ref, head_ref, soil_ref, lo_ref, hi_ref,
    ext_ref, ks_ref, steep_ref, cap_ref, cond_ref, deriv_ref, store_ref, water_ref,
):
    layers, rows, cols = head_ref.shape
    tall = rows + 2 * HALO
    tables = table_rows(table_ref, 8)

    def step(k, _):
        for at in range(0, tall, 8):
            for lane_at in range(0, cols, LANES):
                part = slice(lane_at, lane_at + LANES)
                if at < rows:
                    head = head_ref[k, at : at + 8, part]
                    index = soil_ref[k, at : at + 8, part] + 1
                else:
                    from_ref = hi_ref if at < rows + HALO else lo_ref
                    row = (at - rows) % HALO
                    head = from_ref[k, row : row + 8, part]
                    index = from_ref[layers + k, row : row + 8, part].astype(jnp.int32)
                conduct, steep, capacity = (lookup(row, index) for row in tables)
                values = (head, conduct, steep, capacity) + pointwise(head, conduct, steep, capacity)
                outs = (ext_ref, ks_ref, steep_ref, cap_ref, cond_ref, deriv_ref, store_ref, water_ref)
                for ref, value in zip(outs, values):
                    ref[k, at : at + 8, part] = value
        return 0

    lax.fori_loop(0, layers, step, 0)


def fields(mains, sides):
    return [Field(m, s) for m, s in zip(mains, sides)]


def newton_scratch(layers, tall, cols):
    main, side = ((layers, tall, cols), (layers, tall, LANES))
    shapes = [main] * 6 + [side] * 6 + [(1, tall, cols)] * 2 + [(1, tall, LANES)] * 2
    return [pltpu.VMEM(s, f32) for s in shapes + [(len(PAIRS), 8, LANES)]]


def split_scratch(refs):
    coefs = fields(refs[0:6], refs[6:12])
    zface, mask = fields(refs[12:14], refs[14:16])
    return [(coefs[0], coefs[1]), (coefs[2], coefs[3]), (coefs[4], coefs[5])], zface, mask, refs[16]


def set_mask(mask, conduct):
    for j in range(mask.tiles):
        mask.set(0, j, (conduct.get(0, j) > 0.0).astype(f32))


def first_kernel(
    table_ref, src_ref, slo_ref, shi_ref, ylo_ref, yhi_ref,
    ext_ref, ks_ref, cond_ref, deriv_ref, store_ref, water_ref,
    ext_side, ks_side, steep_side, cap_side, base_ref, base_side,
    p0_ref, p1_ref, p2_ref, p0_side, p1_side, p2_side, gram_ref,
    cond_side, deriv_side, store_side, water_side, *scratch,
):
    layers, rows, cols = src_ref.shape
    tall = rows + 2 * HALO
    tables = table_rows(table_ref, tall)
    lane = lane_iota((tall, LANES))

    def side(field, k):
        right = yhi_ref[field]
        left = ylo_ref[field]
        shift = (-HALO * k) % LANES
        right = pltpu.roll(right, shift, 1) if shift else right
        left = pltpu.roll(left, (LANES - HALO - HALO * k) % LANES, 1)
        return jnp.where(lane < HALO, right, jnp.where(lane >= LANES - HALO, left, 0.0))

    for k in range(layers):
        head = side(0, k)
        index = side(1, k).astype(jnp.int32)
        conduct, steep, capacity = (lookup(row, index) for row in tables)
        cond, deriv, store, water = pointwise(head, conduct, steep, capacity)
        ext_side[k] = head
        ks_side[k] = conduct
        steep_side[k] = steep
        cap_side[k] = capacity
        cond_side[k] = cond
        deriv_side[k] = deriv
        store_side[k] = store
        water_side[k] = water
        base_side[k] = side(2, k) + water

    def add_source(k, _):
        base_ref[k, 0:rows] = water_ref[k, 0:rows] + src_ref[k]
        base_ref[k, rows : rows + HALO] = water_ref[k, rows : rows + HALO] + shi_ref[k]
        base_ref[k, rows + HALO : tall] = water_ref[k, rows + HALO : tall] + slo_ref[k]
        return 0

    lax.fori_loop(0, layers, add_source, 0)
    faces, zface, mask, sums_ref = split_scratch(scratch)
    set_mask(mask, Field(ks_ref, ks_side))
    krylov(
        Field(ext_ref, ext_side), Field(water_ref, water_side), Field(base_ref, base_side),
        Field(cond_ref, cond_side), Field(deriv_ref, deriv_side), Field(store_ref, store_side),
        mask, fields((p0_ref, p1_ref, p2_ref), (p0_side, p1_side, p2_side)), faces, zface,
        sums_ref, (rows, cols),
    )
    emit_gram(sums_ref, gram_ref)


def second_kernel(
    arrived_ref, old_ref, ks_ref, steep_ref, cap_ref, base_ref, q0_ref, q1_ref, q2_ref,
    old_side, ks_side, steep_side, cap_side, base_side, q0_side, q1_side, q2_side,
    part_ref, p0_ref, p1_ref, p2_ref, gram_ref,
    p0_side, p1_side, p2_side, ext_ref, cond_ref, deriv_ref, store_ref, water_ref,
    ext_side, cond_side, deriv_side, store_side, water_side, *scratch,
):
    layers, tall, _ = old_ref.shape
    rows, cols = part_ref.shape[1:]
    x = [jnp.broadcast_to(value, (8, LANES)) for value in solve(arrived_ref)]

    def update(k, old, ks, steep, cap, base, qs, outs, lanes):
        for at in range(0, tall, 8):
            for lane_at in range(0, lanes, LANES):
                here = (k, slice(at, at + 8), slice(lane_at, lane_at + LANES))
                head = old[here]
                for value, q in zip(x, qs):
                    head = head - value * q[here]
                values = (head,) + pointwise(head, ks[here], steep[here], cap[here])
                for ref, value in zip(outs, values):
                    ref[here] = value
                if at < rows and lanes > LANES:
                    part_ref[here] = head

    def step(k, _):
        update(
            k, old_ref, ks_ref, steep_ref, cap_ref, base_ref, (q0_ref, q1_ref, q2_ref),
            (ext_ref, cond_ref, deriv_ref, store_ref, water_ref), cols,
        )
        update(
            k, old_side, ks_side, steep_side, cap_side, base_side, (q0_side, q1_side, q2_side),
            (ext_side, cond_side, deriv_side, store_side, water_side), LANES,
        )
        return 0

    lax.fori_loop(0, layers, step, 0)
    faces, zface, mask, sums_ref = split_scratch(scratch)
    set_mask(mask, Field(ks_ref, ks_side))
    krylov(
        Field(ext_ref, ext_side), Field(water_ref, water_side), Field(base_ref, base_side),
        Field(cond_ref, cond_side), Field(deriv_ref, deriv_side), Field(store_ref, store_side),
        mask, fields((p0_ref, p1_ref, p2_ref), (p0_side, p1_side, p2_side)), faces, zface,
        sums_ref, (rows, cols),
    )
    emit_gram(sums_ref, gram_ref)


def last_kernel(arrived_ref, part_ref, q0_ref, q1_ref, q2_ref, head_ref):
    layers, rows, cols = part_ref.shape
    x = [jnp.broadcast_to(value, (rows, cols)) for value in solve(arrived_ref)]

    def step(k, _):
        head = part_ref[k]
        for value, q in zip(x, (q0_ref, q1_ref, q2_ref)):
            head = head - value * q[k, 0:rows, :]
        head_ref[k] = head
        return 0

    lax.fori_loop(0, layers, step, 0)


def shards(head_old, soil_type, soil_table, forcing, canopy, column_slot):
    layers, rows, cols = head_old.shape
    both = ("gx", "gy")
    devices = lax.axis_size("gx") * lax.axis_size("gy")
    tall = rows + 2 * HALO
    own, edge = ((layers, rows, cols), f32), ((layers, HALO, cols), f32)
    main, side = ((layers, tall, cols), f32), ((layers, tall, LANES), f32)
    gram_block = ((devices, 1, LANES), f32)

    def exchange(to_lower, to_upper, axis):
        size = lax.axis_size(axis)
        up = [(i, i + 1) for i in range(size - 1)]
        down = [(j, i) for i, j in up]
        return lax.ppermute(to_upper, axis, up), lax.ppermute(to_lower, axis, down)

    def spread(x):
        return lax.all_to_all(x, both, split_axis=0, concat_axis=0, tiled=True)

    (send,) = call(pack_kernel, [((devices, 8, LANES), f32)], 1)(canopy)
    arrived = spread(send)
    down, up = call(edge_kernel, [((2 * layers, HALO, cols), f32)] * 2, 2)(head_old, soil_type)
    lo, hi = exchange(down, up, "gx")
    source, sdown, sup, flux = call(
        source_kernel,
        [own, edge, edge, ((2, rows, cols), f32)],
        6,
        scratch=[pltpu.VMEM((devices // 2, 2 + layers, 8, LANES), f32)],
        in_specs=[smem] + [vmem] * 5,
    )(soil_table, arrived, head_old, soil_type, forcing, column_slot)
    slo, shi = exchange(sdown, sup, "gx")
    ext, ks, steep, cap, cond, deriv, store, water = call(
        soil_kernel, [main] * 8, 5, in_specs=[smem] + [vmem] * 4
    )(soil_table, head_old, soil_type, lo, hi)
    ydown, yup = call(strip_kernel, [((3, tall, LANES), f32)] * 2, 7)(
        head_old, soil_type, lo, hi, source, slo, shi
    )
    ylo, yhi = exchange(ydown, yup, "gy")
    ext_s, ks_s, steep_s, cap_s, base, base_s, p0, p1, p2, p0_s, p1_s, p2_s, gram = call(
        first_kernel,
        [side] * 4 + [main, side] + [main] * 3 + [side] * 3 + [gram_block],
        12,
        scratch=[pltpu.VMEM(side[0], f32)] * 4 + newton_scratch(layers, tall, cols),
        in_specs=[smem] + [vmem] * 11,
    )(soil_table, source, slo, shi, ylo, yhi, ext, ks, cond, deriv, store, water)
    sums = spread(gram)
    part, q0, q1, q2, gram = call(
        second_kernel,
        [own] + [main] * 3 + [gram_block],
        17,
        scratch=[pltpu.VMEM(side[0], f32)] * 3
        + [pltpu.VMEM(main[0], f32)] * 5
        + [pltpu.VMEM(side[0], f32)] * 5
        + newton_scratch(layers, tall, cols),
    )(sums, ext, ks, steep, cap, base, p0, p1, p2, ext_s, ks_s, steep_s, cap_s, base_s, p0_s, p1_s, p2_s)
    sums = spread(gram)
    (head,) = call(last_kernel, [own], 5)(sums, part, q0, q1, q2)
    return head, flux


def solution(mesh):
    return jax.shard_map(
        shards,
        mesh=mesh,
        in_specs=(
            P(None, "gx", "gy"),
            P(None, "gx", "gy"),
            P(),
            P(None, "gx", "gy"),
            P(None, ("gx", "gy")),
            P("gx", "gy"),
        ),
        out_specs=(P(None, "gx", "gy"), P(None, "gx", "gy")),
        check_vma=False,
    )
```

```python
import functools

import jax
import jax.numpy as jnp
from jax import lax
from jax.experimental import pallas as pl
from jax.experimental.pallas import tpu as pltpu
from jax.sharding import PartitionSpec as P

NEWTON = 2
KRYLOV = 3
HALO = 8
SOURCE_DEPTH = 6
LANES = 128
SLOT = 64

storage_weight = 4.0
norm_epsilon = 1e-06

VMEM_LIMIT = 40 * 1024 * 1024
PAIRS = [(i, j) for i in range(KRYLOV + 1) for j in range(i, KRYLOV + 1)]

f32 = jnp.float32
vmem = pl.BlockSpec(memory_space=pltpu.VMEM)
smem = pl.BlockSpec(memory_space=pltpu.SMEM)


def call(body, outs, n_in, scratch=(), in_specs=None, flops=1000000):
    return pl.pallas_call(
        body,
        out_shape=[jax.ShapeDtypeStruct(s, d) for s, d in outs],
        in_specs=in_specs or [vmem] * n_in,
        out_specs=[vmem] * len(outs),
        scratch_shapes=list(scratch),
        compiler_params=pltpu.CompilerParams(vmem_limit_bytes=VMEM_LIMIT),
        cost_estimate=pl.CostEstimate(flops=flops, bytes_accessed=1000000, transcendentals=0),
    )


def lane_iota(shape):
    return lax.broadcasted_iota(jnp.int32, shape, len(shape) - 1)


def pack_kernel(
    canopy_hbm, head_hbm, soil_hbm, send_ref, down_ref, up_ref, canopy_ref, head_ref, soil_ref, sems
):
    copies = [
        pltpu.make_async_copy(head_hbm, head_ref, sems.at[0]),
        pltpu.make_async_copy(soil_hbm, soil_ref, sems.at[1]),
        pltpu.make_async_copy(canopy_hbm, canopy_ref, sems.at[2]),
    ]
    for copy in copies:
        copy.start()
    layers, width, _ = head_ref.shape
    copies[0].wait()
    copies[1].wait()
    for out_ref, at in ((down_ref, 0), (up_ref, width - HALO)):
        for k in range(layers):
            out_ref[k] = head_ref[k, at : at + HALO, :]
            out_ref[layers + k] = (soil_ref[k, at : at + HALO, :] + 1).astype(f32)
    copies[2].wait()
    rows = canopy_ref.shape[0]
    low = lane_iota((8, LANES)) < SLOT
    for t in range(canopy_ref.shape[1] // LANES):
        here = slice(t * LANES, (t + 1) * LANES)
        first = canopy_ref[0:8, here]
        rest = jnp.concatenate([canopy_ref[8:rows, here], jnp.zeros((16 - rows, LANES), f32)], axis=0)
        send_ref[2 * t] = jnp.where(low, first, pltpu.roll(rest, SLOT, 1))
        send_ref[2 * t + 1] = jnp.where(low, pltpu.roll(first, SLOT, 1), rest)


def table_rows(table_ref, rows):
    lane = lane_iota((rows, LANES))
    out = []
    for field in range(table_ref.shape[0]):
        row = jnp.zeros((rows, LANES), f32)
        for kind in range(table_ref.shape[1]):
            row = jnp.where(lane == kind + 1, table_ref[field, kind], row)
        out.append(row)
    return out


def lookup(row, index):
    pieces = [
        jnp.take_along_axis(row, index[:, at : at + LANES], axis=1, mode="promise_in_bounds")
        for at in range(0, index.shape[1], LANES)
    ]
    return jnp.concatenate(pieces, axis=1)


def sigmoid(u):
    return 1.0 / (1.0 + jnp.exp(-u))


def source_kernel(
    table_ref, arrived_ref, head_ref, soil_ref, forcing_ref, slot_ref,
    source_ref, down_ref, up_ref, flux_ref, tab_ref,
):
    layers, rows, cols = head_ref.shape
    owners = arrived_ref.shape[0]
    low = lane_iota((8, LANES)) < SLOT
    line = lax.broadcasted_iota(jnp.int32, (16, LANES), 0)
    is_root = (line >= 3) & (line < 3 + layers)

    def unpack(t, _):
        first = arrived_ref[2 * t]
        second = arrived_ref[2 * t + 1]
        both = jnp.concatenate(
            [
                jnp.where(low, first, pltpu.roll(second, SLOT, 1)),
                jnp.where(low, pltpu.roll(first, SLOT, 1), second),
            ],
            axis=0,
        )
        leaf_area, albedo, resist = both[0:1], both[1:2], both[2:3]
        root_sum = jnp.sum(jnp.where(is_root, both, 0.0), axis=0, keepdims=True)
        both = both * (leaf_area / ((leaf_area + resist) * root_sum))
        tab_ref[t, 0] = jnp.broadcast_to(0.5 + 0.3 * leaf_area, (8, LANES))
        tab_ref[t, 1] = jnp.broadcast_to(1.0 - albedo, (8, LANES))
        for k in range(layers):
            tab_ref[t, 2 + k] = jnp.broadcast_to(both[3 + k : 4 + k], (8, LANES))
        return 0

    lax.fori_loop(0, owners // 2, unpack, 0, unroll=16)
    tables = table_rows(table_ref, 8)

    for at_x in range(0, rows, 8):

        def column(j, _):
            here = (slice(at_x, at_x + 8), pl.ds(pl.multiple_of(j * LANES, LANES), LANES))
            slot = slot_ref[here]
            land = slot >= 0
            value = jnp.maximum(slot, 0)
            lane = value & (LANES - 1)
            tile = value >> 7

            def pick(t, held):
                match = tile == t
                return tuple(
                    jnp.where(match, lookup(tab_ref[t, k], lane), held[k]) for k in range(2 + layers)
                )

            start = tuple(jnp.ones((8, LANES), f32) for _ in range(2 + layers))
            exchange_coef, absorbed, *roots = lax.fori_loop(0, owners // 2, pick, start, unroll=8)
            uptake = []
            for k in range(layers):
                index = soil_ref[(k,) + here] + 1
                steep = lookup(tables[1], index)
                uptake.append(roots[k] * sigmoid(steep * head_ref[(k,) + here]))
                if k == 0:
                    ks_top = lookup(tables[0], index)
            conductance = functools.reduce(jnp.add, uptake)
            sunlight, air_temp, humidity, rainfall = (forcing_ref[(i,) + here] for i in range(4))
            radiation = absorbed * sunlight + 0.3
            square = air_temp * air_temp
            excess = radiation - 0.3 * square * square - conductance * (0.5 - humidity)
            slope = -1.2 * square * air_temp - exchange_coef - conductance
            rise = -excess / slope
            surface = air_temp + rise
            vapour = 0.5 * jnp.exp(2.0 * rise)
            square = surface * surface
            excess = (
                radiation
                - 0.3 * square * square
                - exchange_coef * rise
                - conductance * (vapour - humidity)
            )
            slope = -1.2 * square * surface - exchange_coef - 2.0 * conductance * vapour
            rise = rise - excess / slope
            rate = 0.5 * jnp.exp(2.0 * rise) - humidity
            infiltration = rainfall * ks_top / (rainfall + ks_top)
            infiltration = jnp.where(land, infiltration, 0.0)
            rate = jnp.where(land, rate, 0.0)
            flux_ref[(0,) + here] = conductance * rate
            flux_ref[(1,) + here] = infiltration
            for k in range(layers):
                value = -rate * uptake[k]
                if k == 0:
                    value = value + infiltration
                source_ref[(k,) + here] = value
                edge = slice(SOURCE_DEPTH * k, SOURCE_DEPTH * (k + 1))
                if at_x < HALO:
                    down_ref[edge, here[1]] = value[:SOURCE_DEPTH]
                if at_x >= rows - HALO:
                    up_ref[edge, here[1]] = value[HALO - SOURCE_DEPTH :]
            return 0

        lax.fori_loop(0, cols // LANES, column, 0)


def strips(planes, shift_from):
    packed = None
    for k, plane in enumerate(planes):
        lane = lane_iota(plane.shape)
        shift = (HALO * k - shift_from) % LANES
        moved = pltpu.roll(plane, shift, 1) if shift else plane
        inside = (lane >= HALO * k) & (lane < HALO * (k + 1))
        packed = jnp.where(inside, moved, 0.0 if packed is None else packed)
    return packed


def strip_parts(cols):
    return ((slice(0, LANES), 0), (slice(cols - LANES, cols), LANES - HALO))


def state_strip_kernel(head_ref, soil_ref, lo_ref, hi_ref, down_ref, up_ref):
    layers, _, cols = head_ref.shape
    for out_ref, (part, shift) in zip((down_ref, up_ref), strip_parts(cols)):
        heads, soils = [], []
        for k in range(layers):
            heads.append(
                jnp.concatenate([head_ref[k, :, part], hi_ref[k, :, part], lo_ref[k, :, part]], axis=0)
            )
            soil = (soil_ref[k, :, part] + 1).astype(f32)
            ends = [hi_ref[layers + k, :, part], lo_ref[layers + k, :, part]]
            soils.append(jnp.concatenate([soil] + ends, axis=0))
        out_ref[0] = strips(heads, shift)
        out_ref[1] = strips(soils, shift)


def tall_source(src_ref, slo_ref, shi_ref, k, part):
    edge = slice(SOURCE_DEPTH * k, SOURCE_DEPTH * (k + 1))
    own = src_ref[k, :, part]
    gap = jnp.zeros((2 * (HALO - SOURCE_DEPTH), own.shape[1]), f32)
    return jnp.concatenate([own, shi_ref[edge, part], gap, slo_ref[edge, part]], axis=0)


def source_strip_kernel(src_ref, slo_ref, shi_ref, down_ref, up_ref):
    layers, _, cols = src_ref.shape
    for out_ref, (part, shift) in zip((down_ref, up_ref), strip_parts(cols)):
        out_ref[0] = strips([tall_source(src_ref, slo_ref, shi_ref, k, part) for k in range(layers)], shift)


def side(ylo_ref, yhi_ref, field, k):
    right = yhi_ref[field]
    left = ylo_ref[field]
    lane = lane_iota(right.shape)
    shift = (-HALO * k) % LANES
    right = pltpu.roll(right, shift, 1) if shift else right
    left = pltpu.roll(left, (LANES - HALO - HALO * k) % LANES, 1)
    return jnp.where(lane < HALO, right, jnp.where(lane >= LANES - HALO, left, 0.0))


def after(x, axis):
    return pltpu.roll(x, x.shape[axis] - 1, axis)


def before(x, axis):
    return pltpu.roll(x, 1, axis)


def pointwise(head, conduct, steep, capacity):
    sat = 0.5 + 0.5 * jnp.tanh(0.5 * (steep * head))
    slope = steep * sat * (1.0 - sat)
    cond = conduct * (0.1 + 0.9 * sat * sat)
    deriv = 0.9 * conduct * sat * slope
    weighted = storage_weight * capacity
    return cond, deriv, weighted * slope, weighted * sat


def linearize(head_ref, cond_ref, deriv_ref, store_ref, gain_ref, mask, coefs, out_ref, tile):
    diag_ref, xp_ref, xm_ref, yp_ref, ym_ref, az_ref, bz_ref = coefs
    layers = head_ref.shape[0]
    rows, cols = tile

    def masked(value):
        own = value[:rows, cols:] * mask[:rows, cols:]
        top = jnp.concatenate([value[:rows, :cols], own], axis=1)
        return jnp.concatenate([top, value[rows:] * mask[rows:]], axis=0)

    above = None
    for k in range(layers):
        head = head_ref[k]
        cond = cond_ref[k]
        deriv = deriv_ref[k]
        value = gain_ref[k]
        diag = store_ref[k]
        for plus_ref, minus_ref, axis in ((xp_ref, xm_ref, 0), (yp_ref, ym_ref, 1)):
            mean = 0.5 * (cond + after(cond, axis))
            drop = head - after(head, axis)
            a = mean + deriv * drop
            b = mean - after(deriv, axis) * drop
            face = mean * drop
            value = value + (face - before(face, axis))
            diag = diag + (a + before(b, axis))
            plus_ref[k] = masked(b)
            minus_ref[k] = masked(before(a, axis))
        if k + 1 < layers:
            mean = 0.5 * (cond + cond_ref[k + 1])
            drop = head - head_ref[k + 1] + 1.0
            a = mean + deriv * drop
            b = mean - deriv_ref[k + 1] * drop
            az_ref[k] = a
            bz_ref[k] = b
            face = mean * drop
        else:
            a = 2.0 * deriv
            face = cond
        diag = diag + a
        value = value + face
        if above is not None:
            diag = diag + above[1]
            value = value - above[0]
        above = (face, b)
        diag_ref[k] = diag
        out_ref[k] = masked(value)


def apply(v_ref, coefs, k):
    diag_ref, xp_ref, xm_ref, yp_ref, ym_ref, az_ref, bz_ref = coefs
    v = v_ref[k]
    value = diag_ref[k] * v
    value = value - xp_ref[k] * after(v, 0) - xm_ref[k] * before(v, 0)
    value = value - yp_ref[k] * after(v, 1) - ym_ref[k] * before(v, 1)
    if k > 0:
        value = value - az_ref[k - 1] * v_ref[k - 1]
    if k + 1 < v_ref.shape[0]:
        value = value - bz_ref[k] * v_ref[k + 1]
    return value


def powers(basis, coefs, tile, out_ref):
    layers = basis[0].shape[0]
    rows, cols = tile
    for step in range(KRYLOV - 1):
        for k in range(layers):
            basis[step + 1][k] = apply(basis[step], coefs, k)
    sums = [jnp.zeros((8, LANES), f32) for _ in PAIRS]
    for k in range(layers):
        top = apply(basis[-1], coefs, k)
        for at in range(0, rows, 8):
            for lane_at in range(0, cols, LANES):
                part = (slice(at, at + 8), slice(lane_at, lane_at + LANES))
                vs = [b[(k,) + part] for b in basis] + [top[part]]
                for e, (i, j) in enumerate(PAIRS):
                    sums[e] = sums[e] + vs[i] * vs[j]
    lines = [jnp.sum(x, axis=0, keepdims=True) for x in sums]
    lines.append(jnp.zeros((16 - len(PAIRS), LANES), f32))
    block = jnp.sum(jnp.concatenate(lines, axis=0), axis=1, keepdims=True)
    line = lax.broadcasted_iota(jnp.int32, (16, LANES), 0)
    flat = jnp.sum(jnp.where(lane_iota((16, LANES)) == line, block, 0.0), axis=0, keepdims=True)
    for d in range(out_ref.shape[0]):
        out_ref[d] = flat


def solve(gram_ref):
    total = gram_ref[0]
    for d in range(1, gram_ref.shape[0]):
        total = total + gram_ref[d]
    line = lax.broadcasted_iota(jnp.int32, (16, LANES), 0)
    spread = jnp.broadcast_to(total, (16, LANES))
    column = jnp.sum(jnp.where(lane_iota((16, LANES)) == line, spread, 0.0), axis=1, keepdims=True)
    gram = {}
    for e, (i, j) in enumerate(PAIRS):
        gram[i, j] = gram[j, i] = column[e : e + 1, :]

    def times_gram(c):
        out = []
        for i in range(KRYLOV + 1):
            out.append(functools.reduce(jnp.add, [gram[i, m] * c[m] for m in range(len(c))]))
        return out

    def dot(a, b):
        return functools.reduce(jnp.add, [x * y for x, y in zip(a, b)])

    beta = jnp.sqrt(gram[0, 0] + norm_epsilon)
    basis = [[1.0 / beta]]
    images = [times_gram(basis[0])]
    hessen = {}
    for j in range(KRYLOV):
        w = [jnp.zeros_like(beta)] + basis[j]
        for i in range(j + 1):
            product = dot(w, images[i])
            hessen[i, j] = product
            w = [w[m] - product * basis[i][m] if m < len(basis[i]) else w[m] for m in range(len(w))]
        square = jnp.maximum(dot(w, times_gram(w)), 0.0)
        length = jnp.sqrt(square + norm_epsilon)
        hessen[j + 1, j] = length
        if j + 1 < KRYLOV:
            inverse = 1.0 / length
            basis.append([x * inverse for x in w])
            images.append(times_gram(basis[-1]))
    n = KRYLOV
    normal = {}
    for a in range(n):
        for b in range(a + 1):
            normal[a, b] = functools.reduce(
                jnp.add,
                [hessen[i, a] * hessen[i, b] for i in range(n + 1) if (i, a) in hessen and (i, b) in hessen],
            )
    factor = {}
    inverse = []
    for a in range(n):
        for b in range(a + 1):
            value = normal[a, b]
            for m in range(b):
                value = value - factor[a, m] * factor[b, m]
            if a == b:
                inverse.append(lax.rsqrt(value))
            else:
                factor[a, b] = value * inverse[b]
    forward = []
    for a in range(n):
        value = hessen[0, a] * beta
        for m in range(a):
            value = value - factor[a, m] * forward[m]
        forward.append(value * inverse[a])
    backward = [None] * n
    for a in reversed(range(n)):
        value = forward[a]
        for m in range(a + 1, n):
            value = value - factor[m, a] * backward[m]
        backward[a] = value * inverse[a]
    return [
        functools.reduce(jnp.add, [backward[j] * basis[j][i] for j in range(i, n)]) for i in range(n)
    ]


def state_kernel(
    table_ref, head_ref, soil_ref, lo_ref, hi_ref, ylo_ref, yhi_ref,
    ext_ref, ks_ref, steep_ref, cap_ref, water_ref, flow_ref, *rest,
):
    coefs, (cond_ref, deriv_ref, store_ref, gain_ref) = rest[:7], rest[7:]
    layers, rows, cols = head_ref.shape
    tables = table_rows(table_ref, rows + 2 * HALO)
    mask = None
    for k in range(layers):
        head = jnp.concatenate([head_ref[k], hi_ref[k], lo_ref[k]], axis=0)
        head = jnp.concatenate([head, side(ylo_ref, yhi_ref, 0, k)], axis=1)
        ends = jnp.concatenate([hi_ref[layers + k], lo_ref[layers + k]], axis=0).astype(jnp.int32)
        index = jnp.concatenate([soil_ref[k] + 1, ends], axis=0)
        index = jnp.concatenate([index, side(ylo_ref, yhi_ref, 1, k).astype(jnp.int32)], axis=1)
        conduct, steep, capacity = (lookup(row, index) for row in tables)
        if k == 0:
            mask = (index > 0).astype(f32)
        cond, deriv, store, water = pointwise(head, conduct, steep, capacity)
        ext_ref[k] = head
        ks_ref[k] = conduct
        steep_ref[k] = steep
        cap_ref[k] = capacity
        cond_ref[k] = cond
        deriv_ref[k] = deriv
        store_ref[k] = store
        water_ref[k] = water
        gain_ref[k] = water - water_ref[k]
    linearize(ext_ref, cond_ref, deriv_ref, store_ref, gain_ref, mask, coefs, flow_ref, (rows, cols))


def first_kernel(src_ref, slo_ref, shi_ref, ylo_ref, yhi_ref, water_ref, flow_ref, *rest):
    coefs = rest[:7]
    base_ref, p0_ref, p1_ref, p2_ref, gram_ref = rest[7:]
    layers, rows, cols = src_ref.shape
    for k in range(layers):
        source = tall_source(src_ref, slo_ref, shi_ref, k, slice(0, cols))
        source = jnp.concatenate([source, side(ylo_ref, yhi_ref, 0, k)], axis=1)
        p0_ref[k] = flow_ref[k] - source
        base_ref[k] = water_ref[k] + source
    powers((p0_ref, p1_ref, p2_ref), coefs, (rows, cols), gram_ref)


def second_kernel(
    arrived_ref, old_ref, ks_ref, steep_ref, cap_ref, base_ref, q0_ref, q1_ref, q2_ref,
    part_ref, p0_ref, p1_ref, p2_ref, gram_ref, ext_ref, cond_ref, deriv_ref, store_ref, gain_ref, *coefs,
):
    layers = old_ref.shape[0]
    rows, cols = part_ref.shape[1:]
    x = solve(arrived_ref)
    for k in range(layers):
        conduct = ks_ref[k]
        if k == 0:
            mask = (conduct > 0.0).astype(f32)
        head = old_ref[k] - x[0] * q0_ref[k] - x[1] * q1_ref[k] - x[2] * q2_ref[k]
        cond, deriv, store, water = pointwise(head, conduct, steep_ref[k], cap_ref[k])
        ext_ref[k] = head
        part_ref[k] = head[:rows, :cols]
        cond_ref[k] = cond
        deriv_ref[k] = deriv
        store_ref[k] = store
        gain_ref[k] = water - base_ref[k]
    linearize(ext_ref, cond_ref, deriv_ref, store_ref, gain_ref, mask, coefs, p0_ref, (rows, cols))
    powers((p0_ref, p1_ref, p2_ref), coefs, (rows, cols), gram_ref)


def last_kernel(arrived_ref, part_ref, q0_ref, q1_ref, q2_ref, head_ref):
    layers, rows, cols = part_ref.shape
    x = solve(arrived_ref)
    for k in range(layers):
        own = (k, slice(0, rows), slice(0, cols))
        head_ref[k] = part_ref[k] - x[0] * q0_ref[own] - x[1] * q1_ref[own] - x[2] * q2_ref[own]


def shards(head_old, soil_type, soil_table, forcing, canopy, column_slot):
    layers, rows, cols = head_old.shape
    both = ("gx", "gy")
    devices = lax.axis_size("gx") * lax.axis_size("gy")
    tall, wide = rows + 2 * HALO, cols + LANES
    own, ext = ((layers, rows, cols), f32), ((layers, tall, wide), f32)
    gram_block = ((devices, 1, LANES), f32)
    in_hbm = pl.BlockSpec(memory_space=pltpu.HBM)

    def exchange(to_lower, to_upper, axis):
        size = lax.axis_size(axis)
        up = [(i, i + 1) for i in range(size - 1)]
        down = [(j, i) for i, j in up]
        return lax.ppermute(to_upper, axis, up), lax.ppermute(to_lower, axis, down)

    def spread(x):
        return lax.all_to_all(x, both, split_axis=0, concat_axis=0, tiled=True)

    send, down, up = call(
        pack_kernel,
        [((devices, 8, LANES), f32)] + [((2 * layers, HALO, cols), f32)] * 2,
        3,
        scratch=[
            pltpu.VMEM(canopy.shape, f32),
            pltpu.VMEM(head_old.shape, f32),
            pltpu.VMEM(soil_type.shape, jnp.int32),
            pltpu.SemaphoreType.DMA((3,)),
        ],
        in_specs=[in_hbm] * 3,
    )(canopy, head_old, soil_type)
    lo, hi = exchange(down, up, "gx")
    arrived = spread(send)
    edge = ((-(-SOURCE_DEPTH * layers // 8) * 8, cols), f32)
    source, sdown, sup, flux = call(
        source_kernel,
        [own, edge, edge, ((2, rows, cols), f32)],
        6,
        scratch=[pltpu.VMEM((devices // 2, 2 + layers, 8, LANES), f32)],
        in_specs=[smem] + [vmem] * 5,
    )(soil_table, arrived, head_old, soil_type, forcing, column_slot)
    slo, shi = exchange(sdown, sup, "gx")
    ydown, yup = call(state_strip_kernel, [((2, tall, LANES), f32)] * 2, 4)(head_old, soil_type, lo, hi)
    ylo, yhi = exchange(ydown, yup, "gy")
    sydown, syup = call(source_strip_kernel, [((1, tall, LANES), f32)] * 2, 3)(source, slo, shi)
    sylo, syhi = exchange(sydown, syup, "gy")
    held = [pltpu.VMEM(ext[0], f32)]
    old, ks, steep, cap, water, flow, *coefs = call(
        state_kernel, [ext] * 13, 7, scratch=held * 4, in_specs=[smem] + [vmem] * 6, flops=20000000
    )(soil_table, head_old, soil_type, lo, hi, ylo, yhi)
    base, p0, p1, p2, gram = call(first_kernel, [ext] * 4 + [gram_block], 14)(
        source, slo, shi, sylo, syhi, water, flow, *coefs
    )
    sums = spread(gram)
    part, q0, q1, q2, gram = call(
        second_kernel, [own] + [ext] * 3 + [gram_block], 9, scratch=held * 12
    )(sums, old, ks, steep, cap, base, p0, p1, p2)
    sums = spread(gram)
    (head,) = call(last_kernel, [own], 5)(sums, part, q0, q1, q2)
    return head, flux


def solution(mesh):
    return jax.shard_map(
        shards,
        mesh=mesh,
        in_specs=(
            P(None, "gx", "gy"),
            P(None, "gx", "gy"),
            P(),
            P(None, "gx", "gy"),
            P(None, ("gx", "gy")),
            P("gx", "gy"),
        ),
        out_specs=(P(None, "gx", "gy"), P(None, "gx", "gy")),
        check_vma=False,
    )
```

```python
import functools

import jax
import jax.numpy as jnp
from jax import lax
from jax.experimental import pallas as pl
from jax.experimental.pallas import tpu as pltpu
from jax.sharding import PartitionSpec as P

NEWTON = 2
KRYLOV = 3
HALO = 8
SOURCE_DEPTH = 6
LANES = 128
SLOT = 64

storage_weight = 4.0
norm_epsilon = 1e-06

VMEM_LIMIT = 40 * 1024 * 1024
PAIRS = [(i, j) for i in range(KRYLOV + 1) for j in range(i, KRYLOV + 1)]

f32 = jnp.float32
vmem = pl.BlockSpec(memory_space=pltpu.VMEM)
smem = pl.BlockSpec(memory_space=pltpu.SMEM)


def call(body, outs, n_in, scratch=(), in_specs=None, flops=1000000):
    return pl.pallas_call(
        body,
        out_shape=[jax.ShapeDtypeStruct(s, d) for s, d in outs],
        in_specs=in_specs or [vmem] * n_in,
        out_specs=[vmem] * len(outs),
        scratch_shapes=list(scratch),
        compiler_params=pltpu.CompilerParams(vmem_limit_bytes=VMEM_LIMIT),
        cost_estimate=pl.CostEstimate(flops=flops, bytes_accessed=1000000, transcendentals=0),
    )


def lane_iota(shape):
    return lax.broadcasted_iota(jnp.int32, shape, len(shape) - 1)


def edge_kernel(head_ref, soil_ref, down_ref, up_ref):
    layers, rows, _ = head_ref.shape
    for out_ref, at in ((down_ref, 0), (up_ref, rows - HALO)):
        for k in range(layers):
            out_ref[k] = head_ref[k, at : at + HALO, :]
            out_ref[layers + k] = (soil_ref[k, at : at + HALO, :] + 1).astype(f32)


def pack_kernel(canopy_ref, _, send_ref):
    rows = canopy_ref.shape[0]
    low = lane_iota((8, LANES)) < SLOT
    for t in range(canopy_ref.shape[1] // LANES):
        here = slice(t * LANES, (t + 1) * LANES)
        first = canopy_ref[0:8, here]
        rest = jnp.concatenate([canopy_ref[8:rows, here], jnp.zeros((16 - rows, LANES), f32)], axis=0)
        send_ref[2 * t] = jnp.where(low, first, pltpu.roll(rest, SLOT, 1))
        send_ref[2 * t + 1] = jnp.where(low, pltpu.roll(first, SLOT, 1), rest)


def table_rows(table_ref, rows):
    lane = lane_iota((rows, LANES))
    out = []
    for field in range(table_ref.shape[0]):
        row = jnp.zeros((rows, LANES), f32)
        for kind in range(table_ref.shape[1]):
            row = jnp.where(lane == kind + 1, table_ref[field, kind], row)
        out.append(row)
    return out


def lookup(row, index):
    pieces = [
        jnp.take_along_axis(row, index[:, at : at + LANES], axis=1, mode="promise_in_bounds")
        for at in range(0, index.shape[1], LANES)
    ]
    return jnp.concatenate(pieces, axis=1)


def sigmoid(u):
    return 1.0 / (1.0 + jnp.exp(-u))


def source_kernel(
    table_ref, arrived_ref, head_ref, soil_ref, forcing_ref, slot_ref,
    source_ref, down_ref, up_ref, flux_ref, tab_ref,
):
    layers, rows, cols = head_ref.shape
    owners = arrived_ref.shape[0]
    low = lane_iota((8, LANES)) < SLOT
    line = lax.broadcasted_iota(jnp.int32, (16, LANES), 0)
    is_root = (line >= 3) & (line < 3 + layers)

    def unpack(t, _):
        first = arrived_ref[2 * t]
        second = arrived_ref[2 * t + 1]
        both = jnp.concatenate(
            [
                jnp.where(low, first, pltpu.roll(second, SLOT, 1)),
                jnp.where(low, pltpu.roll(first, SLOT, 1), second),
            ],
            axis=0,
        )
        leaf_area, albedo, resist = both[0:1], both[1:2], both[2:3]
        root_sum = jnp.sum(jnp.where(is_root, both, 0.0), axis=0, keepdims=True)
        both = both * (leaf_area / ((leaf_area + resist) * root_sum))
        tab_ref[t, 0] = jnp.broadcast_to(0.5 + 0.3 * leaf_area, (8, LANES))
        tab_ref[t, 1] = jnp.broadcast_to(1.0 - albedo, (8, LANES))
        for k in range(layers):
            tab_ref[t, 2 + k] = jnp.broadcast_to(both[3 + k : 4 + k], (8, LANES))
        return 0

    lax.fori_loop(0, owners // 2, unpack, 0, unroll=16)
    tables = table_rows(table_ref, 8)

    for at_x in range(0, rows, 8):

        def column(j, _):
            here = (slice(at_x, at_x + 8), pl.ds(pl.multiple_of(j * LANES, LANES), LANES))
            slot = slot_ref[here]
            land = slot >= 0
            value = jnp.maximum(slot, 0)
            lane = value & (LANES - 1)
            tile = value >> 7

            def pick(t, held):
                match = tile == t
                return tuple(
                    jnp.where(match, lookup(tab_ref[t, k], lane), held[k]) for k in range(2 + layers)
                )

            start = tuple(jnp.ones((8, LANES), f32) for _ in range(2 + layers))
            exchange_coef, absorbed, *roots = lax.fori_loop(0, owners // 2, pick, start, unroll=8)
            uptake = []
            for k in range(layers):
                index = soil_ref[(k,) + here] + 1
                steep = lookup(tables[1], index)
                uptake.append(roots[k] * sigmoid(steep * head_ref[(k,) + here]))
                if k == 0:
                    ks_top = lookup(tables[0], index)
            conductance = functools.reduce(jnp.add, uptake)
            sunlight, air_temp, humidity, rainfall = (forcing_ref[(i,) + here] for i in range(4))
            radiation = absorbed * sunlight + 0.3
            square = air_temp * air_temp
            excess = radiation - 0.3 * square * square - conductance * (0.5 - humidity)
            slope = -1.2 * square * air_temp - exchange_coef - conductance
            rise = -excess / slope
            surface = air_temp + rise
            vapour = 0.5 * jnp.exp(2.0 * rise)
            square = surface * surface
            excess = (
                radiation
                - 0.3 * square * square
                - exchange_coef * rise
                - conductance * (vapour - humidity)
            )
            slope = -1.2 * square * surface - exchange_coef - 2.0 * conductance * vapour
            rise = rise - excess / slope
            rate = 0.5 * jnp.exp(2.0 * rise) - humidity
            infiltration = rainfall * ks_top / (rainfall + ks_top)
            infiltration = jnp.where(land, infiltration, 0.0)
            rate = jnp.where(land, rate, 0.0)
            flux_ref[(0,) + here] = conductance * rate
            flux_ref[(1,) + here] = infiltration
            for k in range(layers):
                value = -rate * uptake[k]
                if k == 0:
                    value = value + infiltration
                source_ref[(k,) + here] = value
                edge = slice(SOURCE_DEPTH * k, SOURCE_DEPTH * (k + 1))
                if at_x < HALO:
                    down_ref[edge, here[1]] = value[:SOURCE_DEPTH]
                if at_x >= rows - HALO:
                    up_ref[edge, here[1]] = value[HALO - SOURCE_DEPTH :]
            return 0

        lax.fori_loop(0, cols // LANES, column, 0)


def strips(planes, shift_from):
    packed = None
    for k, plane in enumerate(planes):
        lane = lane_iota(plane.shape)
        shift = (HALO * k - shift_from) % LANES
        moved = pltpu.roll(plane, shift, 1) if shift else plane
        inside = (lane >= HALO * k) & (lane < HALO * (k + 1))
        packed = jnp.where(inside, moved, 0.0 if packed is None else packed)
    return packed


def strip_parts(cols):
    return ((slice(0, LANES), 0), (slice(cols - LANES, cols), LANES - HALO))


def send_strips(low, high, field, out_ref):
    me = lax.axis_index("gy")
    for d in range(out_ref.shape[0]):
        out_ref[d, field] = jnp.where(d < me, low, high)


def state_strip_kernel(head_ref, soil_ref, lo_ref, hi_ref, out_ref):
    layers, _, cols = head_ref.shape
    parts = []
    for part, shift in strip_parts(cols):
        heads, soils = [], []
        for k in range(layers):
            heads.append(
                jnp.concatenate([head_ref[k, :, part], hi_ref[k, :, part], lo_ref[k, :, part]], axis=0)
            )
            soil = (soil_ref[k, :, part] + 1).astype(f32)
            ends = [hi_ref[layers + k, :, part], lo_ref[layers + k, :, part]]
            soils.append(jnp.concatenate([soil] + ends, axis=0))
        parts.append((strips(heads, shift), strips(soils, shift)))
    for field in range(2):
        send_strips(parts[0][field], parts[1][field], field, out_ref)


def tall_source(src_ref, slo_ref, shi_ref, k, part):
    edge = slice(SOURCE_DEPTH * k, SOURCE_DEPTH * (k + 1))
    own = src_ref[k, :, part]
    gap = jnp.zeros((2 * (HALO - SOURCE_DEPTH), own.shape[1]), f32)
    return jnp.concatenate([own, shi_ref[edge, part], gap, slo_ref[edge, part]], axis=0)


def source_strip_kernel(src_ref, slo_ref, shi_ref, out_ref):
    layers, _, cols = src_ref.shape
    low, high = (
        strips([tall_source(src_ref, slo_ref, shi_ref, k, part) for k in range(layers)], shift)
        for part, shift in strip_parts(cols)
    )
    send_strips(low, high, 0, out_ref)


def received(strip_ref, field):
    me = lax.axis_index("gy")
    count = strip_ref.shape[0]
    right = strip_ref[jnp.minimum(me + 1, count - 1), field]
    left = strip_ref[jnp.maximum(me - 1, 0), field]
    return jnp.where(me + 1 < count, right, 0.0), jnp.where(me > 0, left, 0.0)


def side(strip, k):
    right, left = strip
    lane = lane_iota(right.shape)
    shift = (-HALO * k) % LANES
    right = pltpu.roll(right, shift, 1) if shift else right
    left = pltpu.roll(left, (LANES - HALO - HALO * k) % LANES, 1)
    return jnp.where(lane < HALO, right, jnp.where(lane >= LANES - HALO, left, 0.0))


def after(x, axis):
    return pltpu.roll(x, x.shape[axis] - 1, axis)


def before(x, axis):
    return pltpu.roll(x, 1, axis)


def pointwise(head, conduct, steep, capacity):
    sat = 0.5 + 0.5 * jnp.tanh(0.5 * (steep * head))
    slope = steep * sat * (1.0 - sat)
    cond = conduct * (0.1 + 0.9 * sat * sat)
    deriv = 0.9 * conduct * sat * slope
    weighted = storage_weight * capacity
    return cond, deriv, weighted * slope, weighted * sat


def linearize(head_ref, cond_ref, deriv_ref, store_ref, gain_ref, mask, coefs, out_ref, tile):
    diag_ref, xp_ref, xm_ref, yp_ref, ym_ref, az_ref, bz_ref = coefs
    layers = head_ref.shape[0]
    rows, cols = tile

    def masked(value):
        own = value[:rows, cols:] * mask[:rows, cols:]
        top = jnp.concatenate([value[:rows, :cols], own], axis=1)
        return jnp.concatenate([top, value[rows:] * mask[rows:]], axis=0)

    above = None
    for k in range(layers):
        head = head_ref[k]
        cond = cond_ref[k]
        deriv = deriv_ref[k]
        value = gain_ref[k]
        diag = store_ref[k]
        for plus_ref, minus_ref, axis in ((xp_ref, xm_ref, 0), (yp_ref, ym_ref, 1)):
            mean = 0.5 * (cond + after(cond, axis))
            drop = head - after(head, axis)
            a = mean + deriv * drop
            b = mean - after(deriv, axis) * drop
            face = mean * drop
            value = value + (face - before(face, axis))
            diag = diag + (a + before(b, axis))
            plus_ref[k] = masked(b)
            minus_ref[k] = masked(before(a, axis))
        if k + 1 < layers:
            mean = 0.5 * (cond + cond_ref[k + 1])
            drop = head - head_ref[k + 1] + 1.0
            a = mean + deriv * drop
            b = mean - deriv_ref[k + 1] * drop
            az_ref[k] = a
            bz_ref[k] = b
            face = mean * drop
        else:
            a = 2.0 * deriv
            face = cond
        diag = diag + a
        value = value + face
        if above is not None:
            diag = diag + above[1]
            value = value - above[0]
        above = (face, b)
        diag_ref[k] = diag
        out_ref[k] = masked(value)


def apply(v_ref, coefs, k):
    diag_ref, xp_ref, xm_ref, yp_ref, ym_ref, az_ref, bz_ref = coefs
    v = v_ref[k]
    value = diag_ref[k] * v
    value = value - xp_ref[k] * after(v, 0) - xm_ref[k] * before(v, 0)
    value = value - yp_ref[k] * after(v, 1) - ym_ref[k] * before(v, 1)
    if k > 0:
        value = value - az_ref[k - 1] * v_ref[k - 1]
    if k + 1 < v_ref.shape[0]:
        value = value - bz_ref[k] * v_ref[k + 1]
    return value


def powers(basis, coefs, tile, out_ref):
    layers = basis[0].shape[0]
    rows, cols = tile
    for step in range(KRYLOV - 1):
        for k in range(layers):
            basis[step + 1][k] = apply(basis[step], coefs, k)
    sums = [jnp.zeros((8, LANES), f32) for _ in PAIRS]
    for k in range(layers):
        top = apply(basis[-1], coefs, k)
        for at in range(0, rows, 8):
            for lane_at in range(0, cols, LANES):
                part = (slice(at, at + 8), slice(lane_at, lane_at + LANES))
                vs = [b[(k,) + part] for b in basis] + [top[part]]
                for e, (i, j) in enumerate(PAIRS):
                    sums[e] = sums[e] + vs[i] * vs[j]
    lines = [jnp.sum(x, axis=0, keepdims=True) for x in sums]
    lines.append(jnp.zeros((16 - len(PAIRS), LANES), f32))
    block = jnp.sum(jnp.concatenate(lines, axis=0), axis=1, keepdims=True)
    line = lax.broadcasted_iota(jnp.int32, (16, LANES), 0)
    flat = jnp.sum(jnp.where(lane_iota((16, LANES)) == line, block, 0.0), axis=0, keepdims=True)
    for d in range(out_ref.shape[0]):
        out_ref[d] = flat


def solve(gram_ref):
    total = gram_ref[0]
    for d in range(1, gram_ref.shape[0]):
        total = total + gram_ref[d]
    line = lax.broadcasted_iota(jnp.int32, (16, LANES), 0)
    spread = jnp.broadcast_to(total, (16, LANES))
    column = jnp.sum(jnp.where(lane_iota((16, LANES)) == line, spread, 0.0), axis=1, keepdims=True)
    gram = {}
    for e, (i, j) in enumerate(PAIRS):
        gram[i, j] = gram[j, i] = column[e : e + 1, :]

    def times_gram(c):
        out = []
        for i in range(KRYLOV + 1):
            out.append(functools.reduce(jnp.add, [gram[i, m] * c[m] for m in range(len(c))]))
        return out

    def dot(a, b):
        return functools.reduce(jnp.add, [x * y for x, y in zip(a, b)])

    square = gram[0, 0] + norm_epsilon
    inverse = lax.rsqrt(square)
    beta = square * inverse
    basis = [[inverse]]
    images = [times_gram(basis[0])]
    hessen = {}
    for j in range(KRYLOV):
        w = [jnp.zeros_like(beta)] + basis[j]
        for i in range(j + 1):
            product = dot(w, images[i])
            hessen[i, j] = product
            w = [w[m] - product * basis[i][m] if m < len(basis[i]) else w[m] for m in range(len(w))]
        square = jnp.maximum(dot(w, times_gram(w)), 0.0) + norm_epsilon
        inverse = lax.rsqrt(square)
        hessen[j + 1, j] = square * inverse
        if j + 1 < KRYLOV:
            basis.append([x * inverse for x in w])
            images.append(times_gram(basis[-1]))
    n = KRYLOV
    normal = {}
    for a in range(n):
        for b in range(a + 1):
            normal[a, b] = functools.reduce(
                jnp.add,
                [hessen[i, a] * hessen[i, b] for i in range(n + 1) if (i, a) in hessen and (i, b) in hessen],
            )
    factor = {}
    inverse = []
    for a in range(n):
        for b in range(a + 1):
            value = normal[a, b]
            for m in range(b):
                value = value - factor[a, m] * factor[b, m]
            if a == b:
                inverse.append(lax.rsqrt(value))
            else:
                factor[a, b] = value * inverse[b]
    forward = []
    for a in range(n):
        value = hessen[0, a] * beta
        for m in range(a):
            value = value - factor[a, m] * forward[m]
        forward.append(value * inverse[a])
    backward = [None] * n
    for a in reversed(range(n)):
        value = forward[a]
        for m in range(a + 1, n):
            value = value - factor[m, a] * backward[m]
        backward[a] = value * inverse[a]
    return [
        functools.reduce(jnp.add, [backward[j] * basis[j][i] for j in range(i, n)]) for i in range(n)
    ]


def state_kernel(
    table_ref, head_ref, soil_ref, lo_ref, hi_ref, strip_ref,
    ext_ref, ks_ref, steep_ref, cap_ref, cond_ref, deriv_ref, store_ref, water_ref,
):
    layers, rows, cols = head_ref.shape
    tables = table_rows(table_ref, rows + 2 * HALO)
    heads, soils = received(strip_ref, 0), received(strip_ref, 1)
    for k in range(layers):
        head = jnp.concatenate([head_ref[k], hi_ref[k], lo_ref[k]], axis=0)
        head = jnp.concatenate([head, side(heads, k)], axis=1)
        ends = jnp.concatenate([hi_ref[layers + k], lo_ref[layers + k]], axis=0).astype(jnp.int32)
        index = jnp.concatenate([soil_ref[k] + 1, ends], axis=0)
        index = jnp.concatenate([index, side(soils, k).astype(jnp.int32)], axis=1)
        conduct, steep, capacity = (lookup(row, index) for row in tables)
        values = (head, conduct, steep, capacity) + pointwise(head, conduct, steep, capacity)
        outs = (ext_ref, ks_ref, steep_ref, cap_ref, cond_ref, deriv_ref, store_ref, water_ref)
        for ref, value in zip(outs, values):
            ref[k] = value


def flow_kernel(ext_ref, ks_ref, cond_ref, deriv_ref, store_ref, water_ref, flow_ref, *rest, tile):
    coefs, gain_ref = rest[:7], rest[7]
    mask = (ks_ref[0] > 0.0).astype(f32)
    for k in range(ext_ref.shape[0]):
        gain_ref[k] = water_ref[k] - water_ref[k]
    linearize(ext_ref, cond_ref, deriv_ref, store_ref, gain_ref, mask, coefs, flow_ref, tile)


def first_kernel(src_ref, slo_ref, shi_ref, strip_ref, water_ref, flow_ref, *rest):
    coefs = rest[:7]
    base_ref, p0_ref, p1_ref, p2_ref, gram_ref = rest[7:]
    layers, rows, cols = src_ref.shape
    strip = received(strip_ref, 0)
    for k in range(layers):
        source = tall_source(src_ref, slo_ref, shi_ref, k, slice(0, cols))
        source = jnp.concatenate([source, side(strip, k)], axis=1)
        p0_ref[k] = flow_ref[k] - source
        base_ref[k] = water_ref[k] + source
    powers((p0_ref, p1_ref, p2_ref), coefs, (rows, cols), gram_ref)


def second_kernel(
    arrived_ref, old_ref, ks_ref, steep_ref, cap_ref, base_ref, q0_ref, q1_ref, q2_ref,
    part_ref, p0_ref, p1_ref, p2_ref, gram_ref, ext_ref, cond_ref, deriv_ref, store_ref, gain_ref, *coefs,
):
    layers = old_ref.shape[0]
    rows, cols = part_ref.shape[1:]
    x = solve(arrived_ref)
    for k in range(layers):
        conduct = ks_ref[k]
        if k == 0:
            mask = (conduct > 0.0).astype(f32)
        head = old_ref[k] - x[0] * q0_ref[k] - x[1] * q1_ref[k] - x[2] * q2_ref[k]
        cond, deriv, store, water = pointwise(head, conduct, steep_ref[k], cap_ref[k])
        ext_ref[k] = head
        part_ref[k] = head[:rows, :cols]
        cond_ref[k] = cond
        deriv_ref[k] = deriv
        store_ref[k] = store
        gain_ref[k] = water - base_ref[k]
    linearize(ext_ref, cond_ref, deriv_ref, store_ref, gain_ref, mask, coefs, p0_ref, (rows, cols))
    powers((p0_ref, p1_ref, p2_ref), coefs, (rows, cols), gram_ref)


def last_kernel(arrived_ref, part_ref, q0_ref, q1_ref, q2_ref, head_ref):
    layers, rows, cols = part_ref.shape
    x = solve(arrived_ref)
    for k in range(layers):
        own = (k, slice(0, rows), slice(0, cols))
        head_ref[k] = part_ref[k] - x[0] * q0_ref[own] - x[1] * q1_ref[own] - x[2] * q2_ref[own]


def shards(head_old, soil_type, soil_table, forcing, canopy, column_slot):
    layers, rows, cols = head_old.shape
    both = ("gx", "gy")
    devices = lax.axis_size("gx") * lax.axis_size("gy")
    tall, wide = rows + 2 * HALO, cols + LANES
    own, ext = ((layers, rows, cols), f32), ((layers, tall, wide), f32)
    gram_block = ((devices, 1, LANES), f32)

    def exchange(to_lower, to_upper, axis):
        size = lax.axis_size(axis)
        up = [(i, i + 1) for i in range(size - 1)]
        down = [(j, i) for i, j in up]
        return lax.ppermute(to_upper, axis, up), lax.ppermute(to_lower, axis, down)

    def spread(x, axes):
        return lax.all_to_all(x, axes, split_axis=0, concat_axis=0, tiled=True)

    down, up = call(edge_kernel, [((2 * layers, HALO, cols), f32)] * 2, 2)(head_old, soil_type)
    lo, hi = exchange(down, up, "gx")
    (send,) = call(
        pack_kernel,
        [((devices, 8, LANES), f32)],
        2,
        in_specs=[vmem, pl.BlockSpec(memory_space=pl.ANY)],
        flops=1000000000,
    )(canopy, down)
    arrived = spread(send, both)
    edge = ((-(-SOURCE_DEPTH * layers // 8) * 8, cols), f32)
    source, sdown, sup, flux = call(
        source_kernel,
        [own, edge, edge, ((2, rows, cols), f32)],
        6,
        scratch=[pltpu.VMEM((devices // 2, 2 + layers, 8, LANES), f32)],
        in_specs=[smem] + [vmem] * 5,
    )(soil_table, arrived, head_old, soil_type, forcing, column_slot)
    slo, shi = exchange(sdown, sup, "gx")
    line = lax.axis_size("gy")
    (strip,) = call(state_strip_kernel, [((line, 2, tall, LANES), f32)], 4)(head_old, soil_type, lo, hi)
    strip = spread(strip, "gy")
    (sstrip,) = call(source_strip_kernel, [((line, 1, tall, LANES), f32)], 3)(source, slo, shi)
    sstrip = spread(sstrip, "gy")
    held = [pltpu.VMEM(ext[0], f32)]
    old, ks, steep, cap, cond, deriv, store, water = call(
        state_kernel, [ext] * 8, 6, in_specs=[smem] + [vmem] * 5, flops=20000000
    )(soil_table, head_old, soil_type, lo, hi, strip)
    flow, *coefs = call(
        functools.partial(flow_kernel, tile=(rows, cols)), [ext] * 8, 6, scratch=held, flops=20000000
    )(old, ks, cond, deriv, store, water)
    base, p0, p1, p2, gram = call(first_kernel, [ext] * 4 + [gram_block], 13)(
        source, slo, shi, sstrip, water, flow, *coefs
    )
    sums = spread(gram, both)
    part, q0, q1, q2, gram = call(
        second_kernel, [own] + [ext] * 3 + [gram_block], 9, scratch=held * 12
    )(sums, old, ks, steep, cap, base, p0, p1, p2)
    sums = spread(gram, both)
    (head,) = call(last_kernel, [own], 5)(sums, part, q0, q1, q2)
    return head, flux


def solution(mesh):
    return jax.shard_map(
        shards,
        mesh=mesh,
        in_specs=(
            P(None, "gx", "gy"),
            P(None, "gx", "gy"),
            P(),
            P(None, "gx", "gy"),
            P(None, ("gx", "gy")),
            P("gx", "gy"),
        ),
        out_specs=(P(None, "gx", "gy"), P(None, "gx", "gy")),
        check_vma=False,
    )
```

```python
import functools

import jax
import jax.numpy as jnp
from jax import lax
from jax.experimental import pallas as pl
from jax.experimental.pallas import tpu as pltpu
from jax.sharding import PartitionSpec as P

NEWTON = 2
KRYLOV = 3
HALO = 8
STATE_DEPTH = 7
SOURCE_DEPTH = 6
LANES = 128
SLOT = 64

storage_weight = 4.0
norm_epsilon = 1e-06

VMEM_LIMIT = 20 * 1024 * 1024
PAIRS = [(i, j) for i in range(KRYLOV + 1) for j in range(i, KRYLOV + 1)]

f32 = jnp.float32
vmem = pl.BlockSpec(memory_space=pltpu.VMEM)
smem = pl.BlockSpec(memory_space=pltpu.SMEM)


def call(body, outs, n_in, scratch=(), in_specs=None, flops=1000000):
    return pl.pallas_call(
        body,
        out_shape=[jax.ShapeDtypeStruct(s, d) for s, d in outs],
        in_specs=in_specs or [vmem] * n_in,
        out_specs=[vmem] * len(outs),
        scratch_shapes=list(scratch),
        compiler_params=pltpu.CompilerParams(vmem_limit_bytes=VMEM_LIMIT),
        cost_estimate=pl.CostEstimate(flops=flops, bytes_accessed=1000000, transcendentals=0),
    )


def lane_iota(shape):
    return lax.broadcasted_iota(jnp.int32, shape, len(shape) - 1)


def edge_kernel(head_ref, soil_ref, down_ref, up_ref):
    layers, rows, _ = head_ref.shape
    for out_ref, part in ((down_ref, slice(0, STATE_DEPTH)), (up_ref, slice(rows - STATE_DEPTH, rows))):
        for k in range(layers):
            out_ref[STATE_DEPTH * k : STATE_DEPTH * (k + 1)] = head_ref[k][part]
        for k in range(layers):
            at = STATE_DEPTH * (layers + k)
            out_ref[at : at + STATE_DEPTH] = (soil_ref[k] + 1).astype(f32)[part]


def pack_kernel(canopy_ref, send_ref):
    rows = canopy_ref.shape[0]
    low = lane_iota((8, LANES)) < SLOT
    for t in range(canopy_ref.shape[1] // LANES):
        here = slice(t * LANES, (t + 1) * LANES)
        first = canopy_ref[0:8, here]
        rest = jnp.concatenate([canopy_ref[8:rows, here], jnp.zeros((16 - rows, LANES), f32)], axis=0)
        send_ref[2 * t] = jnp.where(low, first, pltpu.roll(rest, SLOT, 1))
        send_ref[2 * t + 1] = jnp.where(low, pltpu.roll(first, SLOT, 1), rest)


def table_rows(table_ref, rows):
    lane = lane_iota((rows, LANES))
    out = []
    for field in range(table_ref.shape[0]):
        row = jnp.zeros((rows, LANES), f32)
        for kind in range(table_ref.shape[1]):
            row = jnp.where(lane == kind + 1, table_ref[field, kind], row)
        out.append(row)
    return out


def lookup(row, index):
    pieces = [
        jnp.take_along_axis(row, index[:, at : at + LANES], axis=1, mode="promise_in_bounds")
        for at in range(0, index.shape[1], LANES)
    ]
    return jnp.concatenate(pieces, axis=1)


def sigmoid(u):
    return 1.0 / (1.0 + jnp.exp(-u))


def source_kernel(
    table_ref, arrived_ref, head_ref, soil_ref, forcing_ref, slot_ref,
    source_ref, down_ref, up_ref, flux_ref, tab_ref,
):
    layers, rows, cols = head_ref.shape
    owners = arrived_ref.shape[0]
    low = lane_iota((8, LANES)) < SLOT
    line = lax.broadcasted_iota(jnp.int32, (16, LANES), 0)
    is_root = (line >= 3) & (line < 3 + layers)

    def unpack(t, _):
        first = arrived_ref[2 * t]
        second = arrived_ref[2 * t + 1]
        both = jnp.concatenate(
            [
                jnp.where(low, first, pltpu.roll(second, SLOT, 1)),
                jnp.where(low, pltpu.roll(first, SLOT, 1), second),
            ],
            axis=0,
        )
        leaf_area, albedo, resist = both[0:1], both[1:2], both[2:3]
        root_sum = jnp.sum(jnp.where(is_root, both, 0.0), axis=0, keepdims=True)
        both = both * (leaf_area / ((leaf_area + resist) * root_sum))
        tab_ref[t, 0] = jnp.broadcast_to(0.5 + 0.3 * leaf_area, (8, LANES))
        tab_ref[t, 1] = jnp.broadcast_to(1.0 - albedo, (8, LANES))
        for k in range(layers):
            tab_ref[t, 2 + k] = jnp.broadcast_to(both[3 + k : 4 + k], (8, LANES))
        return 0

    lax.fori_loop(0, owners // 2, unpack, 0, unroll=16)
    tables = table_rows(table_ref, 8)

    for at_x in range(0, rows, 8):

        def column(j, _):
            here = (slice(at_x, at_x + 8), pl.ds(pl.multiple_of(j * LANES, LANES), LANES))
            slot = slot_ref[here]
            land = slot >= 0
            value = jnp.maximum(slot, 0)
            lane = value & (LANES - 1)
            tile = value >> 7

            def pick(t, held):
                match = tile == t
                return tuple(
                    jnp.where(match, lookup(tab_ref[t, k], lane), held[k]) for k in range(2 + layers)
                )

            start = tuple(jnp.ones((8, LANES), f32) for _ in range(2 + layers))
            exchange_coef, absorbed, *roots = lax.fori_loop(0, owners // 2, pick, start, unroll=8)
            uptake = []
            for k in range(layers):
                index = soil_ref[(k,) + here] + 1
                steep = lookup(tables[1], index)
                uptake.append(roots[k] * sigmoid(steep * head_ref[(k,) + here]))
                if k == 0:
                    ks_top = lookup(tables[0], index)
            conductance = functools.reduce(jnp.add, uptake)
            sunlight, air_temp, humidity, rainfall = (forcing_ref[(i,) + here] for i in range(4))
            radiation = absorbed * sunlight + 0.3
            square = air_temp * air_temp
            excess = radiation - 0.3 * square * square - conductance * (0.5 - humidity)
            slope = -1.2 * square * air_temp - exchange_coef - conductance
            rise = -excess / slope
            surface = air_temp + rise
            vapour = 0.5 * jnp.exp(2.0 * rise)
            square = surface * surface
            excess = (
                radiation
                - 0.3 * square * square
                - exchange_coef * rise
                - conductance * (vapour - humidity)
            )
            slope = -1.2 * square * surface - exchange_coef - 2.0 * conductance * vapour
            rise = rise - excess / slope
            rate = 0.5 * jnp.exp(2.0 * rise) - humidity
            infiltration = rainfall * ks_top / (rainfall + ks_top)
            infiltration = jnp.where(land, infiltration, 0.0)
            rate = jnp.where(land, rate, 0.0)
            flux_ref[(0,) + here] = conductance * rate
            flux_ref[(1,) + here] = infiltration
            for k in range(layers):
                value = -rate * uptake[k]
                if k == 0:
                    value = value + infiltration
                source_ref[(k,) + here] = value
                edge = slice(SOURCE_DEPTH * k, SOURCE_DEPTH * (k + 1))
                if at_x < HALO:
                    down_ref[edge, here[1]] = value[:SOURCE_DEPTH]
                if at_x >= rows - HALO:
                    up_ref[edge, here[1]] = value[HALO - SOURCE_DEPTH :]
            return 0

        lax.fori_loop(0, cols // LANES, column, 0)


def strips(planes, shift_from):
    packed = None
    for k, plane in enumerate(planes):
        lane = lane_iota(plane.shape)
        shift = (HALO * k - shift_from) % LANES
        moved = pltpu.roll(plane, shift, 1) if shift else plane
        inside = (lane >= HALO * k) & (lane < HALO * (k + 1))
        packed = jnp.where(inside, moved, 0.0 if packed is None else packed)
    return packed


def strip_parts(cols):
    return ((slice(0, LANES), 0), (slice(cols - LANES, cols), LANES - HALO))


def ends_of(lo_ref, hi_ref, at, depth, part):
    edge = slice(depth * at, depth * (at + 1))
    above, below = hi_ref[edge, part], lo_ref[edge, part]
    gap = jnp.zeros((2 * (HALO - depth), above.shape[1]), f32)
    return jnp.concatenate([above, gap, below], axis=0)


def strip_kernel(head_ref, soil_ref, lo_ref, hi_ref, src_ref, slo_ref, shi_ref, down_ref, up_ref):
    layers, _, cols = head_ref.shape
    every = range(layers)
    for out_ref, (part, shift) in zip((down_ref, up_ref), strip_parts(cols)):
        heads = [(head_ref[k, :, part], ends_of(lo_ref, hi_ref, k, STATE_DEPTH, part)) for k in every]
        soils = [
            (
                (soil_ref[k, :, part] + 1).astype(f32),
                ends_of(lo_ref, hi_ref, layers + k, STATE_DEPTH, part),
            )
            for k in every
        ]
        sources = [(src_ref[k, :, part], ends_of(slo_ref, shi_ref, k, SOURCE_DEPTH, part)) for k in every]
        for field, pairs in enumerate((heads, soils, sources)):
            out_ref[field] = strips([jnp.concatenate(pair, axis=0) for pair in pairs], shift)


def side(ylo_ref, yhi_ref, field, k):
    right = yhi_ref[field]
    left = ylo_ref[field]
    lane = lane_iota(right.shape)
    shift = (-HALO * k) % LANES
    right = pltpu.roll(right, shift, 1) if shift else right
    left = pltpu.roll(left, (LANES - HALO - HALO * k) % LANES, 1)
    return jnp.where(lane < HALO, right, jnp.where(lane >= LANES - HALO, left, 0.0))


def after(x, axis):
    return pltpu.roll(x, x.shape[axis] - 1, axis)


def before(x, axis):
    return pltpu.roll(x, 1, axis)


def pointwise(head, conduct, steep, capacity):
    sat = 0.5 + 0.5 * jnp.tanh(0.5 * (steep * head))
    slope = steep * sat * (1.0 - sat)
    cond = conduct * (0.1 + 0.9 * sat * sat)
    deriv = 0.9 * conduct * sat * slope
    weighted = storage_weight * capacity
    return cond, deriv, weighted * slope, weighted * sat


def joined(main_ref, side_ref):
    return lambda k: jnp.concatenate([main_ref[k], side_ref[k]], axis=1)


def linearize(layers, head_of, cond_of, deriv_of, store_of, gain_of, mask, coefs, out_ref, tile):
    diag_ref, xp_ref, xm_ref, yp_ref, ym_ref, az_ref, bz_ref = coefs
    rows, cols = tile

    def masked(value):
        own = value[:rows, cols:] * mask[:rows, cols:]
        top = jnp.concatenate([value[:rows, :cols], own], axis=1)
        return jnp.concatenate([top, value[rows:] * mask[rows:]], axis=0)

    above = None
    for k in range(layers):
        head = head_of(k)
        cond = cond_of(k)
        deriv = deriv_of(k)
        value = gain_of(k)
        diag = store_of(k)
        for plus_ref, minus_ref, axis in ((xp_ref, xm_ref, 0), (yp_ref, ym_ref, 1)):
            mean = 0.5 * (cond + after(cond, axis))
            drop = head - after(head, axis)
            a = mean + deriv * drop
            b = mean - after(deriv, axis) * drop
            face = mean * drop
            value = value + (face - before(face, axis))
            diag = diag + (a + before(b, axis))
            plus_ref[k] = masked(b)
            minus_ref[k] = masked(before(a, axis))
        if k + 1 < layers:
            mean = 0.5 * (cond + cond_of(k + 1))
            drop = head - head_of(k + 1) + 1.0
            a = mean + deriv * drop
            b = mean - deriv_of(k + 1) * drop
            az_ref[k] = a
            bz_ref[k] = b
            face = mean * drop
        else:
            a = 2.0 * deriv
            face = cond
        diag = diag + a
        value = value + face
        if above is not None:
            diag = diag + above[1]
            value = value - above[0]
        above = (face, b)
        diag_ref[k] = diag
        out_ref[k] = masked(value)


def apply(v_ref, coefs, k):
    diag_ref, xp_ref, xm_ref, yp_ref, ym_ref, az_ref, bz_ref = coefs
    v = v_ref[k]
    value = diag_ref[k] * v
    value = value - xp_ref[k] * after(v, 0) - xm_ref[k] * before(v, 0)
    value = value - yp_ref[k] * after(v, 1) - ym_ref[k] * before(v, 1)
    if k > 0:
        value = value - az_ref[k - 1] * v_ref[k - 1]
    if k + 1 < v_ref.shape[0]:
        value = value - bz_ref[k] * v_ref[k + 1]
    return value


def powers(basis, coefs, tile, out_ref):
    layers = basis[0].shape[0]
    rows, cols = tile
    for step in range(KRYLOV - 1):
        for k in range(layers):
            basis[step + 1][k] = apply(basis[step], coefs, k)
    sums = [jnp.zeros((8, LANES), f32) for _ in PAIRS]
    for k in range(layers):
        top = apply(basis[-1], coefs, k)
        for at in range(0, rows, 8):
            for lane_at in range(0, cols, LANES):
                part = (slice(at, at + 8), slice(lane_at, lane_at + LANES))
                vs = [b[(k,) + part] for b in basis] + [top[part]]
                for e, (i, j) in enumerate(PAIRS):
                    sums[e] = sums[e] + vs[i] * vs[j]
    lines = [jnp.sum(x, axis=0, keepdims=True) for x in sums]
    lines.append(jnp.zeros((16 - len(PAIRS), LANES), f32))
    block = jnp.sum(jnp.concatenate(lines, axis=0), axis=1, keepdims=True)
    line = lax.broadcasted_iota(jnp.int32, (16, LANES), 0)
    flat = jnp.sum(jnp.where(lane_iota((16, LANES)) == line, block, 0.0), axis=0, keepdims=True)
    for d in range(out_ref.shape[0]):
        out_ref[d] = flat


def solve(gram_ref):
    total = gram_ref[0]
    for d in range(1, gram_ref.shape[0]):
        total = total + gram_ref[d]
    line = lax.broadcasted_iota(jnp.int32, (16, LANES), 0)
    spread = jnp.broadcast_to(total, (16, LANES))
    column = jnp.sum(jnp.where(lane_iota((16, LANES)) == line, spread, 0.0), axis=1, keepdims=True)
    gram = {}
    for e, (i, j) in enumerate(PAIRS):
        gram[i, j] = gram[j, i] = column[e : e + 1, :]

    def times_gram(c):
        out = []
        for i in range(KRYLOV + 1):
            out.append(functools.reduce(jnp.add, [gram[i, m] * c[m] for m in range(len(c))]))
        return out

    def dot(a, b):
        return functools.reduce(jnp.add, [x * y for x, y in zip(a, b)])

    square = gram[0, 0] + norm_epsilon
    inverse = lax.rsqrt(square)
    beta = square * inverse
    basis = [[inverse]]
    images = [times_gram(basis[0])]
    hessen = {}
    for j in range(KRYLOV):
        w = [jnp.zeros_like(beta)] + basis[j]
        for i in range(j + 1):
            product = dot(w, images[i])
            hessen[i, j] = product
            w = [w[m] - product * basis[i][m] if m < len(basis[i]) else w[m] for m in range(len(w))]
        square = jnp.maximum(dot(w, times_gram(w)), 0.0) + norm_epsilon
        inverse = lax.rsqrt(square)
        hessen[j + 1, j] = square * inverse
        if j + 1 < KRYLOV:
            basis.append([x * inverse for x in w])
            images.append(times_gram(basis[-1]))
    n = KRYLOV
    normal = {}
    for a in range(n):
        for b in range(a + 1):
            normal[a, b] = functools.reduce(
                jnp.add,
                [hessen[i, a] * hessen[i, b] for i in range(n + 1) if (i, a) in hessen and (i, b) in hessen],
            )
    factor = {}
    inverse = []
    for a in range(n):
        for b in range(a + 1):
            value = normal[a, b]
            for m in range(b):
                value = value - factor[a, m] * factor[b, m]
            if a == b:
                inverse.append(lax.rsqrt(value))
            else:
                factor[a, b] = value * inverse[b]
    forward = []
    for a in range(n):
        value = hessen[0, a] * beta
        for m in range(a):
            value = value - factor[a, m] * forward[m]
        forward.append(value * inverse[a])
    backward = [None] * n
    for a in reversed(range(n)):
        value = forward[a]
        for m in range(a + 1, n):
            value = value - factor[m, a] * backward[m]
        backward[a] = value * inverse[a]
    return [
        functools.reduce(jnp.add, [backward[j] * basis[j][i] for j in range(i, n)]) for i in range(n)
    ]


def state_kernel(
    table_ref, head_ref, soil_ref, lo_ref, hi_ref,
    ext_ref, ks_ref, steep_ref, cap_ref, cond_ref, deriv_ref, store_ref, water_ref,
):
    layers, rows, cols = head_ref.shape
    tables = table_rows(table_ref, rows + 2 * HALO)
    every = slice(0, cols)
    for k in range(layers):
        ends = ends_of(lo_ref, hi_ref, k, STATE_DEPTH, every)
        head = jnp.concatenate([head_ref[k], ends], axis=0)
        ends = ends_of(lo_ref, hi_ref, layers + k, STATE_DEPTH, every)
        index = jnp.concatenate([soil_ref[k] + 1, ends.astype(jnp.int32)], axis=0)
        conduct, steep, capacity = (lookup(row, index) for row in tables)
        values = (head, conduct, steep, capacity) + pointwise(head, conduct, steep, capacity)
        outs = (ext_ref, ks_ref, steep_ref, cap_ref, cond_ref, deriv_ref, store_ref, water_ref)
        for ref, value in zip(outs, values):
            ref[k] = value


def first_kernel(
    table_ref, src_ref, slo_ref, shi_ref, ylo_ref, yhi_ref,
    ext_ref, ks_ref, cond_ref, deriv_ref, store_ref, water_ref,
    ext_side, ks_side, steep_side, cap_side, base_ref, p0_ref, p1_ref, p2_ref, gram_ref,
    cond_side, deriv_side, store_side, water_side, *coefs,
):
    layers, rows, cols = src_ref.shape
    tables = table_rows(table_ref, rows + 2 * HALO)
    for k in range(layers):
        head = side(ylo_ref, yhi_ref, 0, k)
        index = side(ylo_ref, yhi_ref, 1, k).astype(jnp.int32)
        conduct, steep, capacity = (lookup(row, index) for row in tables)
        values = (head, conduct, steep, capacity) + pointwise(head, conduct, steep, capacity)
        outs = (ext_side, ks_side, steep_side, cap_side, cond_side, deriv_side, store_side, water_side)
        for ref, value in zip(outs, values):
            ref[k] = value
    water_of = joined(water_ref, water_side)

    def gain_of(k):
        source = jnp.concatenate([src_ref[k], ends_of(slo_ref, shi_ref, k, SOURCE_DEPTH, slice(0, cols))], axis=0)
        source = jnp.concatenate([source, side(ylo_ref, yhi_ref, 2, k)], axis=1)
        water = water_of(k)
        base_ref[k] = water + source
        return water - base_ref[k]

    linearize(
        layers, joined(ext_ref, ext_side), joined(cond_ref, cond_side), joined(deriv_ref, deriv_side),
        joined(store_ref, store_side), gain_of,
        (joined(ks_ref, ks_side)(0) > 0.0).astype(f32), coefs, p0_ref, (rows, cols),
    )
    powers((p0_ref, p1_ref, p2_ref), coefs, (rows, cols), gram_ref)


def second_kernel(
    arrived_ref, old_ref, ks_ref, steep_ref, cap_ref, old_side, ks_side, steep_side, cap_side,
    base_ref, q0_ref, q1_ref, q2_ref,
    part_ref, p0_ref, p1_ref, p2_ref, gram_ref, ext_ref, cond_ref, deriv_ref, store_ref, gain_ref, *coefs,
):
    layers = old_ref.shape[0]
    rows, cols = part_ref.shape[1:]
    x = solve(arrived_ref)
    old_of, ks_of = joined(old_ref, old_side), joined(ks_ref, ks_side)
    steep_of, cap_of = joined(steep_ref, steep_side), joined(cap_ref, cap_side)
    for k in range(layers):
        head = old_of(k) - x[0] * q0_ref[k] - x[1] * q1_ref[k] - x[2] * q2_ref[k]
        cond, deriv, store, water = pointwise(head, ks_of(k), steep_of(k), cap_of(k))
        ext_ref[k] = head
        part_ref[k] = head[:rows, :cols]
        cond_ref[k] = cond
        deriv_ref[k] = deriv
        store_ref[k] = store
        gain_ref[k] = water - base_ref[k]
    linearize(
        layers, *((lambda k, ref=ref: ref[k]) for ref in (ext_ref, cond_ref, deriv_ref, store_ref, gain_ref)),
        (ks_of(0) > 0.0).astype(f32), coefs, p0_ref, (rows, cols),
    )
    powers((p0_ref, p1_ref, p2_ref), coefs, (rows, cols), gram_ref)


def last_kernel(arrived_ref, part_ref, q0_ref, q1_ref, q2_ref, head_ref):
    layers, rows, cols = part_ref.shape
    x = solve(arrived_ref)
    for k in range(layers):
        own = (k, slice(0, rows), slice(0, cols))
        head_ref[k] = part_ref[k] - x[0] * q0_ref[own] - x[1] * q1_ref[own] - x[2] * q2_ref[own]


def shards(head_old, soil_type, soil_table, forcing, canopy, column_slot):
    layers, rows, cols = head_old.shape
    both = ("gx", "gy")
    devices = lax.axis_size("gx") * lax.axis_size("gy")
    tall, wide = rows + 2 * HALO, cols + LANES
    own, ext = ((layers, rows, cols), f32), ((layers, tall, wide), f32)
    gram_block = ((devices, 1, LANES), f32)

    def exchange(to_lower, to_upper, axis):
        size = lax.axis_size(axis)
        up = [(i, i + 1) for i in range(size - 1)]
        down = [(j, i) for i, j in up]
        return lax.ppermute(to_upper, axis, up), lax.ppermute(to_lower, axis, down)

    def spread(x, axes):
        return lax.all_to_all(x, axes, split_axis=0, concat_axis=0, tiled=True)

    (send,) = call(pack_kernel, [((devices, 8, LANES), f32)], 1)(canopy)
    arrived = spread(send, both)

    def edge(fields, depth):
        return (-(-depth * fields * layers // 8) * 8, cols), f32

    down, up = call(edge_kernel, [edge(2, STATE_DEPTH)] * 2, 2)(head_old, soil_type)
    lo, hi = exchange(down, up, "gx")
    source, sdown, sup, flux = call(
        source_kernel,
        [own] + [edge(1, SOURCE_DEPTH)] * 2 + [((2, rows, cols), f32)],
        6,
        scratch=[pltpu.VMEM((devices // 2, 2 + layers, 8, LANES), f32)],
        in_specs=[smem] + [vmem] * 5,
    )(soil_table, arrived, head_old, soil_type, forcing, column_slot)
    slo, shi = exchange(sdown, sup, "gx")
    main, side_block = ((layers, tall, cols), f32), ((layers, tall, LANES), f32)
    old, ks, steep, cap, cond, deriv, store, water = call(
        state_kernel, [main] * 8, 5, in_specs=[smem] + [vmem] * 4
    )(soil_table, head_old, soil_type, lo, hi)
    ydown, yup = call(strip_kernel, [((3, tall, LANES), f32)] * 2, 7)(
        head_old, soil_type, lo, hi, source, slo, shi
    )
    ylo, yhi = exchange(ydown, yup, "gy")
    held, held_side = [pltpu.VMEM(ext[0], f32)], [pltpu.VMEM(side_block[0], f32)]
    old_s, ks_s, steep_s, cap_s, base, p0, p1, p2, gram = call(
        first_kernel,
        [side_block] * 4 + [ext] * 4 + [gram_block],
        12,
        scratch=held_side * 4 + held * 7,
        in_specs=[smem] + [vmem] * 11,
    )(soil_table, source, slo, shi, ylo, yhi, old, ks, cond, deriv, store, water)
    sums = spread(gram, both)
    part, q0, q1, q2, gram = call(
        second_kernel, [own] + [ext] * 3 + [gram_block], 13, scratch=held * 12
    )(sums, old, ks, steep, cap, old_s, ks_s, steep_s, cap_s, base, p0, p1, p2)
    sums = spread(gram, both)
    (head,) = call(last_kernel, [own], 5)(sums, part, q0, q1, q2)
    return head, flux


def solution(mesh):
    return jax.shard_map(
        shards,
        mesh=mesh,
        in_specs=(
            P(None, "gx", "gy"),
            P(None, "gx", "gy"),
            P(),
            P(None, "gx", "gy"),
            P(None, ("gx", "gy")),
            P("gx", "gy"),
        ),
        out_specs=(P(None, "gx", "gy"), P(None, "gx", "gy")),
        check_vma=False,
    )
```

```python
import functools

import jax
import jax.numpy as jnp
from jax import lax
from jax.experimental import pallas as pl
from jax.experimental.pallas import tpu as pltpu
from jax.sharding import PartitionSpec as P

NEWTON = 2
KRYLOV = 3
HALO = 8
STATE_DEPTH = 7
SOURCE_DEPTH = 6
FIXED = 65535.0
LANES = 128
SLOT = 64

storage_weight = 4.0
norm_epsilon = 1e-06

VMEM_LIMIT = 20 * 1024 * 1024
PAIRS = [(i, j) for i in range(KRYLOV + 1) for j in range(i, KRYLOV + 1)]

f32 = jnp.float32
vmem = pl.BlockSpec(memory_space=pltpu.VMEM)
smem = pl.BlockSpec(memory_space=pltpu.SMEM)


def call(body, outs, n_in, scratch=(), in_specs=None, flops=1000000):
    return pl.pallas_call(
        body,
        out_shape=[jax.ShapeDtypeStruct(s, d) for s, d in outs],
        in_specs=in_specs or [vmem] * n_in,
        out_specs=[vmem] * len(outs),
        scratch_shapes=list(scratch),
        compiler_params=pltpu.CompilerParams(vmem_limit_bytes=VMEM_LIMIT),
        cost_estimate=pl.CostEstimate(flops=flops, bytes_accessed=1000000, transcendentals=0),
    )


def lane_iota(shape):
    return lax.broadcasted_iota(jnp.int32, shape, len(shape) - 1)


def edge_kernel(head_ref, soil_ref, down_ref, up_ref):
    layers, rows, _ = head_ref.shape
    for out_ref, part in ((down_ref, slice(0, STATE_DEPTH)), (up_ref, slice(rows - STATE_DEPTH, rows))):
        for k in range(layers):
            out_ref[STATE_DEPTH * k : STATE_DEPTH * (k + 1)] = head_ref[k][part]
        for k in range(layers):
            at = STATE_DEPTH * (layers + k)
            out_ref[at : at + STATE_DEPTH] = (soil_ref[k] + 1).astype(f32)[part]


def pack_kernel(canopy_ref, send_ref):
    rows = canopy_ref.shape[0]
    low = lane_iota((8, LANES)) < SLOT
    for t in range(canopy_ref.shape[1] // LANES):
        here = slice(t * LANES, (t + 1) * LANES)
        first = canopy_ref[0:8, here]
        rest = jnp.concatenate([canopy_ref[8:rows, here], jnp.zeros((16 - rows, LANES), f32)], axis=0)
        send_ref[2 * t] = jnp.where(low, first, pltpu.roll(rest, SLOT, 1))
        send_ref[2 * t + 1] = jnp.where(low, pltpu.roll(first, SLOT, 1), rest)


def table_rows(table_ref, rows):
    lane = lane_iota((rows, LANES))
    out = []
    for field in range(table_ref.shape[0]):
        row = jnp.zeros((rows, LANES), f32)
        for kind in range(table_ref.shape[1]):
            row = jnp.where(lane == kind + 1, table_ref[field, kind], row)
        out.append(row)
    return out


def lookup(row, index):
    pieces = [
        jnp.take_along_axis(row, index[:, at : at + LANES], axis=1, mode="promise_in_bounds")
        for at in range(0, index.shape[1], LANES)
    ]
    return jnp.concatenate(pieces, axis=1)


def sigmoid(u):
    return 1.0 / (1.0 + jnp.exp(-u))


def source_kernel(
    table_ref, arrived_ref, head_ref, soil_ref, forcing_ref, slot_ref,
    source_ref, flux_ref, tab_ref, factor_ref,
):
    layers, rows, cols = head_ref.shape
    owners = arrived_ref.shape[0]
    pairs = -(-layers // 2)
    low = lane_iota((8, LANES)) < SLOT
    line = lax.broadcasted_iota(jnp.int32, (16, LANES), 0)
    is_root = (line >= 3) & (line < 3 + layers)

    def unpack(t, _):
        first = arrived_ref[2 * t]
        second = arrived_ref[2 * t + 1]
        both = jnp.concatenate(
            [
                jnp.where(low, first, pltpu.roll(second, SLOT, 1)),
                jnp.where(low, pltpu.roll(first, SLOT, 1), second),
            ],
            axis=0,
        )
        leaf_area, albedo, resist = both[0:1], both[1:2], both[2:3]
        root_sum = jnp.sum(jnp.where(is_root, both, 0.0), axis=0, keepdims=True)
        factor = leaf_area / ((leaf_area + resist) * root_sum) * (1.0 / FIXED)
        factor_ref[t] = jnp.broadcast_to(factor, (8, LANES))
        fixed = (both * FIXED + 0.5).astype(jnp.int32)
        for m in range(pairs):
            word = fixed[3 + m : 4 + m]
            if m + pairs < layers:
                word = word | (fixed[3 + m + pairs : 4 + m + pairs] << 16)
            tab_ref[t, m] = jnp.broadcast_to(word, (8, LANES))
        leaf = ((0.5 + 0.3 * leaf_area) * (0.25 * FIXED) + 0.5).astype(jnp.int32)
        bright = ((1.0 - albedo) * FIXED + 0.5).astype(jnp.int32)
        tab_ref[t, pairs] = jnp.broadcast_to(leaf | (bright << 16), (8, LANES))
        return 0

    lax.fori_loop(0, owners // 2, unpack, 0, unroll=16)
    tables = table_rows(table_ref, 8)

    for at_x in range(0, rows, 8):

        def column(j, _):
            here = (slice(at_x, at_x + 8), pl.ds(pl.multiple_of(j * LANES, LANES), LANES))
            slot = slot_ref[here]
            land = slot >= 0
            value = jnp.maximum(slot, 0)
            lane = value & (LANES - 1)
            tile = value >> 7

            def pick(t, held):
                match = tile == t
                found = [lookup(tab_ref[t, m], lane) for m in range(pairs + 1)]
                found.append(lookup(factor_ref[t], lane))
                return tuple(jnp.where(match, new, old) for new, old in zip(found, held))

            start = [jnp.full((8, LANES), 1, jnp.int32)] * (pairs + 1)
            start.append(jnp.full((8, LANES), 1.0 / FIXED, f32))
            *words, terms, factor = lax.fori_loop(0, owners // 2, pick, tuple(start), unroll=8)

            def halves(word):
                upper = lax.shift_right_logical(word, jnp.full((8, LANES), 16, jnp.int32))
                return (word & 0xFFFF).astype(f32), upper.astype(f32)

            leaf, bright = halves(terms)
            exchange_coef = leaf * (4.0 / FIXED)
            absorbed = bright * (1.0 / FIXED)
            split = [halves(word) for word in words]
            roots = [factor * split[k % pairs][k // pairs] for k in range(layers)]
            uptake = []
            for k in range(layers):
                index = soil_ref[(k,) + here] + 1
                steep = lookup(tables[1], index)
                uptake.append(roots[k] * sigmoid(steep * head_ref[(k,) + here]))
                if k == 0:
                    ks_top = lookup(tables[0], index)
            conductance = functools.reduce(jnp.add, uptake)
            sunlight, air_temp, humidity, rainfall = (forcing_ref[(i,) + here] for i in range(4))
            radiation = absorbed * sunlight + 0.3
            square = air_temp * air_temp
            excess = radiation - 0.3 * square * square - conductance * (0.5 - humidity)
            slope = -1.2 * square * air_temp - exchange_coef - conductance
            rise = -excess / slope
            surface = air_temp + rise
            vapour = 0.5 * jnp.exp(2.0 * rise)
            square = surface * surface
            excess = (
                radiation
                - 0.3 * square * square
                - exchange_coef * rise
                - conductance * (vapour - humidity)
            )
            slope = -1.2 * square * surface - exchange_coef - 2.0 * conductance * vapour
            rise = rise - excess / slope
            rate = 0.5 * jnp.exp(2.0 * rise) - humidity
            infiltration = rainfall * ks_top / (rainfall + ks_top)
            infiltration = jnp.where(land, infiltration, 0.0)
            rate = jnp.where(land, rate, 0.0)
            flux_ref[(0,) + here] = conductance * rate
            flux_ref[(1,) + here] = infiltration
            for k in range(layers):
                value = -rate * uptake[k]
                if k == 0:
                    value = value + infiltration
                source_ref[(k,) + here] = value
            return 0

        lax.fori_loop(0, cols // LANES, column, 0)


def strips(planes, shift_from):
    packed = None
    for k, plane in enumerate(planes):
        lane = lane_iota(plane.shape)
        shift = (HALO * k - shift_from) % LANES
        moved = pltpu.roll(plane, shift, 1) if shift else plane
        inside = (lane >= HALO * k) & (lane < HALO * (k + 1))
        packed = jnp.where(inside, moved, 0.0 if packed is None else packed)
    return packed


def strip_parts(cols):
    return ((slice(0, LANES), 0), (slice(cols - LANES, cols), LANES - HALO))


def ends_of(lo_ref, hi_ref, at, depth, part):
    edge = slice(depth * at, depth * (at + 1))
    above, below = hi_ref[edge, part], lo_ref[edge, part]
    gap = jnp.zeros((2 * (HALO - depth), above.shape[1]), f32)
    return jnp.concatenate([above, gap, below], axis=0)


def strip_kernel(head_ref, soil_ref, src_ref, down_ref, up_ref):
    layers, _, cols = head_ref.shape
    for out_ref, (part, shift) in zip((down_ref, up_ref), strip_parts(cols)):
        out_ref[0] = strips([head_ref[k, :, part] for k in range(layers)], shift)
        out_ref[1] = strips([(soil_ref[k, :, part] + 1).astype(f32) for k in range(layers)], shift)
        out_ref[2] = strips([src_ref[k, :, part] for k in range(layers)], shift)


def source_edge_kernel(src_ref, ylo_ref, yhi_ref, down_ref, up_ref):
    layers, rows, _ = src_ref.shape
    at = SOURCE_DEPTH * layers
    for out_ref, first in ((down_ref, 0), (up_ref, rows - HALO)):
        row = 0 if first == 0 else rows - SOURCE_DEPTH
        for k in range(layers):
            part = slice(SOURCE_DEPTH * k, SOURCE_DEPTH * (k + 1))
            out_ref[part] = src_ref[k][row : row + SOURCE_DEPTH]
        blocks = [ref[f, first : first + HALO] for f in range(3) for ref in (ylo_ref, yhi_ref)]
        half = HALO // 2
        tail = [block[h : h + half] for block in blocks[4:6] for h in (0, half)]
        for j in range(4):
            out_ref[at : at + HALO, j * LANES : (j + 1) * LANES] = blocks[j]
            out_ref[at + HALO : at + HALO + half, j * LANES : (j + 1) * LANES] = tail[j]


def corner(edge_ref, at, field, which):
    half = HALO // 2
    if field < 2:
        j = 2 * field + which
        return edge_ref[at : at + HALO, j * LANES : (j + 1) * LANES]
    pieces = [
        edge_ref[at + HALO : at + HALO + half, j * LANES : (j + 1) * LANES]
        for j in (2 * which, 2 * which + 1)
    ]
    return jnp.concatenate(pieces, axis=0)


def tall_strips(layers, ylo_ref, yhi_ref, slo_ref, shi_ref):
    at = SOURCE_DEPTH * layers
    out = []
    for field in range(3):
        pair = []
        for which, ref in ((1, yhi_ref), (0, ylo_ref)):
            ends = [corner(shi_ref, at, field, which), corner(slo_ref, at, field, which)]
            pair.append(jnp.concatenate([ref[field]] + ends, axis=0))
        out.append(pair)
    return out


def side(strip, k):
    right, left = strip
    lane = lane_iota(right.shape)
    shift = (-HALO * k) % LANES
    right = pltpu.roll(right, shift, 1) if shift else right
    left = pltpu.roll(left, (LANES - HALO - HALO * k) % LANES, 1)
    return jnp.where(lane < HALO, right, jnp.where(lane >= LANES - HALO, left, 0.0))


def after(x, axis):
    return pltpu.roll(x, x.shape[axis] - 1, axis)


def before(x, axis):
    return pltpu.roll(x, 1, axis)


def pointwise(head, conduct, steep, capacity):
    sat = 0.5 + 0.5 * jnp.tanh(0.5 * (steep * head))
    slope = steep * sat * (1.0 - sat)
    cond = conduct * (0.1 + 0.9 * sat * sat)
    deriv = 0.9 * conduct * sat * slope
    weighted = storage_weight * capacity
    return cond, deriv, weighted * slope, weighted * sat


def joined(main_ref, side_ref):
    return lambda k: jnp.concatenate([main_ref[k], side_ref[k]], axis=1)


def linearize(layers, head_of, cond_of, deriv_of, store_of, gain_of, mask, coefs, out_ref, tile):
    diag_ref, xp_ref, xm_ref, yp_ref, ym_ref, az_ref, bz_ref = coefs
    rows, cols = tile

    def masked(value):
        own = value[:rows, cols:] * mask[:rows, cols:]
        top = jnp.concatenate([value[:rows, :cols], own], axis=1)
        return jnp.concatenate([top, value[rows:] * mask[rows:]], axis=0)

    above = None
    for k in range(layers):
        head = head_of(k)
        cond = cond_of(k)
        deriv = deriv_of(k)
        value = gain_of(k)
        diag = store_of(k)
        for plus_ref, minus_ref, axis in ((xp_ref, xm_ref, 0), (yp_ref, ym_ref, 1)):
            mean = 0.5 * (cond + after(cond, axis))
            drop = head - after(head, axis)
            a = mean + deriv * drop
            b = mean - after(deriv, axis) * drop
            face = mean * drop
            value = value + (face - before(face, axis))
            diag = diag + (a + before(b, axis))
            plus_ref[k] = masked(b)
            minus_ref[k] = masked(before(a, axis))
        if k + 1 < layers:
            mean = 0.5 * (cond + cond_of(k + 1))
            drop = head - head_of(k + 1) + 1.0
            a = mean + deriv * drop
            b = mean - deriv_of(k + 1) * drop
            az_ref[k] = a
            bz_ref[k] = b
            face = mean * drop
        else:
            a = 2.0 * deriv
            face = cond
        diag = diag + a
        value = value + face
        if above is not None:
            diag = diag + above[1]
            value = value - above[0]
        above = (face, b)
        diag_ref[k] = diag
        out_ref[k] = masked(value)


def apply(v_ref, coefs, k):
    diag_ref, xp_ref, xm_ref, yp_ref, ym_ref, az_ref, bz_ref = coefs
    v = v_ref[k]
    value = diag_ref[k] * v
    value = value - xp_ref[k] * after(v, 0) - xm_ref[k] * before(v, 0)
    value = value - yp_ref[k] * after(v, 1) - ym_ref[k] * before(v, 1)
    if k > 0:
        value = value - az_ref[k - 1] * v_ref[k - 1]
    if k + 1 < v_ref.shape[0]:
        value = value - bz_ref[k] * v_ref[k + 1]
    return value


def powers(basis, coefs, tile, out_ref):
    layers = basis[0].shape[0]
    rows, cols = tile
    for step in range(KRYLOV - 1):
        for k in range(layers):
            basis[step + 1][k] = apply(basis[step], coefs, k)
    sums = [jnp.zeros((8, LANES), f32) for _ in PAIRS]
    for k in range(layers):
        top = apply(basis[-1], coefs, k)
        for at in range(0, rows, 8):
            for lane_at in range(0, cols, LANES):
                part = (slice(at, at + 8), slice(lane_at, lane_at + LANES))
                vs = [b[(k,) + part] for b in basis] + [top[part]]
                for e, (i, j) in enumerate(PAIRS):
                    sums[e] = sums[e] + vs[i] * vs[j]
    lines = [jnp.sum(x, axis=0, keepdims=True) for x in sums]
    lines.append(jnp.zeros((16 - len(PAIRS), LANES), f32))
    block = jnp.sum(jnp.concatenate(lines, axis=0), axis=1, keepdims=True)
    line = lax.broadcasted_iota(jnp.int32, (16, LANES), 0)
    flat = jnp.sum(jnp.where(lane_iota((16, LANES)) == line, block, 0.0), axis=0, keepdims=True)
    for d in range(out_ref.shape[0]):
        out_ref[d] = flat


def solve(gram_ref):
    total = gram_ref[0]
    for d in range(1, gram_ref.shape[0]):
        total = total + gram_ref[d]
    line = lax.broadcasted_iota(jnp.int32, (16, LANES), 0)
    spread = jnp.broadcast_to(total, (16, LANES))
    column = jnp.sum(jnp.where(lane_iota((16, LANES)) == line, spread, 0.0), axis=1, keepdims=True)
    gram = {}
    for e, (i, j) in enumerate(PAIRS):
        gram[i, j] = gram[j, i] = column[e : e + 1, :]

    def times_gram(c):
        out = []
        for i in range(KRYLOV + 1):
            out.append(functools.reduce(jnp.add, [gram[i, m] * c[m] for m in range(len(c))]))
        return out

    def dot(a, b):
        return functools.reduce(jnp.add, [x * y for x, y in zip(a, b)])

    square = gram[0, 0] + norm_epsilon
    inverse = lax.rsqrt(square)
    beta = square * inverse
    basis = [[inverse]]
    images = [times_gram(basis[0])]
    hessen = {}
    for j in range(KRYLOV):
        w = [jnp.zeros_like(beta)] + basis[j]
        for i in range(j + 1):
            product = dot(w, images[i])
            hessen[i, j] = product
            w = [w[m] - product * basis[i][m] if m < len(basis[i]) else w[m] for m in range(len(w))]
        square = jnp.maximum(dot(w, times_gram(w)), 0.0) + norm_epsilon
        inverse = lax.rsqrt(square)
        hessen[j + 1, j] = square * inverse
        if j + 1 < KRYLOV:
            basis.append([x * inverse for x in w])
            images.append(times_gram(basis[-1]))
    n = KRYLOV
    normal = {}
    for a in range(n):
        for b in range(a + 1):
            normal[a, b] = functools.reduce(
                jnp.add,
                [hessen[i, a] * hessen[i, b] for i in range(n + 1) if (i, a) in hessen and (i, b) in hessen],
            )
    factor = {}
    inverse = []
    for a in range(n):
        for b in range(a + 1):
            value = normal[a, b]
            for m in range(b):
                value = value - factor[a, m] * factor[b, m]
            if a == b:
                inverse.append(lax.rsqrt(value))
            else:
                factor[a, b] = value * inverse[b]
    forward = []
    for a in range(n):
        value = hessen[0, a] * beta
        for m in range(a):
            value = value - factor[a, m] * forward[m]
        forward.append(value * inverse[a])
    backward = [None] * n
    for a in reversed(range(n)):
        value = forward[a]
        for m in range(a + 1, n):
            value = value - factor[m, a] * backward[m]
        backward[a] = value * inverse[a]
    return [
        functools.reduce(jnp.add, [backward[j] * basis[j][i] for j in range(i, n)]) for i in range(n)
    ]


def state_kernel(
    table_ref, head_ref, soil_ref, lo_ref, hi_ref,
    ext_ref, ks_ref, steep_ref, cap_ref, cond_ref, deriv_ref, store_ref, water_ref,
):
    layers, rows, cols = head_ref.shape
    tables = table_rows(table_ref, rows + 2 * HALO)
    every = slice(0, cols)
    for k in range(layers):
        ends = ends_of(lo_ref, hi_ref, k, STATE_DEPTH, every)
        head = jnp.concatenate([head_ref[k], ends], axis=0)
        ends = ends_of(lo_ref, hi_ref, layers + k, STATE_DEPTH, every)
        index = jnp.concatenate([soil_ref[k] + 1, ends.astype(jnp.int32)], axis=0)
        conduct, steep, capacity = (lookup(row, index) for row in tables)
        values = (head, conduct, steep, capacity) + pointwise(head, conduct, steep, capacity)
        outs = (ext_ref, ks_ref, steep_ref, cap_ref, cond_ref, deriv_ref, store_ref, water_ref)
        for ref, value in zip(outs, values):
            ref[k] = value


def first_kernel(
    table_ref, src_ref, slo_ref, shi_ref, ylo_ref, yhi_ref,
    ext_ref, ks_ref, cond_ref, deriv_ref, store_ref, water_ref,
    ext_side, ks_side, steep_side, cap_side, base_ref, p0_ref, p1_ref, p2_ref, gram_ref,
    cond_side, deriv_side, store_side, water_side, *coefs,
):
    layers, rows, cols = src_ref.shape
    tables = table_rows(table_ref, rows + 2 * HALO)
    heads, soils, sources = tall_strips(layers, ylo_ref, yhi_ref, slo_ref, shi_ref)
    for k in range(layers):
        head = side(heads, k)
        index = side(soils, k).astype(jnp.int32)
        conduct, steep, capacity = (lookup(row, index) for row in tables)
        values = (head, conduct, steep, capacity) + pointwise(head, conduct, steep, capacity)
        outs = (ext_side, ks_side, steep_side, cap_side, cond_side, deriv_side, store_side, water_side)
        for ref, value in zip(outs, values):
            ref[k] = value
    water_of = joined(water_ref, water_side)

    def gain_of(k):
        source = jnp.concatenate([src_ref[k], ends_of(slo_ref, shi_ref, k, SOURCE_DEPTH, slice(0, cols))], axis=0)
        source = jnp.concatenate([source, side(sources, k)], axis=1)
        water = water_of(k)
        base_ref[k] = water + source
        return water - base_ref[k]

    linearize(
        layers, joined(ext_ref, ext_side), joined(cond_ref, cond_side), joined(deriv_ref, deriv_side),
        joined(store_ref, store_side), gain_of,
        (joined(ks_ref, ks_side)(0) > 0.0).astype(f32), coefs, p0_ref, (rows, cols),
    )
    powers((p0_ref, p1_ref, p2_ref), coefs, (rows, cols), gram_ref)


def second_kernel(
    arrived_ref, old_ref, ks_ref, steep_ref, cap_ref, old_side, ks_side, steep_side, cap_side,
    base_ref, q0_ref, q1_ref, q2_ref,
    part_ref, p0_ref, p1_ref, p2_ref, gram_ref, ext_ref, cond_ref, deriv_ref, store_ref, gain_ref, *coefs,
):
    layers = old_ref.shape[0]
    rows, cols = part_ref.shape[1:]
    x = solve(arrived_ref)
    old_of, ks_of = joined(old_ref, old_side), joined(ks_ref, ks_side)
    steep_of, cap_of = joined(steep_ref, steep_side), joined(cap_ref, cap_side)
    for k in range(layers):
        head = old_of(k) - x[0] * q0_ref[k] - x[1] * q1_ref[k] - x[2] * q2_ref[k]
        cond, deriv, store, water = pointwise(head, ks_of(k), steep_of(k), cap_of(k))
        ext_ref[k] = head
        part_ref[k] = head[:rows, :cols]
        cond_ref[k] = cond
        deriv_ref[k] = deriv
        store_ref[k] = store
        gain_ref[k] = water - base_ref[k]
    linearize(
        layers, *((lambda k, ref=ref: ref[k]) for ref in (ext_ref, cond_ref, deriv_ref, store_ref, gain_ref)),
        (ks_of(0) > 0.0).astype(f32), coefs, p0_ref, (rows, cols),
    )
    powers((p0_ref, p1_ref, p2_ref), coefs, (rows, cols), gram_ref)


def last_kernel(arrived_ref, part_ref, q0_ref, q1_ref, q2_ref, head_ref):
    layers, rows, cols = part_ref.shape
    x = solve(arrived_ref)
    for k in range(layers):
        own = (k, slice(0, rows), slice(0, cols))
        head_ref[k] = part_ref[k] - x[0] * q0_ref[own] - x[1] * q1_ref[own] - x[2] * q2_ref[own]


def shards(head_old, soil_type, soil_table, forcing, canopy, column_slot):
    layers, rows, cols = head_old.shape
    both = ("gx", "gy")
    devices = lax.axis_size("gx") * lax.axis_size("gy")
    tall, wide = rows + 2 * HALO, cols + LANES
    own, ext = ((layers, rows, cols), f32), ((layers, tall, wide), f32)
    gram_block = ((devices, 1, LANES), f32)

    def exchange(to_lower, to_upper, axis):
        size = lax.axis_size(axis)
        up = [(i, i + 1) for i in range(size - 1)]
        down = [(j, i) for i, j in up]
        return lax.ppermute(to_upper, axis, up), lax.ppermute(to_lower, axis, down)

    def spread(x, axes):
        return lax.all_to_all(x, axes, split_axis=0, concat_axis=0, tiled=True)

    (send,) = call(pack_kernel, [((devices, 8, LANES), f32)], 1)(canopy)
    arrived = spread(send, both)

    def edge(count):
        return (-(-count // 8) * 8, cols), f32

    down, up = call(edge_kernel, [edge(2 * STATE_DEPTH * layers)] * 2, 2)(head_old, soil_type)
    lo, hi = exchange(down, up, "gx")
    source, flux = call(
        source_kernel,
        [own, ((2, rows, cols), f32)],
        6,
        scratch=[
            pltpu.VMEM((devices // 2, -(-layers // 2) + 1, 8, LANES), jnp.int32),
            pltpu.VMEM((devices // 2, 8, LANES), f32),
        ],
        in_specs=[smem] + [vmem] * 5,
    )(soil_table, arrived, head_old, soil_type, forcing, column_slot)
    ydown, yup = call(strip_kernel, [((3, rows, LANES), f32)] * 2, 3)(head_old, soil_type, source)
    ylo, yhi = exchange(ydown, yup, "gy")
    sdown, sup = call(source_edge_kernel, [edge(SOURCE_DEPTH * layers + HALO + HALO // 2)] * 2, 3)(
        source, ylo, yhi
    )
    slo, shi = exchange(sdown, sup, "gx")
    main, side_block = ((layers, tall, cols), f32), ((layers, tall, LANES), f32)
    old, ks, steep, cap, cond, deriv, store, water = call(
        state_kernel, [main] * 8, 5, in_specs=[smem] + [vmem] * 4
    )(soil_table, head_old, soil_type, lo, hi)
    held, held_side = [pltpu.VMEM(ext[0], f32)], [pltpu.VMEM(side_block[0], f32)]
    old_s, ks_s, steep_s, cap_s, base, p0, p1, p2, gram = call(
        first_kernel,
        [side_block] * 4 + [ext] * 4 + [gram_block],
        12,
        scratch=held_side * 4 + held * 7,
        in_specs=[smem] + [vmem] * 11,
    )(soil_table, source, slo, shi, ylo, yhi, old, ks, cond, deriv, store, water)
    sums = spread(gram, both)
    part, q0, q1, q2, gram = call(
        second_kernel, [own] + [ext] * 3 + [gram_block], 13, scratch=held * 12
    )(sums, old, ks, steep, cap, old_s, ks_s, steep_s, cap_s, base, p0, p1, p2)
    sums = spread(gram, both)
    (head,) = call(last_kernel, [own], 5)(sums, part, q0, q1, q2)
    return head, flux


def solution(mesh):
    return jax.shard_map(
        shards,
        mesh=mesh,
        in_specs=(
            P(None, "gx", "gy"),
            P(None, "gx", "gy"),
            P(),
            P(None, "gx", "gy"),
            P(None, ("gx", "gy")),
            P("gx", "gy"),
        ),
        out_specs=(P(None, "gx", "gy"), P(None, "gx", "gy")),
        check_vma=False,
    )
```

```python
import functools

import jax
import jax.numpy as jnp
from jax import lax
from jax.experimental import pallas as pl
from jax.experimental.pallas import tpu as pltpu
from jax.sharding import PartitionSpec as P

NEWTON = 2
KRYLOV = 3
HALO = 8
STATE_DEPTH = 7
SOURCE_DEPTH = 6
FIXED = 65535.0
LANES = 128
SLOT = 64

storage_weight = 4.0
norm_epsilon = 1e-06

VMEM_LIMIT = 20 * 1024 * 1024
PAIRS = [(i, j) for i in range(KRYLOV + 1) for j in range(i, KRYLOV + 1)]

f32 = jnp.float32
vmem = pl.BlockSpec(memory_space=pltpu.VMEM)
smem = pl.BlockSpec(memory_space=pltpu.SMEM)


def call(body, outs, n_in, scratch=(), in_specs=None, flops=1000000):
    return pl.pallas_call(
        body,
        out_shape=[jax.ShapeDtypeStruct(s, d) for s, d in outs],
        in_specs=in_specs or [vmem] * n_in,
        out_specs=[vmem] * len(outs),
        scratch_shapes=list(scratch),
        compiler_params=pltpu.CompilerParams(vmem_limit_bytes=VMEM_LIMIT),
        cost_estimate=pl.CostEstimate(flops=flops, bytes_accessed=1000000, transcendentals=0),
    )


def lane_iota(shape):
    return lax.broadcasted_iota(jnp.int32, shape, len(shape) - 1)


def edge_kernel(head_ref, soil_ref, down_ref, up_ref):
    layers, rows, _ = head_ref.shape
    for out_ref, part in ((down_ref, slice(0, STATE_DEPTH)), (up_ref, slice(rows - STATE_DEPTH, rows))):
        for k in range(layers):
            out_ref[STATE_DEPTH * k : STATE_DEPTH * (k + 1)] = head_ref[k][part]
        for k in range(layers):
            at = STATE_DEPTH * (layers + k)
            out_ref[at : at + STATE_DEPTH] = (soil_ref[k] + 1).astype(f32)[part]


def pack_kernel(canopy_ref, send_ref):
    rows = canopy_ref.shape[0]
    low = lane_iota((8, LANES)) < SLOT
    for t in range(canopy_ref.shape[1] // LANES):
        here = slice(t * LANES, (t + 1) * LANES)
        first = canopy_ref[0:8, here]
        rest = jnp.concatenate([canopy_ref[8:rows, here], jnp.zeros((16 - rows, LANES), f32)], axis=0)
        send_ref[2 * t] = jnp.where(low, first, pltpu.roll(rest, SLOT, 1))
        send_ref[2 * t + 1] = jnp.where(low, pltpu.roll(first, SLOT, 1), rest)


def table_rows(table_ref, rows):
    lane = lane_iota((rows, LANES))
    out = []
    for field in range(table_ref.shape[0]):
        row = jnp.zeros((rows, LANES), f32)
        for kind in range(table_ref.shape[1]):
            row = jnp.where(lane == kind + 1, table_ref[field, kind], row)
        out.append(row)
    return out


def lookup(row, index):
    pieces = [
        jnp.take_along_axis(row, index[:, at : at + LANES], axis=1, mode="promise_in_bounds")
        for at in range(0, index.shape[1], LANES)
    ]
    return jnp.concatenate(pieces, axis=1)


def sigmoid(u):
    return 1.0 / (1.0 + jnp.exp(-u))


def source_kernel(
    table_ref, arrived_ref, head_ref, soil_ref, forcing_ref, slot_ref,
    source_ref, flux_ref, tab_ref, factor_ref,
):
    layers, rows, cols = head_ref.shape
    owners = arrived_ref.shape[0]
    pairs = -(-layers // 2)
    low = lane_iota((8, LANES)) < SLOT
    line = lax.broadcasted_iota(jnp.int32, (16, LANES), 0)
    is_root = (line >= 3) & (line < 3 + layers)

    def unpack(t, _):
        first = arrived_ref[2 * t]
        second = arrived_ref[2 * t + 1]
        both = jnp.concatenate(
            [
                jnp.where(low, first, pltpu.roll(second, SLOT, 1)),
                jnp.where(low, pltpu.roll(first, SLOT, 1), second),
            ],
            axis=0,
        )
        leaf_area, albedo, resist = both[0:1], both[1:2], both[2:3]
        root_sum = jnp.sum(jnp.where(is_root, both, 0.0), axis=0, keepdims=True)
        factor = leaf_area / ((leaf_area + resist) * root_sum) * (1.0 / FIXED)
        factor_ref[t] = jnp.broadcast_to(factor, (8, LANES))
        fixed = (both * FIXED + 0.5).astype(jnp.int32)
        for m in range(pairs):
            word = fixed[3 + m : 4 + m]
            if m + pairs < layers:
                word = word | (fixed[3 + m + pairs : 4 + m + pairs] << 16)
            tab_ref[t, m] = jnp.broadcast_to(word, (8, LANES))
        leaf = ((0.5 + 0.3 * leaf_area) * (0.25 * FIXED) + 0.5).astype(jnp.int32)
        bright = ((1.0 - albedo) * FIXED + 0.5).astype(jnp.int32)
        tab_ref[t, pairs] = jnp.broadcast_to(leaf | (bright << 16), (8, LANES))
        return 0

    lax.fori_loop(0, owners // 2, unpack, 0, unroll=16)
    tables = table_rows(table_ref, rows)
    shape = (rows, LANES)

    def whole(block):
        return jnp.concatenate([block] * (rows // 8), axis=0)

    for at_y in range(0, cols, LANES):
        here = (slice(0, rows), slice(at_y, at_y + LANES))
        slot = slot_ref[here]
        land = slot >= 0
        value = jnp.maximum(slot, 0)
        lane = value & (LANES - 1)
        tile = value >> 7

        def pick(t, held):
            match = tile == t
            found = [lookup(whole(tab_ref[t, m]), lane) for m in range(pairs + 1)]
            found.append(lookup(whole(factor_ref[t]), lane))
            return tuple(jnp.where(match, new, old) for new, old in zip(found, held))

        held = tuple([jnp.full(shape, 1, jnp.int32)] * (pairs + 1) + [jnp.full(shape, 1.0 / FIXED, f32)])
        if owners <= 32:
            for t in range(owners // 2):
                held = pick(t, held)
        else:
            held = lax.fori_loop(0, owners // 2, pick, held, unroll=8)
        *words, terms, factor = held

        def halves(word):
            upper = lax.shift_right_logical(word, jnp.full(shape, 16, jnp.int32))
            return (word & 0xFFFF).astype(f32), upper.astype(f32)

        leaf, bright = halves(terms)
        exchange_coef = leaf * (4.0 / FIXED)
        absorbed = bright * (1.0 / FIXED)
        split = [halves(word) for word in words]
        uptake = []
        for k in range(layers):
            index = soil_ref[(k,) + here] + 1
            steep = lookup(tables[1], index)
            root = factor * split[k % pairs][k // pairs]
            uptake.append(root * sigmoid(steep * head_ref[(k,) + here]))
            if k == 0:
                ks_top = lookup(tables[0], index)
        conductance = functools.reduce(jnp.add, uptake)
        sunlight, air_temp, humidity, rainfall = (forcing_ref[(i,) + here] for i in range(4))
        radiation = absorbed * sunlight + 0.3
        square = air_temp * air_temp
        excess = radiation - 0.3 * square * square - conductance * (0.5 - humidity)
        slope = -1.2 * square * air_temp - exchange_coef - conductance
        rise = -excess / slope
        surface = air_temp + rise
        vapour = 0.5 * jnp.exp(2.0 * rise)
        square = surface * surface
        excess = (
            radiation
            - 0.3 * square * square
            - exchange_coef * rise
            - conductance * (vapour - humidity)
        )
        slope = -1.2 * square * surface - exchange_coef - 2.0 * conductance * vapour
        rise = rise - excess / slope
        rate = 0.5 * jnp.exp(2.0 * rise) - humidity
        infiltration = rainfall * ks_top / (rainfall + ks_top)
        infiltration = jnp.where(land, infiltration, 0.0)
        rate = jnp.where(land, rate, 0.0)
        flux_ref[(0,) + here] = conductance * rate
        flux_ref[(1,) + here] = infiltration
        for k in range(layers):
            value = -rate * uptake[k]
            if k == 0:
                value = value + infiltration
            source_ref[(k,) + here] = value


def strips(planes, shift_from):
    packed = None
    for k, plane in enumerate(planes):
        lane = lane_iota(plane.shape)
        shift = (HALO * k - shift_from) % LANES
        moved = pltpu.roll(plane, shift, 1) if shift else plane
        inside = (lane >= HALO * k) & (lane < HALO * (k + 1))
        packed = jnp.where(inside, moved, 0.0 if packed is None else packed)
    return packed


def strip_parts(cols):
    return ((slice(0, LANES), 0), (slice(cols - LANES, cols), LANES - HALO))


def ends_of(lo_ref, hi_ref, at, depth, part):
    edge = slice(depth * at, depth * (at + 1))
    above, below = hi_ref[edge, part], lo_ref[edge, part]
    gap = jnp.zeros((2 * (HALO - depth), above.shape[1]), f32)
    return jnp.concatenate([above, gap, below], axis=0)


def strip_kernel(head_ref, soil_ref, src_ref, down_ref, up_ref):
    layers, _, cols = head_ref.shape
    for out_ref, (part, shift) in zip((down_ref, up_ref), strip_parts(cols)):
        out_ref[0] = strips([head_ref[k, :, part] for k in range(layers)], shift)
        out_ref[1] = strips([(soil_ref[k, :, part] + 1).astype(f32) for k in range(layers)], shift)
        out_ref[2] = strips([src_ref[k, :, part] for k in range(layers)], shift)


def source_edge_kernel(src_ref, ylo_ref, yhi_ref, down_ref, up_ref):
    layers, rows, _ = src_ref.shape
    at = SOURCE_DEPTH * layers
    for out_ref, first in ((down_ref, 0), (up_ref, rows - HALO)):
        row = 0 if first == 0 else rows - SOURCE_DEPTH
        for k in range(layers):
            part = slice(SOURCE_DEPTH * k, SOURCE_DEPTH * (k + 1))
            out_ref[part] = src_ref[k][row : row + SOURCE_DEPTH]
        blocks = [ref[f, first : first + HALO] for f in range(3) for ref in (ylo_ref, yhi_ref)]
        half = HALO // 2
        tail = [block[h : h + half] for block in blocks[4:6] for h in (0, half)]
        for j in range(4):
            out_ref[at : at + HALO, j * LANES : (j + 1) * LANES] = blocks[j]
            out_ref[at + HALO : at + HALO + half, j * LANES : (j + 1) * LANES] = tail[j]


def corner(edge_ref, at, field, which):
    half = HALO // 2
    if field < 2:
        j = 2 * field + which
        return edge_ref[at : at + HALO, j * LANES : (j + 1) * LANES]
    pieces = [
        edge_ref[at + HALO : at + HALO + half, j * LANES : (j + 1) * LANES]
        for j in (2 * which, 2 * which + 1)
    ]
    return jnp.concatenate(pieces, axis=0)


def tall_strips(layers, ylo_ref, yhi_ref, slo_ref, shi_ref):
    at = SOURCE_DEPTH * layers
    out = []
    for field in range(3):
        pair = []
        for which, ref in ((1, yhi_ref), (0, ylo_ref)):
            ends = [corner(shi_ref, at, field, which), corner(slo_ref, at, field, which)]
            pair.append(jnp.concatenate([ref[field]] + ends, axis=0))
        out.append(pair)
    return out


def side(strip, k):
    right, left = strip
    lane = lane_iota(right.shape)
    shift = (-HALO * k) % LANES
    right = pltpu.roll(right, shift, 1) if shift else right
    left = pltpu.roll(left, (LANES - HALO - HALO * k) % LANES, 1)
    return jnp.where(lane < HALO, right, jnp.where(lane >= LANES - HALO, left, 0.0))


def after(x, axis):
    return pltpu.roll(x, x.shape[axis] - 1, axis)


def before(x, axis):
    return pltpu.roll(x, 1, axis)


def pointwise(head, conduct, steep, capacity):
    sat = 0.5 + 0.5 * jnp.tanh(0.5 * (steep * head))
    slope = steep * sat * (1.0 - sat)
    cond = conduct * (0.1 + 0.9 * sat * sat)
    deriv = 0.9 * conduct * sat * slope
    weighted = storage_weight * capacity
    return cond, deriv, weighted * slope, weighted * sat


def joined(main_ref, side_ref):
    return lambda k: jnp.concatenate([main_ref[k], side_ref[k]], axis=1)


def linearize(layers, head_of, cond_of, deriv_of, store_of, gain_of, mask, coefs, out_ref, tile):
    diag_ref, xp_ref, xm_ref, yp_ref, ym_ref, az_ref, bz_ref = coefs
    rows, cols = tile

    def masked(value):
        own = value[:rows, cols:] * mask[:rows, cols:]
        top = jnp.concatenate([value[:rows, :cols], own], axis=1)
        return jnp.concatenate([top, value[rows:] * mask[rows:]], axis=0)

    above = None
    for k in range(layers):
        head = head_of(k)
        cond = cond_of(k)
        deriv = deriv_of(k)
        value = gain_of(k)
        diag = store_of(k)
        for plus_ref, minus_ref, axis in ((xp_ref, xm_ref, 0), (yp_ref, ym_ref, 1)):
            mean = 0.5 * (cond + after(cond, axis))
            drop = head - after(head, axis)
            a = mean + deriv * drop
            b = mean - after(deriv, axis) * drop
            face = mean * drop
            value = value + (face - before(face, axis))
            diag = diag + (a + before(b, axis))
            plus_ref[k] = masked(b)
            minus_ref[k] = masked(before(a, axis))
        if k + 1 < layers:
            mean = 0.5 * (cond + cond_of(k + 1))
            drop = head - head_of(k + 1) + 1.0
            a = mean + deriv * drop
            b = mean - deriv_of(k + 1) * drop
            az_ref[k] = a
            bz_ref[k] = b
            face = mean * drop
        else:
            a = 2.0 * deriv
            face = cond
        diag = diag + a
        value = value + face
        if above is not None:
            diag = diag + above[1]
            value = value - above[0]
        above = (face, b)
        diag_ref[k] = diag
        out_ref[k] = masked(value)


def apply(v_ref, coefs, k):
    diag_ref, xp_ref, xm_ref, yp_ref, ym_ref, az_ref, bz_ref = coefs
    v = v_ref[k]
    value = diag_ref[k] * v
    value = value - xp_ref[k] * after(v, 0) - xm_ref[k] * before(v, 0)
    value = value - yp_ref[k] * after(v, 1) - ym_ref[k] * before(v, 1)
    if k > 0:
        value = value - az_ref[k - 1] * v_ref[k - 1]
    if k + 1 < v_ref.shape[0]:
        value = value - bz_ref[k] * v_ref[k + 1]
    return value


def powers(basis, coefs, tile, out_ref):
    layers = basis[0].shape[0]
    rows, cols = tile
    for step in range(KRYLOV - 1):
        for k in range(layers):
            basis[step + 1][k] = apply(basis[step], coefs, k)
    sums = [jnp.zeros((8, LANES), f32) for _ in PAIRS]
    for k in range(layers):
        top = apply(basis[-1], coefs, k)
        for at in range(0, rows, 8):
            for lane_at in range(0, cols, LANES):
                part = (slice(at, at + 8), slice(lane_at, lane_at + LANES))
                vs = [b[(k,) + part] for b in basis] + [top[part]]
                for e, (i, j) in enumerate(PAIRS):
                    sums[e] = sums[e] + vs[i] * vs[j]
    lines = [jnp.sum(x, axis=0, keepdims=True) for x in sums]
    lines.append(jnp.zeros((16 - len(PAIRS), LANES), f32))
    block = jnp.sum(jnp.concatenate(lines, axis=0), axis=1, keepdims=True)
    line = lax.broadcasted_iota(jnp.int32, (16, LANES), 0)
    flat = jnp.sum(jnp.where(lane_iota((16, LANES)) == line, block, 0.0), axis=0, keepdims=True)
    out_ref[0] = flat


def solve(gram_ref):
    terms = [gram_ref[d] for d in range(gram_ref.shape[0])]
    while len(terms) > 1:
        terms = [functools.reduce(jnp.add, terms[i : i + 2]) for i in range(0, len(terms), 2)]
    total = terms[0]
    line = lax.broadcasted_iota(jnp.int32, (16, LANES), 0)
    spread = jnp.broadcast_to(total, (16, LANES))
    column = jnp.sum(jnp.where(lane_iota((16, LANES)) == line, spread, 0.0), axis=1, keepdims=True)
    gram = {}
    for e, (i, j) in enumerate(PAIRS):
        gram[i, j] = gram[j, i] = column[e : e + 1, :]

    def times_gram(c):
        out = []
        for i in range(KRYLOV + 1):
            out.append(functools.reduce(jnp.add, [gram[i, m] * c[m] for m in range(len(c))]))
        return out

    def dot(a, b):
        return functools.reduce(jnp.add, [x * y for x, y in zip(a, b)])

    square = gram[0, 0] + norm_epsilon
    inverse = lax.rsqrt(square)
    beta = square * inverse
    basis = [[inverse]]
    images = [times_gram(basis[0])]
    hessen = {}
    for j in range(KRYLOV):
        w = [jnp.zeros_like(beta)] + basis[j]
        for i in range(j + 1):
            product = dot(w, images[i])
            hessen[i, j] = product
            w = [w[m] - product * basis[i][m] if m < len(basis[i]) else w[m] for m in range(len(w))]
        square = jnp.maximum(dot(w, times_gram(w)), 0.0) + norm_epsilon
        inverse = lax.rsqrt(square)
        hessen[j + 1, j] = square * inverse
        if j + 1 < KRYLOV:
            basis.append([x * inverse for x in w])
            images.append(times_gram(basis[-1]))
    n = KRYLOV
    normal = {}
    for a in range(n):
        for b in range(a + 1):
            normal[a, b] = functools.reduce(
                jnp.add,
                [hessen[i, a] * hessen[i, b] for i in range(n + 1) if (i, a) in hessen and (i, b) in hessen],
            )
    factor = {}
    inverse = []
    for a in range(n):
        for b in range(a + 1):
            value = normal[a, b]
            for m in range(b):
                value = value - factor[a, m] * factor[b, m]
            if a == b:
                inverse.append(lax.rsqrt(value))
            else:
                factor[a, b] = value * inverse[b]
    forward = []
    for a in range(n):
        value = hessen[0, a] * beta
        for m in range(a):
            value = value - factor[a, m] * forward[m]
        forward.append(value * inverse[a])
    backward = [None] * n
    for a in reversed(range(n)):
        value = forward[a]
        for m in range(a + 1, n):
            value = value - factor[m, a] * backward[m]
        backward[a] = value * inverse[a]
    return [
        functools.reduce(jnp.add, [backward[j] * basis[j][i] for j in range(i, n)]) for i in range(n)
    ]


def state_kernel(
    table_ref, head_ref, soil_ref, lo_ref, hi_ref,
    ext_ref, ks_ref, steep_ref, cap_ref, cond_ref, deriv_ref, store_ref, water_ref,
):
    layers, rows, cols = head_ref.shape
    tables = table_rows(table_ref, rows + 2 * HALO)
    every = slice(0, cols)
    for k in range(layers):
        ends = ends_of(lo_ref, hi_ref, k, STATE_DEPTH, every)
        head = jnp.concatenate([head_ref[k], ends], axis=0)
        ends = ends_of(lo_ref, hi_ref, layers + k, STATE_DEPTH, every)
        index = jnp.concatenate([soil_ref[k] + 1, ends.astype(jnp.int32)], axis=0)
        conduct, steep, capacity = (lookup(row, index) for row in tables)
        values = (head, conduct, steep, capacity) + pointwise(head, conduct, steep, capacity)
        outs = (ext_ref, ks_ref, steep_ref, cap_ref, cond_ref, deriv_ref, store_ref, water_ref)
        for ref, value in zip(outs, values):
            ref[k] = value


def first_kernel(
    table_ref, src_ref, slo_ref, shi_ref, ylo_ref, yhi_ref,
    ext_ref, ks_ref, cond_ref, deriv_ref, store_ref, water_ref,
    ext_side, ks_side, steep_side, cap_side, base_ref, p0_ref, p1_ref, p2_ref, gram_ref,
    cond_side, deriv_side, store_side, water_side, *coefs,
):
    layers, rows, cols = src_ref.shape
    tables = table_rows(table_ref, rows + 2 * HALO)
    heads, soils, sources = tall_strips(layers, ylo_ref, yhi_ref, slo_ref, shi_ref)
    for k in range(layers):
        head = side(heads, k)
        index = side(soils, k).astype(jnp.int32)
        conduct, steep, capacity = (lookup(row, index) for row in tables)
        values = (head, conduct, steep, capacity) + pointwise(head, conduct, steep, capacity)
        outs = (ext_side, ks_side, steep_side, cap_side, cond_side, deriv_side, store_side, water_side)
        for ref, value in zip(outs, values):
            ref[k] = value
    water_of = joined(water_ref, water_side)

    def gain_of(k):
        source = jnp.concatenate([src_ref[k], ends_of(slo_ref, shi_ref, k, SOURCE_DEPTH, slice(0, cols))], axis=0)
        source = jnp.concatenate([source, side(sources, k)], axis=1)
        water = water_of(k)
        base_ref[k] = water + source
        return water - base_ref[k]

    linearize(
        layers, joined(ext_ref, ext_side), joined(cond_ref, cond_side), joined(deriv_ref, deriv_side),
        joined(store_ref, store_side), gain_of,
        (joined(ks_ref, ks_side)(0) > 0.0).astype(f32), coefs, p0_ref, (rows, cols),
    )
    powers((p0_ref, p1_ref, p2_ref), coefs, (rows, cols), gram_ref)


def second_kernel(
    arrived_ref, old_ref, ks_ref, steep_ref, cap_ref, old_side, ks_side, steep_side, cap_side,
    base_ref, q0_ref, q1_ref, q2_ref,
    part_ref, p0_ref, p1_ref, p2_ref, gram_ref, ext_ref, cond_ref, deriv_ref, store_ref, gain_ref, *coefs,
):
    layers = old_ref.shape[0]
    rows, cols = part_ref.shape[1:]
    x = solve(arrived_ref)
    near = lax.broadcasted_iota(jnp.int32, (HALO, cols + LANES), 0) < HALO // 2

    def folded(of):
        def get(k):
            value = of(k)
            ends = jnp.where(near, value[rows : rows + HALO], value[rows + HALO :])
            return jnp.concatenate([value[:rows], ends], axis=0)

        return get

    old_of, ks_of = folded(joined(old_ref, old_side)), folded(joined(ks_ref, ks_side))
    steep_of, cap_of = folded(joined(steep_ref, steep_side)), folded(joined(cap_ref, cap_side))
    base_of, *qs = (folded(lambda k, ref=ref: ref[k]) for ref in (base_ref, q0_ref, q1_ref, q2_ref))
    for k in range(layers):
        head = old_of(k)
        for value, q_of in zip(x, qs):
            head = head - value * q_of(k)
        cond, deriv, store, water = pointwise(head, ks_of(k), steep_of(k), cap_of(k))
        ext_ref[k] = head
        part_ref[k] = head[:rows, :cols]
        cond_ref[k] = cond
        deriv_ref[k] = deriv
        store_ref[k] = store
        gain_ref[k] = water - base_of(k)
    linearize(
        layers, *((lambda k, ref=ref: ref[k]) for ref in (ext_ref, cond_ref, deriv_ref, store_ref, gain_ref)),
        (ks_of(0) > 0.0).astype(f32), coefs, p0_ref, (rows, cols),
    )
    powers((p0_ref, p1_ref, p2_ref), coefs, (rows, cols), gram_ref)


def last_kernel(arrived_ref, part_ref, q0_ref, q1_ref, q2_ref, head_ref):
    layers, rows, cols = part_ref.shape
    x = solve(arrived_ref)
    for k in range(layers):
        own = (k, slice(0, rows), slice(0, cols))
        head_ref[k] = part_ref[k] - x[0] * q0_ref[own] - x[1] * q1_ref[own] - x[2] * q2_ref[own]


def shards(head_old, soil_type, soil_table, forcing, canopy, column_slot):
    layers, rows, cols = head_old.shape
    both = ("gx", "gy")
    devices = lax.axis_size("gx") * lax.axis_size("gy")
    tall, wide = rows + 2 * HALO, cols + LANES
    own, ext = ((layers, rows, cols), f32), ((layers, tall, wide), f32)
    gram_block = ((1, 1, LANES), f32)

    def exchange(to_lower, to_upper, axis):
        size = lax.axis_size(axis)
        up = [(i, i + 1) for i in range(size - 1)]
        down = [(j, i) for i, j in up]
        return lax.ppermute(to_upper, axis, up), lax.ppermute(to_lower, axis, down)

    def spread(x, axes):
        return lax.all_to_all(x, axes, split_axis=0, concat_axis=0, tiled=True)

    (send,) = call(pack_kernel, [((devices, 8, LANES), f32)], 1)(canopy)
    arrived = spread(send, both)

    def edge(count):
        return (-(-count // 8) * 8, cols), f32

    down, up = call(edge_kernel, [edge(2 * STATE_DEPTH * layers)] * 2, 2)(head_old, soil_type)
    lo, hi = exchange(down, up, "gx")
    source, flux = call(
        source_kernel,
        [own, ((2, rows, cols), f32)],
        6,
        scratch=[
            pltpu.VMEM((devices // 2, -(-layers // 2) + 1, 8, LANES), jnp.int32),
            pltpu.VMEM((devices // 2, 8, LANES), f32),
        ],
        in_specs=[smem] + [vmem] * 5,
    )(soil_table, arrived, head_old, soil_type, forcing, column_slot)
    ydown, yup = call(strip_kernel, [((3, rows, LANES), f32)] * 2, 3)(head_old, soil_type, source)
    ylo, yhi = exchange(ydown, yup, "gy")
    sdown, sup = call(source_edge_kernel, [edge(SOURCE_DEPTH * layers + HALO + HALO // 2)] * 2, 3)(
        source, ylo, yhi
    )
    slo, shi = exchange(sdown, sup, "gx")
    main, side_block = ((layers, tall, cols), f32), ((layers, tall, LANES), f32)
    old, ks, steep, cap, cond, deriv, store, water = call(
        state_kernel, [main] * 8, 5, in_specs=[smem] + [vmem] * 4
    )(soil_table, head_old, soil_type, lo, hi)
    held, held_side = [pltpu.VMEM(ext[0], f32)], [pltpu.VMEM(side_block[0], f32)]
    old_s, ks_s, steep_s, cap_s, base, p0, p1, p2, gram = call(
        first_kernel,
        [side_block] * 4 + [ext] * 4 + [gram_block],
        12,
        scratch=held_side * 4 + held * 7,
        in_specs=[smem] + [vmem] * 11,
    )(soil_table, source, slo, shi, ylo, yhi, old, ks, cond, deriv, store, water)
    sums = lax.all_gather(gram, both, axis=0, tiled=True)
    part, q0, q1, q2, gram = call(
        second_kernel,
        [own] + [((layers, rows + HALO, wide), f32)] * 3 + [gram_block],
        13,
        scratch=[pltpu.VMEM((layers, rows + HALO, wide), f32)] * 12,
    )(sums, old, ks, steep, cap, old_s, ks_s, steep_s, cap_s, base, p0, p1, p2)
    sums = lax.all_gather(gram, both, axis=0, tiled=True)
    (head,) = call(last_kernel, [own], 5)(sums, part, q0, q1, q2)
    return head, flux


def solution(mesh):
    return jax.shard_map(
        shards,
        mesh=mesh,
        in_specs=(
            P(None, "gx", "gy"),
            P(None, "gx", "gy"),
            P(),
            P(None, "gx", "gy"),
            P(None, ("gx", "gy")),
            P("gx", "gy"),
        ),
        out_specs=(P(None, "gx", "gy"), P(None, "gx", "gy")),
        check_vma=False,
    )
```

```python
import functools

import jax
import jax.numpy as jnp
from jax import lax
from jax.experimental import pallas as pl
from jax.experimental.pallas import tpu as pltpu
from jax.sharding import PartitionSpec as P

NEWTON = 2
KRYLOV = 3
HALO = 8
STATE_DEPTH = 7
SOURCE_DEPTH = 6
FIXED = 65535.0
LANES = 128
SLOT = 64

storage_weight = 4.0
norm_epsilon = 1e-06

VMEM_LIMIT = 20 * 1024 * 1024
PAIRS = [(i, j) for i in range(KRYLOV + 1) for j in range(i, KRYLOV + 1)]

f32 = jnp.float32
vmem = pl.BlockSpec(memory_space=pltpu.VMEM)
smem = pl.BlockSpec(memory_space=pltpu.SMEM)


def call(body, outs, n_in, scratch=(), in_specs=None, flops=1000000, grant=VMEM_LIMIT):
    return pl.pallas_call(
        body,
        out_shape=[jax.ShapeDtypeStruct(s, d) for s, d in outs],
        in_specs=in_specs or [vmem] * n_in,
        out_specs=[vmem] * len(outs),
        scratch_shapes=list(scratch),
        compiler_params=pltpu.CompilerParams(vmem_limit_bytes=grant),
        cost_estimate=pl.CostEstimate(flops=flops, bytes_accessed=1000000, transcendentals=0),
    )


def lane_iota(shape):
    return lax.broadcasted_iota(jnp.int32, shape, len(shape) - 1)


def pack_kernel(
    canopy_hbm, head_hbm, soil_hbm, send_ref, down_ref, up_ref, canopy_ref, head_ref, soil_ref, sems
):
    copies = [
        pltpu.make_async_copy(canopy_hbm, canopy_ref, sems.at[0]),
        pltpu.make_async_copy(head_hbm, head_ref, sems.at[1]),
        pltpu.make_async_copy(soil_hbm, soil_ref, sems.at[2]),
    ]
    for copy in copies:
        copy.start()
    copies[0].wait()
    rows = canopy_ref.shape[0]
    low = lane_iota((8, LANES)) < SLOT
    for t in range(canopy_ref.shape[1] // LANES):
        here = slice(t * LANES, (t + 1) * LANES)
        first = canopy_ref[0:8, here]
        rest = jnp.concatenate([canopy_ref[8:rows, here], jnp.zeros((16 - rows, LANES), f32)], axis=0)
        send_ref[2 * t] = jnp.where(low, first, pltpu.roll(rest, SLOT, 1))
        send_ref[2 * t + 1] = jnp.where(low, pltpu.roll(first, SLOT, 1), rest)
    layers, rows, _ = head_ref.shape
    copies[1].wait()
    copies[2].wait()
    for out_ref, part in ((down_ref, slice(0, STATE_DEPTH)), (up_ref, slice(rows - STATE_DEPTH, rows))):
        for k in range(layers):
            out_ref[STATE_DEPTH * k : STATE_DEPTH * (k + 1)] = head_ref[k][part]
        for k in range(layers):
            at = STATE_DEPTH * (layers + k)
            out_ref[at : at + STATE_DEPTH] = (soil_ref[k] + 1).astype(f32)[part]


def table_rows(table_ref, rows):
    lane = lane_iota((rows, LANES))
    out = []
    for field in range(table_ref.shape[0]):
        row = jnp.zeros((rows, LANES), f32)
        for kind in range(table_ref.shape[1]):
            row = jnp.where(lane == kind + 1, table_ref[field, kind], row)
        out.append(row)
    return out


def lookup(row, index):
    pieces = [
        jnp.take_along_axis(row, index[:, at : at + LANES], axis=1, mode="promise_in_bounds")
        for at in range(0, index.shape[1], LANES)
    ]
    return jnp.concatenate(pieces, axis=1)


def sigmoid(u):
    return 1.0 / (1.0 + jnp.exp(-u))


def source_kernel(
    table_ref, arrived_ref, head_ref, soil_ref, forcing_ref, slot_ref,
    source_ref, flux_ref, tab_ref, factor_ref,
):
    layers, rows, cols = head_ref.shape
    owners = arrived_ref.shape[0]
    pairs = -(-layers // 2)
    low = lane_iota((8, LANES)) < SLOT
    line = lax.broadcasted_iota(jnp.int32, (16, LANES), 0)
    is_root = (line >= 3) & (line < 3 + layers)

    def unpack(t, _):
        first = arrived_ref[2 * t]
        second = arrived_ref[2 * t + 1]
        both = jnp.concatenate(
            [
                jnp.where(low, first, pltpu.roll(second, SLOT, 1)),
                jnp.where(low, pltpu.roll(first, SLOT, 1), second),
            ],
            axis=0,
        )
        leaf_area, albedo, resist = both[0:1], both[1:2], both[2:3]
        root_sum = jnp.sum(jnp.where(is_root, both, 0.0), axis=0, keepdims=True)
        factor = leaf_area / ((leaf_area + resist) * root_sum) * (1.0 / FIXED)
        factor_ref[t] = jnp.broadcast_to(factor, (8, LANES))
        fixed = (both * FIXED + 0.5).astype(jnp.int32)
        for m in range(pairs):
            word = fixed[3 + m : 4 + m]
            if m + pairs < layers:
                word = word | (fixed[3 + m + pairs : 4 + m + pairs] << 16)
            tab_ref[t, m] = jnp.broadcast_to(word, (8, LANES))
        leaf = ((0.5 + 0.3 * leaf_area) * (0.25 * FIXED) + 0.5).astype(jnp.int32)
        bright = ((1.0 - albedo) * FIXED + 0.5).astype(jnp.int32)
        tab_ref[t, pairs] = jnp.broadcast_to(leaf | (bright << 16), (8, LANES))
        return 0

    lax.fori_loop(0, owners // 2, unpack, 0, unroll=16)
    tables = table_rows(table_ref, rows)
    shape = (rows, LANES)

    def whole(block):
        return jnp.concatenate([block] * (rows // 8), axis=0)

    for at_y in range(0, cols, LANES):
        here = (slice(0, rows), slice(at_y, at_y + LANES))
        slot = slot_ref[here]
        land = slot >= 0
        value = jnp.maximum(slot, 0)
        lane = value & (LANES - 1)
        tile = value >> 7

        def pick(t, held):
            match = tile == t
            found = [lookup(whole(tab_ref[t, m]), lane) for m in range(pairs + 1)]
            found.append(lookup(whole(factor_ref[t]), lane))
            return tuple(jnp.where(match, new, old) for new, old in zip(found, held))

        held = tuple([jnp.full(shape, 1, jnp.int32)] * (pairs + 1) + [jnp.full(shape, 1.0 / FIXED, f32)])
        if owners <= 32:
            for t in range(owners // 2):
                held = pick(t, held)
        else:
            held = lax.fori_loop(0, owners // 2, pick, held, unroll=8)
        *words, terms, factor = held

        def halves(word):
            upper = lax.shift_right_logical(word, jnp.full(shape, 16, jnp.int32))
            return (word & 0xFFFF).astype(f32), upper.astype(f32)

        leaf, bright = halves(terms)
        exchange_coef = leaf * (4.0 / FIXED)
        absorbed = bright * (1.0 / FIXED)
        split = [halves(word) for word in words]
        uptake = []
        for k in range(layers):
            index = soil_ref[(k,) + here] + 1
            steep = lookup(tables[1], index)
            root = factor * split[k % pairs][k // pairs]
            uptake.append(root * sigmoid(steep * head_ref[(k,) + here]))
            if k == 0:
                ks_top = lookup(tables[0], index)
        conductance = functools.reduce(jnp.add, uptake)
        sunlight, air_temp, humidity, rainfall = (forcing_ref[(i,) + here] for i in range(4))
        radiation = absorbed * sunlight + 0.3
        square = air_temp * air_temp
        excess = radiation - 0.3 * square * square - conductance * (0.5 - humidity)
        slope = -1.2 * square * air_temp - exchange_coef - conductance
        rise = -excess / slope
        surface = air_temp + rise
        vapour = 0.5 * jnp.exp(2.0 * rise)
        square = surface * surface
        excess = (
            radiation
            - 0.3 * square * square
            - exchange_coef * rise
            - conductance * (vapour - humidity)
        )
        slope = -1.2 * square * surface - exchange_coef - 2.0 * conductance * vapour
        rise = rise - excess / slope
        rate = 0.5 * jnp.exp(2.0 * rise) - humidity
        infiltration = rainfall * ks_top / (rainfall + ks_top)
        infiltration = jnp.where(land, infiltration, 0.0)
        rate = jnp.where(land, rate, 0.0)
        flux_ref[(0,) + here] = conductance * rate
        flux_ref[(1,) + here] = infiltration
        for k in range(layers):
            value = -rate * uptake[k]
            if k == 0:
                value = value + infiltration
            source_ref[(k,) + here] = value


def strips(planes, shift_from):
    packed = None
    for k, plane in enumerate(planes):
        lane = lane_iota(plane.shape)
        shift = (HALO * k - shift_from) % LANES
        moved = pltpu.roll(plane, shift, 1) if shift else plane
        inside = (lane >= HALO * k) & (lane < HALO * (k + 1))
        packed = jnp.where(inside, moved, 0.0 if packed is None else packed)
    return packed


def strip_parts(cols):
    return ((slice(0, LANES), 0), (slice(cols - LANES, cols), LANES - HALO))


def ends_of(lo_ref, hi_ref, at, depth, part):
    edge = slice(depth * at, depth * (at + 1))
    above, below = hi_ref[edge, part], lo_ref[edge, part]
    gap = jnp.zeros((2 * (HALO - depth), above.shape[1]), f32)
    return jnp.concatenate([above, gap, below], axis=0)


def strip_kernel(head_ref, soil_ref, src_ref, down_ref, up_ref):
    layers, _, cols = head_ref.shape
    for out_ref, (part, shift) in zip((down_ref, up_ref), strip_parts(cols)):
        out_ref[0] = strips([head_ref[k, :, part] for k in range(layers)], shift)
        out_ref[1] = strips([(soil_ref[k, :, part] + 1).astype(f32) for k in range(layers)], shift)
        out_ref[2] = strips([src_ref[k, :, part] for k in range(layers)], shift)


def source_edge_kernel(src_ref, ylo_ref, yhi_ref, down_ref, up_ref):
    layers, rows, _ = src_ref.shape
    at = SOURCE_DEPTH * layers
    for out_ref, first in ((down_ref, 0), (up_ref, rows - HALO)):
        row = 0 if first == 0 else rows - SOURCE_DEPTH
        for k in range(layers):
            part = slice(SOURCE_DEPTH * k, SOURCE_DEPTH * (k + 1))
            out_ref[part] = src_ref[k][row : row + SOURCE_DEPTH]
        blocks = [ref[f, first : first + HALO] for f in range(3) for ref in (ylo_ref, yhi_ref)]
        half = HALO // 2
        tail = [block[h : h + half] for block in blocks[4:6] for h in (0, half)]
        for j in range(4):
            out_ref[at : at + HALO, j * LANES : (j + 1) * LANES] = blocks[j]
            out_ref[at + HALO : at + HALO + half, j * LANES : (j + 1) * LANES] = tail[j]


def corner(edge_ref, at, field, which):
    half = HALO // 2
    if field < 2:
        j = 2 * field + which
        return edge_ref[at : at + HALO, j * LANES : (j + 1) * LANES]
    pieces = [
        edge_ref[at + HALO : at + HALO + half, j * LANES : (j + 1) * LANES]
        for j in (2 * which, 2 * which + 1)
    ]
    return jnp.concatenate(pieces, axis=0)


def tall_strips(layers, ylo_ref, yhi_ref, slo_ref, shi_ref):
    at = SOURCE_DEPTH * layers
    out = []
    for field in range(3):
        pair = []
        for which, ref in ((1, yhi_ref), (0, ylo_ref)):
            ends = [corner(shi_ref, at, field, which), corner(slo_ref, at, field, which)]
            pair.append(jnp.concatenate([ref[field]] + ends, axis=0))
        out.append(pair)
    return out


def side(strip, k):
    right, left = strip
    lane = lane_iota(right.shape)
    shift = (-HALO * k) % LANES
    right = pltpu.roll(right, shift, 1) if shift else right
    left = pltpu.roll(left, (LANES - HALO - HALO * k) % LANES, 1)
    return jnp.where(lane < HALO, right, jnp.where(lane >= LANES - HALO, left, 0.0))


def after(x, axis):
    return pltpu.roll(x, x.shape[axis] - 1, axis)


def before(x, axis):
    return pltpu.roll(x, 1, axis)


def pointwise(head, conduct, steep, capacity):
    sat = 0.5 + 0.5 * jnp.tanh(0.5 * (steep * head))
    slope = steep * sat * (1.0 - sat)
    cond = conduct * (0.1 + 0.9 * sat * sat)
    deriv = 0.9 * conduct * sat * slope
    weighted = storage_weight * capacity
    return cond, deriv, weighted * slope, weighted * sat


def joined(main_ref, side_ref):
    return lambda k: jnp.concatenate([main_ref[k], side_ref[k]], axis=1)


def linearize(layers, head_of, cond_of, deriv_of, store_of, gain_of, mask, coefs, out_ref, tile):
    diag_ref, xp_ref, xm_ref, yp_ref, ym_ref, az_ref, bz_ref = coefs
    rows, cols = tile

    def masked(value):
        own = value[:rows, cols:] * mask[:rows, cols:]
        top = jnp.concatenate([value[:rows, :cols], own], axis=1)
        return jnp.concatenate([top, value[rows:] * mask[rows:]], axis=0)

    above = None
    for k in range(layers):
        head = head_of(k)
        cond = cond_of(k)
        deriv = deriv_of(k)
        value = gain_of(k)
        diag = store_of(k)
        for plus_ref, minus_ref, axis in ((xp_ref, xm_ref, 0), (yp_ref, ym_ref, 1)):
            mean = 0.5 * (cond + after(cond, axis))
            drop = head - after(head, axis)
            a = mean + deriv * drop
            b = mean - after(deriv, axis) * drop
            face = mean * drop
            value = value + (face - before(face, axis))
            diag = diag + (a + before(b, axis))
            plus_ref[k] = masked(b)
            minus_ref[k] = masked(before(a, axis))
        if k + 1 < layers:
            mean = 0.5 * (cond + cond_of(k + 1))
            drop = head - head_of(k + 1) + 1.0
            a = mean + deriv * drop
            b = mean - deriv_of(k + 1) * drop
            az_ref[k] = a
            bz_ref[k] = b
            face = mean * drop
        else:
            a = 2.0 * deriv
            face = cond
        diag = diag + a
        value = value + face
        if above is not None:
            diag = diag + above[1]
            value = value - above[0]
        above = (face, b)
        diag_ref[k] = diag
        out_ref[k] = masked(value)


def apply(v_ref, coefs, k):
    diag_ref, xp_ref, xm_ref, yp_ref, ym_ref, az_ref, bz_ref = coefs
    v = v_ref[k]
    value = diag_ref[k] * v
    value = value - xp_ref[k] * after(v, 0) - xm_ref[k] * before(v, 0)
    value = value - yp_ref[k] * after(v, 1) - ym_ref[k] * before(v, 1)
    if k > 0:
        value = value - az_ref[k - 1] * v_ref[k - 1]
    if k + 1 < v_ref.shape[0]:
        value = value - bz_ref[k] * v_ref[k + 1]
    return value


def powers(basis, coefs, tile, out_ref):
    layers = basis[0].shape[0]
    rows, cols = tile
    for step in range(KRYLOV - 1):
        for k in range(layers):
            basis[step + 1][k] = apply(basis[step], coefs, k)
    sums = [jnp.zeros((8, LANES), f32) for _ in PAIRS]
    for k in range(layers):
        top = apply(basis[-1], coefs, k)
        for at in range(0, rows, 8):
            for lane_at in range(0, cols, LANES):
                part = (slice(at, at + 8), slice(lane_at, lane_at + LANES))
                vs = [b[(k,) + part] for b in basis] + [top[part]]
                for e, (i, j) in enumerate(PAIRS):
                    sums[e] = sums[e] + vs[i] * vs[j]
    lines = [jnp.sum(x, axis=0, keepdims=True) for x in sums]
    lines.append(jnp.zeros((16 - len(PAIRS), LANES), f32))
    block = jnp.sum(jnp.concatenate(lines, axis=0), axis=1, keepdims=True)
    line = lax.broadcasted_iota(jnp.int32, (16, LANES), 0)
    flat = jnp.sum(jnp.where(lane_iota((16, LANES)) == line, block, 0.0), axis=0, keepdims=True)
    for d in range(out_ref.shape[0]):
        out_ref[d] = flat


def solve(gram_ref):
    terms = [gram_ref[d] for d in range(gram_ref.shape[0])]
    while len(terms) > 1:
        terms = [functools.reduce(jnp.add, terms[i : i + 2]) for i in range(0, len(terms), 2)]
    total = terms[0]
    line = lax.broadcasted_iota(jnp.int32, (16, LANES), 0)
    spread = jnp.broadcast_to(total, (16, LANES))
    column = jnp.sum(jnp.where(lane_iota((16, LANES)) == line, spread, 0.0), axis=1, keepdims=True)
    gram = {}
    for e, (i, j) in enumerate(PAIRS):
        gram[i, j] = gram[j, i] = column[e : e + 1, :]

    def times_gram(c):
        out = []
        for i in range(KRYLOV + 1):
            out.append(functools.reduce(jnp.add, [gram[i, m] * c[m] for m in range(len(c))]))
        return out

    def dot(a, b):
        return functools.reduce(jnp.add, [x * y for x, y in zip(a, b)])

    square = gram[0, 0] + norm_epsilon
    inverse = lax.rsqrt(square)
    beta = square * inverse
    basis = [[inverse]]
    images = [times_gram(basis[0])]
    hessen = {}
    for j in range(KRYLOV):
        w = [jnp.zeros_like(beta)] + basis[j]
        for i in range(j + 1):
            product = dot(w, images[i])
            hessen[i, j] = product
            w = [w[m] - product * basis[i][m] if m < len(basis[i]) else w[m] for m in range(len(w))]
        square = jnp.maximum(dot(w, times_gram(w)), 0.0) + norm_epsilon
        inverse = lax.rsqrt(square)
        hessen[j + 1, j] = square * inverse
        if j + 1 < KRYLOV:
            basis.append([x * inverse for x in w])
            images.append(times_gram(basis[-1]))
    n = KRYLOV
    normal = {}
    for a in range(n):
        for b in range(a + 1):
            normal[a, b] = functools.reduce(
                jnp.add,
                [hessen[i, a] * hessen[i, b] for i in range(n + 1) if (i, a) in hessen and (i, b) in hessen],
            )
    factor = {}
    inverse = []
    for a in range(n):
        for b in range(a + 1):
            value = normal[a, b]
            for m in range(b):
                value = value - factor[a, m] * factor[b, m]
            if a == b:
                inverse.append(lax.rsqrt(value))
            else:
                factor[a, b] = value * inverse[b]
    forward = []
    for a in range(n):
        value = hessen[0, a] * beta
        for m in range(a):
            value = value - factor[a, m] * forward[m]
        forward.append(value * inverse[a])
    backward = [None] * n
    for a in reversed(range(n)):
        value = forward[a]
        for m in range(a + 1, n):
            value = value - factor[m, a] * backward[m]
        backward[a] = value * inverse[a]
    return [
        functools.reduce(jnp.add, [backward[j] * basis[j][i] for j in range(i, n)]) for i in range(n)
    ]


def state_kernel(
    table_ref, head_ref, soil_ref, lo_ref, hi_ref,
    ext_ref, ks_ref, steep_ref, cap_ref, cond_ref, deriv_ref, store_ref, water_ref,
):
    layers, rows, cols = head_ref.shape
    tables = table_rows(table_ref, rows + 2 * HALO)
    every = slice(0, cols)
    for k in range(layers):
        ends = ends_of(lo_ref, hi_ref, k, STATE_DEPTH, every)
        head = jnp.concatenate([head_ref[k], ends], axis=0)
        ends = ends_of(lo_ref, hi_ref, layers + k, STATE_DEPTH, every)
        index = jnp.concatenate([soil_ref[k] + 1, ends.astype(jnp.int32)], axis=0)
        conduct, steep, capacity = (lookup(row, index) for row in tables)
        values = (head, conduct, steep, capacity) + pointwise(head, conduct, steep, capacity)
        outs = (ext_ref, ks_ref, steep_ref, cap_ref, cond_ref, deriv_ref, store_ref, water_ref)
        for ref, value in zip(outs, values):
            ref[k] = value


def first_kernel(
    table_ref, src_ref, slo_ref, shi_ref, ylo_ref, yhi_ref,
    ext_ref, ks_ref, cond_ref, deriv_ref, store_ref, water_ref,
    ext_side, ks_side, steep_side, cap_side, base_ref, p0_ref, p1_ref, p2_ref, gram_ref,
    cond_side, deriv_side, store_side, water_side, *coefs,
):
    layers, rows, cols = src_ref.shape
    tables = table_rows(table_ref, rows + 2 * HALO)
    heads, soils, sources = tall_strips(layers, ylo_ref, yhi_ref, slo_ref, shi_ref)
    for k in range(layers):
        head = side(heads, k)
        index = side(soils, k).astype(jnp.int32)
        conduct, steep, capacity = (lookup(row, index) for row in tables)
        values = (head, conduct, steep, capacity) + pointwise(head, conduct, steep, capacity)
        outs = (ext_side, ks_side, steep_side, cap_side, cond_side, deriv_side, store_side, water_side)
        for ref, value in zip(outs, values):
            ref[k] = value
    water_of = joined(water_ref, water_side)

    def gain_of(k):
        source = jnp.concatenate([src_ref[k], ends_of(slo_ref, shi_ref, k, SOURCE_DEPTH, slice(0, cols))], axis=0)
        source = jnp.concatenate([source, side(sources, k)], axis=1)
        water = water_of(k)
        base_ref[k] = water + source
        return water - base_ref[k]

    linearize(
        layers, joined(ext_ref, ext_side), joined(cond_ref, cond_side), joined(deriv_ref, deriv_side),
        joined(store_ref, store_side), gain_of,
        (joined(ks_ref, ks_side)(0) > 0.0).astype(f32), coefs, p0_ref, (rows, cols),
    )
    powers((p0_ref, p1_ref, p2_ref), coefs, (rows, cols), gram_ref)


def second_kernel(
    arrived_ref, old_ref, ks_ref, steep_ref, cap_ref, old_side, ks_side, steep_side, cap_side,
    base_ref, q0_ref, q1_ref, q2_ref,
    part_ref, p0_ref, p1_ref, p2_ref, gram_ref, ext_ref, cond_ref, deriv_ref, store_ref, gain_ref, *coefs,
):
    layers = old_ref.shape[0]
    rows, cols = part_ref.shape[1:]
    x = solve(arrived_ref)
    near = lax.broadcasted_iota(jnp.int32, (HALO, cols + LANES), 0) < HALO // 2

    def folded(of):
        def get(k):
            value = of(k)
            ends = jnp.where(near, value[rows : rows + HALO], value[rows + HALO :])
            return jnp.concatenate([value[:rows], ends], axis=0)

        return get

    old_of, ks_of = folded(joined(old_ref, old_side)), folded(joined(ks_ref, ks_side))
    steep_of, cap_of = folded(joined(steep_ref, steep_side)), folded(joined(cap_ref, cap_side))
    base_of, *qs = (folded(lambda k, ref=ref: ref[k]) for ref in (base_ref, q0_ref, q1_ref, q2_ref))
    for k in range(layers):
        head = old_of(k)
        for value, q_of in zip(x, qs):
            head = head - value * q_of(k)
        cond, deriv, store, water = pointwise(head, ks_of(k), steep_of(k), cap_of(k))
        ext_ref[k] = head
        part_ref[k] = head[:rows, :cols]
        cond_ref[k] = cond
        deriv_ref[k] = deriv
        store_ref[k] = store
        gain_ref[k] = water - base_of(k)
    linearize(
        layers, *((lambda k, ref=ref: ref[k]) for ref in (ext_ref, cond_ref, deriv_ref, store_ref, gain_ref)),
        (ks_of(0) > 0.0).astype(f32), coefs, p0_ref, (rows, cols),
    )
    powers((p0_ref, p1_ref, p2_ref), coefs, (rows, cols), gram_ref)


def last_kernel(arrived_ref, part_ref, q0_ref, q1_ref, q2_ref, head_ref):
    layers, rows, cols = part_ref.shape
    x = solve(arrived_ref)
    for k in range(layers):
        own = (k, slice(0, rows), slice(0, cols))
        head_ref[k] = part_ref[k] - x[0] * q0_ref[own] - x[1] * q1_ref[own] - x[2] * q2_ref[own]


def shards(head_old, soil_type, soil_table, forcing, canopy, column_slot):
    layers, rows, cols = head_old.shape
    both = ("gx", "gy")
    devices = lax.axis_size("gx") * lax.axis_size("gy")
    tall, wide = rows + 2 * HALO, cols + LANES
    own, ext = ((layers, rows, cols), f32), ((layers, tall, wide), f32)
    gram_block = ((devices, 1, LANES), f32)

    def exchange(to_lower, to_upper, axis):
        size = lax.axis_size(axis)
        up = [(i, i + 1) for i in range(size - 1)]
        down = [(j, i) for i, j in up]
        return lax.ppermute(to_upper, axis, up), lax.ppermute(to_lower, axis, down)

    def spread(x, axes):
        return lax.all_to_all(x, axes, split_axis=0, concat_axis=0, tiled=True)

    def edge(count):
        return (-(-count // 8) * 8, cols), f32

    send, down, up = call(
        pack_kernel,
        [((devices, 8, LANES), f32)] + [edge(2 * STATE_DEPTH * layers)] * 2,
        3,
        scratch=[
            pltpu.VMEM(canopy.shape, f32),
            pltpu.VMEM(head_old.shape, f32),
            pltpu.VMEM(soil_type.shape, jnp.int32),
            pltpu.SemaphoreType.DMA((3,)),
        ],
        in_specs=[pl.BlockSpec(memory_space=pl.ANY)] * 3,
        grant=63400000,
    )(canopy, head_old, soil_type)
    arrived = spread(send, both)
    lo, hi = exchange(down, up, "gx")
    source, flux = call(
        source_kernel,
        [own, ((2, rows, cols), f32)],
        6,
        scratch=[
            pltpu.VMEM((devices // 2, -(-layers // 2) + 1, 8, LANES), jnp.int32),
            pltpu.VMEM((devices // 2, 8, LANES), f32),
        ],
        in_specs=[smem] + [vmem] * 5,
    )(soil_table, arrived, head_old, soil_type, forcing, column_slot)
    ydown, yup = call(strip_kernel, [((3, rows, LANES), f32)] * 2, 3)(head_old, soil_type, source)
    ylo, yhi = exchange(ydown, yup, "gy")
    sdown, sup = call(source_edge_kernel, [edge(SOURCE_DEPTH * layers + HALO + HALO // 2)] * 2, 3)(
        source, ylo, yhi
    )
    slo, shi = exchange(sdown, sup, "gx")
    main, side_block = ((layers, tall, cols), f32), ((layers, tall, LANES), f32)
    old, ks, steep, cap, cond, deriv, store, water = call(
        state_kernel, [main] * 8, 5, in_specs=[smem] + [vmem] * 4
    )(soil_table, head_old, soil_type, lo, hi)
    held, held_side = [pltpu.VMEM(ext[0], f32)], [pltpu.VMEM(side_block[0], f32)]
    old_s, ks_s, steep_s, cap_s, base, p0, p1, p2, gram = call(
        first_kernel,
        [side_block] * 4 + [ext] * 4 + [gram_block],
        12,
        scratch=held_side * 4 + held * 7,
        in_specs=[smem] + [vmem] * 11,
    )(soil_table, source, slo, shi, ylo, yhi, old, ks, cond, deriv, store, water)
    sums = spread(gram, both)
    part, q0, q1, q2, gram = call(
        second_kernel,
        [own] + [((layers, rows + HALO, wide), f32)] * 3 + [gram_block],
        13,
        scratch=[pltpu.VMEM((layers, rows + HALO, wide), f32)] * 12,
    )(sums, old, ks, steep, cap, old_s, ks_s, steep_s, cap_s, base, p0, p1, p2)
    sums = spread(gram, both)
    (head,) = call(last_kernel, [own], 5)(sums, part, q0, q1, q2)
    return head, flux


def solution(mesh):
    return jax.shard_map(
        shards,
        mesh=mesh,
        in_specs=(
            P(None, "gx", "gy"),
            P(None, "gx", "gy"),
            P(),
            P(None, "gx", "gy"),
            P(None, ("gx", "gy")),
            P("gx", "gy"),
        ),
        out_specs=(P(None, "gx", "gy"), P(None, "gx", "gy")),
        check_vma=False,
    )
```

```python
import functools

import jax
import jax.numpy as jnp
from jax import lax
from jax.experimental import pallas as pl
from jax.experimental.pallas import tpu as pltpu
from jax.sharding import PartitionSpec as P

NEWTON = 2
KRYLOV = 3
HALO = 8
STATE_DEPTH = 7
SOURCE_DEPTH = 6
FIXED = 65535.0
LANES = 128
SLOT = 64

storage_weight = 4.0
norm_epsilon = 1e-06

VMEM_LIMIT = 20 * 1024 * 1024
PAIRS = [(i, j) for i in range(KRYLOV + 1) for j in range(i, KRYLOV + 1)]

f32 = jnp.float32
vmem = pl.BlockSpec(memory_space=pltpu.VMEM)
smem = pl.BlockSpec(memory_space=pltpu.SMEM)


def call(body, outs, n_in, scratch=(), in_specs=None, flops=1000000, grant=VMEM_LIMIT):
    return pl.pallas_call(
        body,
        out_shape=[jax.ShapeDtypeStruct(s, d) for s, d in outs],
        in_specs=in_specs or [vmem] * n_in,
        out_specs=[vmem] * len(outs),
        scratch_shapes=list(scratch),
        compiler_params=pltpu.CompilerParams(vmem_limit_bytes=grant),
        cost_estimate=pl.CostEstimate(flops=flops, bytes_accessed=1000000, transcendentals=0),
    )


def lane_iota(shape):
    return lax.broadcasted_iota(jnp.int32, shape, len(shape) - 1)


def pack_kernel(
    canopy_hbm, head_hbm, soil_hbm, send_ref, down_ref, up_ref, canopy_ref, head_ref, soil_ref, sems
):
    copies = [
        pltpu.make_async_copy(canopy_hbm, canopy_ref, sems.at[0]),
        pltpu.make_async_copy(head_hbm, head_ref, sems.at[1]),
        pltpu.make_async_copy(soil_hbm, soil_ref, sems.at[2]),
    ]
    for copy in copies:
        copy.start()
    copies[0].wait()
    rows = canopy_ref.shape[0]
    low = lane_iota((8, LANES)) < SLOT
    for t in range(canopy_ref.shape[1] // LANES):
        here = slice(t * LANES, (t + 1) * LANES)
        first = canopy_ref[0:8, here]
        rest = jnp.concatenate([canopy_ref[8:rows, here], jnp.zeros((16 - rows, LANES), f32)], axis=0)
        send_ref[2 * t] = jnp.where(low, first, pltpu.roll(rest, SLOT, 1))
        send_ref[2 * t + 1] = jnp.where(low, pltpu.roll(first, SLOT, 1), rest)
    layers, rows, _ = head_ref.shape
    copies[1].wait()
    copies[2].wait()
    for out_ref, part in ((down_ref, slice(0, STATE_DEPTH)), (up_ref, slice(rows - STATE_DEPTH, rows))):
        for k in range(layers):
            out_ref[STATE_DEPTH * k : STATE_DEPTH * (k + 1)] = head_ref[k][part]
        for k in range(layers):
            at = STATE_DEPTH * (layers + k)
            out_ref[at : at + STATE_DEPTH] = (soil_ref[k] + 1).astype(f32)[part]


def table_rows(table_ref, rows):
    lane = lane_iota((rows, LANES))
    out = []
    for field in range(table_ref.shape[0]):
        row = jnp.zeros((rows, LANES), f32)
        for kind in range(table_ref.shape[1]):
            row = jnp.where(lane == kind + 1, table_ref[field, kind], row)
        out.append(row)
    return out


def lookup(row, index):
    pieces = [
        jnp.take_along_axis(row, index[:, at : at + LANES], axis=1, mode="promise_in_bounds")
        for at in range(0, index.shape[1], LANES)
    ]
    return jnp.concatenate(pieces, axis=1)


def sigmoid(u):
    return 1.0 / (1.0 + jnp.exp(-u))


def edge_source_kernel(
    table_ref, arrived_ref, head_ref, soil_ref, forcing_ref, slot_ref,
    source_ref, flux_ref, tab_ref, factor_ref,
):
    layers, rows, cols = head_ref.shape
    owners = arrived_ref.shape[0]
    pairs = -(-layers // 2)
    low = lane_iota((8, LANES)) < SLOT
    line = lax.broadcasted_iota(jnp.int32, (16, LANES), 0)
    is_root = (line >= 3) & (line < 3 + layers)

    def unpack(t, _):
        first = arrived_ref[2 * t]
        second = arrived_ref[2 * t + 1]
        both = jnp.concatenate(
            [
                jnp.where(low, first, pltpu.roll(second, SLOT, 1)),
                jnp.where(low, pltpu.roll(first, SLOT, 1), second),
            ],
            axis=0,
        )
        leaf_area, albedo, resist = both[0:1], both[1:2], both[2:3]
        root_sum = jnp.sum(jnp.where(is_root, both, 0.0), axis=0, keepdims=True)
        factor = leaf_area / ((leaf_area + resist) * root_sum) * (1.0 / FIXED)
        factor_ref[t] = jnp.broadcast_to(factor, (8, LANES))
        fixed = (both * FIXED + 0.5).astype(jnp.int32)
        for m in range(pairs):
            word = fixed[3 + m : 4 + m]
            if m + pairs < layers:
                word = word | (fixed[3 + m + pairs : 4 + m + pairs] << 16)
            tab_ref[t, m] = jnp.broadcast_to(word, (8, LANES))
        leaf = ((0.5 + 0.3 * leaf_area) * (0.25 * FIXED) + 0.5).astype(jnp.int32)
        bright = ((1.0 - albedo) * FIXED + 0.5).astype(jnp.int32)
        tab_ref[t, pairs] = jnp.broadcast_to(leaf | (bright << 16), (8, LANES))
        return 0

    lax.fori_loop(0, owners // 2, unpack, 0, unroll=16)
    places = [(0, 0), (cols - LANES, LANES)]
    land_columns(
        table_ref, tab_ref, factor_ref, head_ref, soil_ref, forcing_ref, slot_ref, source_ref, flux_ref, places
    )


def inner_source_kernel(
    table_ref, tab_ref, factor_ref, head_ref, soil_ref, forcing_ref, slot_ref, some_ref, part_ref,
    source_ref, flux_ref,
):
    cols = head_ref.shape[2]
    places = [(at, at) for at in range(LANES, cols - LANES, LANES)]
    land_columns(
        table_ref, tab_ref, factor_ref, head_ref, soil_ref, forcing_ref, slot_ref, source_ref, flux_ref, places
    )
    for whole_ref, piece_ref in ((source_ref, some_ref), (flux_ref, part_ref)):
        for k in range(whole_ref.shape[0]):
            whole_ref[k, :, 0:LANES] = piece_ref[k, :, 0:LANES]
            whole_ref[k, :, cols - LANES : cols] = piece_ref[k, :, LANES : 2 * LANES]


def land_columns(
    table_ref, tab_ref, factor_ref, head_ref, soil_ref, forcing_ref, slot_ref, source_ref, flux_ref, places
):
    layers, rows, _ = head_ref.shape
    halves_of = tab_ref.shape[0]
    pairs = tab_ref.shape[1] - 1
    tables = table_rows(table_ref, rows)
    shape = (rows, LANES)

    def whole(block):
        return jnp.concatenate([block] * (rows // 8), axis=0)

    for at_y, put in places:
        here = (slice(0, rows), slice(at_y, at_y + LANES))
        there = (slice(0, rows), slice(put, put + LANES))
        slot = slot_ref[here]
        land = slot >= 0
        value = jnp.maximum(slot, 0)
        lane = value & (LANES - 1)
        tile = value >> 7

        def pick(t, held):
            match = tile == t
            found = [lookup(whole(tab_ref[t, m]), lane) for m in range(pairs + 1)]
            found.append(lookup(whole(factor_ref[t]), lane))
            return tuple(jnp.where(match, new, old) for new, old in zip(found, held))

        held = tuple([jnp.full(shape, 1, jnp.int32)] * (pairs + 1) + [jnp.full(shape, 1.0 / FIXED, f32)])
        if halves_of <= 16:
            for t in range(halves_of):
                held = pick(t, held)
        else:
            held = lax.fori_loop(0, halves_of, pick, held, unroll=8)
        *words, terms, factor = held

        def halves(word):
            upper = lax.shift_right_logical(word, jnp.full(shape, 16, jnp.int32))
            return (word & 0xFFFF).astype(f32), upper.astype(f32)

        leaf, bright = halves(terms)
        exchange_coef = leaf * (4.0 / FIXED)
        absorbed = bright * (1.0 / FIXED)
        split = [halves(word) for word in words]
        uptake = []
        for k in range(layers):
            index = soil_ref[(k,) + here] + 1
            steep = lookup(tables[1], index)
            root = factor * split[k % pairs][k // pairs]
            uptake.append(root * sigmoid(steep * head_ref[(k,) + here]))
            if k == 0:
                ks_top = lookup(tables[0], index)
        conductance = functools.reduce(jnp.add, uptake)
        sunlight, air_temp, humidity, rainfall = (forcing_ref[(i,) + here] for i in range(4))
        radiation = absorbed * sunlight + 0.3
        square = air_temp * air_temp
        excess = radiation - 0.3 * square * square - conductance * (0.5 - humidity)
        slope = -1.2 * square * air_temp - exchange_coef - conductance
        rise = -excess / slope
        surface = air_temp + rise
        vapour = 0.5 * jnp.exp(2.0 * rise)
        square = surface * surface
        excess = (
            radiation
            - 0.3 * square * square
            - exchange_coef * rise
            - conductance * (vapour - humidity)
        )
        slope = -1.2 * square * surface - exchange_coef - 2.0 * conductance * vapour
        rise = rise - excess / slope
        rate = 0.5 * jnp.exp(2.0 * rise) - humidity
        infiltration = rainfall * ks_top / (rainfall + ks_top)
        infiltration = jnp.where(land, infiltration, 0.0)
        rate = jnp.where(land, rate, 0.0)
        flux_ref[(0,) + there] = conductance * rate
        flux_ref[(1,) + there] = infiltration
        for k in range(layers):
            value = -rate * uptake[k]
            if k == 0:
                value = value + infiltration
            source_ref[(k,) + there] = value


def strips(planes, shift_from):
    packed = None
    for k, plane in enumerate(planes):
        lane = lane_iota(plane.shape)
        shift = (HALO * k - shift_from) % LANES
        moved = pltpu.roll(plane, shift, 1) if shift else plane
        inside = (lane >= HALO * k) & (lane < HALO * (k + 1))
        packed = jnp.where(inside, moved, 0.0 if packed is None else packed)
    return packed


def strip_parts(cols):
    return ((slice(0, LANES), 0), (slice(cols - LANES, cols), LANES - HALO))


def ends_of(lo_ref, hi_ref, at, depth, part):
    edge = slice(depth * at, depth * (at + 1))
    above, below = hi_ref[edge, part], lo_ref[edge, part]
    gap = jnp.zeros((2 * (HALO - depth), above.shape[1]), f32)
    return jnp.concatenate([above, gap, below], axis=0)


def strip_kernel(head_ref, soil_ref, some_ref, down_ref, up_ref):
    layers, _, cols = head_ref.shape
    for out_ref, (part, shift), at in zip((down_ref, up_ref), strip_parts(cols), (0, LANES)):
        out_ref[0] = strips([head_ref[k, :, part] for k in range(layers)], shift)
        out_ref[1] = strips([(soil_ref[k, :, part] + 1).astype(f32) for k in range(layers)], shift)
        out_ref[2] = strips([some_ref[k, :, at : at + LANES] for k in range(layers)], shift)


def source_edge_kernel(src_ref, ylo_ref, yhi_ref, down_ref, up_ref):
    layers, rows, _ = src_ref.shape
    at = SOURCE_DEPTH * layers
    for out_ref, first in ((down_ref, 0), (up_ref, rows - HALO)):
        row = 0 if first == 0 else rows - SOURCE_DEPTH
        for k in range(layers):
            part = slice(SOURCE_DEPTH * k, SOURCE_DEPTH * (k + 1))
            out_ref[part] = src_ref[k][row : row + SOURCE_DEPTH]
        blocks = [ref[f, first : first + HALO] for f in range(3) for ref in (ylo_ref, yhi_ref)]
        half = HALO // 2
        tail = [block[h : h + half] for block in blocks[4:6] for h in (0, half)]
        for j in range(4):
            out_ref[at : at + HALO, j * LANES : (j + 1) * LANES] = blocks[j]
            out_ref[at + HALO : at + HALO + half, j * LANES : (j + 1) * LANES] = tail[j]


def corner(edge_ref, at, field, which):
    half = HALO // 2
    if field < 2:
        j = 2 * field + which
        return edge_ref[at : at + HALO, j * LANES : (j + 1) * LANES]
    pieces = [
        edge_ref[at + HALO : at + HALO + half, j * LANES : (j + 1) * LANES]
        for j in (2 * which, 2 * which + 1)
    ]
    return jnp.concatenate(pieces, axis=0)


def tall_strips(layers, ylo_ref, yhi_ref, slo_ref, shi_ref):
    at = SOURCE_DEPTH * layers
    out = []
    for field in range(3):
        pair = []
        for which, ref in ((1, yhi_ref), (0, ylo_ref)):
            ends = [corner(shi_ref, at, field, which), corner(slo_ref, at, field, which)]
            pair.append(jnp.concatenate([ref[field]] + ends, axis=0))
        out.append(pair)
    return out


def side(strip, k):
    right, left = strip
    lane = lane_iota(right.shape)
    shift = (-HALO * k) % LANES
    right = pltpu.roll(right, shift, 1) if shift else right
    left = pltpu.roll(left, (LANES - HALO - HALO * k) % LANES, 1)
    return jnp.where(lane < HALO, right, jnp.where(lane >= LANES - HALO, left, 0.0))


def after(x, axis):
    return pltpu.roll(x, x.shape[axis] - 1, axis)


def before(x, axis):
    return pltpu.roll(x, 1, axis)


def pointwise(head, conduct, steep, capacity):
    sat = 0.5 + 0.5 * jnp.tanh(0.5 * (steep * head))
    slope = steep * sat * (1.0 - sat)
    cond = conduct * (0.1 + 0.9 * sat * sat)
    deriv = 0.9 * conduct * sat * slope
    weighted = storage_weight * capacity
    return cond, deriv, weighted * slope, weighted * sat


def joined(*refs):
    return lambda k: jnp.concatenate([ref[k] for ref in refs], axis=1)


def plain(ref):
    return lambda k: ref[k]


def face_of(here, there, extra=None):
    mean = 0.5 * (here[1] + there[1])
    drop = here[0] - there[0]
    if extra is not None:
        drop = drop + extra
    return mean + here[2] * drop, mean - there[2] * drop, mean * drop


def ring_faces(state, axis, inside=None):
    a, b, face = face_of(state, [after(x, axis) for x in state])
    if inside is not None:
        a, b, face = (jnp.where(inside, x, 0.0) for x in (a, b, face))
    return face - before(face, axis), a + before(b, axis), b, before(a, axis)


def linearize(layers, state_of, store_of, y_faces, masked, coefs, finish):
    diag_ref, xp_ref, xm_ref, yp_ref, ym_ref, az_ref, bz_ref = coefs
    above = None
    for k in range(layers):
        state = state_of(k)
        net_x, diag_x, xp, xm = ring_faces(state, 0)
        net_y, diag_y, yp, ym = y_faces(k, state)
        for ref, value in ((xp_ref, xp), (xm_ref, xm), (yp_ref, yp), (ym_ref, ym)):
            ref[k] = masked(value)
        if k + 1 < layers:
            a, b, face = face_of(state, state_of(k + 1), 1.0)
            az_ref[k] = a
            bz_ref[k] = b
        else:
            a, face = 2.0 * state[2], state[1]
        diag = store_of(k) + diag_x + diag_y + a
        value = net_x + net_y + face
        if above is not None:
            diag = diag + above[1]
            value = value - above[0]
        above = (face, b)
        diag_ref[k] = diag
        finish(k, masked(value))


def apply(v_ref, coefs, k):
    diag_of, xp_of, xm_of, yp_of, ym_of, az_of, bz_of = coefs
    v = v_ref[k]
    value = diag_of(k) * v
    value = value - xp_of(k) * after(v, 0) - xm_of(k) * before(v, 0)
    value = value - yp_of(k) * after(v, 1) - ym_of(k) * before(v, 1)
    if k > 0:
        value = value - az_of(k - 1) * v_ref[k - 1]
    if k + 1 < v_ref.shape[0]:
        value = value - bz_of(k) * v_ref[k + 1]
    return value


def powers(basis, coefs, tile, out_ref):
    layers = basis[0].shape[0]
    rows, cols = tile
    for step in range(KRYLOV - 1):
        for k in range(layers):
            basis[step + 1][k] = apply(basis[step], coefs, k)
    sums = [jnp.zeros((8, LANES), f32) for _ in PAIRS]
    for k in range(layers):
        top = apply(basis[-1], coefs, k)
        for at in range(0, rows, 8):
            for lane_at in range(0, cols, LANES):
                part = (slice(at, at + 8), slice(lane_at, lane_at + LANES))
                vs = [b[(k,) + part] for b in basis] + [top[part]]
                for e, (i, j) in enumerate(PAIRS):
                    sums[e] = sums[e] + vs[i] * vs[j]
    lines = [jnp.sum(x, axis=0, keepdims=True) for x in sums]
    lines.append(jnp.zeros((16 - len(PAIRS), LANES), f32))
    block = jnp.sum(jnp.concatenate(lines, axis=0), axis=1, keepdims=True)
    line = lax.broadcasted_iota(jnp.int32, (16, LANES), 0)
    flat = jnp.sum(jnp.where(lane_iota((16, LANES)) == line, block, 0.0), axis=0, keepdims=True)
    for d in range(out_ref.shape[0]):
        out_ref[d] = flat


def solve(gram_ref):
    terms = [gram_ref[d] for d in range(gram_ref.shape[0])]
    while len(terms) > 1:
        terms = [functools.reduce(jnp.add, terms[i : i + 2]) for i in range(0, len(terms), 2)]
    total = terms[0]
    line = lax.broadcasted_iota(jnp.int32, (16, LANES), 0)
    spread = jnp.broadcast_to(total, (16, LANES))
    column = jnp.sum(jnp.where(lane_iota((16, LANES)) == line, spread, 0.0), axis=1, keepdims=True)
    gram = {}
    for e, (i, j) in enumerate(PAIRS):
        gram[i, j] = gram[j, i] = column[e : e + 1, :]

    def times_gram(c):
        out = []
        for i in range(KRYLOV + 1):
            out.append(functools.reduce(jnp.add, [gram[i, m] * c[m] for m in range(len(c))]))
        return out

    def dot(a, b):
        return functools.reduce(jnp.add, [x * y for x, y in zip(a, b)])

    square = gram[0, 0] + norm_epsilon
    inverse = lax.rsqrt(square)
    beta = square * inverse
    basis = [[inverse]]
    images = [times_gram(basis[0])]
    hessen = {}
    for j in range(KRYLOV):
        w = [jnp.zeros_like(beta)] + basis[j]
        for i in range(j + 1):
            product = dot(w, images[i])
            hessen[i, j] = product
            w = [w[m] - product * basis[i][m] if m < len(basis[i]) else w[m] for m in range(len(w))]
        square = jnp.maximum(dot(w, times_gram(w)), 0.0) + norm_epsilon
        inverse = lax.rsqrt(square)
        hessen[j + 1, j] = square * inverse
        if j + 1 < KRYLOV:
            basis.append([x * inverse for x in w])
            images.append(times_gram(basis[-1]))
    n = KRYLOV
    normal = {}
    for a in range(n):
        for b in range(a + 1):
            normal[a, b] = functools.reduce(
                jnp.add,
                [hessen[i, a] * hessen[i, b] for i in range(n + 1) if (i, a) in hessen and (i, b) in hessen],
            )
    factor = {}
    inverse = []
    for a in range(n):
        for b in range(a + 1):
            value = normal[a, b]
            for m in range(b):
                value = value - factor[a, m] * factor[b, m]
            if a == b:
                inverse.append(lax.rsqrt(value))
            else:
                factor[a, b] = value * inverse[b]
    forward = []
    for a in range(n):
        value = hessen[0, a] * beta
        for m in range(a):
            value = value - factor[a, m] * forward[m]
        forward.append(value * inverse[a])
    backward = [None] * n
    for a in reversed(range(n)):
        value = forward[a]
        for m in range(a + 1, n):
            value = value - factor[m, a] * backward[m]
        backward[a] = value * inverse[a]
    return [
        functools.reduce(jnp.add, [backward[j] * basis[j][i] for j in range(i, n)]) for i in range(n)
    ]


def state_kernel(
    table_ref, head_ref, soil_ref, lo_ref, hi_ref,
    ext_ref, ks_ref, steep_ref, cap_ref, cond_ref, deriv_ref, store_ref, water_ref,
):
    layers, rows, cols = head_ref.shape
    tables = table_rows(table_ref, rows + 2 * HALO)
    every = slice(0, cols)
    for k in range(layers):
        ends = ends_of(lo_ref, hi_ref, k, STATE_DEPTH, every)
        head = jnp.concatenate([head_ref[k], ends], axis=0)
        ends = ends_of(lo_ref, hi_ref, layers + k, STATE_DEPTH, every)
        index = jnp.concatenate([soil_ref[k] + 1, ends.astype(jnp.int32)], axis=0)
        conduct, steep, capacity = (lookup(row, index) for row in tables)
        values = (head, conduct, steep, capacity) + pointwise(head, conduct, steep, capacity)
        outs = (ext_ref, ks_ref, steep_ref, cap_ref, cond_ref, deriv_ref, store_ref, water_ref)
        for ref, value in zip(outs, values):
            ref[k] = value


def flow_kernel(ext_ref, ks_ref, cond_ref, deriv_ref, store_ref, flow_ref, *coefs, rows):
    layers, _, cols = ext_ref.shape
    mask = (ks_ref[0] > 0.0).astype(f32)
    inside = lane_iota(mask.shape) < cols - 1

    def masked(value):
        return jnp.concatenate([value[:rows], value[rows:] * mask[rows:]], axis=0)

    def finish(k, value):
        flow_ref[k] = value

    linearize(
        layers, lambda k: (ext_ref[k], cond_ref[k], deriv_ref[k]), plain(store_ref),
        lambda k, state: ring_faces(state, 1, inside), masked, coefs, finish,
    )


def first_kernel(
    table_ref, src_ref, slo_ref, shi_ref, ylo_ref, yhi_ref,
    ext_ref, ks_ref, cond_ref, deriv_ref, water_ref, flow_ref, *rest,
):
    mains, rest = rest[:7], rest[7:]
    ext_side, ks_side, steep_side, cap_side, base_ref, p0_ref, p1_ref, p2_ref, gram_ref = rest[:9]
    sides, (cond_side, deriv_side, store_side) = rest[9:16], rest[16:19]
    diag_first, diag_last, yp_last, ym_first = rest[19:23]
    layers, rows, cols = src_ref.shape
    tables = table_rows(table_ref, rows + 2 * HALO)
    heads, soils, sources = tall_strips(layers, ylo_ref, yhi_ref, slo_ref, shi_ref)
    start, end, middle = slice(0, LANES), slice(cols - LANES, cols), slice(LANES, cols - LANES)
    lane = lane_iota((rows + 2 * HALO, LANES))
    is_first, is_last = lane == 0, lane == LANES - 1

    def source_of(k):
        ends = ends_of(slo_ref, shi_ref, k, SOURCE_DEPTH, slice(0, cols))
        return jnp.concatenate([src_ref[k], ends], axis=0)

    for k in range(layers):
        head = side(heads, k)
        index = side(soils, k).astype(jnp.int32)
        conduct, steep, capacity = (lookup(row, index) for row in tables)
        cond, deriv, store, water = pointwise(head, conduct, steep, capacity)
        outs = (ext_side, ks_side, steep_side, cap_side, cond_side, deriv_side, store_side)
        for ref, value in zip(outs, (head, conduct, steep, capacity, cond, deriv, store)):
            ref[k] = value
        base_ref[k, :, 0:cols] = water_ref[k] + source_of(k)
        base_ref[k, :, cols:] = water + side(sources, k)
        p0_ref[k, :, middle] = flow_ref[k, :, middle] + (water_ref[k, :, middle] - base_ref[k, :, middle])
        p0_ref[k, :, cols:] = water - base_ref[k, :, cols:]

    masks = [(ref > 0.0).astype(f32) for ref in (ks_ref[0, :, start], ks_ref[0, :, end], ks_side[0])]

    def y_faces(k, state):
        first = (ext_ref[k, :, start], cond_ref[k, :, start], deriv_ref[k, :, start])
        last = (ext_ref[k, :, end], cond_ref[k, :, end], deriv_ref[k, :, end])
        moved = [after(x, 1) for x in state]
        ahead = [jnp.where(is_last, after(x, 1), y) for x, y in zip(first, moved)]
        a, b, face = face_of(state, ahead)
        a_in, b_in, face_in = (jnp.where(is_last, x, 0.0) for x in face_of(last, moved))
        a_out, b_out, face_out = (before(x, 1) for x in (a, b, face))
        a_pre, b_pre, face_pre = (before(x, 1) for x in (a_in, b_in, face_in))
        gain = water_ref[k, :, end] - base_ref[k, :, end]
        p0_ref[k, :, end] = flow_ref[k, :, end] + face_in * masks[1] + gain
        diag_last[k] = mains[0][k, :, end] + a_in
        yp_last[k] = mains[3][k, :, end] + b_in * masks[1]
        gain = water_ref[k, :, start] - base_ref[k, :, start]
        p0_ref[k, :, start] = flow_ref[k, :, start] - jnp.where(is_first, face_out, 0.0) * masks[0] + gain
        diag_first[k] = mains[0][k, :, start] + jnp.where(is_first, b_out, 0.0)
        ym_first[k] = mains[4][k, :, start] + jnp.where(is_first, a_out, 0.0) * masks[0]
        a_pre, b_pre, face_pre = (
            jnp.where(is_first, x, y)
            for x, y in ((a_pre, a_out), (b_pre, b_out), (face_pre, face_out))
        )
        return face - face_pre, a + b_pre, b, a_pre

    def finish(k, value):
        p0_ref[k, :, cols:] = p0_ref[k, :, cols:] + value

    linearize(
        layers, lambda k: (ext_side[k], cond_side[k], deriv_side[k]), plain(store_side),
        y_faces, lambda value: value * masks[2], sides, finish,
    )

    def pieces(n, first_of, last_of):
        main, beside = mains[n], sides[n]
        return lambda k: jnp.concatenate(
            [first_of(main, k), main[k, :, middle], last_of(main, k), beside[k]], axis=1
        )

    def of_start(ref, k):
        return ref[k, :, start]

    def of_end(ref, k):
        return ref[k, :, end]

    coefs = [joined(main, beside) for main, beside in zip(mains, sides)]
    coefs[0] = pieces(0, lambda _, k: diag_first[k], lambda _, k: diag_last[k])
    coefs[3] = pieces(3, of_start, lambda _, k: yp_last[k])
    coefs[4] = pieces(4, lambda _, k: ym_first[k], of_end)
    powers((p0_ref, p1_ref, p2_ref), coefs, (rows, cols), gram_ref)


def second_kernel(
    arrived_ref, old_ref, ks_ref, steep_ref, cap_ref, old_side, ks_side, steep_side, cap_side,
    base_ref, q0_ref, q1_ref, q2_ref,
    part_ref, p0_ref, p1_ref, p2_ref, gram_ref, ext_ref, cond_ref, deriv_ref, store_ref, gain_ref, *coefs,
):
    layers = old_ref.shape[0]
    rows, cols = part_ref.shape[1:]
    x = solve(arrived_ref)
    near = lax.broadcasted_iota(jnp.int32, (HALO, cols + LANES), 0) < HALO // 2

    def folded(of):
        def get(k):
            value = of(k)
            ends = jnp.where(near, value[rows : rows + HALO], value[rows + HALO :])
            return jnp.concatenate([value[:rows], ends], axis=0)

        return get

    old_of, ks_of = folded(joined(old_ref, old_side)), folded(joined(ks_ref, ks_side))
    steep_of, cap_of = folded(joined(steep_ref, steep_side)), folded(joined(cap_ref, cap_side))
    base_of, *qs = (folded(plain(ref)) for ref in (base_ref, q0_ref, q1_ref, q2_ref))
    for k in range(layers):
        head = old_of(k)
        for value, q_of in zip(x, qs):
            head = head - value * q_of(k)
        cond, deriv, store, water = pointwise(head, ks_of(k), steep_of(k), cap_of(k))
        ext_ref[k] = head
        part_ref[k] = head[:rows, :cols]
        cond_ref[k] = cond
        deriv_ref[k] = deriv
        store_ref[k] = store
        gain_ref[k] = water - base_of(k)
    mask = (ks_of(0) > 0.0).astype(f32)

    def masked(value):
        own = value[:rows, cols:] * mask[:rows, cols:]
        top = jnp.concatenate([value[:rows, :cols], own], axis=1)
        return jnp.concatenate([top, value[rows:] * mask[rows:]], axis=0)

    def finish(k, value):
        p0_ref[k] = value + gain_ref[k]

    linearize(
        layers, lambda k: (ext_ref[k], cond_ref[k], deriv_ref[k]), plain(store_ref),
        lambda k, state: ring_faces(state, 1), masked, coefs, finish,
    )
    powers((p0_ref, p1_ref, p2_ref), [plain(ref) for ref in coefs], (rows, cols), gram_ref)


def last_kernel(arrived_ref, part_ref, q0_ref, q1_ref, q2_ref, head_ref):
    layers, rows, cols = part_ref.shape
    x = solve(arrived_ref)
    for k in range(layers):
        own = (k, slice(0, rows), slice(0, cols))
        head_ref[k] = part_ref[k] - x[0] * q0_ref[own] - x[1] * q1_ref[own] - x[2] * q2_ref[own]


def shards(head_old, soil_type, soil_table, forcing, canopy, column_slot):
    layers, rows, cols = head_old.shape
    both = ("gx", "gy")
    devices = lax.axis_size("gx") * lax.axis_size("gy")
    tall, wide = rows + 2 * HALO, cols + LANES
    own, ext = ((layers, rows, cols), f32), ((layers, tall, wide), f32)
    gram_block = ((devices, 1, LANES), f32)

    def exchange(to_lower, to_upper, axis):
        size = lax.axis_size(axis)
        up = [(i, i + 1) for i in range(size - 1)]
        down = [(j, i) for i, j in up]
        return lax.ppermute(to_upper, axis, up), lax.ppermute(to_lower, axis, down)

    def spread(x, axes):
        return lax.all_to_all(x, axes, split_axis=0, concat_axis=0, tiled=True)

    def edge(count):
        return (-(-count // 8) * 8, cols), f32

    send, down, up = call(
        pack_kernel,
        [((devices, 8, LANES), f32)] + [edge(2 * STATE_DEPTH * layers)] * 2,
        3,
        scratch=[
            pltpu.VMEM(canopy.shape, f32),
            pltpu.VMEM(head_old.shape, f32),
            pltpu.VMEM(soil_type.shape, jnp.int32),
            pltpu.SemaphoreType.DMA((3,)),
        ],
        in_specs=[pl.BlockSpec(memory_space=pl.ANY)] * 3,
        grant=63400000,
    )(canopy, head_old, soil_type)
    arrived = spread(send, both)
    lo, hi = exchange(down, up, "gx")
    columns = (head_old, soil_type, forcing, column_slot)
    table = ((devices // 2, -(-layers // 2) + 1, 8, LANES), jnp.int32)
    some, flux, tab, factor = call(
        edge_source_kernel,
        [((layers, rows, 2 * LANES), f32), ((2, rows, 2 * LANES), f32), table, ((devices // 2, 8, LANES), f32)],
        6,
        in_specs=[smem] + [vmem] * 5,
    )(soil_table, arrived, *columns)
    ydown, yup = call(strip_kernel, [((3, rows, LANES), f32)] * 2, 3)(head_old, soil_type, some)
    ylo, yhi = exchange(ydown, yup, "gy")
    source, flux = call(
        inner_source_kernel, [own, ((2, rows, cols), f32)], 9, in_specs=[smem] + [vmem] * 8
    )(soil_table, tab, factor, *columns, some, flux)
    sdown, sup = call(source_edge_kernel, [edge(SOURCE_DEPTH * layers + HALO + HALO // 2)] * 2, 3)(
        source, ylo, yhi
    )
    slo, shi = exchange(sdown, sup, "gx")
    main, side_block = ((layers, tall, cols), f32), ((layers, tall, LANES), f32)
    old, ks, steep, cap, cond, deriv, store, water = call(
        state_kernel, [main] * 8, 5, in_specs=[smem] + [vmem] * 4
    )(soil_table, head_old, soil_type, lo, hi)
    flow, *coefs = call(functools.partial(flow_kernel, rows=rows), [main] * 8, 5)(
        old, ks, cond, deriv, store
    )
    old_s, ks_s, steep_s, cap_s, base, p0, p1, p2, gram = call(
        first_kernel,
        [side_block] * 4 + [ext] * 4 + [gram_block],
        19,
        scratch=[pltpu.VMEM(side_block[0], f32)] * 14,
        in_specs=[smem] + [vmem] * 18,
    )(soil_table, source, slo, shi, ylo, yhi, old, ks, cond, deriv, water, flow, *coefs)
    sums = spread(gram, both)
    part, q0, q1, q2, gram = call(
        second_kernel,
        [own] + [((layers, rows + HALO, wide), f32)] * 3 + [gram_block],
        13,
        scratch=[pltpu.VMEM((layers, rows + HALO, wide), f32)] * 12,
    )(sums, old, ks, steep, cap, old_s, ks_s, steep_s, cap_s, base, p0, p1, p2)
    sums = spread(gram, both)
    (head,) = call(last_kernel, [own], 5)(sums, part, q0, q1, q2)
    return head, flux


def solution(mesh):
    return jax.shard_map(
        shards,
        mesh=mesh,
        in_specs=(
            P(None, "gx", "gy"),
            P(None, "gx", "gy"),
            P(),
            P(None, "gx", "gy"),
            P(None, ("gx", "gy")),
            P("gx", "gy"),
        ),
        out_specs=(P(None, "gx", "gy"), P(None, "gx", "gy")),
        check_vma=False,
    )
```

```python
import functools

import jax
import jax.numpy as jnp
from jax import lax
from jax.experimental import pallas as pl
from jax.experimental.pallas import tpu as pltpu
from jax.sharding import PartitionSpec as P

NEWTON = 2
KRYLOV = 3
HALO = 8
STATE_DEPTH = 7
SOURCE_DEPTH = 6
FIXED = 65535.0
LANES = 128
SLOT = 64

storage_weight = 4.0
norm_epsilon = 1e-06

VMEM_LIMIT = 20 * 1024 * 1024
PAIRS = [(i, j) for i in range(KRYLOV + 1) for j in range(i, KRYLOV + 1)]

f32 = jnp.float32
vmem = pl.BlockSpec(memory_space=pltpu.VMEM)
smem = pl.BlockSpec(memory_space=pltpu.SMEM)


def call(body, outs, n_in, scratch=(), in_specs=None, flops=1000000, grant=VMEM_LIMIT):
    return pl.pallas_call(
        body,
        out_shape=[jax.ShapeDtypeStruct(s, d) for s, d in outs],
        in_specs=in_specs or [vmem] * n_in,
        out_specs=[vmem] * len(outs),
        scratch_shapes=list(scratch),
        compiler_params=pltpu.CompilerParams(vmem_limit_bytes=grant),
        cost_estimate=pl.CostEstimate(flops=flops, bytes_accessed=1000000, transcendentals=0),
    )


def lane_iota(shape):
    return lax.broadcasted_iota(jnp.int32, shape, len(shape) - 1)


def pack_kernel(
    canopy_hbm, head_hbm, soil_hbm, send_ref, down_ref, up_ref, canopy_ref, head_ref, soil_ref, sems
):
    copies = [
        pltpu.make_async_copy(canopy_hbm, canopy_ref, sems.at[0]),
        pltpu.make_async_copy(head_hbm, head_ref, sems.at[1]),
        pltpu.make_async_copy(soil_hbm, soil_ref, sems.at[2]),
    ]
    for copy in copies:
        copy.start()
    copies[0].wait()
    rows = canopy_ref.shape[0]
    low = lane_iota((8, LANES)) < SLOT
    for t in range(canopy_ref.shape[1] // LANES):
        here = slice(t * LANES, (t + 1) * LANES)
        first = canopy_ref[0:8, here]
        rest = jnp.concatenate([canopy_ref[8:rows, here], jnp.zeros((16 - rows, LANES), f32)], axis=0)
        send_ref[2 * t] = jnp.where(low, first, pltpu.roll(rest, SLOT, 1))
        send_ref[2 * t + 1] = jnp.where(low, pltpu.roll(first, SLOT, 1), rest)
    layers, rows, _ = head_ref.shape
    copies[1].wait()
    copies[2].wait()
    for out_ref, part in ((down_ref, slice(0, STATE_DEPTH)), (up_ref, slice(rows - STATE_DEPTH, rows))):
        for k in range(layers):
            out_ref[STATE_DEPTH * k : STATE_DEPTH * (k + 1)] = head_ref[k][part]
        for k in range(layers):
            at = STATE_DEPTH * (layers + k)
            out_ref[at : at + STATE_DEPTH] = (soil_ref[k] + 1).astype(f32)[part]


def table_rows(table_ref, rows):
    lane = lane_iota((rows, LANES))
    out = []
    for field in range(table_ref.shape[0]):
        row = jnp.zeros((rows, LANES), f32)
        for kind in range(table_ref.shape[1]):
            row = jnp.where(lane == kind + 1, table_ref[field, kind], row)
        out.append(row)
    return out


def lookup(row, index):
    pieces = [
        jnp.take_along_axis(row, index[:, at : at + LANES], axis=1, mode="promise_in_bounds")
        for at in range(0, index.shape[1], LANES)
    ]
    return jnp.concatenate(pieces, axis=1)


def sigmoid(u):
    return 1.0 / (1.0 + jnp.exp(-u))


def edge_source_kernel(
    table_ref, arrived_ref, head_ref, soil_ref, forcing_ref, slot_ref,
    source_ref, flux_ref, tab_ref, factor_ref,
):
    layers, rows, cols = head_ref.shape
    owners = arrived_ref.shape[0]
    pairs = -(-layers // 2)
    low = lane_iota((8, LANES)) < SLOT
    line = lax.broadcasted_iota(jnp.int32, (16, LANES), 0)
    is_root = (line >= 3) & (line < 3 + layers)

    def unpack(t, _):
        first = arrived_ref[2 * t]
        second = arrived_ref[2 * t + 1]
        both = jnp.concatenate(
            [
                jnp.where(low, first, pltpu.roll(second, SLOT, 1)),
                jnp.where(low, pltpu.roll(first, SLOT, 1), second),
            ],
            axis=0,
        )
        leaf_area, albedo, resist = both[0:1], both[1:2], both[2:3]
        root_sum = jnp.sum(jnp.where(is_root, both, 0.0), axis=0, keepdims=True)
        factor = leaf_area / ((leaf_area + resist) * root_sum) * (1.0 / FIXED)
        factor_ref[t] = jnp.broadcast_to(factor, (8, LANES))
        fixed = (both * FIXED + 0.5).astype(jnp.int32)
        for m in range(pairs):
            word = fixed[3 + m : 4 + m]
            if m + pairs < layers:
                word = word | (fixed[3 + m + pairs : 4 + m + pairs] << 16)
            tab_ref[t, m] = jnp.broadcast_to(word, (8, LANES))
        leaf = ((0.5 + 0.3 * leaf_area) * (0.25 * FIXED) + 0.5).astype(jnp.int32)
        bright = ((1.0 - albedo) * FIXED + 0.5).astype(jnp.int32)
        tab_ref[t, pairs] = jnp.broadcast_to(leaf | (bright << 16), (8, LANES))
        return 0

    lax.fori_loop(0, owners // 2, unpack, 0, unroll=16)
    places = [(0, 0), (cols - LANES, LANES)]
    land_columns(
        table_ref, tab_ref, factor_ref, head_ref, soil_ref, forcing_ref, slot_ref, source_ref, flux_ref, places
    )


def inner_source_kernel(
    table_ref, tab_ref, factor_ref, head_ref, soil_ref, forcing_ref, slot_ref, some_ref, part_ref,
    source_ref, flux_ref,
):
    cols = head_ref.shape[2]
    places = [(at, at) for at in range(LANES, cols - LANES, LANES)]
    land_columns(
        table_ref, tab_ref, factor_ref, head_ref, soil_ref, forcing_ref, slot_ref, source_ref, flux_ref, places
    )
    for whole_ref, piece_ref in ((source_ref, some_ref), (flux_ref, part_ref)):
        for k in range(whole_ref.shape[0]):
            whole_ref[k, :, 0:LANES] = piece_ref[k, :, 0:LANES]
            whole_ref[k, :, cols - LANES : cols] = piece_ref[k, :, LANES : 2 * LANES]


def land_columns(
    table_ref, tab_ref, factor_ref, head_ref, soil_ref, forcing_ref, slot_ref, source_ref, flux_ref, places
):
    layers, rows, _ = head_ref.shape
    halves_of = tab_ref.shape[0]
    pairs = tab_ref.shape[1] - 1
    tables = table_rows(table_ref, rows)
    shape = (rows, LANES)

    def whole(block):
        return jnp.concatenate([block] * (rows // 8), axis=0)

    for at_y, put in places:
        here = (slice(0, rows), slice(at_y, at_y + LANES))
        there = (slice(0, rows), slice(put, put + LANES))
        slot = slot_ref[here]
        land = slot >= 0
        value = jnp.maximum(slot, 0)
        lane = value & (LANES - 1)
        tile = value >> 7

        def pick(t, held):
            match = tile == t
            found = [lookup(whole(tab_ref[t, m]), lane) for m in range(pairs + 1)]
            found.append(lookup(whole(factor_ref[t]), lane))
            return tuple(jnp.where(match, new, old) for new, old in zip(found, held))

        held = tuple([jnp.full(shape, 1, jnp.int32)] * (pairs + 1) + [jnp.full(shape, 1.0 / FIXED, f32)])
        if halves_of <= 16:
            for t in range(halves_of):
                held = pick(t, held)
        else:
            held = lax.fori_loop(0, halves_of, pick, held, unroll=8)
        *words, terms, factor = held

        def halves(word):
            upper = lax.shift_right_logical(word, jnp.full(shape, 16, jnp.int32))
            return (word & 0xFFFF).astype(f32), upper.astype(f32)

        leaf, bright = halves(terms)
        exchange_coef = leaf * (4.0 / FIXED)
        absorbed = bright * (1.0 / FIXED)
        split = [halves(word) for word in words]
        uptake = []
        for k in range(layers):
            index = soil_ref[(k,) + here] + 1
            steep = lookup(tables[1], index)
            root = factor * split[k % pairs][k // pairs]
            uptake.append(root * sigmoid(steep * head_ref[(k,) + here]))
            if k == 0:
                ks_top = lookup(tables[0], index)
        conductance = functools.reduce(jnp.add, uptake)
        sunlight, air_temp, humidity, rainfall = (forcing_ref[(i,) + here] for i in range(4))
        radiation = absorbed * sunlight + 0.3
        square = air_temp * air_temp
        excess = radiation - 0.3 * square * square - conductance * (0.5 - humidity)
        slope = -1.2 * square * air_temp - exchange_coef - conductance
        rise = -excess / slope
        surface = air_temp + rise
        vapour = 0.5 * jnp.exp(2.0 * rise)
        square = surface * surface
        excess = (
            radiation
            - 0.3 * square * square
            - exchange_coef * rise
            - conductance * (vapour - humidity)
        )
        slope = -1.2 * square * surface - exchange_coef - 2.0 * conductance * vapour
        rise = rise - excess / slope
        rate = 0.5 * jnp.exp(2.0 * rise) - humidity
        infiltration = rainfall * ks_top / (rainfall + ks_top)
        infiltration = jnp.where(land, infiltration, 0.0)
        rate = jnp.where(land, rate, 0.0)
        flux_ref[(0,) + there] = conductance * rate
        flux_ref[(1,) + there] = infiltration
        for k in range(layers):
            value = -rate * uptake[k]
            if k == 0:
                value = value + infiltration
            source_ref[(k,) + there] = value


def strips(planes, shift_from):
    packed = None
    for k, plane in enumerate(planes):
        lane = lane_iota(plane.shape)
        shift = (HALO * k - shift_from) % LANES
        moved = pltpu.roll(plane, shift, 1) if shift else plane
        inside = (lane >= HALO * k) & (lane < HALO * (k + 1))
        packed = jnp.where(inside, moved, 0.0 if packed is None else packed)
    return packed


def strip_parts(cols):
    return ((slice(0, LANES), 0), (slice(cols - LANES, cols), LANES - HALO))


def ends_of(lo_ref, hi_ref, at, depth, part):
    edge = slice(depth * at, depth * (at + 1))
    above, below = hi_ref[edge, part], lo_ref[edge, part]
    gap = jnp.zeros((2 * (HALO - depth), above.shape[1]), f32)
    return jnp.concatenate([above, gap, below], axis=0)


def strip_kernel(head_ref, soil_ref, some_ref, out_ref):
    layers, _, cols = head_ref.shape
    me = lax.axis_index("gy")
    blocks = []
    for (part, shift), at in zip(strip_parts(cols), (0, LANES)):
        blocks.append(
            (
                strips([head_ref[k, :, part] for k in range(layers)], shift),
                strips([(soil_ref[k, :, part] + 1).astype(f32) for k in range(layers)], shift),
                strips([some_ref[k, :, at : at + LANES] for k in range(layers)], shift),
            )
        )
    for field, (low, high) in enumerate(zip(*blocks)):
        for d in range(out_ref.shape[0]):
            out_ref[d, field] = jnp.where(d < me, low, high)


def received(strip_ref, field):
    me = lax.axis_index("gy")
    count = strip_ref.shape[0]
    below = strip_ref[jnp.maximum(me - 1, 0), field]
    above = strip_ref[jnp.minimum(me + 1, count - 1), field]
    return jnp.where(me > 0, below, 0.0), jnp.where(me + 1 < count, above, 0.0)


def source_edge_kernel(src_ref, strip_ref, down_ref, up_ref):
    layers, rows, _ = src_ref.shape
    at = SOURCE_DEPTH * layers
    pieces = [x for field in range(3) for x in received(strip_ref, field)]
    for out_ref, first in ((down_ref, 0), (up_ref, rows - HALO)):
        row = 0 if first == 0 else rows - SOURCE_DEPTH
        for k in range(layers):
            part = slice(SOURCE_DEPTH * k, SOURCE_DEPTH * (k + 1))
            out_ref[part] = src_ref[k][row : row + SOURCE_DEPTH]
        blocks = [x[first : first + HALO] for x in pieces]
        half = HALO // 2
        tail = [block[h : h + half] for block in blocks[4:6] for h in (0, half)]
        for j in range(4):
            out_ref[at : at + HALO, j * LANES : (j + 1) * LANES] = blocks[j]
            out_ref[at + HALO : at + HALO + half, j * LANES : (j + 1) * LANES] = tail[j]


def corner(edge_ref, at, field, which):
    half = HALO // 2
    if field < 2:
        j = 2 * field + which
        return edge_ref[at : at + HALO, j * LANES : (j + 1) * LANES]
    pieces = [
        edge_ref[at + HALO : at + HALO + half, j * LANES : (j + 1) * LANES]
        for j in (2 * which, 2 * which + 1)
    ]
    return jnp.concatenate(pieces, axis=0)


def tall_strips(layers, strip_ref, slo_ref, shi_ref):
    at = SOURCE_DEPTH * layers
    out = []
    for field in range(3):
        pair = []
        below, above = received(strip_ref, field)
        for which, piece in ((1, above), (0, below)):
            ends = [corner(shi_ref, at, field, which), corner(slo_ref, at, field, which)]
            pair.append(jnp.concatenate([piece] + ends, axis=0))
        out.append(pair)
    return out


def side(strip, k):
    right, left = strip
    lane = lane_iota(right.shape)
    shift = (-HALO * k) % LANES
    right = pltpu.roll(right, shift, 1) if shift else right
    left = pltpu.roll(left, (LANES - HALO - HALO * k) % LANES, 1)
    return jnp.where(lane < HALO, right, jnp.where(lane >= LANES - HALO, left, 0.0))


def after(x, axis):
    return pltpu.roll(x, x.shape[axis] - 1, axis)


def before(x, axis):
    return pltpu.roll(x, 1, axis)


def pointwise(head, conduct, steep, capacity):
    sat = 0.5 + 0.5 * jnp.tanh(0.5 * (steep * head))
    slope = steep * sat * (1.0 - sat)
    cond = conduct * (0.1 + 0.9 * sat * sat)
    deriv = 0.9 * conduct * sat * slope
    weighted = storage_weight * capacity
    return cond, deriv, weighted * slope, weighted * sat


def joined(*refs):
    return lambda k: jnp.concatenate([ref[k] for ref in refs], axis=1)


def plain(ref):
    return lambda k: ref[k]


def face_of(here, there, extra=None):
    mean = 0.5 * (here[1] + there[1])
    drop = here[0] - there[0]
    if extra is not None:
        drop = drop + extra
    return mean + here[2] * drop, mean - there[2] * drop, mean * drop


def ring_faces(state, axis, inside=None):
    a, b, face = face_of(state, [after(x, axis) for x in state])
    if inside is not None:
        a, b, face = (jnp.where(inside, x, 0.0) for x in (a, b, face))
    return face - before(face, axis), a + before(b, axis), b, before(a, axis)


def linearize(layers, state_of, store_of, y_faces, masked, coefs, finish):
    diag_ref, xp_ref, xm_ref, yp_ref, ym_ref, az_ref, bz_ref = coefs
    above = None
    for k in range(layers):
        state = state_of(k)
        net_x, diag_x, xp, xm = ring_faces(state, 0)
        net_y, diag_y, yp, ym = y_faces(k, state)
        for ref, value in ((xp_ref, xp), (xm_ref, xm), (yp_ref, yp), (ym_ref, ym)):
            ref[k] = masked(value)
        if k + 1 < layers:
            a, b, face = face_of(state, state_of(k + 1), 1.0)
            az_ref[k] = a
            bz_ref[k] = b
        else:
            a, face = 2.0 * state[2], state[1]
        diag = store_of(k) + diag_x + diag_y + a
        value = net_x + net_y + face
        if above is not None:
            diag = diag + above[1]
            value = value - above[0]
        above = (face, b)
        diag_ref[k] = diag
        finish(k, masked(value))


def apply(v_ref, coefs, k):
    diag_of, xp_of, xm_of, yp_of, ym_of, az_of, bz_of = coefs
    v = v_ref[k]
    value = diag_of(k) * v
    value = value - xp_of(k) * after(v, 0) - xm_of(k) * before(v, 0)
    value = value - yp_of(k) * after(v, 1) - ym_of(k) * before(v, 1)
    if k > 0:
        value = value - az_of(k - 1) * v_ref[k - 1]
    if k + 1 < v_ref.shape[0]:
        value = value - bz_of(k) * v_ref[k + 1]
    return value


def powers(basis, coefs, tile, out_ref):
    layers = basis[0].shape[0]
    rows, cols = tile
    for step in range(KRYLOV - 1):
        for k in range(layers):
            basis[step + 1][k] = apply(basis[step], coefs, k)
    sums = [jnp.zeros((8, LANES), f32) for _ in PAIRS]
    for k in range(layers):
        top = apply(basis[-1], coefs, k)
        for at in range(0, rows, 8):
            for lane_at in range(0, cols, LANES):
                part = (slice(at, at + 8), slice(lane_at, lane_at + LANES))
                vs = [b[(k,) + part] for b in basis] + [top[part]]
                for e, (i, j) in enumerate(PAIRS):
                    sums[e] = sums[e] + vs[i] * vs[j]
    lines = [jnp.sum(x, axis=0, keepdims=True) for x in sums]
    lines.append(jnp.zeros((16 - len(PAIRS), LANES), f32))
    block = jnp.sum(jnp.concatenate(lines, axis=0), axis=1, keepdims=True)
    line = lax.broadcasted_iota(jnp.int32, (16, LANES), 0)
    flat = jnp.sum(jnp.where(lane_iota((16, LANES)) == line, block, 0.0), axis=0, keepdims=True)
    for d in range(out_ref.shape[0]):
        out_ref[d] = flat


def solve(gram_ref):
    terms = [gram_ref[d] for d in range(gram_ref.shape[0])]
    while len(terms) > 1:
        terms = [functools.reduce(jnp.add, terms[i : i + 2]) for i in range(0, len(terms), 2)]
    total = terms[0]
    line = lax.broadcasted_iota(jnp.int32, (16, LANES), 0)
    spread = jnp.broadcast_to(total, (16, LANES))
    column = jnp.sum(jnp.where(lane_iota((16, LANES)) == line, spread, 0.0), axis=1, keepdims=True)
    gram = {}
    for e, (i, j) in enumerate(PAIRS):
        gram[i, j] = gram[j, i] = column[e : e + 1, :]

    def times_gram(c):
        out = []
        for i in range(KRYLOV + 1):
            out.append(functools.reduce(jnp.add, [gram[i, m] * c[m] for m in range(len(c))]))
        return out

    def dot(a, b):
        return functools.reduce(jnp.add, [x * y for x, y in zip(a, b)])

    square = gram[0, 0] + norm_epsilon
    inverse = lax.rsqrt(square)
    beta = square * inverse
    basis = [[inverse]]
    images = [times_gram(basis[0])]
    hessen = {}
    for j in range(KRYLOV):
        w = [jnp.zeros_like(beta)] + basis[j]
        for i in range(j + 1):
            product = dot(w, images[i])
            hessen[i, j] = product
            w = [w[m] - product * basis[i][m] if m < len(basis[i]) else w[m] for m in range(len(w))]
        square = jnp.maximum(dot(w, times_gram(w)), 0.0) + norm_epsilon
        inverse = lax.rsqrt(square)
        hessen[j + 1, j] = square * inverse
        if j + 1 < KRYLOV:
            basis.append([x * inverse for x in w])
            images.append(times_gram(basis[-1]))
    n = KRYLOV
    normal = {}
    for a in range(n):
        for b in range(a + 1):
            normal[a, b] = functools.reduce(
                jnp.add,
                [hessen[i, a] * hessen[i, b] for i in range(n + 1) if (i, a) in hessen and (i, b) in hessen],
            )
    factor = {}
    inverse = []
    for a in range(n):
        for b in range(a + 1):
            value = normal[a, b]
            for m in range(b):
                value = value - factor[a, m] * factor[b, m]
            if a == b:
                inverse.append(lax.rsqrt(value))
            else:
                factor[a, b] = value * inverse[b]
    forward = []
    for a in range(n):
        value = hessen[0, a] * beta
        for m in range(a):
            value = value - factor[a, m] * forward[m]
        forward.append(value * inverse[a])
    backward = [None] * n
    for a in reversed(range(n)):
        value = forward[a]
        for m in range(a + 1, n):
            value = value - factor[m, a] * backward[m]
        backward[a] = value * inverse[a]
    return [
        functools.reduce(jnp.add, [backward[j] * basis[j][i] for j in range(i, n)]) for i in range(n)
    ]


def state_kernel(
    table_ref, head_ref, soil_ref, lo_ref, hi_ref,
    ext_ref, ks_ref, steep_ref, cap_ref, cond_ref, deriv_ref, store_ref, water_ref,
):
    layers, rows, cols = head_ref.shape
    tables = table_rows(table_ref, rows + 2 * HALO)
    every = slice(0, cols)
    for k in range(layers):
        ends = ends_of(lo_ref, hi_ref, k, STATE_DEPTH, every)
        head = jnp.concatenate([head_ref[k], ends], axis=0)
        ends = ends_of(lo_ref, hi_ref, layers + k, STATE_DEPTH, every)
        index = jnp.concatenate([soil_ref[k] + 1, ends.astype(jnp.int32)], axis=0)
        conduct, steep, capacity = (lookup(row, index) for row in tables)
        values = (head, conduct, steep, capacity) + pointwise(head, conduct, steep, capacity)
        outs = (ext_ref, ks_ref, steep_ref, cap_ref, cond_ref, deriv_ref, store_ref, water_ref)
        for ref, value in zip(outs, values):
            ref[k] = value


def flow_kernel(ext_ref, ks_ref, cond_ref, deriv_ref, store_ref, flow_ref, *coefs, rows):
    layers, _, cols = ext_ref.shape
    mask = (ks_ref[0] > 0.0).astype(f32)
    inside = lane_iota(mask.shape) < cols - 1

    def masked(value):
        return jnp.concatenate([value[:rows], value[rows:] * mask[rows:]], axis=0)

    def finish(k, value):
        flow_ref[k] = value

    linearize(
        layers, lambda k: (ext_ref[k], cond_ref[k], deriv_ref[k]), plain(store_ref),
        lambda k, state: ring_faces(state, 1, inside), masked, coefs, finish,
    )


def first_kernel(
    table_ref, src_ref, slo_ref, shi_ref, strip_ref,
    ext_ref, ks_ref, cond_ref, deriv_ref, water_ref, flow_ref, *rest,
):
    mains, rest = rest[:7], rest[7:]
    ext_side, ks_side, steep_side, cap_side, base_ref, p0_ref, p1_ref, p2_ref, gram_ref = rest[:9]
    sides, (cond_side, deriv_side, store_side) = rest[9:16], rest[16:19]
    diag_first, diag_last, yp_last, ym_first = rest[19:23]
    layers, rows, cols = src_ref.shape
    tables = table_rows(table_ref, rows + 2 * HALO)
    heads, soils, sources = tall_strips(layers, strip_ref, slo_ref, shi_ref)
    start, end, middle = slice(0, LANES), slice(cols - LANES, cols), slice(LANES, cols - LANES)
    lane = lane_iota((rows + 2 * HALO, LANES))
    is_first, is_last = lane == 0, lane == LANES - 1

    def source_of(k):
        ends = ends_of(slo_ref, shi_ref, k, SOURCE_DEPTH, slice(0, cols))
        return jnp.concatenate([src_ref[k], ends], axis=0)

    for k in range(layers):
        head = side(heads, k)
        index = side(soils, k).astype(jnp.int32)
        conduct, steep, capacity = (lookup(row, index) for row in tables)
        cond, deriv, store, water = pointwise(head, conduct, steep, capacity)
        outs = (ext_side, ks_side, steep_side, cap_side, cond_side, deriv_side, store_side)
        for ref, value in zip(outs, (head, conduct, steep, capacity, cond, deriv, store)):
            ref[k] = value
        base_ref[k, :, 0:cols] = water_ref[k] + source_of(k)
        base_ref[k, :, cols:] = water + side(sources, k)
        p0_ref[k, :, middle] = flow_ref[k, :, middle] + (water_ref[k, :, middle] - base_ref[k, :, middle])
        p0_ref[k, :, cols:] = water - base_ref[k, :, cols:]

    masks = [(ref > 0.0).astype(f32) for ref in (ks_ref[0, :, start], ks_ref[0, :, end], ks_side[0])]

    def y_faces(k, state):
        first = (ext_ref[k, :, start], cond_ref[k, :, start], deriv_ref[k, :, start])
        last = (ext_ref[k, :, end], cond_ref[k, :, end], deriv_ref[k, :, end])
        moved = [after(x, 1) for x in state]
        ahead = [jnp.where(is_last, after(x, 1), y) for x, y in zip(first, moved)]
        a, b, face = face_of(state, ahead)
        a_in, b_in, face_in = (jnp.where(is_last, x, 0.0) for x in face_of(last, moved))
        a_out, b_out, face_out = (before(x, 1) for x in (a, b, face))
        a_pre, b_pre, face_pre = (before(x, 1) for x in (a_in, b_in, face_in))
        gain = water_ref[k, :, end] - base_ref[k, :, end]
        p0_ref[k, :, end] = flow_ref[k, :, end] + face_in * masks[1] + gain
        diag_last[k] = mains[0][k, :, end] + a_in
        yp_last[k] = mains[3][k, :, end] + b_in * masks[1]
        gain = water_ref[k, :, start] - base_ref[k, :, start]
        p0_ref[k, :, start] = flow_ref[k, :, start] - jnp.where(is_first, face_out, 0.0) * masks[0] + gain
        diag_first[k] = mains[0][k, :, start] + jnp.where(is_first, b_out, 0.0)
        ym_first[k] = mains[4][k, :, start] + jnp.where(is_first, a_out, 0.0) * masks[0]
        a_pre, b_pre, face_pre = (
            jnp.where(is_first, x, y)
            for x, y in ((a_pre, a_out), (b_pre, b_out), (face_pre, face_out))
        )
        return face - face_pre, a + b_pre, b, a_pre

    def finish(k, value):
        p0_ref[k, :, cols:] = p0_ref[k, :, cols:] + value

    linearize(
        layers, lambda k: (ext_side[k], cond_side[k], deriv_side[k]), plain(store_side),
        y_faces, lambda value: value * masks[2], sides, finish,
    )

    def pieces(n, first_of, last_of):
        main, beside = mains[n], sides[n]
        return lambda k: jnp.concatenate(
            [first_of(main, k), main[k, :, middle], last_of(main, k), beside[k]], axis=1
        )

    def of_start(ref, k):
        return ref[k, :, start]

    def of_end(ref, k):
        return ref[k, :, end]

    coefs = [joined(main, beside) for main, beside in zip(mains, sides)]
    coefs[0] = pieces(0, lambda _, k: diag_first[k], lambda _, k: diag_last[k])
    coefs[3] = pieces(3, of_start, lambda _, k: yp_last[k])
    coefs[4] = pieces(4, lambda _, k: ym_first[k], of_end)
    powers((p0_ref, p1_ref, p2_ref), coefs, (rows, cols), gram_ref)


def second_kernel(
    arrived_ref, old_ref, ks_ref, steep_ref, cap_ref, old_side, ks_side, steep_side, cap_side,
    base_ref, q0_ref, q1_ref, q2_ref,
    part_ref, p0_ref, p1_ref, p2_ref, gram_ref, ext_ref, cond_ref, deriv_ref, store_ref, gain_ref, *coefs,
):
    layers = old_ref.shape[0]
    rows, cols = part_ref.shape[1:]
    x = solve(arrived_ref)
    near = lax.broadcasted_iota(jnp.int32, (HALO, cols + LANES), 0) < HALO // 2

    def folded(of):
        def get(k):
            value = of(k)
            ends = jnp.where(near, value[rows : rows + HALO], value[rows + HALO :])
            return jnp.concatenate([value[:rows], ends], axis=0)

        return get

    old_of, ks_of = folded(joined(old_ref, old_side)), folded(joined(ks_ref, ks_side))
    steep_of, cap_of = folded(joined(steep_ref, steep_side)), folded(joined(cap_ref, cap_side))
    base_of, *qs = (folded(plain(ref)) for ref in (base_ref, q0_ref, q1_ref, q2_ref))
    for k in range(layers):
        head = old_of(k)
        for value, q_of in zip(x, qs):
            head = head - value * q_of(k)
        cond, deriv, store, water = pointwise(head, ks_of(k), steep_of(k), cap_of(k))
        ext_ref[k] = head
        part_ref[k] = head[:rows, :cols]
        cond_ref[k] = cond
        deriv_ref[k] = deriv
        store_ref[k] = store
        gain_ref[k] = water - base_of(k)
    mask = (ks_of(0) > 0.0).astype(f32)

    def masked(value):
        own = value[:rows, cols:] * mask[:rows, cols:]
        top = jnp.concatenate([value[:rows, :cols], own], axis=1)
        return jnp.concatenate([top, value[rows:] * mask[rows:]], axis=0)

    def finish(k, value):
        p0_ref[k] = value + gain_ref[k]

    linearize(
        layers, lambda k: (ext_ref[k], cond_ref[k], deriv_ref[k]), plain(store_ref),
        lambda k, state: ring_faces(state, 1), masked, coefs, finish,
    )
    powers((p0_ref, p1_ref, p2_ref), [plain(ref) for ref in coefs], (rows, cols), gram_ref)


def last_kernel(arrived_ref, part_ref, q0_ref, q1_ref, q2_ref, head_ref):
    layers, rows, cols = part_ref.shape
    x = solve(arrived_ref)
    for k in range(layers):
        own = (k, slice(0, rows), slice(0, cols))
        head_ref[k] = part_ref[k] - x[0] * q0_ref[own] - x[1] * q1_ref[own] - x[2] * q2_ref[own]


def shards(head_old, soil_type, soil_table, forcing, canopy, column_slot):
    layers, rows, cols = head_old.shape
    both = ("gx", "gy")
    devices = lax.axis_size("gx") * lax.axis_size("gy")
    tall, wide = rows + 2 * HALO, cols + LANES
    own, ext = ((layers, rows, cols), f32), ((layers, tall, wide), f32)
    gram_block = ((devices, 1, LANES), f32)

    def exchange(to_lower, to_upper, axis):
        size = lax.axis_size(axis)
        up = [(i, i + 1) for i in range(size - 1)]
        down = [(j, i) for i, j in up]
        return lax.ppermute(to_upper, axis, up), lax.ppermute(to_lower, axis, down)

    def spread(x, axes):
        return lax.all_to_all(x, axes, split_axis=0, concat_axis=0, tiled=True)

    def edge(count):
        return (-(-count // 8) * 8, cols), f32

    send, down, up = call(
        pack_kernel,
        [((devices, 8, LANES), f32)] + [edge(2 * STATE_DEPTH * layers)] * 2,
        3,
        scratch=[
            pltpu.VMEM(canopy.shape, f32),
            pltpu.VMEM(head_old.shape, f32),
            pltpu.VMEM(soil_type.shape, jnp.int32),
            pltpu.SemaphoreType.DMA((3,)),
        ],
        in_specs=[pl.BlockSpec(memory_space=pl.ANY)] * 3,
        grant=63400000,
    )(canopy, head_old, soil_type)
    arrived = spread(send, both)
    lo, hi = exchange(down, up, "gx")
    columns = (head_old, soil_type, forcing, column_slot)
    table = ((devices // 2, -(-layers // 2) + 1, 8, LANES), jnp.int32)
    some, flux, tab, factor = call(
        edge_source_kernel,
        [((layers, rows, 2 * LANES), f32), ((2, rows, 2 * LANES), f32), table, ((devices // 2, 8, LANES), f32)],
        6,
        in_specs=[smem] + [vmem] * 5,
    )(soil_table, arrived, *columns)
    (strip,) = call(strip_kernel, [((lax.axis_size("gy"), 3, rows, LANES), f32)], 3)(
        head_old, soil_type, some
    )
    strip = spread(strip, "gy")
    source, flux = call(
        inner_source_kernel, [own, ((2, rows, cols), f32)], 9, in_specs=[smem] + [vmem] * 8
    )(soil_table, tab, factor, *columns, some, flux)
    sdown, sup = call(source_edge_kernel, [edge(SOURCE_DEPTH * layers + HALO + HALO // 2)] * 2, 2)(
        source, strip
    )
    slo, shi = exchange(sdown, sup, "gx")
    main, side_block = ((layers, tall, cols), f32), ((layers, tall, LANES), f32)
    old, ks, steep, cap, cond, deriv, store, water = call(
        state_kernel, [main] * 8, 5, in_specs=[smem] + [vmem] * 4
    )(soil_table, head_old, soil_type, lo, hi)
    flow, *coefs = call(functools.partial(flow_kernel, rows=rows), [main] * 8, 5)(
        old, ks, cond, deriv, store
    )
    old_s, ks_s, steep_s, cap_s, base, p0, p1, p2, gram = call(
        first_kernel,
        [side_block] * 4 + [ext] * 4 + [gram_block],
        18,
        scratch=[pltpu.VMEM(side_block[0], f32)] * 14,
        in_specs=[smem] + [vmem] * 17,
    )(soil_table, source, slo, shi, strip, old, ks, cond, deriv, water, flow, *coefs)
    sums = spread(gram, both)
    part, q0, q1, q2, gram = call(
        second_kernel,
        [own] + [((layers, rows + HALO, wide), f32)] * 3 + [gram_block],
        13,
        scratch=[pltpu.VMEM((layers, rows + HALO, wide), f32)] * 12,
    )(sums, old, ks, steep, cap, old_s, ks_s, steep_s, cap_s, base, p0, p1, p2)
    sums = spread(gram, both)
    (head,) = call(last_kernel, [own], 5)(sums, part, q0, q1, q2)
    return head, flux


def solution(mesh):
    return jax.shard_map(
        shards,
        mesh=mesh,
        in_specs=(
            P(None, "gx", "gy"),
            P(None, "gx", "gy"),
            P(),
            P(None, "gx", "gy"),
            P(None, ("gx", "gy")),
            P("gx", "gy"),
        ),
        out_specs=(P(None, "gx", "gy"), P(None, "gx", "gy")),
        check_vma=False,
    )
```

```python
import functools

import jax
import jax.numpy as jnp
from jax import lax
from jax.experimental import pallas as pl
from jax.experimental.pallas import tpu as pltpu
from jax.sharding import PartitionSpec as P

NEWTON = 2
KRYLOV = 3
HALO = 8
STATE_DEPTH = 7
SOURCE_DEPTH = 6
FIXED = 65535.0
LANES = 128
SLOT = 64

storage_weight = 4.0
norm_epsilon = 1e-06

VMEM_LIMIT = 20 * 1024 * 1024
PAIRS = [(i, j) for i in range(KRYLOV + 1) for j in range(i, KRYLOV + 1)]

f32 = jnp.float32
vmem = pl.BlockSpec(memory_space=pltpu.VMEM)
smem = pl.BlockSpec(memory_space=pltpu.SMEM)


def call(body, outs, n_in, scratch=(), in_specs=None, flops=1000000, grant=VMEM_LIMIT):
    return pl.pallas_call(
        body,
        out_shape=[jax.ShapeDtypeStruct(s, d) for s, d in outs],
        in_specs=in_specs or [vmem] * n_in,
        out_specs=[vmem] * len(outs),
        scratch_shapes=list(scratch),
        compiler_params=pltpu.CompilerParams(vmem_limit_bytes=grant),
        cost_estimate=pl.CostEstimate(flops=flops, bytes_accessed=1000000, transcendentals=0),
    )


def lane_iota(shape):
    return lax.broadcasted_iota(jnp.int32, shape, len(shape) - 1)


def pack_kernel(
    canopy_hbm, head_hbm, soil_hbm, send_ref, near_ref, far_ref, canopy_ref, head_ref, soil_ref, sems
):
    copies = [
        pltpu.make_async_copy(canopy_hbm, canopy_ref, sems.at[0]),
        pltpu.make_async_copy(head_hbm, head_ref, sems.at[1]),
        pltpu.make_async_copy(soil_hbm, soil_ref, sems.at[2]),
    ]
    for copy in copies:
        copy.start()
    copies[0].wait()
    rows = canopy_ref.shape[0]
    low = lane_iota((8, LANES)) < SLOT
    for t in range(canopy_ref.shape[1] // LANES):
        here = slice(t * LANES, (t + 1) * LANES)
        first = canopy_ref[0:8, here]
        rest = jnp.concatenate([canopy_ref[8:rows, here], jnp.zeros((16 - rows, LANES), f32)], axis=0)
        send_ref[2 * t] = jnp.where(low, first, pltpu.roll(rest, SLOT, 1))
        send_ref[2 * t + 1] = jnp.where(low, pltpu.roll(first, SLOT, 1), rest)
    layers, rows, _ = head_ref.shape
    copies[1].wait()
    copies[2].wait()
    low_rows, high_rows = slice(0, STATE_DEPTH), slice(rows - STATE_DEPTH, rows)
    upward = near_is_above()
    for n in range(2 * layers):
        plane = head_ref[n] if n < layers else (soil_ref[n - layers] + 1).astype(f32)
        part = slice(STATE_DEPTH * n, STATE_DEPTH * (n + 1))
        near_ref[part] = jnp.where(upward, plane[high_rows], plane[low_rows])
        far_ref[part] = jnp.where(upward, plane[low_rows], plane[high_rows])


def near_is_above():
    return lax.rem(lax.axis_index("gx"), 2) == 0


def below_above(near, far):
    upward = near_is_above()
    return jnp.where(upward, far, near), jnp.where(upward, near, far)


def table_rows(table_ref, rows):
    lane = lane_iota((rows, LANES))
    out = []
    for field in range(table_ref.shape[0]):
        row = jnp.zeros((rows, LANES), f32)
        for kind in range(table_ref.shape[1]):
            row = jnp.where(lane == kind + 1, table_ref[field, kind], row)
        out.append(row)
    return out


def lookup(row, index):
    pieces = [
        jnp.take_along_axis(row, index[:, at : at + LANES], axis=1, mode="promise_in_bounds")
        for at in range(0, index.shape[1], LANES)
    ]
    return jnp.concatenate(pieces, axis=1)


def sigmoid(u):
    return 1.0 / (1.0 + jnp.exp(-u))


def edge_source_kernel(
    table_ref, arrived_ref, head_ref, soil_ref, forcing_ref, slot_ref,
    source_ref, flux_ref, tab_ref, factor_ref,
):
    layers, rows, cols = head_ref.shape
    owners = arrived_ref.shape[0]
    pairs = -(-layers // 2)
    low = lane_iota((8, LANES)) < SLOT
    line = lax.broadcasted_iota(jnp.int32, (16, LANES), 0)
    is_root = (line >= 3) & (line < 3 + layers)

    def unpack(t, _):
        first = arrived_ref[2 * t]
        second = arrived_ref[2 * t + 1]
        both = jnp.concatenate(
            [
                jnp.where(low, first, pltpu.roll(second, SLOT, 1)),
                jnp.where(low, pltpu.roll(first, SLOT, 1), second),
            ],
            axis=0,
        )
        leaf_area, albedo, resist = both[0:1], both[1:2], both[2:3]
        root_sum = jnp.sum(jnp.where(is_root, both, 0.0), axis=0, keepdims=True)
        factor = leaf_area / ((leaf_area + resist) * root_sum) * (1.0 / FIXED)
        factor_ref[t] = jnp.broadcast_to(factor, (8, LANES))
        fixed = (both * FIXED + 0.5).astype(jnp.int32)
        for m in range(pairs):
            word = fixed[3 + m : 4 + m]
            if m + pairs < layers:
                word = word | (fixed[3 + m + pairs : 4 + m + pairs] << 16)
            tab_ref[t, m] = jnp.broadcast_to(word, (8, LANES))
        leaf = ((0.5 + 0.3 * leaf_area) * (0.25 * FIXED) + 0.5).astype(jnp.int32)
        bright = ((1.0 - albedo) * FIXED + 0.5).astype(jnp.int32)
        tab_ref[t, pairs] = jnp.broadcast_to(leaf | (bright << 16), (8, LANES))
        return 0

    lax.fori_loop(0, owners // 2, unpack, 0, unroll=16)
    places = [(0, 0), (cols - LANES, LANES)]
    land_columns(
        table_ref, tab_ref, factor_ref, head_ref, soil_ref, forcing_ref, slot_ref, source_ref, flux_ref, places
    )


def inner_source_kernel(
    table_ref, tab_ref, factor_ref, head_ref, soil_ref, forcing_ref, slot_ref, some_ref, part_ref,
    source_ref, flux_ref,
):
    cols = head_ref.shape[2]
    places = [(at, at) for at in range(LANES, cols - LANES, LANES)]
    land_columns(
        table_ref, tab_ref, factor_ref, head_ref, soil_ref, forcing_ref, slot_ref, source_ref, flux_ref, places
    )
    for whole_ref, piece_ref in ((source_ref, some_ref), (flux_ref, part_ref)):
        for k in range(whole_ref.shape[0]):
            whole_ref[k, :, 0:LANES] = piece_ref[k, :, 0:LANES]
            whole_ref[k, :, cols - LANES : cols] = piece_ref[k, :, LANES : 2 * LANES]


def land_columns(
    table_ref, tab_ref, factor_ref, head_ref, soil_ref, forcing_ref, slot_ref, source_ref, flux_ref, places
):
    layers, rows, _ = head_ref.shape
    halves_of = tab_ref.shape[0]
    pairs = tab_ref.shape[1] - 1
    tables = table_rows(table_ref, rows)
    shape = (rows, LANES)

    def whole(block):
        return jnp.concatenate([block] * (rows // 8), axis=0)

    for at_y, put in places:
        here = (slice(0, rows), slice(at_y, at_y + LANES))
        there = (slice(0, rows), slice(put, put + LANES))
        slot = slot_ref[here]
        land = slot >= 0
        value = jnp.maximum(slot, 0)
        lane = value & (LANES - 1)
        tile = value >> 7

        def pick(t, held):
            match = tile == t
            found = [lookup(whole(tab_ref[t, m]), lane) for m in range(pairs + 1)]
            found.append(lookup(whole(factor_ref[t]), lane))
            return tuple(jnp.where(match, new, old) for new, old in zip(found, held))

        held = tuple([jnp.full(shape, 1, jnp.int32)] * (pairs + 1) + [jnp.full(shape, 1.0 / FIXED, f32)])
        if halves_of <= 16:
            for t in range(halves_of):
                held = pick(t, held)
        else:
            held = lax.fori_loop(0, halves_of, pick, held, unroll=8)
        *words, terms, factor = held

        def halves(word):
            upper = lax.shift_right_logical(word, jnp.full(shape, 16, jnp.int32))
            return (word & 0xFFFF).astype(f32), upper.astype(f32)

        leaf, bright = halves(terms)
        exchange_coef = leaf * (4.0 / FIXED)
        absorbed = bright * (1.0 / FIXED)
        split = [halves(word) for word in words]
        uptake = []
        for k in range(layers):
            index = soil_ref[(k,) + here] + 1
            steep = lookup(tables[1], index)
            root = factor * split[k % pairs][k // pairs]
            uptake.append(root * sigmoid(steep * head_ref[(k,) + here]))
            if k == 0:
                ks_top = lookup(tables[0], index)
        conductance = functools.reduce(jnp.add, uptake)
        sunlight, air_temp, humidity, rainfall = (forcing_ref[(i,) + here] for i in range(4))
        radiation = absorbed * sunlight + 0.3
        square = air_temp * air_temp
        excess = radiation - 0.3 * square * square - conductance * (0.5 - humidity)
        slope = -1.2 * square * air_temp - exchange_coef - conductance
        rise = -excess / slope
        surface = air_temp + rise
        vapour = 0.5 * jnp.exp(2.0 * rise)
        square = surface * surface
        excess = (
            radiation
            - 0.3 * square * square
            - exchange_coef * rise
            - conductance * (vapour - humidity)
        )
        slope = -1.2 * square * surface - exchange_coef - 2.0 * conductance * vapour
        rise = rise - excess / slope
        rate = 0.5 * jnp.exp(2.0 * rise) - humidity
        infiltration = rainfall * ks_top / (rainfall + ks_top)
        infiltration = jnp.where(land, infiltration, 0.0)
        rate = jnp.where(land, rate, 0.0)
        flux_ref[(0,) + there] = conductance * rate
        flux_ref[(1,) + there] = infiltration
        for k in range(layers):
            value = -rate * uptake[k]
            if k == 0:
                value = value + infiltration
            source_ref[(k,) + there] = value


def strips(planes, shift_from):
    packed = None
    for k, plane in enumerate(planes):
        lane = lane_iota(plane.shape)
        shift = (HALO * k - shift_from) % LANES
        moved = pltpu.roll(plane, shift, 1) if shift else plane
        inside = (lane >= HALO * k) & (lane < HALO * (k + 1))
        packed = jnp.where(inside, moved, 0.0 if packed is None else packed)
    return packed


def strip_parts(cols):
    return ((slice(0, LANES), 0), (slice(cols - LANES, cols), LANES - HALO))


def ends_of(near_ref, far_ref, at, depth, part):
    edge = slice(depth * at, depth * (at + 1))
    below, above = below_above(near_ref[edge, part], far_ref[edge, part])
    gap = jnp.zeros((2 * (HALO - depth), above.shape[1]), f32)
    return jnp.concatenate([above, gap, below], axis=0)


def strip_kernel(head_ref, soil_ref, some_ref, out_ref):
    layers, _, cols = head_ref.shape
    me = lax.axis_index("gy")
    blocks = []
    for (part, shift), at in zip(strip_parts(cols), (0, LANES)):
        blocks.append(
            (
                strips([head_ref[k, :, part] for k in range(layers)], shift),
                strips([(soil_ref[k, :, part] + 1).astype(f32) for k in range(layers)], shift),
                strips([some_ref[k, :, at : at + LANES] for k in range(layers)], shift),
            )
        )
    for field, (low, high) in enumerate(zip(*blocks)):
        for d in range(out_ref.shape[0]):
            out_ref[d, field] = jnp.where(d < me, low, high)


def received(strip_ref, field):
    me = lax.axis_index("gy")
    count = strip_ref.shape[0]
    below = strip_ref[jnp.maximum(me - 1, 0), field]
    above = strip_ref[jnp.minimum(me + 1, count - 1), field]
    return jnp.where(me > 0, below, 0.0), jnp.where(me + 1 < count, above, 0.0)


def source_edge_kernel(src_ref, strip_ref, near_ref, far_ref):
    layers, rows, _ = src_ref.shape
    at = SOURCE_DEPTH * layers
    half = HALO // 2
    upward = near_is_above()
    pieces = [x for field in range(3) for x in received(strip_ref, field)]
    for out_ref, up in ((near_ref, upward), (far_ref, jnp.logical_not(upward))):
        for k in range(layers):
            part = slice(SOURCE_DEPTH * k, SOURCE_DEPTH * (k + 1))
            plane = src_ref[k]
            out_ref[part] = jnp.where(up, plane[rows - SOURCE_DEPTH :], plane[:SOURCE_DEPTH])
        blocks = [jnp.where(up, x[rows - HALO :], x[:HALO]) for x in pieces]
        tail = [block[h : h + half] for block in blocks[4:6] for h in (0, half)]
        for j in range(4):
            out_ref[at : at + HALO, j * LANES : (j + 1) * LANES] = blocks[j]
            out_ref[at + HALO : at + HALO + half, j * LANES : (j + 1) * LANES] = tail[j]


def corner(edge_ref, at, field, which):
    half = HALO // 2
    if field < 2:
        j = 2 * field + which
        return edge_ref[at : at + HALO, j * LANES : (j + 1) * LANES]
    pieces = [
        edge_ref[at + HALO : at + HALO + half, j * LANES : (j + 1) * LANES]
        for j in (2 * which, 2 * which + 1)
    ]
    return jnp.concatenate(pieces, axis=0)


def tall_strips(layers, strip_ref, snear_ref, sfar_ref):
    at = SOURCE_DEPTH * layers
    out = []
    for field in range(3):
        pair = []
        below, above = received(strip_ref, field)
        for which, piece in ((1, above), (0, below)):
            lower, upper = below_above(
                corner(snear_ref, at, field, which), corner(sfar_ref, at, field, which)
            )
            pair.append(jnp.concatenate([piece, upper, lower], axis=0))
        out.append(pair)
    return out


def side(strip, k):
    right, left = strip
    lane = lane_iota(right.shape)
    shift = (-HALO * k) % LANES
    right = pltpu.roll(right, shift, 1) if shift else right
    left = pltpu.roll(left, (LANES - HALO - HALO * k) % LANES, 1)
    return jnp.where(lane < HALO, right, jnp.where(lane >= LANES - HALO, left, 0.0))


def after(x, axis):
    return pltpu.roll(x, x.shape[axis] - 1, axis)


def before(x, axis):
    return pltpu.roll(x, 1, axis)


def pointwise(head, conduct, steep, capacity):
    sat = 0.5 + 0.5 * jnp.tanh(0.5 * (steep * head))
    slope = steep * sat * (1.0 - sat)
    cond = conduct * (0.1 + 0.9 * sat * sat)
    deriv = 0.9 * conduct * sat * slope
    weighted = storage_weight * capacity
    return cond, deriv, weighted * slope, weighted * sat


def joined(*refs):
    return lambda k: jnp.concatenate([ref[k] for ref in refs], axis=1)


def plain(ref):
    return lambda k: ref[k]


def face_of(here, there, extra=None):
    mean = 0.5 * (here[1] + there[1])
    drop = here[0] - there[0]
    if extra is not None:
        drop = drop + extra
    return mean + here[2] * drop, mean - there[2] * drop, mean * drop


def ring_faces(state, axis, inside=None):
    a, b, face = face_of(state, [after(x, axis) for x in state])
    if inside is not None:
        a, b, face = (jnp.where(inside, x, 0.0) for x in (a, b, face))
    return face - before(face, axis), a + before(b, axis), b, before(a, axis)


def linearize(layers, state_of, store_of, y_faces, masked, coefs, finish):
    diag_ref, xp_ref, xm_ref, yp_ref, ym_ref, az_ref, bz_ref = coefs
    above = None
    for k in range(layers):
        state = state_of(k)
        net_x, diag_x, xp, xm = ring_faces(state, 0)
        net_y, diag_y, yp, ym = y_faces(k, state)
        for ref, value in ((xp_ref, xp), (xm_ref, xm), (yp_ref, yp), (ym_ref, ym)):
            ref[k] = masked(value)
        if k + 1 < layers:
            a, b, face = face_of(state, state_of(k + 1), 1.0)
            az_ref[k] = a
            bz_ref[k] = b
        else:
            a, face = 2.0 * state[2], state[1]
        diag = store_of(k) + diag_x + diag_y + a
        value = net_x + net_y + face
        if above is not None:
            diag = diag + above[1]
            value = value - above[0]
        above = (face, b)
        diag_ref[k] = diag
        finish(k, masked(value))


def apply(v_ref, coefs, k):
    diag_of, xp_of, xm_of, yp_of, ym_of, az_of, bz_of = coefs
    v = v_ref[k]
    value = diag_of(k) * v
    value = value - xp_of(k) * after(v, 0) - xm_of(k) * before(v, 0)
    value = value - yp_of(k) * after(v, 1) - ym_of(k) * before(v, 1)
    if k > 0:
        value = value - az_of(k - 1) * v_ref[k - 1]
    if k + 1 < v_ref.shape[0]:
        value = value - bz_of(k) * v_ref[k + 1]
    return value


def powers(basis, coefs, tile, out_ref):
    layers = basis[0].shape[0]
    rows, cols = tile
    for step in range(KRYLOV - 1):
        for k in range(layers):
            basis[step + 1][k] = apply(basis[step], coefs, k)
    sums = [jnp.zeros((8, LANES), f32) for _ in PAIRS]
    for k in range(layers):
        top = apply(basis[-1], coefs, k)
        for at in range(0, rows, 8):
            for lane_at in range(0, cols, LANES):
                part = (slice(at, at + 8), slice(lane_at, lane_at + LANES))
                vs = [b[(k,) + part] for b in basis] + [top[part]]
                for e, (i, j) in enumerate(PAIRS):
                    sums[e] = sums[e] + vs[i] * vs[j]
    lines = [jnp.sum(x, axis=0, keepdims=True) for x in sums]
    lines.append(jnp.zeros((16 - len(PAIRS), LANES), f32))
    block = jnp.sum(jnp.concatenate(lines, axis=0), axis=1, keepdims=True)
    line = lax.broadcasted_iota(jnp.int32, (16, LANES), 0)
    flat = jnp.sum(jnp.where(lane_iota((16, LANES)) == line, block, 0.0), axis=0, keepdims=True)
    for d in range(out_ref.shape[0]):
        out_ref[d] = flat


def solve(gram_ref):
    terms = [gram_ref[d] for d in range(gram_ref.shape[0])]
    while len(terms) > 1:
        terms = [functools.reduce(jnp.add, terms[i : i + 2]) for i in range(0, len(terms), 2)]
    total = terms[0]
    line = lax.broadcasted_iota(jnp.int32, (16, LANES), 0)
    spread = jnp.broadcast_to(total, (16, LANES))
    column = jnp.sum(jnp.where(lane_iota((16, LANES)) == line, spread, 0.0), axis=1, keepdims=True)
    gram = {}
    for e, (i, j) in enumerate(PAIRS):
        gram[i, j] = gram[j, i] = column[e : e + 1, :]

    def times_gram(c):
        out = []
        for i in range(KRYLOV + 1):
            out.append(functools.reduce(jnp.add, [gram[i, m] * c[m] for m in range(len(c))]))
        return out

    def dot(a, b):
        return functools.reduce(jnp.add, [x * y for x, y in zip(a, b)])

    square = gram[0, 0] + norm_epsilon
    inverse = lax.rsqrt(square)
    beta = square * inverse
    basis = [[inverse]]
    images = [times_gram(basis[0])]
    hessen = {}
    for j in range(KRYLOV):
        w = [jnp.zeros_like(beta)] + basis[j]
        for i in range(j + 1):
            product = dot(w, images[i])
            hessen[i, j] = product
            w = [w[m] - product * basis[i][m] if m < len(basis[i]) else w[m] for m in range(len(w))]
        square = jnp.maximum(dot(w, times_gram(w)), 0.0) + norm_epsilon
        inverse = lax.rsqrt(square)
        hessen[j + 1, j] = square * inverse
        if j + 1 < KRYLOV:
            basis.append([x * inverse for x in w])
            images.append(times_gram(basis[-1]))
    n = KRYLOV
    normal = {}
    for a in range(n):
        for b in range(a + 1):
            normal[a, b] = functools.reduce(
                jnp.add,
                [hessen[i, a] * hessen[i, b] for i in range(n + 1) if (i, a) in hessen and (i, b) in hessen],
            )
    factor = {}
    inverse = []
    for a in range(n):
        for b in range(a + 1):
            value = normal[a, b]
            for m in range(b):
                value = value - factor[a, m] * factor[b, m]
            if a == b:
                inverse.append(lax.rsqrt(value))
            else:
                factor[a, b] = value * inverse[b]
    forward = []
    for a in range(n):
        value = hessen[0, a] * beta
        for m in range(a):
            value = value - factor[a, m] * forward[m]
        forward.append(value * inverse[a])
    backward = [None] * n
    for a in reversed(range(n)):
        value = forward[a]
        for m in range(a + 1, n):
            value = value - factor[m, a] * backward[m]
        backward[a] = value * inverse[a]
    return [
        functools.reduce(jnp.add, [backward[j] * basis[j][i] for j in range(i, n)]) for i in range(n)
    ]


def state_kernel(
    table_ref, head_ref, soil_ref, near_ref, far_ref,
    ext_ref, ks_ref, steep_ref, cap_ref, cond_ref, deriv_ref, store_ref, water_ref,
):
    layers, rows, cols = head_ref.shape
    tables = table_rows(table_ref, rows + 2 * HALO)
    every = slice(0, cols)
    for k in range(layers):
        ends = ends_of(near_ref, far_ref, k, STATE_DEPTH, every)
        head = jnp.concatenate([head_ref[k], ends], axis=0)
        ends = ends_of(near_ref, far_ref, layers + k, STATE_DEPTH, every)
        index = jnp.concatenate([soil_ref[k] + 1, ends.astype(jnp.int32)], axis=0)
        conduct, steep, capacity = (lookup(row, index) for row in tables)
        values = (head, conduct, steep, capacity) + pointwise(head, conduct, steep, capacity)
        outs = (ext_ref, ks_ref, steep_ref, cap_ref, cond_ref, deriv_ref, store_ref, water_ref)
        for ref, value in zip(outs, values):
            ref[k] = value


def flow_kernel(ext_ref, ks_ref, cond_ref, deriv_ref, store_ref, flow_ref, *coefs, rows):
    layers, _, cols = ext_ref.shape
    mask = (ks_ref[0] > 0.0).astype(f32)
    inside = lane_iota(mask.shape) < cols - 1

    def masked(value):
        return jnp.concatenate([value[:rows], value[rows:] * mask[rows:]], axis=0)

    def finish(k, value):
        flow_ref[k] = value

    linearize(
        layers, lambda k: (ext_ref[k], cond_ref[k], deriv_ref[k]), plain(store_ref),
        lambda k, state: ring_faces(state, 1, inside), masked, coefs, finish,
    )


def first_kernel(
    table_ref, src_ref, snear_ref, sfar_ref, strip_ref,
    ext_ref, ks_ref, cond_ref, deriv_ref, water_ref, flow_ref, *rest,
):
    mains, rest = rest[:7], rest[7:]
    ext_side, ks_side, steep_side, cap_side, base_ref, p0_ref, p1_ref, p2_ref, gram_ref = rest[:9]
    sides, (cond_side, deriv_side, store_side) = rest[9:16], rest[16:19]
    diag_first, diag_last, yp_last, ym_first = rest[19:23]
    layers, rows, cols = src_ref.shape
    tables = table_rows(table_ref, rows + 2 * HALO)
    heads, soils, sources = tall_strips(layers, strip_ref, snear_ref, sfar_ref)
    start, end, middle = slice(0, LANES), slice(cols - LANES, cols), slice(LANES, cols - LANES)
    lane = lane_iota((rows + 2 * HALO, LANES))
    is_first, is_last = lane == 0, lane == LANES - 1

    def source_of(k):
        ends = ends_of(snear_ref, sfar_ref, k, SOURCE_DEPTH, slice(0, cols))
        return jnp.concatenate([src_ref[k], ends], axis=0)

    for k in range(layers):
        head = side(heads, k)
        index = side(soils, k).astype(jnp.int32)
        conduct, steep, capacity = (lookup(row, index) for row in tables)
        cond, deriv, store, water = pointwise(head, conduct, steep, capacity)
        outs = (ext_side, ks_side, steep_side, cap_side, cond_side, deriv_side, store_side)
        for ref, value in zip(outs, (head, conduct, steep, capacity, cond, deriv, store)):
            ref[k] = value
        base_ref[k, :, 0:cols] = water_ref[k] + source_of(k)
        base_ref[k, :, cols:] = water + side(sources, k)
        p0_ref[k, :, middle] = flow_ref[k, :, middle] + (water_ref[k, :, middle] - base_ref[k, :, middle])
        p0_ref[k, :, cols:] = water - base_ref[k, :, cols:]

    masks = [(ref > 0.0).astype(f32) for ref in (ks_ref[0, :, start], ks_ref[0, :, end], ks_side[0])]

    def y_faces(k, state):
        first = (ext_ref[k, :, start], cond_ref[k, :, start], deriv_ref[k, :, start])
        last = (ext_ref[k, :, end], cond_ref[k, :, end], deriv_ref[k, :, end])
        moved = [after(x, 1) for x in state]
        ahead = [jnp.where(is_last, after(x, 1), y) for x, y in zip(first, moved)]
        a, b, face = face_of(state, ahead)
        a_in, b_in, face_in = (jnp.where(is_last, x, 0.0) for x in face_of(last, moved))
        a_out, b_out, face_out = (before(x, 1) for x in (a, b, face))
        a_pre, b_pre, face_pre = (before(x, 1) for x in (a_in, b_in, face_in))
        gain = water_ref[k, :, end] - base_ref[k, :, end]
        p0_ref[k, :, end] = flow_ref[k, :, end] + face_in * masks[1] + gain
        diag_last[k] = mains[0][k, :, end] + a_in
        yp_last[k] = mains[3][k, :, end] + b_in * masks[1]
        gain = water_ref[k, :, start] - base_ref[k, :, start]
        p0_ref[k, :, start] = flow_ref[k, :, start] - jnp.where(is_first, face_out, 0.0) * masks[0] + gain
        diag_first[k] = mains[0][k, :, start] + jnp.where(is_first, b_out, 0.0)
        ym_first[k] = mains[4][k, :, start] + jnp.where(is_first, a_out, 0.0) * masks[0]
        a_pre, b_pre, face_pre = (
            jnp.where(is_first, x, y)
            for x, y in ((a_pre, a_out), (b_pre, b_out), (face_pre, face_out))
        )
        return face - face_pre, a + b_pre, b, a_pre

    def finish(k, value):
        p0_ref[k, :, cols:] = p0_ref[k, :, cols:] + value

    linearize(
        layers, lambda k: (ext_side[k], cond_side[k], deriv_side[k]), plain(store_side),
        y_faces, lambda value: value * masks[2], sides, finish,
    )

    def pieces(n, first_of, last_of):
        main, beside = mains[n], sides[n]
        return lambda k: jnp.concatenate(
            [first_of(main, k), main[k, :, middle], last_of(main, k), beside[k]], axis=1
        )

    def of_start(ref, k):
        return ref[k, :, start]

    def of_end(ref, k):
        return ref[k, :, end]

    coefs = [joined(main, beside) for main, beside in zip(mains, sides)]
    coefs[0] = pieces(0, lambda _, k: diag_first[k], lambda _, k: diag_last[k])
    coefs[3] = pieces(3, of_start, lambda _, k: yp_last[k])
    coefs[4] = pieces(4, lambda _, k: ym_first[k], of_end)
    powers((p0_ref, p1_ref, p2_ref), coefs, (rows, cols), gram_ref)


def second_kernel(
    arrived_ref, old_ref, ks_ref, steep_ref, cap_ref, old_side, ks_side, steep_side, cap_side,
    base_ref, q0_ref, q1_ref, q2_ref,
    part_ref, p0_ref, p1_ref, p2_ref, gram_ref, ext_ref, cond_ref, deriv_ref, store_ref, gain_ref, *coefs,
):
    layers = old_ref.shape[0]
    rows, cols = part_ref.shape[1:]
    x = solve(arrived_ref)
    near = lax.broadcasted_iota(jnp.int32, (HALO, cols + LANES), 0) < HALO // 2

    def folded(of):
        def get(k):
            value = of(k)
            ends = jnp.where(near, value[rows : rows + HALO], value[rows + HALO :])
            return jnp.concatenate([value[:rows], ends], axis=0)

        return get

    old_of, ks_of = folded(joined(old_ref, old_side)), folded(joined(ks_ref, ks_side))
    steep_of, cap_of = folded(joined(steep_ref, steep_side)), folded(joined(cap_ref, cap_side))
    base_of, *qs = (folded(plain(ref)) for ref in (base_ref, q0_ref, q1_ref, q2_ref))
    for k in range(layers):
        head = old_of(k)
        for value, q_of in zip(x, qs):
            head = head - value * q_of(k)
        cond, deriv, store, water = pointwise(head, ks_of(k), steep_of(k), cap_of(k))
        ext_ref[k] = head
        part_ref[k] = head[:rows, :cols]
        cond_ref[k] = cond
        deriv_ref[k] = deriv
        store_ref[k] = store
        gain_ref[k] = water - base_of(k)
    mask = (ks_of(0) > 0.0).astype(f32)

    def masked(value):
        own = value[:rows, cols:] * mask[:rows, cols:]
        top = jnp.concatenate([value[:rows, :cols], own], axis=1)
        return jnp.concatenate([top, value[rows:] * mask[rows:]], axis=0)

    def finish(k, value):
        p0_ref[k] = value + gain_ref[k]

    linearize(
        layers, lambda k: (ext_ref[k], cond_ref[k], deriv_ref[k]), plain(store_ref),
        lambda k, state: ring_faces(state, 1), masked, coefs, finish,
    )
    powers((p0_ref, p1_ref, p2_ref), [plain(ref) for ref in coefs], (rows, cols), gram_ref)


def last_kernel(arrived_ref, part_ref, q0_ref, q1_ref, q2_ref, head_ref):
    layers, rows, cols = part_ref.shape
    x = solve(arrived_ref)
    for k in range(layers):
        own = (k, slice(0, rows), slice(0, cols))
        head_ref[k] = part_ref[k] - x[0] * q0_ref[own] - x[1] * q1_ref[own] - x[2] * q2_ref[own]


def shards(head_old, soil_type, soil_table, forcing, canopy, column_slot):
    layers, rows, cols = head_old.shape
    both = ("gx", "gy")
    devices = lax.axis_size("gx") * lax.axis_size("gy")
    tall, wide = rows + 2 * HALO, cols + LANES
    own, ext = ((layers, rows, cols), f32), ((layers, tall, wide), f32)
    gram_block = ((devices, 1, LANES), f32)

    def exchange(to_near, to_far):
        size = lax.axis_size("gx")
        near = [(i, i + 1) for i in range(0, size - 1, 2)]
        far = [(i, i + 1) for i in range(1, size - 1, 2)]
        return tuple(
            lax.ppermute(x, "gx", pairs + [(j, i) for i, j in pairs])
            for x, pairs in ((to_near, near), (to_far, far))
        )

    def spread(x, axes):
        return lax.all_to_all(x, axes, split_axis=0, concat_axis=0, tiled=True)

    def edge(count):
        return (-(-count // 8) * 8, cols), f32

    send, to_near, to_far = call(
        pack_kernel,
        [((devices, 8, LANES), f32)] + [edge(2 * STATE_DEPTH * layers)] * 2,
        3,
        scratch=[
            pltpu.VMEM(canopy.shape, f32),
            pltpu.VMEM(head_old.shape, f32),
            pltpu.VMEM(soil_type.shape, jnp.int32),
            pltpu.SemaphoreType.DMA((3,)),
        ],
        in_specs=[pl.BlockSpec(memory_space=pl.ANY)] * 3,
        grant=63400000,
    )(canopy, head_old, soil_type)
    arrived = spread(send, both)
    near, far = exchange(to_near, to_far)
    columns = (head_old, soil_type, forcing, column_slot)
    table = ((devices // 2, -(-layers // 2) + 1, 8, LANES), jnp.int32)
    some, flux, tab, factor = call(
        edge_source_kernel,
        [((layers, rows, 2 * LANES), f32), ((2, rows, 2 * LANES), f32), table, ((devices // 2, 8, LANES), f32)],
        6,
        in_specs=[smem] + [vmem] * 5,
    )(soil_table, arrived, *columns)
    (strip,) = call(strip_kernel, [((lax.axis_size("gy"), 3, rows, LANES), f32)], 3)(
        head_old, soil_type, some
    )
    strip = spread(strip, "gy")
    source, flux = call(
        inner_source_kernel, [own, ((2, rows, cols), f32)], 9, in_specs=[smem] + [vmem] * 8
    )(soil_table, tab, factor, *columns, some, flux)
    to_near, to_far = call(source_edge_kernel, [edge(SOURCE_DEPTH * layers + HALO + HALO // 2)] * 2, 2)(
        source, strip
    )
    snear, sfar = exchange(to_near, to_far)
    main, side_block = ((layers, tall, cols), f32), ((layers, tall, LANES), f32)
    old, ks, steep, cap, cond, deriv, store, water = call(
        state_kernel, [main] * 8, 5, in_specs=[smem] + [vmem] * 4
    )(soil_table, head_old, soil_type, near, far)
    flow, *coefs = call(functools.partial(flow_kernel, rows=rows), [main] * 8, 5)(
        old, ks, cond, deriv, store
    )
    old_s, ks_s, steep_s, cap_s, base, p0, p1, p2, gram = call(
        first_kernel,
        [side_block] * 4 + [ext] * 4 + [gram_block],
        18,
        scratch=[pltpu.VMEM(side_block[0], f32)] * 14,
        in_specs=[smem] + [vmem] * 17,
    )(soil_table, source, snear, sfar, strip, old, ks, cond, deriv, water, flow, *coefs)
    sums = spread(gram, both)
    part, q0, q1, q2, gram = call(
        second_kernel,
        [own] + [((layers, rows + HALO, wide), f32)] * 3 + [gram_block],
        13,
        scratch=[pltpu.VMEM((layers, rows + HALO, wide), f32)] * 12,
    )(sums, old, ks, steep, cap, old_s, ks_s, steep_s, cap_s, base, p0, p1, p2)
    sums = spread(gram, both)
    (head,) = call(last_kernel, [own], 5)(sums, part, q0, q1, q2)
    return head, flux


def solution(mesh):
    return jax.shard_map(
        shards,
        mesh=mesh,
        in_specs=(
            P(None, "gx", "gy"),
            P(None, "gx", "gy"),
            P(),
            P(None, "gx", "gy"),
            P(None, ("gx", "gy")),
            P("gx", "gy"),
        ),
        out_specs=(P(None, "gx", "gy"), P(None, "gx", "gy")),
        check_vma=False,
    )
```

```python
import functools

import jax
import jax.numpy as jnp
from jax import lax
from jax.experimental import pallas as pl
from jax.experimental.pallas import tpu as pltpu
from jax.sharding import PartitionSpec as P

NEWTON = 2
KRYLOV = 3
HALO = 8
STATE_DEPTH = 7
SOURCE_DEPTH = 6
FIXED = 65535.0
LANES = 128
SLOT = 64

storage_weight = 4.0
norm_epsilon = 1e-06

VMEM_LIMIT = 20 * 1024 * 1024
PAIRS = [(i, j) for i in range(KRYLOV + 1) for j in range(i, KRYLOV + 1)]

f32 = jnp.float32
vmem = pl.BlockSpec(memory_space=pltpu.VMEM)
smem = pl.BlockSpec(memory_space=pltpu.SMEM)


def call(body, outs, n_in, scratch=(), in_specs=None, flops=1000000, grant=VMEM_LIMIT):
    return pl.pallas_call(
        body,
        out_shape=[jax.ShapeDtypeStruct(s, d) for s, d in outs],
        in_specs=in_specs or [vmem] * n_in,
        out_specs=[vmem] * len(outs),
        scratch_shapes=list(scratch),
        compiler_params=pltpu.CompilerParams(vmem_limit_bytes=grant),
        cost_estimate=pl.CostEstimate(flops=flops, bytes_accessed=1000000, transcendentals=0),
    )


def lane_iota(shape):
    return lax.broadcasted_iota(jnp.int32, shape, len(shape) - 1)


def pack_kernel(
    canopy_hbm, head_hbm, soil_hbm, send_ref, near_ref, far_ref, canopy_ref, head_ref, soil_ref, sems
):
    copies = [
        pltpu.make_async_copy(canopy_hbm, canopy_ref, sems.at[0]),
        pltpu.make_async_copy(head_hbm, head_ref, sems.at[1]),
        pltpu.make_async_copy(soil_hbm, soil_ref, sems.at[2]),
    ]
    for copy in copies:
        copy.start()
    copies[0].wait()
    rows = canopy_ref.shape[0]
    low = lane_iota((8, LANES)) < SLOT
    for t in range(canopy_ref.shape[1] // LANES):
        here = slice(t * LANES, (t + 1) * LANES)
        first = canopy_ref[0:8, here]
        rest = jnp.concatenate([canopy_ref[8:rows, here], jnp.zeros((16 - rows, LANES), f32)], axis=0)
        send_ref[2 * t] = jnp.where(low, first, pltpu.roll(rest, SLOT, 1))
        send_ref[2 * t + 1] = jnp.where(low, pltpu.roll(first, SLOT, 1), rest)
    layers, rows, _ = head_ref.shape
    copies[1].wait()
    copies[2].wait()
    low_rows, high_rows = slice(0, STATE_DEPTH), slice(rows - STATE_DEPTH, rows)
    upward = near_is_above("gx")
    for n in range(2 * layers):
        plane = head_ref[n] if n < layers else (soil_ref[n - layers] + 1).astype(f32)
        part = slice(STATE_DEPTH * n, STATE_DEPTH * (n + 1))
        near_ref[part] = jnp.where(upward, plane[high_rows], plane[low_rows])
        far_ref[part] = jnp.where(upward, plane[low_rows], plane[high_rows])


def near_is_above(axis):
    return lax.rem(lax.axis_index(axis), 2) == 0


def below_above(near, far, axis):
    upward = near_is_above(axis)
    return jnp.where(upward, far, near), jnp.where(upward, near, far)


def table_rows(table_ref, rows):
    lane = lane_iota((rows, LANES))
    out = []
    for field in range(table_ref.shape[0]):
        row = jnp.zeros((rows, LANES), f32)
        for kind in range(table_ref.shape[1]):
            row = jnp.where(lane == kind + 1, table_ref[field, kind], row)
        out.append(row)
    return out


def lookup(row, index):
    pieces = [
        jnp.take_along_axis(row, index[:, at : at + LANES], axis=1, mode="promise_in_bounds")
        for at in range(0, index.shape[1], LANES)
    ]
    return jnp.concatenate(pieces, axis=1)


def sigmoid(u):
    return 1.0 / (1.0 + jnp.exp(-u))


def edge_source_kernel(
    table_ref, arrived_ref, head_ref, soil_ref, forcing_ref, slot_ref,
    source_ref, flux_ref, tab_ref, factor_ref,
):
    layers, rows, cols = head_ref.shape
    owners = arrived_ref.shape[0]
    pairs = -(-layers // 2)
    low = lane_iota((8, LANES)) < SLOT
    line = lax.broadcasted_iota(jnp.int32, (16, LANES), 0)
    is_root = (line >= 3) & (line < 3 + layers)

    def unpack(t, _):
        first = arrived_ref[2 * t]
        second = arrived_ref[2 * t + 1]
        both = jnp.concatenate(
            [
                jnp.where(low, first, pltpu.roll(second, SLOT, 1)),
                jnp.where(low, pltpu.roll(first, SLOT, 1), second),
            ],
            axis=0,
        )
        leaf_area, albedo, resist = both[0:1], both[1:2], both[2:3]
        root_sum = jnp.sum(jnp.where(is_root, both, 0.0), axis=0, keepdims=True)
        factor = leaf_area / ((leaf_area + resist) * root_sum) * (1.0 / FIXED)
        factor_ref[t] = jnp.broadcast_to(factor, (8, LANES))
        fixed = (both * FIXED + 0.5).astype(jnp.int32)
        for m in range(pairs):
            word = fixed[3 + m : 4 + m]
            if m + pairs < layers:
                word = word | (fixed[3 + m + pairs : 4 + m + pairs] << 16)
            tab_ref[t, m] = jnp.broadcast_to(word, (8, LANES))
        leaf = ((0.5 + 0.3 * leaf_area) * (0.25 * FIXED) + 0.5).astype(jnp.int32)
        bright = ((1.0 - albedo) * FIXED + 0.5).astype(jnp.int32)
        tab_ref[t, pairs] = jnp.broadcast_to(leaf | (bright << 16), (8, LANES))
        return 0

    lax.fori_loop(0, owners // 2, unpack, 0, unroll=16)
    places = [(0, 0), (cols - LANES, LANES)]
    land_columns(
        table_ref, tab_ref, factor_ref, head_ref, soil_ref, forcing_ref, slot_ref, source_ref, flux_ref, places
    )


def inner_source_kernel(
    table_ref, tab_ref, factor_ref, head_ref, soil_ref, forcing_ref, slot_ref, some_ref, part_ref,
    source_ref, flux_ref,
):
    cols = head_ref.shape[2]
    places = [(at, at) for at in range(LANES, cols - LANES, LANES)]
    land_columns(
        table_ref, tab_ref, factor_ref, head_ref, soil_ref, forcing_ref, slot_ref, source_ref, flux_ref, places
    )
    for whole_ref, piece_ref in ((source_ref, some_ref), (flux_ref, part_ref)):
        for k in range(whole_ref.shape[0]):
            whole_ref[k, :, 0:LANES] = piece_ref[k, :, 0:LANES]
            whole_ref[k, :, cols - LANES : cols] = piece_ref[k, :, LANES : 2 * LANES]


def land_columns(
    table_ref, tab_ref, factor_ref, head_ref, soil_ref, forcing_ref, slot_ref, source_ref, flux_ref, places
):
    layers, rows, _ = head_ref.shape
    halves_of = tab_ref.shape[0]
    pairs = tab_ref.shape[1] - 1
    tables = table_rows(table_ref, rows)
    shape = (rows, LANES)

    def whole(block):
        return jnp.concatenate([block] * (rows // 8), axis=0)

    for at_y, put in places:
        here = (slice(0, rows), slice(at_y, at_y + LANES))
        there = (slice(0, rows), slice(put, put + LANES))
        slot = slot_ref[here]
        land = slot >= 0
        value = jnp.maximum(slot, 0)
        lane = value & (LANES - 1)
        tile = value >> 7

        def pick(t, held):
            match = tile == t
            found = [lookup(whole(tab_ref[t, m]), lane) for m in range(pairs + 1)]
            found.append(lookup(whole(factor_ref[t]), lane))
            return tuple(jnp.where(match, new, old) for new, old in zip(found, held))

        held = tuple([jnp.full(shape, 1, jnp.int32)] * (pairs + 1) + [jnp.full(shape, 1.0 / FIXED, f32)])
        if halves_of <= 16:
            for t in range(halves_of):
                held = pick(t, held)
        else:
            held = lax.fori_loop(0, halves_of, pick, held, unroll=8)
        *words, terms, factor = held

        def halves(word):
            upper = lax.shift_right_logical(word, jnp.full(shape, 16, jnp.int32))
            return (word & 0xFFFF).astype(f32), upper.astype(f32)

        leaf, bright = halves(terms)
        exchange_coef = leaf * (4.0 / FIXED)
        absorbed = bright * (1.0 / FIXED)
        split = [halves(word) for word in words]
        uptake = []
        for k in range(layers):
            index = soil_ref[(k,) + here] + 1
            steep = lookup(tables[1], index)
            root = factor * split[k % pairs][k // pairs]
            uptake.append(root * sigmoid(steep * head_ref[(k,) + here]))
            if k == 0:
                ks_top = lookup(tables[0], index)
        conductance = functools.reduce(jnp.add, uptake)
        sunlight, air_temp, humidity, rainfall = (forcing_ref[(i,) + here] for i in range(4))
        radiation = absorbed * sunlight + 0.3
        square = air_temp * air_temp
        excess = radiation - 0.3 * square * square - conductance * (0.5 - humidity)
        slope = -1.2 * square * air_temp - exchange_coef - conductance
        rise = -excess / slope
        surface = air_temp + rise
        vapour = 0.5 * jnp.exp(2.0 * rise)
        square = surface * surface
        excess = (
            radiation
            - 0.3 * square * square
            - exchange_coef * rise
            - conductance * (vapour - humidity)
        )
        slope = -1.2 * square * surface - exchange_coef - 2.0 * conductance * vapour
        rise = rise - excess / slope
        rate = 0.5 * jnp.exp(2.0 * rise) - humidity
        infiltration = rainfall * ks_top / (rainfall + ks_top)
        infiltration = jnp.where(land, infiltration, 0.0)
        rate = jnp.where(land, rate, 0.0)
        flux_ref[(0,) + there] = conductance * rate
        flux_ref[(1,) + there] = infiltration
        for k in range(layers):
            value = -rate * uptake[k]
            if k == 0:
                value = value + infiltration
            source_ref[(k,) + there] = value


def strips(planes, shift_from):
    packed = None
    for k, plane in enumerate(planes):
        lane = lane_iota(plane.shape)
        shift = (HALO * k - shift_from) % LANES
        moved = pltpu.roll(plane, shift, 1) if shift else plane
        inside = (lane >= HALO * k) & (lane < HALO * (k + 1))
        packed = jnp.where(inside, moved, 0.0 if packed is None else packed)
    return packed


def strip_parts(cols):
    return ((slice(0, LANES), 0), (slice(cols - LANES, cols), LANES - HALO))


def ends_of(near_ref, far_ref, at, depth, part):
    edge = slice(depth * at, depth * (at + 1))
    below, above = below_above(near_ref[edge, part], far_ref[edge, part], "gx")
    gap = jnp.zeros((2 * (HALO - depth), above.shape[1]), f32)
    return jnp.concatenate([above, gap, below], axis=0)


def strip_kernel(head_ref, soil_ref, some_ref, near_ref, far_ref):
    layers, _, cols = head_ref.shape
    upward = near_is_above("gy")
    blocks = []
    for (part, shift), at in zip(strip_parts(cols), (0, LANES)):
        blocks.append(
            (
                strips([head_ref[k, :, part] for k in range(layers)], shift),
                strips([(soil_ref[k, :, part] + 1).astype(f32) for k in range(layers)], shift),
                strips([some_ref[k, :, at : at + LANES] for k in range(layers)], shift),
            )
        )
    for field, (low, high) in enumerate(zip(*blocks)):
        near_ref[field] = jnp.where(upward, high, low)
        far_ref[field] = jnp.where(upward, low, high)


def source_edge_kernel(src_ref, ynear_ref, yfar_ref, near_ref, far_ref):
    layers, rows, _ = src_ref.shape
    at = SOURCE_DEPTH * layers
    half = HALO // 2
    upward = near_is_above("gx")
    pieces = [x for field in range(3) for x in below_above(ynear_ref[field], yfar_ref[field], "gy")]
    for out_ref, up in ((near_ref, upward), (far_ref, jnp.logical_not(upward))):
        for k in range(layers):
            part = slice(SOURCE_DEPTH * k, SOURCE_DEPTH * (k + 1))
            plane = src_ref[k]
            out_ref[part] = jnp.where(up, plane[rows - SOURCE_DEPTH :], plane[:SOURCE_DEPTH])
        blocks = [jnp.where(up, x[rows - HALO :], x[:HALO]) for x in pieces]
        tail = [block[h : h + half] for block in blocks[4:6] for h in (0, half)]
        for j in range(4):
            out_ref[at : at + HALO, j * LANES : (j + 1) * LANES] = blocks[j]
            out_ref[at + HALO : at + HALO + half, j * LANES : (j + 1) * LANES] = tail[j]


def corner(edge_ref, at, field, which):
    half = HALO // 2
    if field < 2:
        j = 2 * field + which
        return edge_ref[at : at + HALO, j * LANES : (j + 1) * LANES]
    pieces = [
        edge_ref[at + HALO : at + HALO + half, j * LANES : (j + 1) * LANES]
        for j in (2 * which, 2 * which + 1)
    ]
    return jnp.concatenate(pieces, axis=0)


def tall_strips(layers, ynear_ref, yfar_ref, snear_ref, sfar_ref):
    at = SOURCE_DEPTH * layers
    out = []
    for field in range(3):
        pair = []
        below, above = below_above(ynear_ref[field], yfar_ref[field], "gy")
        for which, piece in ((1, above), (0, below)):
            lower, upper = below_above(
                corner(snear_ref, at, field, which), corner(sfar_ref, at, field, which), "gx"
            )
            pair.append(jnp.concatenate([piece, upper, lower], axis=0))
        out.append(pair)
    return out


def side(strip, k):
    right, left = strip
    lane = lane_iota(right.shape)
    shift = (-HALO * k) % LANES
    right = pltpu.roll(right, shift, 1) if shift else right
    left = pltpu.roll(left, (LANES - HALO - HALO * k) % LANES, 1)
    return jnp.where(lane < HALO, right, jnp.where(lane >= LANES - HALO, left, 0.0))


def after(x, axis):
    return pltpu.roll(x, x.shape[axis] - 1, axis)


def before(x, axis):
    return pltpu.roll(x, 1, axis)


def pointwise(head, conduct, steep, capacity):
    sat = 0.5 + 0.5 * jnp.tanh(0.5 * (steep * head))
    slope = steep * sat * (1.0 - sat)
    cond = conduct * (0.1 + 0.9 * sat * sat)
    deriv = 0.9 * conduct * sat * slope
    weighted = storage_weight * capacity
    return cond, deriv, weighted * slope, weighted * sat


def joined(*refs):
    return lambda k: jnp.concatenate([ref[k] for ref in refs], axis=1)


def plain(ref):
    return lambda k: ref[k]


def face_of(here, there, extra=None):
    mean = 0.5 * (here[1] + there[1])
    drop = here[0] - there[0]
    if extra is not None:
        drop = drop + extra
    return mean + here[2] * drop, mean - there[2] * drop, mean * drop


def ring_faces(state, axis, inside=None):
    a, b, face = face_of(state, [after(x, axis) for x in state])
    if inside is not None:
        a, b, face = (jnp.where(inside, x, 0.0) for x in (a, b, face))
    return face - before(face, axis), a + before(b, axis), b, before(a, axis)


def linearize(layers, state_of, store_of, y_faces, masked, coefs, finish):
    diag_ref, xp_ref, xm_ref, yp_ref, ym_ref, az_ref, bz_ref = coefs
    above = None
    for k in range(layers):
        state = state_of(k)
        net_x, diag_x, xp, xm = ring_faces(state, 0)
        net_y, diag_y, yp, ym = y_faces(k, state)
        for ref, value in ((xp_ref, xp), (xm_ref, xm), (yp_ref, yp), (ym_ref, ym)):
            ref[k] = masked(value)
        if k + 1 < layers:
            a, b, face = face_of(state, state_of(k + 1), 1.0)
            az_ref[k] = a
            bz_ref[k] = b
        else:
            a, face = 2.0 * state[2], state[1]
        diag = store_of(k) + diag_x + diag_y + a
        value = net_x + net_y + face
        if above is not None:
            diag = diag + above[1]
            value = value - above[0]
        above = (face, b)
        diag_ref[k] = diag
        finish(k, masked(value))


def apply(v_ref, coefs, k):
    diag_of, xp_of, xm_of, yp_of, ym_of, az_of, bz_of = coefs
    v = v_ref[k]
    value = diag_of(k) * v
    value = value - xp_of(k) * after(v, 0) - xm_of(k) * before(v, 0)
    value = value - yp_of(k) * after(v, 1) - ym_of(k) * before(v, 1)
    if k > 0:
        value = value - az_of(k - 1) * v_ref[k - 1]
    if k + 1 < v_ref.shape[0]:
        value = value - bz_of(k) * v_ref[k + 1]
    return value


def powers(basis, coefs, tile, out_ref):
    layers = basis[0].shape[0]
    rows, cols = tile
    for step in range(KRYLOV - 1):
        for k in range(layers):
            basis[step + 1][k] = apply(basis[step], coefs, k)
    sums = [jnp.zeros((8, LANES), f32) for _ in PAIRS]
    for k in range(layers):
        top = apply(basis[-1], coefs, k)
        for at in range(0, rows, 8):
            for lane_at in range(0, cols, LANES):
                part = (slice(at, at + 8), slice(lane_at, lane_at + LANES))
                vs = [b[(k,) + part] for b in basis] + [top[part]]
                for e, (i, j) in enumerate(PAIRS):
                    sums[e] = sums[e] + vs[i] * vs[j]
    lines = [jnp.sum(x, axis=0, keepdims=True) for x in sums]
    lines.append(jnp.zeros((16 - len(PAIRS), LANES), f32))
    block = jnp.sum(jnp.concatenate(lines, axis=0), axis=1, keepdims=True)
    line = lax.broadcasted_iota(jnp.int32, (16, LANES), 0)
    flat = jnp.sum(jnp.where(lane_iota((16, LANES)) == line, block, 0.0), axis=0, keepdims=True)
    for d in range(out_ref.shape[0]):
        out_ref[d] = flat


def solve(gram_ref):
    terms = [gram_ref[d] for d in range(gram_ref.shape[0])]
    while len(terms) > 1:
        terms = [functools.reduce(jnp.add, terms[i : i + 2]) for i in range(0, len(terms), 2)]
    total = terms[0]
    line = lax.broadcasted_iota(jnp.int32, (16, LANES), 0)
    spread = jnp.broadcast_to(total, (16, LANES))
    column = jnp.sum(jnp.where(lane_iota((16, LANES)) == line, spread, 0.0), axis=1, keepdims=True)
    gram = {}
    for e, (i, j) in enumerate(PAIRS):
        gram[i, j] = gram[j, i] = column[e : e + 1, :]

    def times_gram(c):
        out = []
        for i in range(KRYLOV + 1):
            out.append(functools.reduce(jnp.add, [gram[i, m] * c[m] for m in range(len(c))]))
        return out

    def dot(a, b):
        return functools.reduce(jnp.add, [x * y for x, y in zip(a, b)])

    square = gram[0, 0] + norm_epsilon
    inverse = lax.rsqrt(square)
    beta = square * inverse
    basis = [[inverse]]
    images = [times_gram(basis[0])]
    hessen = {}
    for j in range(KRYLOV):
        w = [jnp.zeros_like(beta)] + basis[j]
        for i in range(j + 1):
            product = dot(w, images[i])
            hessen[i, j] = product
            w = [w[m] - product * basis[i][m] if m < len(basis[i]) else w[m] for m in range(len(w))]
        square = jnp.maximum(dot(w, times_gram(w)), 0.0) + norm_epsilon
        inverse = lax.rsqrt(square)
        hessen[j + 1, j] = square * inverse
        if j + 1 < KRYLOV:
            basis.append([x * inverse for x in w])
            images.append(times_gram(basis[-1]))
    n = KRYLOV
    normal = {}
    for a in range(n):
        for b in range(a + 1):
            normal[a, b] = functools.reduce(
                jnp.add,
                [hessen[i, a] * hessen[i, b] for i in range(n + 1) if (i, a) in hessen and (i, b) in hessen],
            )
    factor = {}
    inverse = []
    for a in range(n):
        for b in range(a + 1):
            value = normal[a, b]
            for m in range(b):
                value = value - factor[a, m] * factor[b, m]
            if a == b:
                inverse.append(lax.rsqrt(value))
            else:
                factor[a, b] = value * inverse[b]
    forward = []
    for a in range(n):
        value = hessen[0, a] * beta
        for m in range(a):
            value = value - factor[a, m] * forward[m]
        forward.append(value * inverse[a])
    backward = [None] * n
    for a in reversed(range(n)):
        value = forward[a]
        for m in range(a + 1, n):
            value = value - factor[m, a] * backward[m]
        backward[a] = value * inverse[a]
    return [
        functools.reduce(jnp.add, [backward[j] * basis[j][i] for j in range(i, n)]) for i in range(n)
    ]


def state_kernel(
    table_ref, head_ref, soil_ref, near_ref, far_ref,
    ext_ref, ks_ref, steep_ref, cap_ref, cond_ref, deriv_ref, store_ref, water_ref,
):
    layers, rows, cols = head_ref.shape
    tables = table_rows(table_ref, rows + 2 * HALO)
    every = slice(0, cols)
    for k in range(layers):
        ends = ends_of(near_ref, far_ref, k, STATE_DEPTH, every)
        head = jnp.concatenate([head_ref[k], ends], axis=0)
        ends = ends_of(near_ref, far_ref, layers + k, STATE_DEPTH, every)
        index = jnp.concatenate([soil_ref[k] + 1, ends.astype(jnp.int32)], axis=0)
        conduct, steep, capacity = (lookup(row, index) for row in tables)
        values = (head, conduct, steep, capacity) + pointwise(head, conduct, steep, capacity)
        outs = (ext_ref, ks_ref, steep_ref, cap_ref, cond_ref, deriv_ref, store_ref, water_ref)
        for ref, value in zip(outs, values):
            ref[k] = value


def flow_kernel(ext_ref, ks_ref, cond_ref, deriv_ref, store_ref, flow_ref, *coefs, rows):
    layers, _, cols = ext_ref.shape
    mask = (ks_ref[0] > 0.0).astype(f32)
    inside = lane_iota(mask.shape) < cols - 1

    def masked(value):
        return jnp.concatenate([value[:rows], value[rows:] * mask[rows:]], axis=0)

    def finish(k, value):
        flow_ref[k] = value

    linearize(
        layers, lambda k: (ext_ref[k], cond_ref[k], deriv_ref[k]), plain(store_ref),
        lambda k, state: ring_faces(state, 1, inside), masked, coefs, finish,
    )


def first_kernel(
    table_ref, src_ref, snear_ref, sfar_ref, ynear_ref, yfar_ref,
    ext_ref, ks_ref, cond_ref, deriv_ref, water_ref, flow_ref, *rest,
):
    mains, rest = rest[:7], rest[7:]
    ext_side, ks_side, steep_side, cap_side, base_ref, p0_ref, p1_ref, p2_ref, gram_ref = rest[:9]
    sides, (cond_side, deriv_side, store_side) = rest[9:16], rest[16:19]
    diag_first, diag_last, yp_last, ym_first = rest[19:23]
    layers, rows, cols = src_ref.shape
    tables = table_rows(table_ref, rows + 2 * HALO)
    heads, soils, sources = tall_strips(layers, ynear_ref, yfar_ref, snear_ref, sfar_ref)
    start, end, middle = slice(0, LANES), slice(cols - LANES, cols), slice(LANES, cols - LANES)
    lane = lane_iota((rows + 2 * HALO, LANES))
    is_first, is_last = lane == 0, lane == LANES - 1

    def source_of(k):
        ends = ends_of(snear_ref, sfar_ref, k, SOURCE_DEPTH, slice(0, cols))
        return jnp.concatenate([src_ref[k], ends], axis=0)

    for k in range(layers):
        head = side(heads, k)
        index = side(soils, k).astype(jnp.int32)
        conduct, steep, capacity = (lookup(row, index) for row in tables)
        cond, deriv, store, water = pointwise(head, conduct, steep, capacity)
        outs = (ext_side, ks_side, steep_side, cap_side, cond_side, deriv_side, store_side)
        for ref, value in zip(outs, (head, conduct, steep, capacity, cond, deriv, store)):
            ref[k] = value
        base_ref[k, :, 0:cols] = water_ref[k] + source_of(k)
        base_ref[k, :, cols:] = water + side(sources, k)
        p0_ref[k, :, middle] = flow_ref[k, :, middle] + (water_ref[k, :, middle] - base_ref[k, :, middle])
        p0_ref[k, :, cols:] = water - base_ref[k, :, cols:]

    masks = [(ref > 0.0).astype(f32) for ref in (ks_ref[0, :, start], ks_ref[0, :, end], ks_side[0])]

    def y_faces(k, state):
        first = (ext_ref[k, :, start], cond_ref[k, :, start], deriv_ref[k, :, start])
        last = (ext_ref[k, :, end], cond_ref[k, :, end], deriv_ref[k, :, end])
        moved = [after(x, 1) for x in state]
        ahead = [jnp.where(is_last, after(x, 1), y) for x, y in zip(first, moved)]
        a, b, face = face_of(state, ahead)
        a_in, b_in, face_in = (jnp.where(is_last, x, 0.0) for x in face_of(last, moved))
        a_out, b_out, face_out = (before(x, 1) for x in (a, b, face))
        a_pre, b_pre, face_pre = (before(x, 1) for x in (a_in, b_in, face_in))
        gain = water_ref[k, :, end] - base_ref[k, :, end]
        p0_ref[k, :, end] = flow_ref[k, :, end] + face_in * masks[1] + gain
        diag_last[k] = mains[0][k, :, end] + a_in
        yp_last[k] = mains[3][k, :, end] + b_in * masks[1]
        gain = water_ref[k, :, start] - base_ref[k, :, start]
        p0_ref[k, :, start] = flow_ref[k, :, start] - jnp.where(is_first, face_out, 0.0) * masks[0] + gain
        diag_first[k] = mains[0][k, :, start] + jnp.where(is_first, b_out, 0.0)
        ym_first[k] = mains[4][k, :, start] + jnp.where(is_first, a_out, 0.0) * masks[0]
        a_pre, b_pre, face_pre = (
            jnp.where(is_first, x, y)
            for x, y in ((a_pre, a_out), (b_pre, b_out), (face_pre, face_out))
        )
        return face - face_pre, a + b_pre, b, a_pre

    def finish(k, value):
        p0_ref[k, :, cols:] = p0_ref[k, :, cols:] + value

    linearize(
        layers, lambda k: (ext_side[k], cond_side[k], deriv_side[k]), plain(store_side),
        y_faces, lambda value: value * masks[2], sides, finish,
    )

    def pieces(n, first_of, last_of):
        main, beside = mains[n], sides[n]
        return lambda k: jnp.concatenate(
            [first_of(main, k), main[k, :, middle], last_of(main, k), beside[k]], axis=1
        )

    def of_start(ref, k):
        return ref[k, :, start]

    def of_end(ref, k):
        return ref[k, :, end]

    coefs = [joined(main, beside) for main, beside in zip(mains, sides)]
    coefs[0] = pieces(0, lambda _, k: diag_first[k], lambda _, k: diag_last[k])
    coefs[3] = pieces(3, of_start, lambda _, k: yp_last[k])
    coefs[4] = pieces(4, lambda _, k: ym_first[k], of_end)
    powers((p0_ref, p1_ref, p2_ref), coefs, (rows, cols), gram_ref)


def second_kernel(
    arrived_ref, old_ref, ks_ref, steep_ref, cap_ref, old_side, ks_side, steep_side, cap_side,
    base_ref, q0_ref, q1_ref, q2_ref,
    part_ref, p0_ref, p1_ref, p2_ref, gram_ref, ext_ref, cond_ref, deriv_ref, store_ref, gain_ref, *coefs,
):
    layers = old_ref.shape[0]
    rows, cols = part_ref.shape[1:]
    x = solve(arrived_ref)
    near = lax.broadcasted_iota(jnp.int32, (HALO, cols + LANES), 0) < HALO // 2

    def folded(of):
        def get(k):
            value = of(k)
            ends = jnp.where(near, value[rows : rows + HALO], value[rows + HALO :])
            return jnp.concatenate([value[:rows], ends], axis=0)

        return get

    old_of, ks_of = folded(joined(old_ref, old_side)), folded(joined(ks_ref, ks_side))
    steep_of, cap_of = folded(joined(steep_ref, steep_side)), folded(joined(cap_ref, cap_side))
    base_of, *qs = (folded(plain(ref)) for ref in (base_ref, q0_ref, q1_ref, q2_ref))
    for k in range(layers):
        head = old_of(k)
        for value, q_of in zip(x, qs):
            head = head - value * q_of(k)
        cond, deriv, store, water = pointwise(head, ks_of(k), steep_of(k), cap_of(k))
        ext_ref[k] = head
        part_ref[k] = head[:rows, :cols]
        cond_ref[k] = cond
        deriv_ref[k] = deriv
        store_ref[k] = store
        gain_ref[k] = water - base_of(k)
    mask = (ks_of(0) > 0.0).astype(f32)

    def masked(value):
        own = value[:rows, cols:] * mask[:rows, cols:]
        top = jnp.concatenate([value[:rows, :cols], own], axis=1)
        return jnp.concatenate([top, value[rows:] * mask[rows:]], axis=0)

    def finish(k, value):
        p0_ref[k] = value + gain_ref[k]

    linearize(
        layers, lambda k: (ext_ref[k], cond_ref[k], deriv_ref[k]), plain(store_ref),
        lambda k, state: ring_faces(state, 1), masked, coefs, finish,
    )
    powers((p0_ref, p1_ref, p2_ref), [plain(ref) for ref in coefs], (rows, cols), gram_ref)


def last_kernel(arrived_ref, part_ref, q0_ref, q1_ref, q2_ref, head_ref):
    layers, rows, cols = part_ref.shape
    x = solve(arrived_ref)
    for k in range(layers):
        own = (k, slice(0, rows), slice(0, cols))
        head_ref[k] = part_ref[k] - x[0] * q0_ref[own] - x[1] * q1_ref[own] - x[2] * q2_ref[own]


def shards(head_old, soil_type, soil_table, forcing, canopy, column_slot):
    layers, rows, cols = head_old.shape
    both = ("gx", "gy")
    devices = lax.axis_size("gx") * lax.axis_size("gy")
    tall, wide = rows + 2 * HALO, cols + LANES
    own, ext = ((layers, rows, cols), f32), ((layers, tall, wide), f32)
    gram_block = ((devices, 1, LANES), f32)

    def exchange(to_near, to_far, axis):
        size = lax.axis_size(axis)
        near = [(i, i + 1) for i in range(0, size - 1, 2)]
        far = [(i, i + 1) for i in range(1, size - 1, 2)]
        return tuple(
            lax.ppermute(x, axis, pairs + [(j, i) for i, j in pairs])
            for x, pairs in ((to_near, near), (to_far, far))
        )

    def spread(x, axes):
        return lax.all_to_all(x, axes, split_axis=0, concat_axis=0, tiled=True)

    def edge(count):
        return (-(-count // 8) * 8, cols), f32

    send, to_near, to_far = call(
        pack_kernel,
        [((devices, 8, LANES), f32)] + [edge(2 * STATE_DEPTH * layers)] * 2,
        3,
        scratch=[
            pltpu.VMEM(canopy.shape, f32),
            pltpu.VMEM(head_old.shape, f32),
            pltpu.VMEM(soil_type.shape, jnp.int32),
            pltpu.SemaphoreType.DMA((3,)),
        ],
        in_specs=[pl.BlockSpec(memory_space=pl.ANY)] * 3,
        grant=63400000,
    )(canopy, head_old, soil_type)
    arrived = spread(send, both)
    near, far = exchange(to_near, to_far, "gx")
    columns = (head_old, soil_type, forcing, column_slot)
    table = ((devices // 2, -(-layers // 2) + 1, 8, LANES), jnp.int32)
    some, flux, tab, factor = call(
        edge_source_kernel,
        [((layers, rows, 2 * LANES), f32), ((2, rows, 2 * LANES), f32), table, ((devices // 2, 8, LANES), f32)],
        6,
        in_specs=[smem] + [vmem] * 5,
    )(soil_table, arrived, *columns)
    to_near, to_far = call(strip_kernel, [((3, rows, LANES), f32)] * 2, 3)(head_old, soil_type, some)
    ynear, yfar = exchange(to_near, to_far, "gy")
    source, flux = call(
        inner_source_kernel, [own, ((2, rows, cols), f32)], 9, in_specs=[smem] + [vmem] * 8
    )(soil_table, tab, factor, *columns, some, flux)
    to_near, to_far = call(source_edge_kernel, [edge(SOURCE_DEPTH * layers + HALO + HALO // 2)] * 2, 3)(
        source, ynear, yfar
    )
    snear, sfar = exchange(to_near, to_far, "gx")
    main, side_block = ((layers, tall, cols), f32), ((layers, tall, LANES), f32)
    old, ks, steep, cap, cond, deriv, store, water = call(
        state_kernel, [main] * 8, 5, in_specs=[smem] + [vmem] * 4
    )(soil_table, head_old, soil_type, near, far)
    flow, *coefs = call(functools.partial(flow_kernel, rows=rows), [main] * 8, 5)(
        old, ks, cond, deriv, store
    )
    old_s, ks_s, steep_s, cap_s, base, p0, p1, p2, gram = call(
        first_kernel,
        [side_block] * 4 + [ext] * 4 + [gram_block],
        19,
        scratch=[pltpu.VMEM(side_block[0], f32)] * 14,
        in_specs=[smem] + [vmem] * 18,
    )(soil_table, source, snear, sfar, ynear, yfar, old, ks, cond, deriv, water, flow, *coefs)
    sums = spread(gram, both)
    part, q0, q1, q2, gram = call(
        second_kernel,
        [own] + [((layers, rows + HALO, wide), f32)] * 3 + [gram_block],
        13,
        scratch=[pltpu.VMEM((layers, rows + HALO, wide), f32)] * 12,
    )(sums, old, ks, steep, cap, old_s, ks_s, steep_s, cap_s, base, p0, p1, p2)
    sums = spread(gram, both)
    (head,) = call(last_kernel, [own], 5)(sums, part, q0, q1, q2)
    return head, flux


def solution(mesh):
    return jax.shard_map(
        shards,
        mesh=mesh,
        in_specs=(
            P(None, "gx", "gy"),
            P(None, "gx", "gy"),
            P(),
            P(None, "gx", "gy"),
            P(None, ("gx", "gy")),
            P("gx", "gy"),
        ),
        out_specs=(P(None, "gx", "gy"), P(None, "gx", "gy")),
        check_vma=False,
    )
```

```python
import functools

import jax
import jax.numpy as jnp
from jax import lax
from jax.experimental import pallas as pl
from jax.experimental.pallas import tpu as pltpu
from jax.sharding import PartitionSpec as P

NEWTON = 2
KRYLOV = 3
HALO = 8
STATE_DEPTH = 7
SOURCE_DEPTH = 6
FIXED = 65535.0
LANES = 128
SLOT = 64

storage_weight = 4.0
norm_epsilon = 1e-06

VMEM_LIMIT = 20 * 1024 * 1024
PAIRS = [(i, j) for i in range(KRYLOV + 1) for j in range(i, KRYLOV + 1)]

f32 = jnp.float32
vmem = pl.BlockSpec(memory_space=pltpu.VMEM)
smem = pl.BlockSpec(memory_space=pltpu.SMEM)


def call(body, outs, n_in, scratch=(), in_specs=None, flops=1000000, grant=VMEM_LIMIT):
    return pl.pallas_call(
        body,
        out_shape=[jax.ShapeDtypeStruct(s, d) for s, d in outs],
        in_specs=in_specs or [vmem] * n_in,
        out_specs=[vmem] * len(outs),
        scratch_shapes=list(scratch),
        compiler_params=pltpu.CompilerParams(vmem_limit_bytes=grant),
        cost_estimate=pl.CostEstimate(flops=flops, bytes_accessed=1000000, transcendentals=0),
    )


def lane_iota(shape):
    return lax.broadcasted_iota(jnp.int32, shape, len(shape) - 1)


def pack_kernel(
    canopy_hbm, head_hbm, soil_hbm, send_ref, near_ref, canopy_ref, head_ref, soil_ref, sems
):
    copies = [
        pltpu.make_async_copy(canopy_hbm, canopy_ref, sems.at[0]),
        pltpu.make_async_copy(head_hbm, head_ref, sems.at[1]),
        pltpu.make_async_copy(soil_hbm, soil_ref, sems.at[2]),
    ]
    for copy in copies:
        copy.start()
    copies[0].wait()
    rows = canopy_ref.shape[0]
    low = lane_iota((8, LANES)) < SLOT
    for t in range(canopy_ref.shape[1] // LANES):
        here = slice(t * LANES, (t + 1) * LANES)
        first = canopy_ref[0:8, here]
        rest = jnp.concatenate([canopy_ref[8:rows, here], jnp.zeros((16 - rows, LANES), f32)], axis=0)
        send_ref[2 * t] = jnp.where(low, first, pltpu.roll(rest, SLOT, 1))
        send_ref[2 * t + 1] = jnp.where(low, pltpu.roll(first, SLOT, 1), rest)
    layers, rows, _ = head_ref.shape
    copies[1].wait()
    copies[2].wait()
    state_edge(head_ref, soil_ref, near_ref, near_is_above("gx"))


def state_edge(head_ref, soil_ref, out_ref, upward):
    layers, rows, _ = head_ref.shape
    for n in range(2 * layers):
        plane = head_ref[n] if n < layers else (soil_ref[n - layers] + 1).astype(f32)
        value = jnp.where(upward, plane[rows - STATE_DEPTH :], plane[:STATE_DEPTH])
        out_ref[STATE_DEPTH * n : STATE_DEPTH * (n + 1)] = value


def far_edge_kernel(head_ref, soil_ref, _, far_ref):
    state_edge(head_ref, soil_ref, far_ref, jnp.logical_not(near_is_above("gx")))


def near_is_above(axis):
    return lax.rem(lax.axis_index(axis), 2) == 0


def below_above(near, far, axis):
    upward = near_is_above(axis)
    return jnp.where(upward, far, near), jnp.where(upward, near, far)


def table_rows(table_ref, rows):
    lane = lane_iota((rows, LANES))
    out = []
    for field in range(table_ref.shape[0]):
        row = jnp.zeros((rows, LANES), f32)
        for kind in range(table_ref.shape[1]):
            row = jnp.where(lane == kind + 1, table_ref[field, kind], row)
        out.append(row)
    return out


def lookup(row, index):
    pieces = [
        jnp.take_along_axis(row, index[:, at : at + LANES], axis=1, mode="promise_in_bounds")
        for at in range(0, index.shape[1], LANES)
    ]
    return jnp.concatenate(pieces, axis=1)


def sigmoid(u):
    return 1.0 / (1.0 + jnp.exp(-u))


def edge_source_kernel(
    table_ref, arrived_ref, head_ref, soil_ref, forcing_ref, slot_ref,
    source_ref, flux_ref, tab_ref, factor_ref,
):
    layers, rows, cols = head_ref.shape
    owners = arrived_ref.shape[0]
    pairs = -(-layers // 2)
    low = lane_iota((8, LANES)) < SLOT
    line = lax.broadcasted_iota(jnp.int32, (16, LANES), 0)
    is_root = (line >= 3) & (line < 3 + layers)

    def unpack(t, _):
        first = arrived_ref[2 * t]
        second = arrived_ref[2 * t + 1]
        both = jnp.concatenate(
            [
                jnp.where(low, first, pltpu.roll(second, SLOT, 1)),
                jnp.where(low, pltpu.roll(first, SLOT, 1), second),
            ],
            axis=0,
        )
        leaf_area, albedo, resist = both[0:1], both[1:2], both[2:3]
        root_sum = jnp.sum(jnp.where(is_root, both, 0.0), axis=0, keepdims=True)
        factor = leaf_area / ((leaf_area + resist) * root_sum) * (1.0 / FIXED)
        factor_ref[t] = jnp.broadcast_to(factor, (8, LANES))
        fixed = (both * FIXED + 0.5).astype(jnp.int32)
        for m in range(pairs):
            word = fixed[3 + m : 4 + m]
            if m + pairs < layers:
                word = word | (fixed[3 + m + pairs : 4 + m + pairs] << 16)
            tab_ref[t, m] = jnp.broadcast_to(word, (8, LANES))
        leaf = ((0.5 + 0.3 * leaf_area) * (0.25 * FIXED) + 0.5).astype(jnp.int32)
        bright = ((1.0 - albedo) * FIXED + 0.5).astype(jnp.int32)
        tab_ref[t, pairs] = jnp.broadcast_to(leaf | (bright << 16), (8, LANES))
        return 0

    lax.fori_loop(0, owners // 2, unpack, 0, unroll=16)
    places = [(0, 0), (cols - LANES, LANES)]
    land_columns(
        table_ref, tab_ref, factor_ref, head_ref, soil_ref, forcing_ref, slot_ref, source_ref, flux_ref, places
    )


def inner_source_kernel(
    table_ref, tab_ref, factor_ref, head_ref, soil_ref, forcing_ref, slot_ref, some_ref, part_ref,
    source_ref, flux_ref,
):
    cols = head_ref.shape[2]
    places = [(at, at) for at in range(LANES, cols - LANES, LANES)]
    land_columns(
        table_ref, tab_ref, factor_ref, head_ref, soil_ref, forcing_ref, slot_ref, source_ref, flux_ref, places
    )
    for whole_ref, piece_ref in ((source_ref, some_ref), (flux_ref, part_ref)):
        for k in range(whole_ref.shape[0]):
            whole_ref[k, :, 0:LANES] = piece_ref[k, :, 0:LANES]
            whole_ref[k, :, cols - LANES : cols] = piece_ref[k, :, LANES : 2 * LANES]


def land_columns(
    table_ref, tab_ref, factor_ref, head_ref, soil_ref, forcing_ref, slot_ref, source_ref, flux_ref, places
):
    layers, rows, _ = head_ref.shape
    halves_of = tab_ref.shape[0]
    pairs = tab_ref.shape[1] - 1
    tables = table_rows(table_ref, rows)
    shape = (rows, LANES)

    def whole(block):
        return jnp.concatenate([block] * (rows // 8), axis=0)

    for at_y, put in places:
        here = (slice(0, rows), slice(at_y, at_y + LANES))
        there = (slice(0, rows), slice(put, put + LANES))
        slot = slot_ref[here]
        land = slot >= 0
        value = jnp.maximum(slot, 0)
        lane = value & (LANES - 1)
        tile = value >> 7

        def pick(t, held):
            match = tile == t
            found = [lookup(whole(tab_ref[t, m]), lane) for m in range(pairs + 1)]
            found.append(lookup(whole(factor_ref[t]), lane))
            return tuple(jnp.where(match, new, old) for new, old in zip(found, held))

        held = tuple([jnp.full(shape, 1, jnp.int32)] * (pairs + 1) + [jnp.full(shape, 1.0 / FIXED, f32)])
        if halves_of <= 16:
            for t in range(halves_of):
                held = pick(t, held)
        else:
            held = lax.fori_loop(0, halves_of, pick, held, unroll=8)
        *words, terms, factor = held

        def halves(word):
            upper = lax.shift_right_logical(word, jnp.full(shape, 16, jnp.int32))
            return (word & 0xFFFF).astype(f32), upper.astype(f32)

        leaf, bright = halves(terms)
        exchange_coef = leaf * (4.0 / FIXED)
        absorbed = bright * (1.0 / FIXED)
        split = [halves(word) for word in words]
        uptake = []
        for k in range(layers):
            index = soil_ref[(k,) + here] + 1
            steep = lookup(tables[1], index)
            root = factor * split[k % pairs][k // pairs]
            uptake.append(root * sigmoid(steep * head_ref[(k,) + here]))
            if k == 0:
                ks_top = lookup(tables[0], index)
        conductance = functools.reduce(jnp.add, uptake)
        sunlight, air_temp, humidity, rainfall = (forcing_ref[(i,) + here] for i in range(4))
        radiation = absorbed * sunlight + 0.3
        square = air_temp * air_temp
        excess = radiation - 0.3 * square * square - conductance * (0.5 - humidity)
        slope = -1.2 * square * air_temp - exchange_coef - conductance
        rise = -excess / slope
        surface = air_temp + rise
        vapour = 0.5 * jnp.exp(2.0 * rise)
        square = surface * surface
        excess = (
            radiation
            - 0.3 * square * square
            - exchange_coef * rise
            - conductance * (vapour - humidity)
        )
        slope = -1.2 * square * surface - exchange_coef - 2.0 * conductance * vapour
        rise = rise - excess / slope
        rate = 0.5 * jnp.exp(2.0 * rise) - humidity
        infiltration = rainfall * ks_top / (rainfall + ks_top)
        infiltration = jnp.where(land, infiltration, 0.0)
        rate = jnp.where(land, rate, 0.0)
        flux_ref[(0,) + there] = conductance * rate
        flux_ref[(1,) + there] = infiltration
        for k in range(layers):
            value = -rate * uptake[k]
            if k == 0:
                value = value + infiltration
            source_ref[(k,) + there] = value


def strips(planes, shift_from):
    packed = None
    for k, plane in enumerate(planes):
        lane = lane_iota(plane.shape)
        shift = (HALO * k - shift_from) % LANES
        moved = pltpu.roll(plane, shift, 1) if shift else plane
        inside = (lane >= HALO * k) & (lane < HALO * (k + 1))
        packed = jnp.where(inside, moved, 0.0 if packed is None else packed)
    return packed


def strip_parts(cols):
    return ((slice(0, LANES), 0), (slice(cols - LANES, cols), LANES - HALO))


def ends_of(near_ref, far_ref, at, depth, part):
    edge = slice(depth * at, depth * (at + 1))
    below, above = below_above(near_ref[edge, part], far_ref[edge, part], "gx")
    gap = jnp.zeros((2 * (HALO - depth), above.shape[1]), f32)
    return jnp.concatenate([above, gap, below], axis=0)


def strip_kernel(head_ref, soil_ref, src_ref, out_ref, *, near, end):
    layers, _, cols = head_ref.shape
    upward = near_is_above("gy")
    if not near:
        upward = jnp.logical_not(upward)
    blocks = []
    for (part, shift), at in zip(strip_parts(cols), (0, end)):
        blocks.append(
            (
                strips([head_ref[k, :, part] for k in range(layers)], shift),
                strips([(soil_ref[k, :, part] + 1).astype(f32) for k in range(layers)], shift),
                strips([src_ref[k, :, at : at + LANES] for k in range(layers)], shift),
            )
        )
    for field, (low, high) in enumerate(zip(*blocks)):
        out_ref[field] = jnp.where(upward, high, low)


def source_edge_kernel(src_ref, ynear_ref, yfar_ref, near_ref, far_ref):
    layers, rows, _ = src_ref.shape
    at = SOURCE_DEPTH * layers
    half = HALO // 2
    upward = near_is_above("gx")
    pieces = [x for field in range(3) for x in below_above(ynear_ref[field], yfar_ref[field], "gy")]
    for out_ref, up in ((near_ref, upward), (far_ref, jnp.logical_not(upward))):
        for k in range(layers):
            part = slice(SOURCE_DEPTH * k, SOURCE_DEPTH * (k + 1))
            plane = src_ref[k]
            out_ref[part] = jnp.where(up, plane[rows - SOURCE_DEPTH :], plane[:SOURCE_DEPTH])
        blocks = [jnp.where(up, x[rows - HALO :], x[:HALO]) for x in pieces]
        tail = [block[h : h + half] for block in blocks[4:6] for h in (0, half)]
        for j in range(4):
            out_ref[at : at + HALO, j * LANES : (j + 1) * LANES] = blocks[j]
            out_ref[at + HALO : at + HALO + half, j * LANES : (j + 1) * LANES] = tail[j]


def corner(edge_ref, at, field, which):
    half = HALO // 2
    if field < 2:
        j = 2 * field + which
        return edge_ref[at : at + HALO, j * LANES : (j + 1) * LANES]
    pieces = [
        edge_ref[at + HALO : at + HALO + half, j * LANES : (j + 1) * LANES]
        for j in (2 * which, 2 * which + 1)
    ]
    return jnp.concatenate(pieces, axis=0)


def tall_strips(layers, ynear_ref, yfar_ref, snear_ref, sfar_ref):
    at = SOURCE_DEPTH * layers
    out = []
    for field in range(3):
        pair = []
        below, above = below_above(ynear_ref[field], yfar_ref[field], "gy")
        for which, piece in ((1, above), (0, below)):
            lower, upper = below_above(
                corner(snear_ref, at, field, which), corner(sfar_ref, at, field, which), "gx"
            )
            pair.append(jnp.concatenate([piece, upper, lower], axis=0))
        out.append(pair)
    return out


def side(strip, k):
    right, left = strip
    lane = lane_iota(right.shape)
    shift = (-HALO * k) % LANES
    right = pltpu.roll(right, shift, 1) if shift else right
    left = pltpu.roll(left, (LANES - HALO - HALO * k) % LANES, 1)
    return jnp.where(lane < HALO, right, jnp.where(lane >= LANES - HALO, left, 0.0))


def after(x, axis):
    return pltpu.roll(x, x.shape[axis] - 1, axis)


def before(x, axis):
    return pltpu.roll(x, 1, axis)


def pointwise(head, conduct, steep, capacity):
    sat = 0.5 + 0.5 * jnp.tanh(0.5 * (steep * head))
    slope = steep * sat * (1.0 - sat)
    cond = conduct * (0.1 + 0.9 * sat * sat)
    deriv = 0.9 * conduct * sat * slope
    weighted = storage_weight * capacity
    return cond, deriv, weighted * slope, weighted * sat


def joined(*refs):
    return lambda k: jnp.concatenate([ref[k] for ref in refs], axis=1)


def plain(ref):
    return lambda k: ref[k]


def face_of(here, there, extra=None):
    mean = 0.5 * (here[1] + there[1])
    drop = here[0] - there[0]
    if extra is not None:
        drop = drop + extra
    return mean + here[2] * drop, mean - there[2] * drop, mean * drop


def ring_faces(state, axis, inside=None):
    a, b, face = face_of(state, [after(x, axis) for x in state])
    if inside is not None:
        a, b, face = (jnp.where(inside, x, 0.0) for x in (a, b, face))
    return face - before(face, axis), a + before(b, axis), b, before(a, axis)


def linearize(layers, state_of, store_of, y_faces, masked, coefs, finish):
    diag_ref, xp_ref, xm_ref, yp_ref, ym_ref, az_ref, bz_ref = coefs
    above = None
    for k in range(layers):
        state = state_of(k)
        net_x, diag_x, xp, xm = ring_faces(state, 0)
        net_y, diag_y, yp, ym = y_faces(k, state)
        for ref, value in ((xp_ref, xp), (xm_ref, xm), (yp_ref, yp), (ym_ref, ym)):
            ref[k] = masked(value)
        if k + 1 < layers:
            a, b, face = face_of(state, state_of(k + 1), 1.0)
            az_ref[k] = a
            bz_ref[k] = b
        else:
            a, face = 2.0 * state[2], state[1]
        diag = store_of(k) + diag_x + diag_y + a
        value = net_x + net_y + face
        if above is not None:
            diag = diag + above[1]
            value = value - above[0]
        above = (face, b)
        diag_ref[k] = diag
        finish(k, masked(value))


def apply(v_ref, coefs, k):
    diag_of, xp_of, xm_of, yp_of, ym_of, az_of, bz_of = coefs
    v = v_ref[k]
    value = diag_of(k) * v
    value = value - xp_of(k) * after(v, 0) - xm_of(k) * before(v, 0)
    value = value - yp_of(k) * after(v, 1) - ym_of(k) * before(v, 1)
    if k > 0:
        value = value - az_of(k - 1) * v_ref[k - 1]
    if k + 1 < v_ref.shape[0]:
        value = value - bz_of(k) * v_ref[k + 1]
    return value


def powers(basis, coefs, tile, out_ref):
    layers = basis[0].shape[0]
    rows, cols = tile
    for step in range(KRYLOV - 1):
        for k in range(layers):
            basis[step + 1][k] = apply(basis[step], coefs, k)
    sums = [jnp.zeros((8, LANES), f32) for _ in PAIRS]
    for k in range(layers):
        top = apply(basis[-1], coefs, k)
        for at in range(0, rows, 8):
            for lane_at in range(0, cols, LANES):
                part = (slice(at, at + 8), slice(lane_at, lane_at + LANES))
                vs = [b[(k,) + part] for b in basis] + [top[part]]
                for e, (i, j) in enumerate(PAIRS):
                    sums[e] = sums[e] + vs[i] * vs[j]
    lines = [jnp.sum(x, axis=0, keepdims=True) for x in sums]
    lines.append(jnp.zeros((16 - len(PAIRS), LANES), f32))
    block = jnp.sum(jnp.concatenate(lines, axis=0), axis=1, keepdims=True)
    line = lax.broadcasted_iota(jnp.int32, (16, LANES), 0)
    flat = jnp.sum(jnp.where(lane_iota((16, LANES)) == line, block, 0.0), axis=0, keepdims=True)
    for d in range(out_ref.shape[0]):
        out_ref[d] = flat


def solve(gram_ref):
    terms = [gram_ref[d] for d in range(gram_ref.shape[0])]
    while len(terms) > 1:
        terms = [functools.reduce(jnp.add, terms[i : i + 2]) for i in range(0, len(terms), 2)]
    total = terms[0]
    line = lax.broadcasted_iota(jnp.int32, (16, LANES), 0)
    spread = jnp.broadcast_to(total, (16, LANES))
    column = jnp.sum(jnp.where(lane_iota((16, LANES)) == line, spread, 0.0), axis=1, keepdims=True)
    gram = {}
    for e, (i, j) in enumerate(PAIRS):
        gram[i, j] = gram[j, i] = column[e : e + 1, :]

    def times_gram(c):
        out = []
        for i in range(KRYLOV + 1):
            out.append(functools.reduce(jnp.add, [gram[i, m] * c[m] for m in range(len(c))]))
        return out

    def dot(a, b):
        return functools.reduce(jnp.add, [x * y for x, y in zip(a, b)])

    square = gram[0, 0] + norm_epsilon
    inverse = lax.rsqrt(square)
    beta = square * inverse
    basis = [[inverse]]
    images = [times_gram(basis[0])]
    hessen = {}
    for j in range(KRYLOV):
        w = [jnp.zeros_like(beta)] + basis[j]
        for i in range(j + 1):
            product = dot(w, images[i])
            hessen[i, j] = product
            w = [w[m] - product * basis[i][m] if m < len(basis[i]) else w[m] for m in range(len(w))]
        square = jnp.maximum(dot(w, times_gram(w)), 0.0) + norm_epsilon
        inverse = lax.rsqrt(square)
        hessen[j + 1, j] = square * inverse
        if j + 1 < KRYLOV:
            basis.append([x * inverse for x in w])
            images.append(times_gram(basis[-1]))
    n = KRYLOV
    normal = {}
    for a in range(n):
        for b in range(a + 1):
            normal[a, b] = functools.reduce(
                jnp.add,
                [hessen[i, a] * hessen[i, b] for i in range(n + 1) if (i, a) in hessen and (i, b) in hessen],
            )
    factor = {}
    inverse = []
    for a in range(n):
        for b in range(a + 1):
            value = normal[a, b]
            for m in range(b):
                value = value - factor[a, m] * factor[b, m]
            if a == b:
                inverse.append(lax.rsqrt(value))
            else:
                factor[a, b] = value * inverse[b]
    forward = []
    for a in range(n):
        value = hessen[0, a] * beta
        for m in range(a):
            value = value - factor[a, m] * forward[m]
        forward.append(value * inverse[a])
    backward = [None] * n
    for a in reversed(range(n)):
        value = forward[a]
        for m in range(a + 1, n):
            value = value - factor[m, a] * backward[m]
        backward[a] = value * inverse[a]
    return [
        functools.reduce(jnp.add, [backward[j] * basis[j][i] for j in range(i, n)]) for i in range(n)
    ]


def state_kernel(
    table_ref, head_ref, soil_ref, near_ref, far_ref,
    ext_ref, ks_ref, steep_ref, cap_ref, cond_ref, deriv_ref, store_ref, water_ref,
):
    layers, rows, cols = head_ref.shape
    tables = table_rows(table_ref, rows + 2 * HALO)
    every = slice(0, cols)
    for k in range(layers):
        ends = ends_of(near_ref, far_ref, k, STATE_DEPTH, every)
        head = jnp.concatenate([head_ref[k], ends], axis=0)
        ends = ends_of(near_ref, far_ref, layers + k, STATE_DEPTH, every)
        index = jnp.concatenate([soil_ref[k] + 1, ends.astype(jnp.int32)], axis=0)
        conduct, steep, capacity = (lookup(row, index) for row in tables)
        values = (head, conduct, steep, capacity) + pointwise(head, conduct, steep, capacity)
        outs = (ext_ref, ks_ref, steep_ref, cap_ref, cond_ref, deriv_ref, store_ref, water_ref)
        for ref, value in zip(outs, values):
            ref[k] = value


def flow_kernel(ext_ref, ks_ref, cond_ref, deriv_ref, store_ref, flow_ref, *coefs, rows):
    layers, _, cols = ext_ref.shape
    mask = (ks_ref[0] > 0.0).astype(f32)
    inside = lane_iota(mask.shape) < cols - 1

    def masked(value):
        return jnp.concatenate([value[:rows], value[rows:] * mask[rows:]], axis=0)

    def finish(k, value):
        flow_ref[k] = value

    linearize(
        layers, lambda k: (ext_ref[k], cond_ref[k], deriv_ref[k]), plain(store_ref),
        lambda k, state: ring_faces(state, 1, inside), masked, coefs, finish,
    )


def first_kernel(
    table_ref, src_ref, snear_ref, sfar_ref, ynear_ref, yfar_ref,
    ext_ref, ks_ref, cond_ref, deriv_ref, water_ref, flow_ref, *rest,
):
    mains, rest = rest[:7], rest[7:]
    ext_side, ks_side, steep_side, cap_side, base_ref, p0_ref, p1_ref, p2_ref, gram_ref = rest[:9]
    sides, (cond_side, deriv_side, store_side) = rest[9:16], rest[16:19]
    diag_first, diag_last, yp_last, ym_first = rest[19:23]
    layers, rows, cols = src_ref.shape
    tables = table_rows(table_ref, rows + 2 * HALO)
    heads, soils, sources = tall_strips(layers, ynear_ref, yfar_ref, snear_ref, sfar_ref)
    start, end, middle = slice(0, LANES), slice(cols - LANES, cols), slice(LANES, cols - LANES)
    lane = lane_iota((rows + 2 * HALO, LANES))
    is_first, is_last = lane == 0, lane == LANES - 1

    def source_of(k):
        ends = ends_of(snear_ref, sfar_ref, k, SOURCE_DEPTH, slice(0, cols))
        return jnp.concatenate([src_ref[k], ends], axis=0)

    for k in range(layers):
        head = side(heads, k)
        index = side(soils, k).astype(jnp.int32)
        conduct, steep, capacity = (lookup(row, index) for row in tables)
        cond, deriv, store, water = pointwise(head, conduct, steep, capacity)
        outs = (ext_side, ks_side, steep_side, cap_side, cond_side, deriv_side, store_side)
        for ref, value in zip(outs, (head, conduct, steep, capacity, cond, deriv, store)):
            ref[k] = value
        base_ref[k, :, 0:cols] = water_ref[k] + source_of(k)
        base_ref[k, :, cols:] = water + side(sources, k)
        p0_ref[k, :, middle] = flow_ref[k, :, middle] + (water_ref[k, :, middle] - base_ref[k, :, middle])
        p0_ref[k, :, cols:] = water - base_ref[k, :, cols:]

    masks = [(ref > 0.0).astype(f32) for ref in (ks_ref[0, :, start], ks_ref[0, :, end], ks_side[0])]

    def y_faces(k, state):
        first = (ext_ref[k, :, start], cond_ref[k, :, start], deriv_ref[k, :, start])
        last = (ext_ref[k, :, end], cond_ref[k, :, end], deriv_ref[k, :, end])
        moved = [after(x, 1) for x in state]
        ahead = [jnp.where(is_last, after(x, 1), y) for x, y in zip(first, moved)]
        a, b, face = face_of(state, ahead)
        a_in, b_in, face_in = (jnp.where(is_last, x, 0.0) for x in face_of(last, moved))
        a_out, b_out, face_out = (before(x, 1) for x in (a, b, face))
        a_pre, b_pre, face_pre = (before(x, 1) for x in (a_in, b_in, face_in))
        gain = water_ref[k, :, end] - base_ref[k, :, end]
        p0_ref[k, :, end] = flow_ref[k, :, end] + face_in * masks[1] + gain
        diag_last[k] = mains[0][k, :, end] + a_in
        yp_last[k] = mains[3][k, :, end] + b_in * masks[1]
        gain = water_ref[k, :, start] - base_ref[k, :, start]
        p0_ref[k, :, start] = flow_ref[k, :, start] - jnp.where(is_first, face_out, 0.0) * masks[0] + gain
        diag_first[k] = mains[0][k, :, start] + jnp.where(is_first, b_out, 0.0)
        ym_first[k] = mains[4][k, :, start] + jnp.where(is_first, a_out, 0.0) * masks[0]
        a_pre, b_pre, face_pre = (
            jnp.where(is_first, x, y)
            for x, y in ((a_pre, a_out), (b_pre, b_out), (face_pre, face_out))
        )
        return face - face_pre, a + b_pre, b, a_pre

    def finish(k, value):
        p0_ref[k, :, cols:] = p0_ref[k, :, cols:] + value

    linearize(
        layers, lambda k: (ext_side[k], cond_side[k], deriv_side[k]), plain(store_side),
        y_faces, lambda value: value * masks[2], sides, finish,
    )

    def pieces(n, first_of, last_of):
        main, beside = mains[n], sides[n]
        return lambda k: jnp.concatenate(
            [first_of(main, k), main[k, :, middle], last_of(main, k), beside[k]], axis=1
        )

    def of_start(ref, k):
        return ref[k, :, start]

    def of_end(ref, k):
        return ref[k, :, end]

    coefs = [joined(main, beside) for main, beside in zip(mains, sides)]
    coefs[0] = pieces(0, lambda _, k: diag_first[k], lambda _, k: diag_last[k])
    coefs[3] = pieces(3, of_start, lambda _, k: yp_last[k])
    coefs[4] = pieces(4, lambda _, k: ym_first[k], of_end)
    powers((p0_ref, p1_ref, p2_ref), coefs, (rows, cols), gram_ref)


def second_kernel(
    arrived_ref, old_ref, ks_ref, steep_ref, cap_ref, old_side, ks_side, steep_side, cap_side,
    base_ref, q0_ref, q1_ref, q2_ref,
    part_ref, p0_ref, p1_ref, p2_ref, gram_ref, ext_ref, cond_ref, deriv_ref, store_ref, gain_ref, *coefs,
):
    layers = old_ref.shape[0]
    rows, cols = part_ref.shape[1:]
    x = solve(arrived_ref)
    near = lax.broadcasted_iota(jnp.int32, (HALO, cols + LANES), 0) < HALO // 2

    def folded(of):
        def get(k):
            value = of(k)
            ends = jnp.where(near, value[rows : rows + HALO], value[rows + HALO :])
            return jnp.concatenate([value[:rows], ends], axis=0)

        return get

    old_of, ks_of = folded(joined(old_ref, old_side)), folded(joined(ks_ref, ks_side))
    steep_of, cap_of = folded(joined(steep_ref, steep_side)), folded(joined(cap_ref, cap_side))
    base_of, *qs = (folded(plain(ref)) for ref in (base_ref, q0_ref, q1_ref, q2_ref))
    for k in range(layers):
        head = old_of(k)
        for value, q_of in zip(x, qs):
            head = head - value * q_of(k)
        cond, deriv, store, water = pointwise(head, ks_of(k), steep_of(k), cap_of(k))
        ext_ref[k] = head
        part_ref[k] = head[:rows, :cols]
        cond_ref[k] = cond
        deriv_ref[k] = deriv
        store_ref[k] = store
        gain_ref[k] = water - base_of(k)
    mask = (ks_of(0) > 0.0).astype(f32)

    def masked(value):
        own = value[:rows, cols:] * mask[:rows, cols:]
        top = jnp.concatenate([value[:rows, :cols], own], axis=1)
        return jnp.concatenate([top, value[rows:] * mask[rows:]], axis=0)

    def finish(k, value):
        p0_ref[k] = value + gain_ref[k]

    linearize(
        layers, lambda k: (ext_ref[k], cond_ref[k], deriv_ref[k]), plain(store_ref),
        lambda k, state: ring_faces(state, 1), masked, coefs, finish,
    )
    powers((p0_ref, p1_ref, p2_ref), [plain(ref) for ref in coefs], (rows, cols), gram_ref)


def last_kernel(arrived_ref, part_ref, q0_ref, q1_ref, q2_ref, head_ref):
    layers, rows, cols = part_ref.shape
    x = solve(arrived_ref)
    for k in range(layers):
        own = (k, slice(0, rows), slice(0, cols))
        head_ref[k] = part_ref[k] - x[0] * q0_ref[own] - x[1] * q1_ref[own] - x[2] * q2_ref[own]


def shards(head_old, soil_type, soil_table, forcing, canopy, column_slot):
    layers, rows, cols = head_old.shape
    both = ("gx", "gy")
    devices = lax.axis_size("gx") * lax.axis_size("gy")
    tall, wide = rows + 2 * HALO, cols + LANES
    own, ext = ((layers, rows, cols), f32), ((layers, tall, wide), f32)
    gram_block = ((devices, 1, LANES), f32)

    def to_partner(x, axis, first):
        pairs = [(i, i + 1) for i in range(first, lax.axis_size(axis) - 1, 2)]
        return lax.ppermute(x, axis, pairs + [(j, i) for i, j in pairs])

    def spread(x, axes):
        return lax.all_to_all(x, axes, split_axis=0, concat_axis=0, tiled=True)

    def edge(count):
        return (-(-count // 8) * 8, cols), f32

    send, to_near = call(
        pack_kernel,
        [((devices, 8, LANES), f32), edge(2 * STATE_DEPTH * layers)],
        3,
        scratch=[
            pltpu.VMEM(canopy.shape, f32),
            pltpu.VMEM(head_old.shape, f32),
            pltpu.VMEM(soil_type.shape, jnp.int32),
            pltpu.SemaphoreType.DMA((3,)),
        ],
        in_specs=[pl.BlockSpec(memory_space=pl.ANY)] * 3,
        grant=63400000,
    )(canopy, head_old, soil_type)
    arrived = spread(send, both)
    near = to_partner(to_near, "gx", 0)
    columns = (head_old, soil_type, forcing, column_slot)
    table = ((devices // 2, -(-layers // 2) + 1, 8, LANES), jnp.int32)
    some, flux, tab, factor = call(
        edge_source_kernel,
        [((layers, rows, 2 * LANES), f32), ((2, rows, 2 * LANES), f32), table, ((devices // 2, 8, LANES), f32)],
        6,
        in_specs=[smem] + [vmem] * 5,
    )(soil_table, arrived, *columns)
    (to_far,) = call(
        far_edge_kernel,
        [edge(2 * STATE_DEPTH * layers)],
        3,
        in_specs=[vmem] * 2 + [pl.BlockSpec(memory_space=pl.ANY)],
    )(head_old, soil_type, some)
    far = to_partner(to_far, "gx", 1)
    strip = [((3, rows, LANES), f32)]
    (to_near,) = call(functools.partial(strip_kernel, near=True, end=LANES), strip, 3)(
        head_old, soil_type, some
    )
    ynear = to_partner(to_near, "gy", 0)
    source, flux = call(
        inner_source_kernel, [own, ((2, rows, cols), f32)], 9, in_specs=[smem] + [vmem] * 8
    )(soil_table, tab, factor, *columns, some, flux)
    (to_far,) = call(functools.partial(strip_kernel, near=False, end=cols - LANES), strip, 3)(
        head_old, soil_type, source
    )
    yfar = to_partner(to_far, "gy", 1)
    to_near, to_far = call(source_edge_kernel, [edge(SOURCE_DEPTH * layers + HALO + HALO // 2)] * 2, 3)(
        source, ynear, yfar
    )
    snear, sfar = to_partner(to_near, "gx", 0), to_partner(to_far, "gx", 1)
    main, side_block = ((layers, tall, cols), f32), ((layers, tall, LANES), f32)
    old, ks, steep, cap, cond, deriv, store, water = call(
        state_kernel, [main] * 8, 5, in_specs=[smem] + [vmem] * 4
    )(soil_table, head_old, soil_type, near, far)
    flow, *coefs = call(functools.partial(flow_kernel, rows=rows), [main] * 8, 5)(
        old, ks, cond, deriv, store
    )
    old_s, ks_s, steep_s, cap_s, base, p0, p1, p2, gram = call(
        first_kernel,
        [side_block] * 4 + [ext] * 4 + [gram_block],
        19,
        scratch=[pltpu.VMEM(side_block[0], f32)] * 14,
        in_specs=[smem] + [vmem] * 18,
    )(soil_table, source, snear, sfar, ynear, yfar, old, ks, cond, deriv, water, flow, *coefs)
    sums = spread(gram, both)
    part, q0, q1, q2, gram = call(
        second_kernel,
        [own] + [((layers, rows + HALO, wide), f32)] * 3 + [gram_block],
        13,
        scratch=[pltpu.VMEM((layers, rows + HALO, wide), f32)] * 12,
    )(sums, old, ks, steep, cap, old_s, ks_s, steep_s, cap_s, base, p0, p1, p2)
    sums = spread(gram, both)
    (head,) = call(last_kernel, [own], 5)(sums, part, q0, q1, q2)
    return head, flux


def solution(mesh):
    return jax.shard_map(
        shards,
        mesh=mesh,
        in_specs=(
            P(None, "gx", "gy"),
            P(None, "gx", "gy"),
            P(),
            P(None, "gx", "gy"),
            P(None, ("gx", "gy")),
            P("gx", "gy"),
        ),
        out_specs=(P(None, "gx", "gy"), P(None, "gx", "gy")),
        check_vma=False,
    )
```

```python
import functools

import jax
import jax.numpy as jnp
from jax import lax
from jax.experimental import pallas as pl
from jax.experimental.pallas import tpu as pltpu
from jax.sharding import PartitionSpec as P

NEWTON = 2
KRYLOV = 3
HALO = 8
STATE_DEPTH = 7
SOURCE_DEPTH = 6
FIXED = 65535.0
LANES = 128
SLOT = 64

storage_weight = 4.0
norm_epsilon = 1e-06

VMEM_LIMIT = 20 * 1024 * 1024
PAIRS = [(i, j) for i in range(KRYLOV + 1) for j in range(i, KRYLOV + 1)]

f32 = jnp.float32
vmem = pl.BlockSpec(memory_space=pltpu.VMEM)
smem = pl.BlockSpec(memory_space=pltpu.SMEM)


def call(body, outs, n_in, scratch=(), in_specs=None, flops=1000000, grant=VMEM_LIMIT):
    return pl.pallas_call(
        body,
        out_shape=[jax.ShapeDtypeStruct(s, d) for s, d in outs],
        in_specs=in_specs or [vmem] * n_in,
        out_specs=[vmem] * len(outs),
        scratch_shapes=list(scratch),
        compiler_params=pltpu.CompilerParams(vmem_limit_bytes=grant),
        cost_estimate=pl.CostEstimate(flops=flops, bytes_accessed=1000000, transcendentals=0),
    )


def lane_iota(shape):
    return lax.broadcasted_iota(jnp.int32, shape, len(shape) - 1)


def pack_kernel(
    canopy_hbm, head_hbm, soil_hbm, send_ref, near_ref, far_ref, canopy_ref, head_ref, soil_ref, sems
):
    copies = [
        pltpu.make_async_copy(canopy_hbm, canopy_ref, sems.at[0]),
        pltpu.make_async_copy(head_hbm, head_ref, sems.at[1]),
        pltpu.make_async_copy(soil_hbm, soil_ref, sems.at[2]),
    ]
    for copy in copies:
        copy.start()
    copies[0].wait()
    rows = canopy_ref.shape[0]
    low = lane_iota((8, LANES)) < SLOT
    for t in range(canopy_ref.shape[1] // LANES):
        here = slice(t * LANES, (t + 1) * LANES)
        first = canopy_ref[0:8, here]
        rest = jnp.concatenate([canopy_ref[8:rows, here], jnp.zeros((16 - rows, LANES), f32)], axis=0)
        send_ref[2 * t] = jnp.where(low, first, pltpu.roll(rest, SLOT, 1))
        send_ref[2 * t + 1] = jnp.where(low, pltpu.roll(first, SLOT, 1), rest)
    layers, rows, _ = head_ref.shape
    copies[1].wait()
    copies[2].wait()
    low_rows, high_rows = slice(0, STATE_DEPTH), slice(rows - STATE_DEPTH, rows)
    upward = near_is_above("gx")
    for n in range(2 * layers):
        plane = head_ref[n] if n < layers else (soil_ref[n - layers] + 1).astype(f32)
        part = slice(STATE_DEPTH * n, STATE_DEPTH * (n + 1))
        near_ref[part] = jnp.where(upward, plane[high_rows], plane[low_rows])
        far_ref[part] = jnp.where(upward, plane[low_rows], plane[high_rows])


def near_is_above(axis):
    return lax.rem(lax.axis_index(axis), 2) == 0


def below_above(near, far, axis):
    upward = near_is_above(axis)
    return jnp.where(upward, far, near), jnp.where(upward, near, far)


def table_rows(table_ref, rows):
    lane = lane_iota((rows, LANES))
    out = []
    for field in range(table_ref.shape[0]):
        row = jnp.zeros((rows, LANES), f32)
        for kind in range(table_ref.shape[1]):
            row = jnp.where(lane == kind + 1, table_ref[field, kind], row)
        out.append(row)
    return out


def lookup(row, index):
    pieces = [
        jnp.take_along_axis(row, index[:, at : at + LANES], axis=1, mode="promise_in_bounds")
        for at in range(0, index.shape[1], LANES)
    ]
    return jnp.concatenate(pieces, axis=1)


def sigmoid(u):
    return 1.0 / (1.0 + jnp.exp(-u))


def edge_source_kernel(
    table_ref, arrived_ref, head_ref, soil_ref, forcing_ref, slot_ref,
    source_ref, flux_ref, tab_ref, factor_ref,
):
    layers, rows, cols = head_ref.shape
    owners = arrived_ref.shape[0]
    pairs = -(-layers // 2)
    low = lane_iota((8, LANES)) < SLOT
    line = lax.broadcasted_iota(jnp.int32, (16, LANES), 0)
    is_root = (line >= 3) & (line < 3 + layers)

    def unpack(t, _):
        first = arrived_ref[2 * t]
        second = arrived_ref[2 * t + 1]
        both = jnp.concatenate(
            [
                jnp.where(low, first, pltpu.roll(second, SLOT, 1)),
                jnp.where(low, pltpu.roll(first, SLOT, 1), second),
            ],
            axis=0,
        )
        leaf_area, albedo, resist = both[0:1], both[1:2], both[2:3]
        root_sum = jnp.sum(jnp.where(is_root, both, 0.0), axis=0, keepdims=True)
        factor = leaf_area / ((leaf_area + resist) * root_sum) * (1.0 / FIXED)
        factor_ref[t] = jnp.broadcast_to(factor, (8, LANES))
        fixed = (both * FIXED + 0.5).astype(jnp.int32)
        for m in range(pairs):
            word = fixed[3 + m : 4 + m]
            if m + pairs < layers:
                word = word | (fixed[3 + m + pairs : 4 + m + pairs] << 16)
            tab_ref[t, m] = jnp.broadcast_to(word, (8, LANES))
        leaf = ((0.5 + 0.3 * leaf_area) * (0.25 * FIXED) + 0.5).astype(jnp.int32)
        bright = ((1.0 - albedo) * FIXED + 0.5).astype(jnp.int32)
        tab_ref[t, pairs] = jnp.broadcast_to(leaf | (bright << 16), (8, LANES))
        return 0

    lax.fori_loop(0, owners // 2, unpack, 0, unroll=16)
    places = [(0, 0), (cols - LANES, LANES)]
    land_columns(
        table_ref, tab_ref, factor_ref, head_ref, soil_ref, forcing_ref, slot_ref, source_ref, flux_ref, places
    )


def inner_source_kernel(
    table_ref, tab_ref, factor_ref, head_ref, soil_ref, forcing_ref, slot_ref, some_ref,
    source_ref, flux_ref,
):
    cols = head_ref.shape[2]
    places = [(at, at) for at in range(LANES, cols - LANES, LANES)]
    land_columns(
        table_ref, tab_ref, factor_ref, head_ref, soil_ref, forcing_ref, slot_ref, source_ref, flux_ref, places
    )
    put_edges(source_ref, some_ref)


def put_edges(whole_ref, piece_ref):
    cols = whole_ref.shape[2]
    for k in range(whole_ref.shape[0]):
        whole_ref[k, :, 0:LANES] = piece_ref[k, :, 0:LANES]
        whole_ref[k, :, cols - LANES : cols] = piece_ref[k, :, LANES : 2 * LANES]


def land_columns(
    table_ref, tab_ref, factor_ref, head_ref, soil_ref, forcing_ref, slot_ref, source_ref, flux_ref, places
):
    layers, rows, _ = head_ref.shape
    halves_of = tab_ref.shape[0]
    pairs = tab_ref.shape[1] - 1
    tables = table_rows(table_ref, rows)
    shape = (rows, LANES)

    def whole(block):
        return jnp.concatenate([block] * (rows // 8), axis=0)

    for at_y, put in places:
        here = (slice(0, rows), slice(at_y, at_y + LANES))
        there = (slice(0, rows), slice(put, put + LANES))
        slot = slot_ref[here]
        land = slot >= 0
        value = jnp.maximum(slot, 0)
        lane = value & (LANES - 1)
        tile = value >> 7

        def pick(t, held):
            match = tile == t
            found = [lookup(whole(tab_ref[t, m]), lane) for m in range(pairs + 1)]
            found.append(lookup(whole(factor_ref[t]), lane))
            return tuple(jnp.where(match, new, old) for new, old in zip(found, held))

        held = tuple([jnp.full(shape, 1, jnp.int32)] * (pairs + 1) + [jnp.full(shape, 1.0 / FIXED, f32)])
        if halves_of <= 16:
            for t in range(halves_of):
                held = pick(t, held)
        else:
            held = lax.fori_loop(0, halves_of, pick, held, unroll=8)
        *words, terms, factor = held

        def halves(word):
            upper = lax.shift_right_logical(word, jnp.full(shape, 16, jnp.int32))
            return (word & 0xFFFF).astype(f32), upper.astype(f32)

        leaf, bright = halves(terms)
        exchange_coef = leaf * (4.0 / FIXED)
        absorbed = bright * (1.0 / FIXED)
        split = [halves(word) for word in words]
        uptake = []
        for k in range(layers):
            index = soil_ref[(k,) + here] + 1
            steep = lookup(tables[1], index)
            root = factor * split[k % pairs][k // pairs]
            uptake.append(root * sigmoid(steep * head_ref[(k,) + here]))
            if k == 0:
                ks_top = lookup(tables[0], index)
        conductance = functools.reduce(jnp.add, uptake)
        sunlight, air_temp, humidity, rainfall = (forcing_ref[(i,) + here] for i in range(4))
        radiation = absorbed * sunlight + 0.3
        square = air_temp * air_temp
        excess = radiation - 0.3 * square * square - conductance * (0.5 - humidity)
        slope = -1.2 * square * air_temp - exchange_coef - conductance
        rise = -excess / slope
        surface = air_temp + rise
        vapour = 0.5 * jnp.exp(2.0 * rise)
        square = surface * surface
        excess = (
            radiation
            - 0.3 * square * square
            - exchange_coef * rise
            - conductance * (vapour - humidity)
        )
        slope = -1.2 * square * surface - exchange_coef - 2.0 * conductance * vapour
        rise = rise - excess / slope
        rate = 0.5 * jnp.exp(2.0 * rise) - humidity
        infiltration = rainfall * ks_top / (rainfall + ks_top)
        infiltration = jnp.where(land, infiltration, 0.0)
        rate = jnp.where(land, rate, 0.0)
        flux_ref[(0,) + there] = conductance * rate
        flux_ref[(1,) + there] = infiltration
        for k in range(layers):
            value = -rate * uptake[k]
            if k == 0:
                value = value + infiltration
            source_ref[(k,) + there] = value


def strips(planes, shift_from):
    packed = None
    for k, plane in enumerate(planes):
        lane = lane_iota(plane.shape)
        shift = (HALO * k - shift_from) % LANES
        moved = pltpu.roll(plane, shift, 1) if shift else plane
        inside = (lane >= HALO * k) & (lane < HALO * (k + 1))
        packed = jnp.where(inside, moved, 0.0 if packed is None else packed)
    return packed


def strip_parts(cols):
    return ((slice(0, LANES), 0), (slice(cols - LANES, cols), LANES - HALO))


def ends_of(near_ref, far_ref, at, depth, part):
    edge = slice(depth * at, depth * (at + 1))
    below, above = below_above(near_ref[edge, part], far_ref[edge, part], "gx")
    gap = jnp.zeros((2 * (HALO - depth), above.shape[1]), f32)
    return jnp.concatenate([above, gap, below], axis=0)


def strip_kernel(head_ref, soil_ref, some_ref, near_ref, far_ref):
    layers, _, cols = head_ref.shape
    upward = near_is_above("gy")
    blocks = []
    for (part, shift), at in zip(strip_parts(cols), (0, LANES)):
        blocks.append(
            (
                strips([head_ref[k, :, part] for k in range(layers)], shift),
                strips([(soil_ref[k, :, part] + 1).astype(f32) for k in range(layers)], shift),
                strips([some_ref[k, :, at : at + LANES] for k in range(layers)], shift),
            )
        )
    for field, (low, high) in enumerate(zip(*blocks)):
        near_ref[field] = jnp.where(upward, high, low)
        far_ref[field] = jnp.where(upward, low, high)


def source_edge_kernel(src_ref, ynear_ref, yfar_ref, near_ref, far_ref):
    layers, rows, _ = src_ref.shape
    at = SOURCE_DEPTH * layers
    half = HALO // 2
    upward = near_is_above("gx")
    pieces = [x for field in range(3) for x in below_above(ynear_ref[field], yfar_ref[field], "gy")]
    for out_ref, up in ((near_ref, upward), (far_ref, jnp.logical_not(upward))):
        for k in range(layers):
            part = slice(SOURCE_DEPTH * k, SOURCE_DEPTH * (k + 1))
            plane = src_ref[k]
            out_ref[part] = jnp.where(up, plane[rows - SOURCE_DEPTH :], plane[:SOURCE_DEPTH])
        blocks = [jnp.where(up, x[rows - HALO :], x[:HALO]) for x in pieces]
        tail = [block[h : h + half] for block in blocks[4:6] for h in (0, half)]
        for j in range(4):
            out_ref[at : at + HALO, j * LANES : (j + 1) * LANES] = blocks[j]
            out_ref[at + HALO : at + HALO + half, j * LANES : (j + 1) * LANES] = tail[j]


def corner(edge_ref, at, field, which):
    half = HALO // 2
    if field < 2:
        j = 2 * field + which
        return edge_ref[at : at + HALO, j * LANES : (j + 1) * LANES]
    pieces = [
        edge_ref[at + HALO : at + HALO + half, j * LANES : (j + 1) * LANES]
        for j in (2 * which, 2 * which + 1)
    ]
    return jnp.concatenate(pieces, axis=0)


def tall_strips(layers, ynear_ref, yfar_ref, snear_ref, sfar_ref):
    at = SOURCE_DEPTH * layers
    out = []
    for field in range(3):
        pair = []
        below, above = below_above(ynear_ref[field], yfar_ref[field], "gy")
        for which, piece in ((1, above), (0, below)):
            lower, upper = below_above(
                corner(snear_ref, at, field, which), corner(sfar_ref, at, field, which), "gx"
            )
            pair.append(jnp.concatenate([piece, upper, lower], axis=0))
        out.append(pair)
    return out


def side(strip, k):
    right, left = strip
    lane = lane_iota(right.shape)
    shift = (-HALO * k) % LANES
    right = pltpu.roll(right, shift, 1) if shift else right
    left = pltpu.roll(left, (LANES - HALO - HALO * k) % LANES, 1)
    return jnp.where(lane < HALO, right, jnp.where(lane >= LANES - HALO, left, 0.0))


def after(x, axis):
    return pltpu.roll(x, x.shape[axis] - 1, axis)


def before(x, axis):
    return pltpu.roll(x, 1, axis)


def pointwise(head, conduct, steep, capacity):
    sat = 0.5 + 0.5 * jnp.tanh(0.5 * (steep * head))
    slope = steep * sat * (1.0 - sat)
    cond = conduct * (0.1 + 0.9 * sat * sat)
    deriv = 0.9 * conduct * sat * slope
    weighted = storage_weight * capacity
    return cond, deriv, weighted * slope, weighted * sat


def joined(*refs):
    return lambda k: jnp.concatenate([ref[k] for ref in refs], axis=1)


def plain(ref):
    return lambda k: ref[k]


def face_of(here, there, extra=None):
    mean = 0.5 * (here[1] + there[1])
    drop = here[0] - there[0]
    if extra is not None:
        drop = drop + extra
    return mean + here[2] * drop, mean - there[2] * drop, mean * drop


def ring_faces(state, axis, inside=None):
    a, b, face = face_of(state, [after(x, axis) for x in state])
    if inside is not None:
        a, b, face = (jnp.where(inside, x, 0.0) for x in (a, b, face))
    return face - before(face, axis), a + before(b, axis), b, before(a, axis)


def linearize(layers, state_of, store_of, y_faces, masked, coefs, finish):
    diag_ref, xp_ref, xm_ref, yp_ref, ym_ref, az_ref, bz_ref = coefs
    above = None
    for k in range(layers):
        state = state_of(k)
        net_x, diag_x, xp, xm = ring_faces(state, 0)
        net_y, diag_y, yp, ym = y_faces(k, state)
        for ref, value in ((xp_ref, xp), (xm_ref, xm), (yp_ref, yp), (ym_ref, ym)):
            ref[k] = masked(value)
        if k + 1 < layers:
            a, b, face = face_of(state, state_of(k + 1), 1.0)
            az_ref[k] = a
            bz_ref[k] = b
        else:
            a, face = 2.0 * state[2], state[1]
        diag = store_of(k) + diag_x + diag_y + a
        value = net_x + net_y + face
        if above is not None:
            diag = diag + above[1]
            value = value - above[0]
        above = (face, b)
        diag_ref[k] = diag
        finish(k, masked(value))


def apply(v_ref, coefs, k):
    diag_of, xp_of, xm_of, yp_of, ym_of, az_of, bz_of = coefs
    v = v_ref[k]
    value = diag_of(k) * v
    value = value - xp_of(k) * after(v, 0) - xm_of(k) * before(v, 0)
    value = value - yp_of(k) * after(v, 1) - ym_of(k) * before(v, 1)
    if k > 0:
        value = value - az_of(k - 1) * v_ref[k - 1]
    if k + 1 < v_ref.shape[0]:
        value = value - bz_of(k) * v_ref[k + 1]
    return value


def powers(basis, coefs, tile, out_ref):
    layers = basis[0].shape[0]
    rows, cols = tile
    for step in range(KRYLOV - 1):
        for k in range(layers):
            basis[step + 1][k] = apply(basis[step], coefs, k)
    sums = [jnp.zeros((8, LANES), f32) for _ in PAIRS]
    for k in range(layers):
        top = apply(basis[-1], coefs, k)
        for at in range(0, rows, 8):
            for lane_at in range(0, cols, LANES):
                part = (slice(at, at + 8), slice(lane_at, lane_at + LANES))
                vs = [b[(k,) + part] for b in basis] + [top[part]]
                for e, (i, j) in enumerate(PAIRS):
                    sums[e] = sums[e] + vs[i] * vs[j]
    lines = [jnp.sum(x, axis=0, keepdims=True) for x in sums]
    lines.append(jnp.zeros((16 - len(PAIRS), LANES), f32))
    block = jnp.sum(jnp.concatenate(lines, axis=0), axis=1, keepdims=True)
    line = lax.broadcasted_iota(jnp.int32, (16, LANES), 0)
    flat = jnp.sum(jnp.where(lane_iota((16, LANES)) == line, block, 0.0), axis=0, keepdims=True)
    for d in range(out_ref.shape[0]):
        out_ref[d] = flat


def solve(gram_ref):
    terms = [gram_ref[d] for d in range(gram_ref.shape[0])]
    while len(terms) > 1:
        terms = [functools.reduce(jnp.add, terms[i : i + 2]) for i in range(0, len(terms), 2)]
    total = terms[0]
    line = lax.broadcasted_iota(jnp.int32, (16, LANES), 0)
    spread = jnp.broadcast_to(total, (16, LANES))
    column = jnp.sum(jnp.where(lane_iota((16, LANES)) == line, spread, 0.0), axis=1, keepdims=True)
    gram = {}
    for e, (i, j) in enumerate(PAIRS):
        gram[i, j] = gram[j, i] = column[e : e + 1, :]

    def times_gram(c):
        out = []
        for i in range(KRYLOV + 1):
            out.append(functools.reduce(jnp.add, [gram[i, m] * c[m] for m in range(len(c))]))
        return out

    def dot(a, b):
        return functools.reduce(jnp.add, [x * y for x, y in zip(a, b)])

    square = gram[0, 0] + norm_epsilon
    inverse = lax.rsqrt(square)
    beta = square * inverse
    basis = [[inverse]]
    images = [times_gram(basis[0])]
    hessen = {}
    for j in range(KRYLOV):
        w = [jnp.zeros_like(beta)] + basis[j]
        for i in range(j + 1):
            product = dot(w, images[i])
            hessen[i, j] = product
            w = [w[m] - product * basis[i][m] if m < len(basis[i]) else w[m] for m in range(len(w))]
        square = jnp.maximum(dot(w, times_gram(w)), 0.0) + norm_epsilon
        inverse = lax.rsqrt(square)
        hessen[j + 1, j] = square * inverse
        if j + 1 < KRYLOV:
            basis.append([x * inverse for x in w])
            images.append(times_gram(basis[-1]))
    n = KRYLOV
    normal = {}
    for a in range(n):
        for b in range(a + 1):
            normal[a, b] = functools.reduce(
                jnp.add,
                [hessen[i, a] * hessen[i, b] for i in range(n + 1) if (i, a) in hessen and (i, b) in hessen],
            )
    factor = {}
    inverse = []
    for a in range(n):
        for b in range(a + 1):
            value = normal[a, b]
            for m in range(b):
                value = value - factor[a, m] * factor[b, m]
            if a == b:
                inverse.append(lax.rsqrt(value))
            else:
                factor[a, b] = value * inverse[b]
    forward = []
    for a in range(n):
        value = hessen[0, a] * beta
        for m in range(a):
            value = value - factor[a, m] * forward[m]
        forward.append(value * inverse[a])
    backward = [None] * n
    for a in reversed(range(n)):
        value = forward[a]
        for m in range(a + 1, n):
            value = value - factor[m, a] * backward[m]
        backward[a] = value * inverse[a]
    return [
        functools.reduce(jnp.add, [backward[j] * basis[j][i] for j in range(i, n)]) for i in range(n)
    ]


def state_kernel(
    table_ref, head_ref, soil_ref, near_ref, far_ref,
    ext_ref, ks_ref, steep_ref, cap_ref, cond_ref, deriv_ref, store_ref, water_ref,
):
    layers, rows, cols = head_ref.shape
    tables = table_rows(table_ref, rows + 2 * HALO)
    every = slice(0, cols)
    for k in range(layers):
        ends = ends_of(near_ref, far_ref, k, STATE_DEPTH, every)
        head = jnp.concatenate([head_ref[k], ends], axis=0)
        ends = ends_of(near_ref, far_ref, layers + k, STATE_DEPTH, every)
        index = jnp.concatenate([soil_ref[k] + 1, ends.astype(jnp.int32)], axis=0)
        conduct, steep, capacity = (lookup(row, index) for row in tables)
        values = (head, conduct, steep, capacity) + pointwise(head, conduct, steep, capacity)
        outs = (ext_ref, ks_ref, steep_ref, cap_ref, cond_ref, deriv_ref, store_ref, water_ref)
        for ref, value in zip(outs, values):
            ref[k] = value


def flow_kernel(ext_ref, ks_ref, cond_ref, deriv_ref, store_ref, flow_ref, *coefs, rows):
    layers, _, cols = ext_ref.shape
    mask = (ks_ref[0] > 0.0).astype(f32)
    inside = lane_iota(mask.shape) < cols - 1

    def masked(value):
        return jnp.concatenate([value[:rows], value[rows:] * mask[rows:]], axis=0)

    def finish(k, value):
        flow_ref[k] = value

    linearize(
        layers, lambda k: (ext_ref[k], cond_ref[k], deriv_ref[k]), plain(store_ref),
        lambda k, state: ring_faces(state, 1, inside), masked, coefs, finish,
    )


def first_kernel(
    table_ref, src_ref, snear_ref, sfar_ref, ynear_ref, yfar_ref,
    ext_ref, ks_ref, cond_ref, deriv_ref, water_ref, flow_ref, *rest,
):
    mains, rest = rest[:7], rest[7:]
    ext_side, ks_side, steep_side, cap_side, base_ref, p0_ref, p1_ref, p2_ref, gram_ref = rest[:9]
    sides, (cond_side, deriv_side, store_side) = rest[9:16], rest[16:19]
    diag_first, diag_last, yp_last, ym_first = rest[19:23]
    layers, rows, cols = src_ref.shape
    tables = table_rows(table_ref, rows + 2 * HALO)
    heads, soils, sources = tall_strips(layers, ynear_ref, yfar_ref, snear_ref, sfar_ref)
    start, end, middle = slice(0, LANES), slice(cols - LANES, cols), slice(LANES, cols - LANES)
    lane = lane_iota((rows + 2 * HALO, LANES))
    is_first, is_last = lane == 0, lane == LANES - 1

    def source_of(k):
        ends = ends_of(snear_ref, sfar_ref, k, SOURCE_DEPTH, slice(0, cols))
        return jnp.concatenate([src_ref[k], ends], axis=0)

    for k in range(layers):
        head = side(heads, k)
        index = side(soils, k).astype(jnp.int32)
        conduct, steep, capacity = (lookup(row, index) for row in tables)
        cond, deriv, store, water = pointwise(head, conduct, steep, capacity)
        outs = (ext_side, ks_side, steep_side, cap_side, cond_side, deriv_side, store_side)
        for ref, value in zip(outs, (head, conduct, steep, capacity, cond, deriv, store)):
            ref[k] = value
        base_ref[k, :, 0:cols] = water_ref[k] + source_of(k)
        base_ref[k, :, cols:] = water + side(sources, k)
        p0_ref[k, :, middle] = flow_ref[k, :, middle] + (water_ref[k, :, middle] - base_ref[k, :, middle])
        p0_ref[k, :, cols:] = water - base_ref[k, :, cols:]

    masks = [(ref > 0.0).astype(f32) for ref in (ks_ref[0, :, start], ks_ref[0, :, end], ks_side[0])]

    def y_faces(k, state):
        first = (ext_ref[k, :, start], cond_ref[k, :, start], deriv_ref[k, :, start])
        last = (ext_ref[k, :, end], cond_ref[k, :, end], deriv_ref[k, :, end])
        moved = [after(x, 1) for x in state]
        ahead = [jnp.where(is_last, after(x, 1), y) for x, y in zip(first, moved)]
        a, b, face = face_of(state, ahead)
        a_in, b_in, face_in = (jnp.where(is_last, x, 0.0) for x in face_of(last, moved))
        a_out, b_out, face_out = (before(x, 1) for x in (a, b, face))
        a_pre, b_pre, face_pre = (before(x, 1) for x in (a_in, b_in, face_in))
        gain = water_ref[k, :, end] - base_ref[k, :, end]
        p0_ref[k, :, end] = flow_ref[k, :, end] + face_in * masks[1] + gain
        diag_last[k] = mains[0][k, :, end] + a_in
        yp_last[k] = mains[3][k, :, end] + b_in * masks[1]
        gain = water_ref[k, :, start] - base_ref[k, :, start]
        p0_ref[k, :, start] = flow_ref[k, :, start] - jnp.where(is_first, face_out, 0.0) * masks[0] + gain
        diag_first[k] = mains[0][k, :, start] + jnp.where(is_first, b_out, 0.0)
        ym_first[k] = mains[4][k, :, start] + jnp.where(is_first, a_out, 0.0) * masks[0]
        a_pre, b_pre, face_pre = (
            jnp.where(is_first, x, y)
            for x, y in ((a_pre, a_out), (b_pre, b_out), (face_pre, face_out))
        )
        return face - face_pre, a + b_pre, b, a_pre

    def finish(k, value):
        p0_ref[k, :, cols:] = p0_ref[k, :, cols:] + value

    linearize(
        layers, lambda k: (ext_side[k], cond_side[k], deriv_side[k]), plain(store_side),
        y_faces, lambda value: value * masks[2], sides, finish,
    )

    def pieces(n, first_of, last_of):
        main, beside = mains[n], sides[n]
        return lambda k: jnp.concatenate(
            [first_of(main, k), main[k, :, middle], last_of(main, k), beside[k]], axis=1
        )

    def of_start(ref, k):
        return ref[k, :, start]

    def of_end(ref, k):
        return ref[k, :, end]

    coefs = [joined(main, beside) for main, beside in zip(mains, sides)]
    coefs[0] = pieces(0, lambda _, k: diag_first[k], lambda _, k: diag_last[k])
    coefs[3] = pieces(3, of_start, lambda _, k: yp_last[k])
    coefs[4] = pieces(4, lambda _, k: ym_first[k], of_end)
    powers((p0_ref, p1_ref, p2_ref), coefs, (rows, cols), gram_ref)


def second_kernel(
    arrived_ref, old_ref, ks_ref, steep_ref, cap_ref, old_side, ks_side, steep_side, cap_side,
    base_ref, q0_ref, q1_ref, q2_ref,
    part_ref, p0_ref, p1_ref, p2_ref, gram_ref, ext_ref, cond_ref, deriv_ref, store_ref, gain_ref, *coefs,
):
    layers = old_ref.shape[0]
    rows, cols = part_ref.shape[1:]
    x = solve(arrived_ref)
    near = lax.broadcasted_iota(jnp.int32, (HALO, cols + LANES), 0) < HALO // 2

    def folded(of):
        def get(k):
            value = of(k)
            ends = jnp.where(near, value[rows : rows + HALO], value[rows + HALO :])
            return jnp.concatenate([value[:rows], ends], axis=0)

        return get

    old_of, ks_of = folded(joined(old_ref, old_side)), folded(joined(ks_ref, ks_side))
    steep_of, cap_of = folded(joined(steep_ref, steep_side)), folded(joined(cap_ref, cap_side))
    base_of, *qs = (folded(plain(ref)) for ref in (base_ref, q0_ref, q1_ref, q2_ref))
    for k in range(layers):
        head = old_of(k)
        for value, q_of in zip(x, qs):
            head = head - value * q_of(k)
        cond, deriv, store, water = pointwise(head, ks_of(k), steep_of(k), cap_of(k))
        ext_ref[k] = head
        part_ref[k] = head[:rows, :cols]
        cond_ref[k] = cond
        deriv_ref[k] = deriv
        store_ref[k] = store
        gain_ref[k] = water - base_of(k)
    mask = (ks_of(0) > 0.0).astype(f32)

    def masked(value):
        own = value[:rows, cols:] * mask[:rows, cols:]
        top = jnp.concatenate([value[:rows, :cols], own], axis=1)
        return jnp.concatenate([top, value[rows:] * mask[rows:]], axis=0)

    def finish(k, value):
        p0_ref[k] = value + gain_ref[k]

    linearize(
        layers, lambda k: (ext_ref[k], cond_ref[k], deriv_ref[k]), plain(store_ref),
        lambda k, state: ring_faces(state, 1), masked, coefs, finish,
    )
    powers((p0_ref, p1_ref, p2_ref), [plain(ref) for ref in coefs], (rows, cols), gram_ref)


def last_kernel(
    arrived_ref, part_ref, q0_ref, q1_ref, q2_ref, inner_ref, piece_ref, head_ref, flux_ref
):
    layers, rows, cols = part_ref.shape
    middle = slice(LANES, cols - LANES)
    for n in range(flux_ref.shape[0]):
        flux_ref[n, :, middle] = inner_ref[n, :, middle]
    put_edges(flux_ref, piece_ref)
    x = solve(arrived_ref)
    for k in range(layers):
        own = (k, slice(0, rows), slice(0, cols))
        head_ref[k] = part_ref[k] - x[0] * q0_ref[own] - x[1] * q1_ref[own] - x[2] * q2_ref[own]


def shards(head_old, soil_type, soil_table, forcing, canopy, column_slot):
    layers, rows, cols = head_old.shape
    both = ("gx", "gy")
    devices = lax.axis_size("gx") * lax.axis_size("gy")
    tall, wide = rows + 2 * HALO, cols + LANES
    own, ext = ((layers, rows, cols), f32), ((layers, tall, wide), f32)
    gram_block = ((devices, 1, LANES), f32)

    def exchange(to_near, to_far, axis):
        size = lax.axis_size(axis)
        near = [(i, i + 1) for i in range(0, size - 1, 2)]
        far = [(i, i + 1) for i in range(1, size - 1, 2)]
        return tuple(
            lax.ppermute(x, axis, pairs + [(j, i) for i, j in pairs])
            for x, pairs in ((to_near, near), (to_far, far))
        )

    def spread(x, axes):
        return lax.all_to_all(x, axes, split_axis=0, concat_axis=0, tiled=True)

    def edge(count):
        return (-(-count // 8) * 8, cols), f32

    send, to_near, to_far = call(
        pack_kernel,
        [((devices, 8, LANES), f32)] + [edge(2 * STATE_DEPTH * layers)] * 2,
        3,
        scratch=[
            pltpu.VMEM(canopy.shape, f32),
            pltpu.VMEM(head_old.shape, f32),
            pltpu.VMEM(soil_type.shape, jnp.int32),
            pltpu.SemaphoreType.DMA((3,)),
        ],
        in_specs=[pl.BlockSpec(memory_space=pl.ANY)] * 3,
        grant=63400000,
    )(canopy, head_old, soil_type)
    arrived = spread(send, both)
    near, far = exchange(to_near, to_far, "gx")
    columns = (head_old, soil_type, forcing, column_slot)
    table = ((devices // 2, -(-layers // 2) + 1, 8, LANES), jnp.int32)
    some, piece, tab, factor = call(
        edge_source_kernel,
        [((layers, rows, 2 * LANES), f32), ((2, rows, 2 * LANES), f32), table, ((devices // 2, 8, LANES), f32)],
        6,
        in_specs=[smem] + [vmem] * 5,
    )(soil_table, arrived, *columns)
    to_near, to_far = call(strip_kernel, [((3, rows, LANES), f32)] * 2, 3)(head_old, soil_type, some)
    ynear, yfar = exchange(to_near, to_far, "gy")
    both_fluxes = ((2, rows, cols), f32)
    source, inner = call(inner_source_kernel, [own, both_fluxes], 8, in_specs=[smem] + [vmem] * 7)(
        soil_table, tab, factor, *columns, some
    )
    to_near, to_far = call(source_edge_kernel, [edge(SOURCE_DEPTH * layers + HALO + HALO // 2)] * 2, 3)(
        source, ynear, yfar
    )
    snear, sfar = exchange(to_near, to_far, "gx")
    main, side_block = ((layers, tall, cols), f32), ((layers, tall, LANES), f32)
    old, ks, steep, cap, cond, deriv, store, water = call(
        state_kernel, [main] * 8, 5, in_specs=[smem] + [vmem] * 4
    )(soil_table, head_old, soil_type, near, far)
    flow, *coefs = call(functools.partial(flow_kernel, rows=rows), [main] * 8, 5)(
        old, ks, cond, deriv, store
    )
    old_s, ks_s, steep_s, cap_s, base, p0, p1, p2, gram = call(
        first_kernel,
        [side_block] * 4 + [ext] * 4 + [gram_block],
        19,
        scratch=[pltpu.VMEM(side_block[0], f32)] * 14,
        in_specs=[smem] + [vmem] * 18,
    )(soil_table, source, snear, sfar, ynear, yfar, old, ks, cond, deriv, water, flow, *coefs)
    sums = spread(gram, both)
    part, q0, q1, q2, gram = call(
        second_kernel,
        [own] + [((layers, rows + HALO, wide), f32)] * 3 + [gram_block],
        13,
        scratch=[pltpu.VMEM((layers, rows + HALO, wide), f32)] * 12,
    )(sums, old, ks, steep, cap, old_s, ks_s, steep_s, cap_s, base, p0, p1, p2)
    sums = spread(gram, both)
    head, flux = call(last_kernel, [own, both_fluxes], 7)(sums, part, q0, q1, q2, inner, piece)
    return head, flux


def solution(mesh):
    return jax.shard_map(
        shards,
        mesh=mesh,
        in_specs=(
            P(None, "gx", "gy"),
            P(None, "gx", "gy"),
            P(),
            P(None, "gx", "gy"),
            P(None, ("gx", "gy")),
            P("gx", "gy"),
        ),
        out_specs=(P(None, "gx", "gy"), P(None, "gx", "gy")),
        check_vma=False,
    )
```

```python
import functools

import jax
import jax.numpy as jnp
from jax import lax
from jax.experimental import pallas as pl
from jax.experimental.pallas import tpu as pltpu
from jax.sharding import PartitionSpec as P

NEWTON = 2
KRYLOV = 3
HALO = 8
STATE_DEPTH = 7
SOURCE_DEPTH = 6
FIXED = 65535.0
LANES = 128
SLOT = 64

storage_weight = 4.0
norm_epsilon = 1e-06

VMEM_LIMIT = 20 * 1024 * 1024
PAIRS = [(i, j) for i in range(KRYLOV + 1) for j in range(i, KRYLOV + 1)]

f32 = jnp.float32
vmem = pl.BlockSpec(memory_space=pltpu.VMEM)
smem = pl.BlockSpec(memory_space=pltpu.SMEM)


def call(body, outs, n_in, scratch=(), in_specs=None, flops=1000000, grant=VMEM_LIMIT):
    return pl.pallas_call(
        body,
        out_shape=[jax.ShapeDtypeStruct(s, d) for s, d in outs],
        in_specs=in_specs or [vmem] * n_in,
        out_specs=[vmem] * len(outs),
        scratch_shapes=list(scratch),
        compiler_params=pltpu.CompilerParams(vmem_limit_bytes=grant),
        cost_estimate=pl.CostEstimate(flops=flops, bytes_accessed=1000000, transcendentals=0),
    )


def lane_iota(shape):
    return lax.broadcasted_iota(jnp.int32, shape, len(shape) - 1)


def pack_kernel(
    canopy_hbm, head_hbm, soil_hbm, send_ref, near_ref, far_ref, canopy_ref, head_ref, soil_ref, sems
):
    copies = [
        pltpu.make_async_copy(canopy_hbm, canopy_ref, sems.at[0]),
        pltpu.make_async_copy(head_hbm, head_ref, sems.at[1]),
        pltpu.make_async_copy(soil_hbm, soil_ref, sems.at[2]),
    ]
    for copy in copies:
        copy.start()
    copies[0].wait()
    rows = canopy_ref.shape[0]
    low = lane_iota((8, LANES)) < SLOT
    for t in range(canopy_ref.shape[1] // LANES):
        here = slice(t * LANES, (t + 1) * LANES)
        first = canopy_ref[0:8, here]
        rest = jnp.concatenate([canopy_ref[8:rows, here], jnp.zeros((16 - rows, LANES), f32)], axis=0)
        send_ref[2 * t] = jnp.where(low, first, pltpu.roll(rest, SLOT, 1))
        send_ref[2 * t + 1] = jnp.where(low, pltpu.roll(first, SLOT, 1), rest)
    layers, rows, _ = head_ref.shape
    copies[1].wait()
    copies[2].wait()
    low_rows, high_rows = slice(0, STATE_DEPTH), slice(rows - STATE_DEPTH, rows)
    upward = near_is_above("gx")
    for n in range(2 * layers):
        plane = head_ref[n] if n < layers else (soil_ref[n - layers] + 1).astype(f32)
        part = slice(STATE_DEPTH * n, STATE_DEPTH * (n + 1))
        near_ref[part] = jnp.where(upward, plane[high_rows], plane[low_rows])
        far_ref[part] = jnp.where(upward, plane[low_rows], plane[high_rows])


def pass_kernel(*_):
    pass


def near_is_above(axis):
    return lax.rem(lax.axis_index(axis), 2) == 0


def below_above(near, far, axis):
    upward = near_is_above(axis)
    return jnp.where(upward, far, near), jnp.where(upward, near, far)


def table_rows(table_ref, rows):
    lane = lane_iota((rows, LANES))
    out = []
    for field in range(table_ref.shape[0]):
        row = jnp.zeros((rows, LANES), f32)
        for kind in range(table_ref.shape[1]):
            row = jnp.where(lane == kind + 1, table_ref[field, kind], row)
        out.append(row)
    return out


def lookup(row, index):
    pieces = [
        jnp.take_along_axis(row, index[:, at : at + LANES], axis=1, mode="promise_in_bounds")
        for at in range(0, index.shape[1], LANES)
    ]
    return jnp.concatenate(pieces, axis=1)


def sigmoid(u):
    return 1.0 / (1.0 + jnp.exp(-u))


def edge_source_kernel(
    table_ref, arrived_ref, head_ref, soil_ref, forcing_ref, slot_ref,
    source_ref, flux_ref, tab_ref, factor_ref,
):
    layers, rows, cols = head_ref.shape
    owners = arrived_ref.shape[0]
    pairs = -(-layers // 2)
    low = lane_iota((8, LANES)) < SLOT
    line = lax.broadcasted_iota(jnp.int32, (16, LANES), 0)
    is_root = (line >= 3) & (line < 3 + layers)

    def unpack(t, _):
        first = arrived_ref[2 * t]
        second = arrived_ref[2 * t + 1]
        both = jnp.concatenate(
            [
                jnp.where(low, first, pltpu.roll(second, SLOT, 1)),
                jnp.where(low, pltpu.roll(first, SLOT, 1), second),
            ],
            axis=0,
        )
        leaf_area, albedo, resist = both[0:1], both[1:2], both[2:3]
        root_sum = jnp.sum(jnp.where(is_root, both, 0.0), axis=0, keepdims=True)
        factor = leaf_area / ((leaf_area + resist) * root_sum) * (1.0 / FIXED)
        factor_ref[t] = jnp.broadcast_to(factor, (8, LANES))
        fixed = (both * FIXED + 0.5).astype(jnp.int32)
        for m in range(pairs):
            word = fixed[3 + m : 4 + m]
            if m + pairs < layers:
                word = word | (fixed[3 + m + pairs : 4 + m + pairs] << 16)
            tab_ref[t, m] = jnp.broadcast_to(word, (8, LANES))
        leaf = ((0.5 + 0.3 * leaf_area) * (0.25 * FIXED) + 0.5).astype(jnp.int32)
        bright = ((1.0 - albedo) * FIXED + 0.5).astype(jnp.int32)
        tab_ref[t, pairs] = jnp.broadcast_to(leaf | (bright << 16), (8, LANES))
        return 0

    lax.fori_loop(0, owners // 2, unpack, 0, unroll=16)
    places = [(0, 0), (cols - LANES, LANES)]
    land_columns(
        table_ref, tab_ref, factor_ref, head_ref, soil_ref, forcing_ref, slot_ref, source_ref, flux_ref, places
    )


def inner_source_kernel(
    table_ref, tab_ref, factor_ref, head_ref, soil_ref, forcing_ref, slot_ref, some_ref,
    source_ref, flux_ref,
):
    cols = head_ref.shape[2]
    places = [(at, at) for at in range(LANES, cols - LANES, LANES)]
    land_columns(
        table_ref, tab_ref, factor_ref, head_ref, soil_ref, forcing_ref, slot_ref, source_ref, flux_ref, places
    )
    put_edges(source_ref, some_ref)


def put_edges(whole_ref, piece_ref):
    cols = whole_ref.shape[2]
    for k in range(whole_ref.shape[0]):
        whole_ref[k, :, 0:LANES] = piece_ref[k, :, 0:LANES]
        whole_ref[k, :, cols - LANES : cols] = piece_ref[k, :, LANES : 2 * LANES]


def land_columns(
    table_ref, tab_ref, factor_ref, head_ref, soil_ref, forcing_ref, slot_ref, source_ref, flux_ref, places
):
    layers, rows, _ = head_ref.shape
    halves_of = tab_ref.shape[0]
    pairs = tab_ref.shape[1] - 1
    tables = table_rows(table_ref, rows)
    shape = (rows, LANES)

    def whole(block):
        return jnp.concatenate([block] * (rows // 8), axis=0)

    for at_y, put in places:
        here = (slice(0, rows), slice(at_y, at_y + LANES))
        there = (slice(0, rows), slice(put, put + LANES))
        slot = slot_ref[here]
        land = slot >= 0
        value = jnp.maximum(slot, 0)
        lane = value & (LANES - 1)
        tile = value >> 7

        def pick(t, held):
            match = tile == t
            found = [lookup(whole(tab_ref[t, m]), lane) for m in range(pairs + 1)]
            found.append(lookup(whole(factor_ref[t]), lane))
            return tuple(jnp.where(match, new, old) for new, old in zip(found, held))

        held = tuple([jnp.full(shape, 1, jnp.int32)] * (pairs + 1) + [jnp.full(shape, 1.0 / FIXED, f32)])
        if halves_of <= 16:
            for t in range(halves_of):
                held = pick(t, held)
        else:
            held = lax.fori_loop(0, halves_of, pick, held, unroll=8)
        *words, terms, factor = held

        def halves(word):
            upper = lax.shift_right_logical(word, jnp.full(shape, 16, jnp.int32))
            return (word & 0xFFFF).astype(f32), upper.astype(f32)

        leaf, bright = halves(terms)
        exchange_coef = leaf * (4.0 / FIXED)
        absorbed = bright * (1.0 / FIXED)
        split = [halves(word) for word in words]
        uptake = []
        for k in range(layers):
            index = soil_ref[(k,) + here] + 1
            steep = lookup(tables[1], index)
            root = factor * split[k % pairs][k // pairs]
            uptake.append(root * sigmoid(steep * head_ref[(k,) + here]))
            if k == 0:
                ks_top = lookup(tables[0], index)
        conductance = functools.reduce(jnp.add, uptake)
        sunlight, air_temp, humidity, rainfall = (forcing_ref[(i,) + here] for i in range(4))
        radiation = absorbed * sunlight + 0.3
        square = air_temp * air_temp
        excess = radiation - 0.3 * square * square - conductance * (0.5 - humidity)
        slope = -1.2 * square * air_temp - exchange_coef - conductance
        rise = -excess / slope
        surface = air_temp + rise
        vapour = 0.5 * jnp.exp(2.0 * rise)
        square = surface * surface
        excess = (
            radiation
            - 0.3 * square * square
            - exchange_coef * rise
            - conductance * (vapour - humidity)
        )
        slope = -1.2 * square * surface - exchange_coef - 2.0 * conductance * vapour
        rise = rise - excess / slope
        rate = 0.5 * jnp.exp(2.0 * rise) - humidity
        infiltration = rainfall * ks_top / (rainfall + ks_top)
        infiltration = jnp.where(land, infiltration, 0.0)
        rate = jnp.where(land, rate, 0.0)
        flux_ref[(0,) + there] = conductance * rate
        flux_ref[(1,) + there] = infiltration
        for k in range(layers):
            value = -rate * uptake[k]
            if k == 0:
                value = value + infiltration
            source_ref[(k,) + there] = value


def strips(planes, shift_from):
    packed = None
    for k, plane in enumerate(planes):
        lane = lane_iota(plane.shape)
        shift = (HALO * k - shift_from) % LANES
        moved = pltpu.roll(plane, shift, 1) if shift else plane
        inside = (lane >= HALO * k) & (lane < HALO * (k + 1))
        packed = jnp.where(inside, moved, 0.0 if packed is None else packed)
    return packed


def strip_parts(cols):
    return ((slice(0, LANES), 0), (slice(cols - LANES, cols), LANES - HALO))


def ends_of(near_ref, far_ref, at, depth, part):
    edge = slice(depth * at, depth * (at + 1))
    below, above = below_above(near_ref[edge, part], far_ref[edge, part], "gx")
    gap = jnp.zeros((2 * (HALO - depth), above.shape[1]), f32)
    return jnp.concatenate([above, gap, below], axis=0)


def strip_kernel(head_ref, soil_ref, some_ref, near_ref, far_ref):
    layers, _, cols = head_ref.shape
    upward = near_is_above("gy")
    blocks = []
    for (part, shift), at in zip(strip_parts(cols), (0, LANES)):
        blocks.append(
            (
                strips([head_ref[k, :, part] for k in range(layers)], shift),
                strips([(soil_ref[k, :, part] + 1).astype(f32) for k in range(layers)], shift),
                strips([some_ref[k, :, at : at + LANES] for k in range(layers)], shift),
            )
        )
    for field, (low, high) in enumerate(zip(*blocks)):
        near_ref[field] = jnp.where(upward, high, low)
        far_ref[field] = jnp.where(upward, low, high)


def source_edge_kernel(src_ref, ynear_ref, yfar_ref, near_ref, far_ref):
    layers, rows, _ = src_ref.shape
    at = SOURCE_DEPTH * layers
    half = HALO // 2
    upward = near_is_above("gx")
    pieces = [x for field in range(3) for x in below_above(ynear_ref[field], yfar_ref[field], "gy")]
    for out_ref, up in ((near_ref, upward), (far_ref, jnp.logical_not(upward))):
        for k in range(layers):
            part = slice(SOURCE_DEPTH * k, SOURCE_DEPTH * (k + 1))
            plane = src_ref[k]
            out_ref[part] = jnp.where(up, plane[rows - SOURCE_DEPTH :], plane[:SOURCE_DEPTH])
        blocks = [jnp.where(up, x[rows - HALO :], x[:HALO]) for x in pieces]
        tail = [block[h : h + half] for block in blocks[4:6] for h in (0, half)]
        for j in range(4):
            out_ref[at : at + HALO, j * LANES : (j + 1) * LANES] = blocks[j]
            out_ref[at + HALO : at + HALO + half, j * LANES : (j + 1) * LANES] = tail[j]


def corner(edge_ref, at, field, which):
    half = HALO // 2
    if field < 2:
        j = 2 * field + which
        return edge_ref[at : at + HALO, j * LANES : (j + 1) * LANES]
    pieces = [
        edge_ref[at + HALO : at + HALO + half, j * LANES : (j + 1) * LANES]
        for j in (2 * which, 2 * which + 1)
    ]
    return jnp.concatenate(pieces, axis=0)


def tall_strips(layers, ynear_ref, yfar_ref, snear_ref, sfar_ref):
    at = SOURCE_DEPTH * layers
    out = []
    for field in range(3):
        pair = []
        below, above = below_above(ynear_ref[field], yfar_ref[field], "gy")
        for which, piece in ((1, above), (0, below)):
            lower, upper = below_above(
                corner(snear_ref, at, field, which), corner(sfar_ref, at, field, which), "gx"
            )
            pair.append(jnp.concatenate([piece, upper, lower], axis=0))
        out.append(pair)
    return out


def side(strip, k):
    right, left = strip
    lane = lane_iota(right.shape)
    shift = (-HALO * k) % LANES
    right = pltpu.roll(right, shift, 1) if shift else right
    left = pltpu.roll(left, (LANES - HALO - HALO * k) % LANES, 1)
    return jnp.where(lane < HALO, right, jnp.where(lane >= LANES - HALO, left, 0.0))


def after(x, axis):
    return pltpu.roll(x, x.shape[axis] - 1, axis)


def before(x, axis):
    return pltpu.roll(x, 1, axis)


def pointwise(head, conduct, steep, capacity):
    sat = 0.5 + 0.5 * jnp.tanh(0.5 * (steep * head))
    slope = steep * sat * (1.0 - sat)
    cond = conduct * (0.1 + 0.9 * sat * sat)
    deriv = 0.9 * conduct * sat * slope
    weighted = storage_weight * capacity
    return cond, deriv, weighted * slope, weighted * sat


def joined(*refs):
    return lambda k: jnp.concatenate([ref[k] for ref in refs], axis=1)


def plain(ref):
    return lambda k: ref[k]


def face_of(here, there, extra=None):
    mean = 0.5 * (here[1] + there[1])
    drop = here[0] - there[0]
    if extra is not None:
        drop = drop + extra
    return mean + here[2] * drop, mean - there[2] * drop, mean * drop


def ring_faces(state, axis, inside=None):
    a, b, face = face_of(state, [after(x, axis) for x in state])
    if inside is not None:
        a, b, face = (jnp.where(inside, x, 0.0) for x in (a, b, face))
    return face - before(face, axis), a + before(b, axis), b, before(a, axis)


def linearize(layers, state_of, store_of, y_faces, masked, coefs, finish):
    diag_ref, xp_ref, xm_ref, yp_ref, ym_ref, az_ref, bz_ref = coefs
    above = None
    for k in range(layers):
        state = state_of(k)
        net_x, diag_x, xp, xm = ring_faces(state, 0)
        net_y, diag_y, yp, ym = y_faces(k, state)
        for ref, value in ((xp_ref, xp), (xm_ref, xm), (yp_ref, yp), (ym_ref, ym)):
            ref[k] = masked(value)
        if k + 1 < layers:
            a, b, face = face_of(state, state_of(k + 1), 1.0)
            az_ref[k] = a
            bz_ref[k] = b
        else:
            a, face = 2.0 * state[2], state[1]
        diag = store_of(k) + diag_x + diag_y + a
        value = net_x + net_y + face
        if above is not None:
            diag = diag + above[1]
            value = value - above[0]
        above = (face, b)
        diag_ref[k] = diag
        finish(k, masked(value))


def apply(v_ref, coefs, k):
    diag_of, xp_of, xm_of, yp_of, ym_of, az_of, bz_of = coefs
    v = v_ref[k]
    value = diag_of(k) * v
    value = value - xp_of(k) * after(v, 0) - xm_of(k) * before(v, 0)
    value = value - yp_of(k) * after(v, 1) - ym_of(k) * before(v, 1)
    if k > 0:
        value = value - az_of(k - 1) * v_ref[k - 1]
    if k + 1 < v_ref.shape[0]:
        value = value - bz_of(k) * v_ref[k + 1]
    return value


def powers(basis, coefs, tile, out_ref):
    layers = basis[0].shape[0]
    rows, cols = tile
    for step in range(KRYLOV - 1):
        for k in range(layers):
            basis[step + 1][k] = apply(basis[step], coefs, k)
    sums = [jnp.zeros((8, LANES), f32) for _ in PAIRS]
    for k in range(layers):
        top = apply(basis[-1], coefs, k)
        for at in range(0, rows, 8):
            for lane_at in range(0, cols, LANES):
                part = (slice(at, at + 8), slice(lane_at, lane_at + LANES))
                vs = [b[(k,) + part] for b in basis] + [top[part]]
                for e, (i, j) in enumerate(PAIRS):
                    sums[e] = sums[e] + vs[i] * vs[j]
    lines = [jnp.sum(x, axis=0, keepdims=True) for x in sums]
    lines.append(jnp.zeros((16 - len(PAIRS), LANES), f32))
    block = jnp.sum(jnp.concatenate(lines, axis=0), axis=1, keepdims=True)
    line = lax.broadcasted_iota(jnp.int32, (16, LANES), 0)
    flat = jnp.sum(jnp.where(lane_iota((16, LANES)) == line, block, 0.0), axis=0, keepdims=True)
    for d in range(out_ref.shape[0]):
        out_ref[d] = flat


def solve(gram_ref):
    terms = [gram_ref[d] for d in range(gram_ref.shape[0])]
    while len(terms) > 1:
        terms = [functools.reduce(jnp.add, terms[i : i + 2]) for i in range(0, len(terms), 2)]
    total = terms[0]
    line = lax.broadcasted_iota(jnp.int32, (16, LANES), 0)
    spread = jnp.broadcast_to(total, (16, LANES))
    column = jnp.sum(jnp.where(lane_iota((16, LANES)) == line, spread, 0.0), axis=1, keepdims=True)
    gram = {}
    for e, (i, j) in enumerate(PAIRS):
        gram[i, j] = gram[j, i] = column[e : e + 1, :]

    def times_gram(c):
        out = []
        for i in range(KRYLOV + 1):
            out.append(functools.reduce(jnp.add, [gram[i, m] * c[m] for m in range(len(c))]))
        return out

    def dot(a, b):
        return functools.reduce(jnp.add, [x * y for x, y in zip(a, b)])

    square = gram[0, 0] + norm_epsilon
    inverse = lax.rsqrt(square)
    beta = square * inverse
    basis = [[inverse]]
    images = [times_gram(basis[0])]
    hessen = {}
    for j in range(KRYLOV):
        w = [jnp.zeros_like(beta)] + basis[j]
        for i in range(j + 1):
            product = dot(w, images[i])
            hessen[i, j] = product
            w = [w[m] - product * basis[i][m] if m < len(basis[i]) else w[m] for m in range(len(w))]
        square = jnp.maximum(dot(w, times_gram(w)), 0.0) + norm_epsilon
        inverse = lax.rsqrt(square)
        hessen[j + 1, j] = square * inverse
        if j + 1 < KRYLOV:
            basis.append([x * inverse for x in w])
            images.append(times_gram(basis[-1]))
    n = KRYLOV
    normal = {}
    for a in range(n):
        for b in range(a + 1):
            normal[a, b] = functools.reduce(
                jnp.add,
                [hessen[i, a] * hessen[i, b] for i in range(n + 1) if (i, a) in hessen and (i, b) in hessen],
            )
    factor = {}
    inverse = []
    for a in range(n):
        for b in range(a + 1):
            value = normal[a, b]
            for m in range(b):
                value = value - factor[a, m] * factor[b, m]
            if a == b:
                inverse.append(lax.rsqrt(value))
            else:
                factor[a, b] = value * inverse[b]
    forward = []
    for a in range(n):
        value = hessen[0, a] * beta
        for m in range(a):
            value = value - factor[a, m] * forward[m]
        forward.append(value * inverse[a])
    backward = [None] * n
    for a in reversed(range(n)):
        value = forward[a]
        for m in range(a + 1, n):
            value = value - factor[m, a] * backward[m]
        backward[a] = value * inverse[a]
    return [
        functools.reduce(jnp.add, [backward[j] * basis[j][i] for j in range(i, n)]) for i in range(n)
    ]


def state_kernel(
    table_ref, head_ref, soil_ref, near_ref, far_ref,
    ext_ref, ks_ref, steep_ref, cap_ref, cond_ref, deriv_ref, store_ref, water_ref,
):
    layers, rows, cols = head_ref.shape
    tables = table_rows(table_ref, rows + 2 * HALO)
    every = slice(0, cols)
    for k in range(layers):
        ends = ends_of(near_ref, far_ref, k, STATE_DEPTH, every)
        head = jnp.concatenate([head_ref[k], ends], axis=0)
        ends = ends_of(near_ref, far_ref, layers + k, STATE_DEPTH, every)
        index = jnp.concatenate([soil_ref[k] + 1, ends.astype(jnp.int32)], axis=0)
        conduct, steep, capacity = (lookup(row, index) for row in tables)
        values = (head, conduct, steep, capacity) + pointwise(head, conduct, steep, capacity)
        outs = (ext_ref, ks_ref, steep_ref, cap_ref, cond_ref, deriv_ref, store_ref, water_ref)
        for ref, value in zip(outs, values):
            ref[k] = value


def flow_kernel(ext_ref, ks_ref, cond_ref, deriv_ref, store_ref, flow_ref, *coefs, rows):
    layers, _, cols = ext_ref.shape
    mask = (ks_ref[0] > 0.0).astype(f32)
    inside = lane_iota(mask.shape) < cols - 1

    def masked(value):
        return jnp.concatenate([value[:rows], value[rows:] * mask[rows:]], axis=0)

    def finish(k, value):
        flow_ref[k] = value

    linearize(
        layers, lambda k: (ext_ref[k], cond_ref[k], deriv_ref[k]), plain(store_ref),
        lambda k, state: ring_faces(state, 1, inside), masked, coefs, finish,
    )


def first_kernel(
    table_ref, src_ref, snear_ref, sfar_ref, ynear_ref, yfar_ref,
    ext_ref, ks_ref, cond_ref, deriv_ref, water_ref, flow_ref, *rest,
):
    mains, rest = rest[:7], rest[7:]
    ext_side, ks_side, steep_side, cap_side, base_ref, p0_ref, p1_ref, p2_ref, gram_ref = rest[:9]
    sides, (cond_side, deriv_side, store_side) = rest[9:16], rest[16:19]
    diag_first, diag_last, yp_last, ym_first = rest[19:23]
    layers, rows, cols = src_ref.shape
    tables = table_rows(table_ref, rows + 2 * HALO)
    heads, soils, sources = tall_strips(layers, ynear_ref, yfar_ref, snear_ref, sfar_ref)
    start, end, middle = slice(0, LANES), slice(cols - LANES, cols), slice(LANES, cols - LANES)
    lane = lane_iota((rows + 2 * HALO, LANES))
    is_first, is_last = lane == 0, lane == LANES - 1

    def source_of(k):
        ends = ends_of(snear_ref, sfar_ref, k, SOURCE_DEPTH, slice(0, cols))
        return jnp.concatenate([src_ref[k], ends], axis=0)

    for k in range(layers):
        head = side(heads, k)
        index = side(soils, k).astype(jnp.int32)
        conduct, steep, capacity = (lookup(row, index) for row in tables)
        cond, deriv, store, water = pointwise(head, conduct, steep, capacity)
        outs = (ext_side, ks_side, steep_side, cap_side, cond_side, deriv_side, store_side)
        for ref, value in zip(outs, (head, conduct, steep, capacity, cond, deriv, store)):
            ref[k] = value
        base_ref[k, :, 0:cols] = water_ref[k] + source_of(k)
        base_ref[k, :, cols:] = water + side(sources, k)
        p0_ref[k, :, middle] = flow_ref[k, :, middle] + (water_ref[k, :, middle] - base_ref[k, :, middle])
        p0_ref[k, :, cols:] = water - base_ref[k, :, cols:]

    masks = [(ref > 0.0).astype(f32) for ref in (ks_ref[0, :, start], ks_ref[0, :, end], ks_side[0])]

    def y_faces(k, state):
        first = (ext_ref[k, :, start], cond_ref[k, :, start], deriv_ref[k, :, start])
        last = (ext_ref[k, :, end], cond_ref[k, :, end], deriv_ref[k, :, end])
        moved = [after(x, 1) for x in state]
        ahead = [jnp.where(is_last, after(x, 1), y) for x, y in zip(first, moved)]
        a, b, face = face_of(state, ahead)
        a_in, b_in, face_in = (jnp.where(is_last, x, 0.0) for x in face_of(last, moved))
        a_out, b_out, face_out = (before(x, 1) for x in (a, b, face))
        a_pre, b_pre, face_pre = (before(x, 1) for x in (a_in, b_in, face_in))
        gain = water_ref[k, :, end] - base_ref[k, :, end]
        p0_ref[k, :, end] = flow_ref[k, :, end] + face_in * masks[1] + gain
        diag_last[k] = mains[0][k, :, end] + a_in
        yp_last[k] = mains[3][k, :, end] + b_in * masks[1]
        gain = water_ref[k, :, start] - base_ref[k, :, start]
        p0_ref[k, :, start] = flow_ref[k, :, start] - jnp.where(is_first, face_out, 0.0) * masks[0] + gain
        diag_first[k] = mains[0][k, :, start] + jnp.where(is_first, b_out, 0.0)
        ym_first[k] = mains[4][k, :, start] + jnp.where(is_first, a_out, 0.0) * masks[0]
        a_pre, b_pre, face_pre = (
            jnp.where(is_first, x, y)
            for x, y in ((a_pre, a_out), (b_pre, b_out), (face_pre, face_out))
        )
        return face - face_pre, a + b_pre, b, a_pre

    def finish(k, value):
        p0_ref[k, :, cols:] = p0_ref[k, :, cols:] + value

    linearize(
        layers, lambda k: (ext_side[k], cond_side[k], deriv_side[k]), plain(store_side),
        y_faces, lambda value: value * masks[2], sides, finish,
    )

    def pieces(n, first_of, last_of):
        main, beside = mains[n], sides[n]
        return lambda k: jnp.concatenate(
            [first_of(main, k), main[k, :, middle], last_of(main, k), beside[k]], axis=1
        )

    def of_start(ref, k):
        return ref[k, :, start]

    def of_end(ref, k):
        return ref[k, :, end]

    coefs = [joined(main, beside) for main, beside in zip(mains, sides)]
    coefs[0] = pieces(0, lambda _, k: diag_first[k], lambda _, k: diag_last[k])
    coefs[3] = pieces(3, of_start, lambda _, k: yp_last[k])
    coefs[4] = pieces(4, lambda _, k: ym_first[k], of_end)
    powers((p0_ref, p1_ref, p2_ref), coefs, (rows, cols), gram_ref)


def second_kernel(
    arrived_ref, old_ref, ks_ref, steep_ref, cap_ref, old_side, ks_side, steep_side, cap_side,
    base_ref, q0_ref, q1_ref, q2_ref,
    part_ref, p0_ref, p1_ref, p2_ref, gram_ref, ext_ref, cond_ref, deriv_ref, store_ref, gain_ref, *coefs,
):
    layers = old_ref.shape[0]
    rows, cols = part_ref.shape[1:]
    x = solve(arrived_ref)
    near = lax.broadcasted_iota(jnp.int32, (HALO, cols + LANES), 0) < HALO // 2

    def folded(of):
        def get(k):
            value = of(k)
            ends = jnp.where(near, value[rows : rows + HALO], value[rows + HALO :])
            return jnp.concatenate([value[:rows], ends], axis=0)

        return get

    old_of, ks_of = folded(joined(old_ref, old_side)), folded(joined(ks_ref, ks_side))
    steep_of, cap_of = folded(joined(steep_ref, steep_side)), folded(joined(cap_ref, cap_side))
    base_of, *qs = (folded(plain(ref)) for ref in (base_ref, q0_ref, q1_ref, q2_ref))
    for k in range(layers):
        head = old_of(k)
        for value, q_of in zip(x, qs):
            head = head - value * q_of(k)
        cond, deriv, store, water = pointwise(head, ks_of(k), steep_of(k), cap_of(k))
        ext_ref[k] = head
        part_ref[k] = head[:rows, :cols]
        cond_ref[k] = cond
        deriv_ref[k] = deriv
        store_ref[k] = store
        gain_ref[k] = water - base_of(k)
    mask = (ks_of(0) > 0.0).astype(f32)

    def masked(value):
        own = value[:rows, cols:] * mask[:rows, cols:]
        top = jnp.concatenate([value[:rows, :cols], own], axis=1)
        return jnp.concatenate([top, value[rows:] * mask[rows:]], axis=0)

    def finish(k, value):
        p0_ref[k] = value + gain_ref[k]

    linearize(
        layers, lambda k: (ext_ref[k], cond_ref[k], deriv_ref[k]), plain(store_ref),
        lambda k, state: ring_faces(state, 1), masked, coefs, finish,
    )
    powers((p0_ref, p1_ref, p2_ref), [plain(ref) for ref in coefs], (rows, cols), gram_ref)


def last_kernel(
    arrived_ref, part_ref, q0_ref, q1_ref, q2_ref, inner_ref, piece_ref, head_ref, flux_ref
):
    layers, rows, cols = part_ref.shape
    middle = slice(LANES, cols - LANES)
    for n in range(flux_ref.shape[0]):
        flux_ref[n, :, middle] = inner_ref[n, :, middle]
    put_edges(flux_ref, piece_ref)
    x = solve(arrived_ref)
    for k in range(layers):
        own = (k, slice(0, rows), slice(0, cols))
        head_ref[k] = part_ref[k] - x[0] * q0_ref[own] - x[1] * q1_ref[own] - x[2] * q2_ref[own]


def shards(head_old, soil_type, soil_table, forcing, canopy, column_slot):
    layers, rows, cols = head_old.shape
    both = ("gx", "gy")
    devices = lax.axis_size("gx") * lax.axis_size("gy")
    tall, wide = rows + 2 * HALO, cols + LANES
    own, ext = ((layers, rows, cols), f32), ((layers, tall, wide), f32)
    gram_block = ((devices, 1, LANES), f32)

    def to_partner(x, axis, first):
        pairs = [(i, i + 1) for i in range(first, lax.axis_size(axis) - 1, 2)]
        return lax.ppermute(x, axis, pairs + [(j, i) for i, j in pairs])

    def exchange(to_near, to_far, axis):
        return to_partner(to_near, axis, 0), to_partner(to_far, axis, 1)

    def spread(x, axes):
        return lax.all_to_all(x, axes, split_axis=0, concat_axis=0, tiled=True)

    def edge(count):
        return (-(-count // 8) * 8, cols), f32

    send, to_near, to_far = call(
        pack_kernel,
        [((devices, 8, LANES), f32)] + [edge(2 * STATE_DEPTH * layers)] * 2,
        3,
        scratch=[
            pltpu.VMEM(canopy.shape, f32),
            pltpu.VMEM(head_old.shape, f32),
            pltpu.VMEM(soil_type.shape, jnp.int32),
            pltpu.SemaphoreType.DMA((3,)),
        ],
        in_specs=[pl.BlockSpec(memory_space=pl.ANY)] * 3,
        grant=63400000,
    )(canopy, head_old, soil_type)
    near = to_partner(to_near, "gx", 0)
    anywhere = pl.BlockSpec(memory_space=pl.ANY)
    send, to_far = pl.pallas_call(
        pass_kernel,
        out_shape=[jax.ShapeDtypeStruct(x.shape, x.dtype) for x in (send, to_far)],
        in_specs=[anywhere] * 2,
        out_specs=[anywhere] * 2,
        input_output_aliases={0: 0, 1: 1},
        compiler_params=pltpu.CompilerParams(vmem_limit_bytes=63400000),
        cost_estimate=pl.CostEstimate(flops=1000000000, bytes_accessed=1000000, transcendentals=0),
    )(send, to_far)
    arrived = spread(send, both)
    far = to_partner(to_far, "gx", 1)
    columns = (head_old, soil_type, forcing, column_slot)
    table = ((devices // 2, -(-layers // 2) + 1, 8, LANES), jnp.int32)
    some, piece, tab, factor = call(
        edge_source_kernel,
        [((layers, rows, 2 * LANES), f32), ((2, rows, 2 * LANES), f32), table, ((devices // 2, 8, LANES), f32)],
        6,
        in_specs=[smem] + [vmem] * 5,
    )(soil_table, arrived, *columns)
    to_near, to_far = call(strip_kernel, [((3, rows, LANES), f32)] * 2, 3)(head_old, soil_type, some)
    ynear, yfar = exchange(to_near, to_far, "gy")
    both_fluxes = ((2, rows, cols), f32)
    source, inner = call(inner_source_kernel, [own, both_fluxes], 8, in_specs=[smem] + [vmem] * 7)(
        soil_table, tab, factor, *columns, some
    )
    to_near, to_far = call(source_edge_kernel, [edge(SOURCE_DEPTH * layers + HALO + HALO // 2)] * 2, 3)(
        source, ynear, yfar
    )
    snear, sfar = exchange(to_near, to_far, "gx")
    main, side_block = ((layers, tall, cols), f32), ((layers, tall, LANES), f32)
    old, ks, steep, cap, cond, deriv, store, water = call(
        state_kernel, [main] * 8, 5, in_specs=[smem] + [vmem] * 4
    )(soil_table, head_old, soil_type, near, far)
    flow, *coefs = call(functools.partial(flow_kernel, rows=rows), [main] * 8, 5)(
        old, ks, cond, deriv, store
    )
    old_s, ks_s, steep_s, cap_s, base, p0, p1, p2, gram = call(
        first_kernel,
        [side_block] * 4 + [ext] * 4 + [gram_block],
        19,
        scratch=[pltpu.VMEM(side_block[0], f32)] * 14,
        in_specs=[smem] + [vmem] * 18,
    )(soil_table, source, snear, sfar, ynear, yfar, old, ks, cond, deriv, water, flow, *coefs)
    sums = spread(gram, both)
    part, q0, q1, q2, gram = call(
        second_kernel,
        [own] + [((layers, rows + HALO, wide), f32)] * 3 + [gram_block],
        13,
        scratch=[pltpu.VMEM((layers, rows + HALO, wide), f32)] * 12,
    )(sums, old, ks, steep, cap, old_s, ks_s, steep_s, cap_s, base, p0, p1, p2)
    sums = spread(gram, both)
    head, flux = call(last_kernel, [own, both_fluxes], 7)(sums, part, q0, q1, q2, inner, piece)
    return head, flux


def solution(mesh):
    return jax.shard_map(
        shards,
        mesh=mesh,
        in_specs=(
            P(None, "gx", "gy"),
            P(None, "gx", "gy"),
            P(),
            P(None, "gx", "gy"),
            P(None, ("gx", "gy")),
            P("gx", "gy"),
        ),
        out_specs=(P(None, "gx", "gy"), P(None, "gx", "gy")),
        check_vma=False,
    )
```
